32 devices in a mesh: ha: 8 (over z, core), ba: 4 (over y, x).
Axes of the slice: x: 2, y: 2, z: 4, core: 2. Of those that a mesh axis runs over, the one named last changes fastest.
Arguments:
- canvas: float32 [4, 64, 64, 512], P('ba', 'ha'), may hold values from -6 to 6
- image_id: int32 [4, 64, 64], P('ba'), may hold values from -1 to 35, as said below
- keep_first: int32 [4, 36], P('ba'), may hold values 0 or 1
- keep_second: int32 [4, 36], P('ba'), may hold values 0 or 1
- first_gain: float32 [512], replicated, may hold values from 0.1 to 1.9
- weight_in: float32 [512, 1024], replicated, may hold values from -0.25 to 0.25
- depth_kernel: float32 [49, 960], replicated, may hold values from -2.5 to 2.5
- gate_first: float32 [64, 128], replicated, may hold values from -0.75 to 0.75
- gate_second: float32 [128, 256], replicated, may hold values from -0.5 to 0.5
- gate_third: float32 [256, 512], replicated, may hold values from -0.375 to 0.375
- weight_out: float32 [512, 512], replicated, may hold values from -0.25 to 0.25
- scale_first: float32 [512], replicated, may hold values from 0.5 to 1.5
- second_gain: float32 [512], replicated, may hold values from 0.1 to 1.9
- weight_up: float32 [512, 2048], replicated, may hold values from -0.25 to 0.25
- weight_down: float32 [2048, 512], replicated, may hold values from -0.125 to 0.125
- scale_second: float32 [512], replicated, may hold values from 0.5 to 1.5
- cotangent: float32 [4, 64, 64, 512], P('ba', 'ha'), may hold values from -6 to 6
Outputs:
- output: float32 [4, 64, 64, 512], P('ba', 'ha')
- grad_canvas: float32 [4, 64, 64, 512], P('ba', 'ha')
- grad_first_gain: float32 [512], replicated
- grad_weight_in: float32 [512, 1024], P('ba', 'ha')
- grad_depth_kernel: float32 [49, 960], replicated
- grad_gate_first: float32 [64, 128], replicated
- grad_gate_second: float32 [128, 256], replicated
- grad_gate_third: float32 [256, 512], replicated
- grad_weight_out: float32 [512, 512], P('ba', 'ha')
- grad_scale_first: float32 [512], replicated
- grad_second_gain: float32 [512], replicated
- grad_weight_up: float32 [512, 2048], P('ba', 'ha')
- grad_weight_down: float32 [2048, 512], P('ba', 'ha')
- grad_scale_second: float32 [512], replicated
The draws below stay inside these ranges and needn't reach their ends.
Inputs may be any that keep to these rules, and one draw needn't show every extreme that they name: `image_id`: each canvas holds either one image on all its cells (number 0) or 36 images of 10 x 10 cells in a 6 x 6 arrangement, numbered 0 to 35 in row order, at a row and column offset of 0 to 4 cells, with -1 on the cells that no image covers. Canvas 0 holds one image, canvas 1 holds 36.
All inputs are finite; a program needn't handle non-finite values. No bound on the sum of `keep_first` or of `keep_second` on one device may be relied on, other than what follows from the above.
Results may differ from the reference program's by a relative error of at most 0.0003.
Values sent between devices are 32-bit elements; how exact they have to be, the bound alone decides.
No kernel may reach another device: no remote copies, remote signals or barrier semaphores. Data moves between devices by JAX's collectives and lax.ppermute only.
A program may use at most 320 MiB of HBM per device.

```python
import jax
import jax.numpy as jnp
from jax import lax

DIM = 512
FF = 2048
KERN = 7
HEIGHT = 64
SLOTS = 36
CANVASES = 4
MIX = 960


def draw_image_id(key, part):
    key = jax.random.fold_in(key, 11)
    kind_key, row_key, col_key = jax.random.split(key, 3)
    canvas_index = jnp.arange(CANVASES, dtype=jnp.int32)
    chosen = jax.random.randint(kind_key, (CANVASES,), 0, 4) == 0
    small = (chosen | (canvas_index == 1)) & (canvas_index != 0)
    offset_rows = jax.random.randint(row_key, (CANVASES, 1, 1), 0, 5)
    offset_cols = jax.random.randint(col_key, (CANVASES, 1, 1), 0, 5)
    cell_rows = jnp.arange(HEIGHT, dtype=jnp.int32)[None, :, None] - offset_rows
    cell_cols = jnp.arange(HEIGHT, dtype=jnp.int32)[None, None, :] - offset_cols
    inside = (cell_rows >= 0) & (cell_rows < 60) & (cell_cols >= 0) & (cell_cols < 60)
    tile = jnp.clip(cell_rows, 0, 59) // 10 * 6 + jnp.clip(cell_cols, 0, 59) // 10
    small_ids = jnp.where(inside, tile, -1)
    return jnp.where(small[:, None, None], small_ids, 0).astype(jnp.int32)


def with_ends(values, stream_key, least, largest):
    place = [jax.random.randint(jax.random.fold_in(stream_key, axis), (), 0, length) for axis, length in enumerate(values.shape)]
    widest = values.shape.index(max(values.shape))
    beside = place[:widest] + [(place[widest] + 1) % values.shape[widest]] + place[widest + 1:]
    return values.at[tuple(place)].set(least).at[tuple(beside)].set(largest)


def block_scale(key, shape, cuts, least, largest):
    def one(axis_at, shards_of):
        steps = jax.random.uniform(jax.random.fold_in(jax.random.fold_in(key, 6), axis_at), (shards_of,), jnp.float32, least / len(cuts), largest / len(cuts))
        return jnp.repeat(jnp.exp(steps), shape[axis_at] // shards_of).reshape((-1,) + (1,) * (len(shape) - axis_at - 1))

    factor_of = one(*cuts[0])
    for cut in cuts[1:]:
        factor_of = factor_of * one(*cut)
    return factor_of


def noise(own_key, extent, deviation, reach, pieces=(), kind=jnp.bfloat16):
    entries = deviation * jax.random.normal(own_key, extent, jnp.float32)
    if pieces:
        entries = entries * block_scale(own_key, extent, pieces, -0.22, 0.18)
    return jnp.clip(entries, -reach, reach).astype(kind)


def setup_inputs(seed: int = 0) -> dict:
    key_of = jax.random.split(jax.random.key(seed), 18)
    canvas = noise(key_of[0], (CANVASES, HEIGHT, HEIGHT, DIM), 1.0, 6.0, ((0, 4), (1, 8)), jnp.float32)
    image_id = draw_image_id(jax.random.fold_in(key_of[17], 71), 0)
    keep_first = with_ends((jax.random.randint(key_of[2], (CANVASES, SLOTS), 0, 5) < 4).astype(jnp.int32), jax.random.fold_in(key_of[2], 1), 0, 1)
    keep_second = with_ends((jax.random.randint(key_of[3], (CANVASES, SLOTS), 0, 5) < 4).astype(jnp.int32), jax.random.fold_in(key_of[3], 1), 0, 1)
    first_gain = jnp.clip(1.0 + 0.18 * jax.random.normal(key_of[4], (DIM,), jnp.float32), 0.1, 1.9)
    weight_in = noise(key_of[5], (DIM, 2 * DIM), DIM ** -0.5, 0.25, (), jnp.float32)
    depth_kernel = noise(key_of[6], (KERN * KERN, MIX), 5 ** -0.5, 2.5, (), jnp.float32)
    gate_first = noise(key_of[7], (DIM // 8, DIM // 4), (DIM // 8) ** -0.5, 0.75, (), jnp.float32)
    gate_second = noise(key_of[8], (DIM // 4, DIM // 2), (DIM // 4) ** -0.5, 0.5, (), jnp.float32)
    gate_third = noise(key_of[9], (DIM // 2, DIM), (DIM // 2) ** -0.5, 0.375, (), jnp.float32)
    weight_out = noise(key_of[10], (DIM, DIM), DIM ** -0.5, 0.25, (), jnp.float32)
    scale_first = jnp.clip(jax.random.uniform(key_of[11], (DIM,), jnp.float32, 0.5, 1.5), 0.5, 1.5)
    second_gain = jnp.clip(1.0 + 0.18 * jax.random.normal(key_of[12], (DIM,), jnp.float32), 0.1, 1.9)
    weight_up = noise(key_of[13], (DIM, FF), DIM ** -0.5, 0.25, (), jnp.float32)
    weight_down = noise(key_of[14], (FF, DIM), FF ** -0.5, 0.125, (), jnp.float32)
    scale_second = jnp.clip(jax.random.uniform(key_of[15], (DIM,), jnp.float32, 0.5, 1.5), 0.5, 1.5)
    cotangent = noise(key_of[16], (CANVASES, HEIGHT, HEIGHT, DIM), 1.0, 6.0, ((0, 4), (1, 8)), jnp.float32)
    return dict(canvas=canvas, image_id=image_id, keep_first=keep_first, keep_second=keep_second, first_gain=first_gain, weight_in=weight_in, depth_kernel=depth_kernel, gate_first=gate_first, gate_second=gate_second, gate_third=gate_third, weight_out=weight_out, scale_first=scale_first, second_gain=second_gain, weight_up=weight_up, weight_down=weight_down, scale_second=scale_second, cotangent=cotangent)


KEEP_RATE = 0.8
SPREAD = 1.0 / 3.0
EPSILON = 1e-06

def matmul(left, right):
    return jnp.dot(left, right, precision=lax.Precision.HIGHEST, preferred_element_type=jnp.float32)

def layer_norm(values, gain):
    centered = values - lax.optimization_barrier(jnp.mean(values, axis=-1, keepdims=True))
    variance = lax.optimization_barrier(jnp.mean(centered * centered, axis=-1, keepdims=True))
    return centered * lax.rsqrt(variance + EPSILON) * gain

def masked_depthwise(padded, padded_ids, own_ids, kernel, row_count, col_count):
    total = jnp.zeros(own_ids.shape + (padded.shape[-1],), jnp.float32)
    for tap_row in range(KERN):
        for tap_col in range(KERN):
            window = padded[..., tap_row:tap_row + row_count, tap_col:tap_col + col_count, :]
            same = padded_ids[..., tap_row:tap_row + row_count, tap_col:tap_col + col_count] == own_ids
            total = total + kernel[tap_row * KERN + tap_col] * window * same.astype(jnp.float32)[..., None]
    return total * SPREAD

def keep_lookup(ids, table):
    slots = jnp.arange(table.shape[-1], dtype=jnp.int32)
    hits = (ids[..., None] == slots).astype(jnp.float32)
    return lax.optimization_barrier(jnp.sum(hits * table, axis=-1)) / KEEP_RATE

def recursive_gates(gate_base, conv, gates, weight_out):
    width = gate_base.shape[-1]
    mixed = gate_base * conv[..., :width]
    start = width
    for level in range(len(gates)):
        width = gates[level].shape[1]
        mixed = matmul(mixed, gates[level]) * conv[..., start:start + width]
        start = start + width
    return matmul(mixed, weight_out)

def residual_tail(masked, branch, keep_one, keep_two, scale_first, second_gain, weight_up, weight_down, scale_second):
    middle = masked + keep_one[..., None] * scale_first * branch
    hidden = jax.nn.gelu(matmul(layer_norm(middle, second_gain), weight_up), approximate=False)
    return middle + keep_two[..., None] * scale_second * matmul(hidden, weight_down)

def canvas_forward(pixels, ids, keep_one, keep_two, params):
    first_gain, weight_in, depth_kernel, gate_first, gate_second, gate_third, weight_out, scale_first, second_gain, weight_up, weight_down, scale_second = params
    reach_rows = KERN // 2
    valid = (ids >= 0).astype(jnp.float32)[..., None]
    masked = pixels * valid
    joined = matmul(layer_norm(masked, first_gain), weight_in)
    split = weight_in.shape[1] - depth_kernel.shape[1]
    gate_base = joined[..., :split]
    padded = jnp.pad(joined[..., split:], ((reach_rows, reach_rows), (reach_rows, reach_rows), (0, 0)))
    padded_ids = jnp.pad(ids, reach_rows, constant_values=-1)
    conv_fn = jax.checkpoint(lambda padded_v, kernel_v: masked_depthwise(padded_v, padded_ids, ids, kernel_v, HEIGHT, HEIGHT))
    conv = conv_fn(padded, depth_kernel)
    branch = recursive_gates(gate_base, conv, (gate_first, gate_second, gate_third), weight_out)
    return residual_tail(masked, branch, keep_one, keep_two, scale_first, second_gain, weight_up, weight_down, scale_second)

def reference(canvas, image_id, keep_first, keep_second, first_gain, weight_in, depth_kernel, gate_first, gate_second, gate_third, weight_out, scale_first, second_gain, weight_up, weight_down, scale_second, cotangent):
    params = (first_gain, weight_in, depth_kernel, gate_first, gate_second, gate_third, weight_out, scale_first, second_gain, weight_up, weight_down, scale_second)

    def one_canvas(totals, items):
        pixels, ids, keep_a, keep_b, incoming = items
        keep_one = keep_lookup(ids, keep_a.astype(jnp.float32))
        keep_two = keep_lookup(ids, keep_b.astype(jnp.float32))

        def forward(pixels_v, params_v):
            return canvas_forward(pixels_v, ids, keep_one, keep_two, params_v)
        result, pull = jax.vjp(forward, pixels, params)
        grad_pixels, grad_params = pull(incoming)
        return (jax.tree.map(jnp.add, totals, grad_params), (result, grad_pixels))
    start = jax.tree.map(jnp.zeros_like, params)
    totals, outputs = lax.scan(one_canvas, start, (canvas, image_id, keep_first, keep_second, cotangent))
    return (outputs[0], outputs[1], totals[0], totals[1], totals[2], totals[3], totals[4], totals[5], totals[6], totals[7], totals[8], totals[9], totals[10], totals[11])
```

```python
import functools

import jax
import jax.numpy as jnp
from jax import lax
from jax.experimental import pallas as pl
from jax.experimental.pallas import tpu as pltpu
from jax.sharding import PartitionSpec as P

KERN = 7
REACH = KERN // 2
KEEP_RATE = 0.8
SPREAD = 1.0 / 3.0
EPSILON = 1e-06
LANES = 128
EDGE = 8
VMEM_BYTES = 56 << 20
F32 = jnp.float32
BF16 = jnp.bfloat16
INV_SQRT_2 = 0.7071067811865476
INV_SQRT_2PI = 0.3989422804014327
NN = (((1,), (0,)), ((), ()))
NT = (((1,), (1,)), ((), ()))
TN = (((0,), (0,)), ((), ()))


def halves(x):
    high = x.astype(BF16)
    return high, (x - high.astype(F32)).astype(BF16)


def dot_once(left, right, dims):
    return lax.dot_general(left, right, dims, preferred_element_type=F32)


def dot_pairs(left, right, dims=NN):
    return dot_once(left[0], right[0], dims) + (
        dot_once(left[0], right[1], dims) + dot_once(left[1], right[0], dims)
    )


def dot(left, right, dims=NN):
    return dot_pairs(halves(left), halves(right), dims)


def normalized(values):
    centered = values - jnp.mean(values, axis=-1, keepdims=True)
    scale = lax.rsqrt(jnp.mean(centered * centered, axis=-1, keepdims=True) + EPSILON)
    return centered * scale, scale


def norm_backward(grad_hat, hat, scale):
    return scale * (
        grad_hat
        - jnp.mean(grad_hat, axis=-1, keepdims=True)
        - hat * jnp.mean(grad_hat * hat, axis=-1, keepdims=True)
    )


def params():
    return pltpu.CompilerParams(vmem_limit_bytes=VMEM_BYTES)


def lasting(microseconds):
    return pl.CostEstimate(flops=int(microseconds * 1.1e9), bytes_accessed=0, transcendentals=0)


def whole(shape):
    return pl.BlockSpec(shape, lambda *_: (0,) * len(shape))


def shape_of(*shape):
    return jax.ShapeDtypeStruct(shape, F32)


def masks_kernel(
    first_row, keep_one, keep_two, ids_ref, middle_ref, valid_ref, one_ref, two_ref, row_ref, col_ref, *, rows, height
):
    cols = ids_ref.shape[1]
    slots = keep_one.shape[1]
    start = first_row[0]
    ids = ids_ref[pl.ds(start, rows + 2 * REACH), :]
    turned = jnp.concatenate([ids, jnp.full((-ids.shape[0] % 8, cols), -1, jnp.int32)], axis=0).T
    own = turned[:, REACH : REACH + rows]
    one = jnp.zeros(own.shape, F32)
    two = jnp.zeros(own.shape, F32)
    for slot in range(slots):
        hit = own == slot
        one = jnp.where(hit, keep_one[0, slot].astype(F32) / KEEP_RATE, one)
        two = jnp.where(hit, keep_two[0, slot].astype(F32) / KEEP_RATE, two)
    valid = (turned >= 0).astype(F32)
    for r in range(rows + 2 * REACH):
        valid_ref[r] = jnp.broadcast_to(valid[:, r : r + 1], (cols, LANES))
    for r in range(rows):
        one_ref[r] = jnp.broadcast_to(one[:, r : r + 1], (cols, LANES))
        two_ref[r] = jnp.broadcast_to(two[:, r : r + 1], (cols, LANES))
    tall = middle_ref[...]
    wide_ids = jnp.broadcast_to(tall, (cols, LANES))
    column = lax.broadcasted_iota(jnp.int32, (cols, LANES), 0)
    for b in range(KERN):
        shift = b - REACH
        moved = pltpu.roll(wide_ids, (-shift) % cols, 0)
        inside = (column + shift >= 0) & (column + shift < cols)
        same = (moved == wide_ids) & inside
        col_ref[b] = same.astype(F32).reshape(cols // 8, 8, LANES)
    across = ids_ref[pl.ds(start, rows + 2 * REACH), cols // 2 : cols // 2 + 1]
    place = start - REACH + lax.broadcasted_iota(jnp.int32, across.shape, 0)
    across = jnp.where((place >= 0) & (place < height), across, -2)
    lane = lax.broadcasted_iota(jnp.int32, (rows, LANES), 1)
    mask = jnp.zeros((rows, LANES), F32)
    for a in range(KERN):
        same = (across[a : a + rows] == across[REACH : REACH + rows]).astype(F32)
        mask = jnp.where(lane == a + 1, same, mask)
    row_ref[...] = mask


def masks(first_row, keep_one, keep_two, ids, rows):
    cols = ids.shape[1]
    padded = jnp.pad(ids, ((REACH, 16 - REACH), (0, 0)), constant_values=-1)
    middle = ids[ids.shape[0] // 2][:, None]
    smem = pl.BlockSpec(memory_space=pltpu.SMEM)
    return pl.pallas_call(
        functools.partial(masks_kernel, rows=rows, height=ids.shape[0]),
        in_specs=[smem, smem, smem, whole(padded.shape), whole(middle.shape)],
        out_shape=[
            shape_of(rows + 2 * REACH, cols, LANES),
            shape_of(rows, cols, LANES),
            shape_of(rows, cols, LANES),
            shape_of(rows, LANES),
            shape_of(KERN, cols // 8, 8, LANES),
        ],
        compiler_params=params(),
        cost_estimate=lasting(2),
    )(first_row, keep_one, keep_two, padded, middle)


def head_kernel(canvas_ref, valid_ref, gain_ref, weight_ref, out_ref, high, low):
    @pl.when(pl.program_id(0) == 0)
    def _():
        hat, _ = normalized(canvas_ref[...] * valid_ref[:, :1])
        high[...], low[...] = halves(hat * gain_ref[...])

    joined = dot_pairs((high[...], low[...]), halves(weight_ref[...]))
    for k in range(out_ref.shape[0]):
        out_ref[k] = joined[:, k * LANES : (k + 1) * LANES]


def head_forward(canvas, valid, gain, weight):
    cells, dim = canvas.shape
    blocks = weight.shape[1] // LANES
    return pl.pallas_call(
        head_kernel,
        grid=(blocks // 2,),
        in_specs=[
            whole((cells, dim)),
            whole((cells, LANES)),
            whole((1, dim)),
            pl.BlockSpec((dim, 2 * LANES), lambda i: (0, i)),
        ],
        out_specs=pl.BlockSpec((2, cells, LANES), lambda i: (i, 0, 0)),
        out_shape=shape_of(blocks, cells, LANES),
        scratch_shapes=[pltpu.VMEM((cells, dim), BF16), pltpu.VMEM((cells, dim), BF16)],
        compiler_params=params(),
        cost_estimate=lasting(4),
    )(canvas, valid, gain, weight)


def fill_shifted(above_ref, own_ref, below_ref, col_ref, flat, shifted, rows_ext, cols):
    groups = cols // 8
    reach = above_ref.shape[1]
    cells = own_ref.shape[1]
    flat[:EDGE] = jnp.zeros((EDGE, LANES), F32)
    flat[EDGE : EDGE + reach] = above_ref[0]
    flat[EDGE + reach : EDGE + reach + cells] = own_ref[0]
    flat[EDGE + reach + cells : EDGE + 2 * reach + cells] = below_ref[0]
    flat[EDGE + 2 * reach + cells :] = jnp.zeros((EDGE, LANES), F32)
    for b in range(KERN):
        mask = col_ref[b]

        def some(h, _, b=b, mask=mask):
            for k in range(2):
                r = 2 * h + k
                start = pl.multiple_of(r * cols, cols) + (EDGE + b - REACH)
                x = flat[pl.ds(start, cols), :].reshape(groups, 8, LANES)
                shifted[b, r] = x if b == REACH else x * mask
            return 0

        lax.fori_loop(0, rows_ext // 2, some, 0)


def conv_kernel(
    row_mask, above_ref, own_ref, below_ref, kern_ref, col_ref, out_ref, flat, shifted, wide, *, rows, cols
):
    groups = cols // 8
    fill_shifted(above_ref, own_ref, below_ref, col_ref, flat, shifted, rows + 2 * REACH, cols)
    for t in range(KERN):
        wide[t] = jnp.zeros((8, LANES), F32)
        wide[KERN * (KERN + 1) + t] = jnp.zeros((8, LANES), F32)
    for t in range(KERN * KERN):
        wide[KERN + t] = jnp.broadcast_to(kern_ref[t : t + 1, :] * SPREAD, (8, LANES))

    def pair(h, _):
        r = 2 * h

        def step(i, totals):
            first, second = totals
            mask_first = row_mask[r, i + 1]
            mask_second = row_mask[r + 1, i]
            for b in range(KERN):
                x = shifted[b, r + i]
                first = first + (wide[(i + 1) * KERN + b] * mask_first)[None] * x
                second = second + (wide[i * KERN + b] * mask_second)[None] * x
            return first, second

        zero = jnp.zeros((groups, 8, LANES), F32)
        first, second = lax.fori_loop(0, KERN + 1, step, (zero, zero))
        out_ref[pl.ds(pl.multiple_of(r * cols, cols), cols), :] = first.reshape(cols, LANES)
        out_ref[pl.ds(pl.multiple_of((r + 1) * cols, cols), cols), :] = second.reshape(cols, LANES)
        return 0

    lax.fori_loop(0, rows // 2, pair, 0)


def conv_specs(reach, cells):
    return [
        pl.BlockSpec(memory_space=pltpu.SMEM),
        pl.BlockSpec((1, reach, LANES), lambda i: (i, 0, 0)),
        pl.BlockSpec((1, cells, LANES), lambda i: (i, 0, 0)),
        pl.BlockSpec((1, reach, LANES), lambda i: (i, 0, 0)),
    ]


def conv_scratch(rows, cols):
    cells_ext = (rows + 2 * REACH) * cols
    return [
        pltpu.VMEM((cells_ext + 2 * EDGE, LANES), F32),
        pltpu.VMEM((KERN, rows + 2 * REACH, cols // 8, 8, LANES), F32),
    ]


def conv_forward(row_mask, above, own, below, kern, col_mask, rows, cols):
    blocks = own.shape[0]
    taps = KERN * KERN
    return pl.pallas_call(
        functools.partial(conv_kernel, rows=rows, cols=cols),
        grid=(blocks,),
        in_specs=conv_specs(REACH * cols, rows * cols)
        + [pl.BlockSpec((taps, LANES), lambda i: (0, i)), whole((KERN, cols // 8, 8, LANES))],
        out_specs=pl.BlockSpec((rows * cols, LANES), lambda i: (0, i)),
        out_shape=shape_of(rows * cols, blocks * LANES),
        scratch_shapes=conv_scratch(rows, cols) + [pltpu.VMEM((KERN * (KERN + 2), 8, LANES), F32)],
        compiler_params=params(),
        cost_estimate=lasting(16),
    )(row_mask, above, own, below, kern, col_mask)


def conv_grad_kernel(
    row_mask, above_ref, own_ref, below_ref, mix_ref, kern_ref, col_ref, out_ref, dk_ref, flat, shifted, wide, dk,
    *, rows, cols,
):
    groups = cols // 8
    taps = KERN * KERN
    fill_shifted(above_ref, own_ref, below_ref, col_ref, flat, shifted, rows + 2 * REACH, cols)
    for t in range(taps):
        wide[t] = jnp.broadcast_to(kern_ref[taps - 1 - t : taps - t, :] * SPREAD, (8, LANES))
        dk[t] = jnp.zeros((8, LANES), F32)

    def one(r, _):
        mix = mix_ref[0, pl.ds(pl.multiple_of(r * cols, cols), cols), :].reshape(groups, 8, LANES)

        def step(i, total):
            mask = row_mask[r, i + 1]
            for b in range(KERN):
                x = shifted[b, r + i]
                total = total + (wide[i * KERN + b] * mask)[None] * x
                dk[i * KERN + b] += jnp.sum(mix * x, axis=0) * mask
            return total

        total = lax.fori_loop(0, KERN, step, jnp.zeros((groups, 8, LANES), F32))
        out_ref[pl.ds(pl.multiple_of(r * cols, cols), cols), :] = total.reshape(cols, LANES)
        return 0

    lax.fori_loop(0, rows, one, 0)
    for t in range(taps):
        dk_ref[0, taps - 1 - t : taps - t, :] = jnp.sum(dk[t], axis=0, keepdims=True) * SPREAD
    dk_ref[0, taps:, :] = jnp.zeros((dk_ref.shape[1] - taps, LANES), F32)


def conv_backward(row_mask, above, own, below, mix, kern, col_mask, rows, cols):
    blocks = own.shape[0]
    taps = KERN * KERN
    tall = -(-taps // 8) * 8
    return pl.pallas_call(
        functools.partial(conv_grad_kernel, rows=rows, cols=cols),
        grid=(blocks,),
        in_specs=conv_specs(REACH * cols, rows * cols)
        + [
            pl.BlockSpec((1, rows * cols, LANES), lambda i: (i, 0, 0)),
            pl.BlockSpec((taps, LANES), lambda i: (0, i)),
            whole((KERN, cols // 8, 8, LANES)),
        ],
        out_specs=[
            pl.BlockSpec((rows * cols, LANES), lambda i: (0, i)),
            pl.BlockSpec((1, tall, LANES), lambda i: (i, 0, 0)),
        ],
        out_shape=[shape_of(rows * cols, blocks * LANES), shape_of(blocks, tall, LANES)],
        scratch_shapes=conv_scratch(rows, cols)
        + [pltpu.VMEM((taps, 8, LANES), F32), pltpu.VMEM((taps, 8, LANES), F32)],
        compiler_params=params(),
        cost_estimate=lasting(24),
    )(row_mask, above, own, below, mix, kern, col_mask)


def gates_kernel(
    conv_ref, canvas_ref, valid_ref, keep_ref, scale_ref, one_ref, two_ref, three_ref, out_ref,
    middle_ref, mixed_ref, mapped_ref,
):
    split = one_ref.shape[0]
    mixed = conv_ref[:, :split] * conv_ref[:, split : 2 * split]
    mixed_ref[:, :split] = mixed
    mixed_ref[:, split : 2 * split] = jnp.zeros_like(mixed)
    start = 2 * split
    for ref in (one_ref, two_ref, three_ref):
        width = ref.shape[1]
        mapped = dot(mixed, ref[...])
        mapped_ref[:, start - 2 * split : start - 2 * split + width] = mapped
        mixed = mapped * conv_ref[:, start : start + width]
        mixed_ref[:, start : start + width] = mixed
        start += width
    branch = dot(mixed, out_ref[...])
    middle_ref[...] = canvas_ref[...] * valid_ref[:, :1] + keep_ref[:, :1] * scale_ref[...] * branch


def row_blocks(cells, width, tile):
    return pl.BlockSpec((tile, width), lambda i: (i, 0))


def gates_forward(conv, canvas, valid, keep, scale, gates, weight_out, tile=256):
    cells, dim = canvas.shape
    wide = conv.shape[1]
    narrow = wide - 2 * gates[0].shape[0]
    return pl.pallas_call(
        gates_kernel,
        grid=(cells // tile,),
        in_specs=[
            row_blocks(cells, wide, tile),
            row_blocks(cells, dim, tile),
            row_blocks(cells, LANES, tile),
            row_blocks(cells, LANES, tile),
            whole(scale.shape),
        ]
        + [whole(g.shape) for g in gates]
        + [whole(weight_out.shape)],
        out_specs=[row_blocks(cells, dim, tile), row_blocks(cells, wide, tile), row_blocks(cells, narrow, tile)],
        out_shape=[shape_of(cells, dim), shape_of(cells, wide), shape_of(cells, narrow)],
        compiler_params=params(),
        cost_estimate=lasting(6),
    )(conv, canvas, valid, keep, scale, *gates, weight_out)


def gates_grad_kernel(
    grad_ref, conv_ref, mapped_ref, keep_ref, scale_ref, one_ref, two_ref, three_ref, out_ref, dconv_ref, dmapped_ref
):
    split = one_ref.shape[0]
    grad = dot(keep_ref[:, :1] * grad_ref[...] * scale_ref[...], out_ref[...], NT)
    start = conv_ref.shape[1]
    for ref in (three_ref, two_ref, one_ref):
        width = ref.shape[1]
        start -= width
        dconv = grad * mapped_ref[:, start - 2 * split : start - 2 * split + width]
        for k in range(width // LANES):
            dconv_ref[start // LANES + k] = dconv[:, k * LANES : (k + 1) * LANES]
        grad_mapped = grad * conv_ref[:, start : start + width]
        dmapped_ref[:, start - 2 * split : start - 2 * split + width] = grad_mapped
        grad = dot(grad_mapped, ref[...], NT)
    dconv_ref[0, :, split : 2 * split] = grad * conv_ref[:, :split]
    dconv_ref[0, :, :split] = grad * conv_ref[:, split : 2 * split]


def gates_backward(grad, conv, mapped, keep, scale, gates, weight_out, tile=256):
    cells, dim = grad.shape
    wide = conv.shape[1]
    narrow = mapped.shape[1]
    return pl.pallas_call(
        gates_grad_kernel,
        grid=(cells // tile,),
        in_specs=[
            row_blocks(cells, dim, tile),
            row_blocks(cells, wide, tile),
            row_blocks(cells, narrow, tile),
            row_blocks(cells, LANES, tile),
            whole(scale.shape),
        ]
        + [whole(g.shape) for g in gates]
        + [whole(weight_out.shape)],
        out_specs=[
            pl.BlockSpec((wide // LANES, tile, LANES), lambda i: (0, i, 0)),
            row_blocks(cells, narrow, tile),
        ],
        out_shape=[shape_of(wide // LANES, cells, LANES), shape_of(cells, narrow)],
        compiler_params=params(),
        cost_estimate=lasting(5),
    )(grad, conv, mapped, keep, scale, *gates, weight_out)


def share(core, first, second, kept_ref, sent_ref, place):
    mine = core == 0
    kept_ref[place] = jnp.where(mine, first, second)
    sent_ref[place] = jnp.where(mine, second, first)


def gates_weight_kernel(
    core_ref, grad_ref, keep_ref, scale_ref, out_ref, mixed_ref, dmapped_ref, dgain_ref, dscale_ref,
    kept_ref, sent_ref, packed_ref, *, widths,
):
    split = widths[0]
    kept = keep_ref[:, :1] * grad_ref[...]
    start = 2 * split
    source = 0
    row = 0
    for level in range(len(widths) - 1):
        tall, width = widths[level], widths[level + 1]
        part = dot(
            mixed_ref[:, source : source + tall], dmapped_ref[:, start - 2 * split : start - 2 * split + width], TN
        )
        for k in range(width // LANES):
            packed_ref[row : row + tall] = part[:, k * LANES : (k + 1) * LANES]
            row += tall
        source = start
        start += width
    crossed = dot(mixed_ref[:, source:], kept, TN)
    dscale = jnp.sum(crossed * out_ref[...], axis=0, keepdims=True)
    packed_ref[row:] = jnp.zeros((packed_ref.shape[0] - row, LANES), F32)
    for vector in (dscale, dgain_ref[...], dscale_ref[...]):
        for k in range(vector.shape[1] // LANES):
            packed_ref[row : row + 1] = vector[:, k * LANES : (k + 1) * LANES]
            row += 1
    turned = (crossed * scale_ref[...]).T
    groups, parts, tall, width = kept_ref.shape
    for z in range(groups):
        for p in range(parts):
            base = 2 * z * tall
            columns = slice(p * width, (p + 1) * width)
            share(
                core_ref[0],
                turned[base : base + tall, columns],
                turned[base + tall : base + 2 * tall, columns],
                kept_ref,
                sent_ref,
                (z, p),
            )


def gates_weights(core, grad, keep, scale, weight_out, mixed, dmapped, dgain, dscale, widths, count_ha, count_ba):
    dim, width = weight_out.shape
    chunks = shape_of(count_ha // 2, count_ba, width // count_ha, dim // count_ba)
    rows = sum(a * b for a, b in zip(widths[:-1], widths[1:])) // LANES + 3 * width // LANES
    rows = -(-rows // 16) * 16
    return pl.pallas_call(
        functools.partial(gates_weight_kernel, widths=widths),
        in_specs=[pl.BlockSpec(memory_space=pltpu.SMEM)] + [pl.BlockSpec(memory_space=pltpu.VMEM)] * 8,
        out_shape=[chunks, chunks, shape_of(rows, LANES)],
        compiler_params=params(),
        cost_estimate=lasting(5),
    )(core, grad, keep, scale, weight_out, mixed, dmapped, dgain, dscale)


def share_columns(core, grad, kept_ref, sent_ref):
    groups, parts, tall, width = kept_ref.shape
    for z in range(groups):
        first = grad[:, 2 * z * width : (2 * z + 1) * width].reshape(parts, tall, width)
        second = grad[:, (2 * z + 1) * width : (2 * z + 2) * width].reshape(parts, tall, width)
        share(core, first, second, kept_ref, sent_ref, z)


def ffn_kernel(
    core_ref, middle_ref, cot_ref, keep_ref, gain_ref, scale_ref, up_ref, down_ref,
    out_ref, dmiddle_ref, up_kept_ref, up_sent_ref, down_kept_ref, down_sent_ref, dgain_ref, dscale_ref,
    n_high, n_low, nt_high, nt_low, y_high, y_low, yt_high, yt_low, result, dnorm,
):
    step = pl.program_id(0)

    @pl.when(step == 0)
    def _():
        hat, _ = normalized(middle_ref[...])
        normed = hat * gain_ref[...]
        n_high[...], n_low[...] = halves(normed)
        nt_high[...], nt_low[...] = halves(normed.T)
        grad = keep_ref[:, :1] * scale_ref[...] * cot_ref[...]
        y_high[...], y_low[...] = halves(grad)
        yt_high[...], yt_low[...] = halves(grad.T)
        result[...] = jnp.zeros_like(result)
        dnorm[...] = jnp.zeros_like(dnorm)

    up = halves(up_ref[...])
    down = halves(down_ref[...])
    pre = dot_pairs((n_high[...], n_low[...]), up)
    cdf = 0.5 + 0.5 * lax.erf(pre * INV_SQRT_2)
    slope = cdf + pre * (INV_SQRT_2PI * jnp.exp(-0.5 * pre * pre))
    hidden = halves(pre * cdf)
    result[...] += dot_pairs(hidden, down)
    grad_pre = halves(dot_pairs((y_high[...], y_low[...]), down, NT) * slope)
    ddown = dot_pairs((yt_high[...], yt_low[...]), hidden)
    groups, parts, tall, width = down_kept_ref.shape
    for z in range(groups):
        for p in range(parts):
            base = 2 * z * tall
            columns = slice(p * width, (p + 1) * width)
            share(
                core_ref[0],
                ddown[base : base + tall, columns],
                ddown[base + tall : base + 2 * tall, columns],
                down_kept_ref,
                down_sent_ref,
                (z, p),
            )
    share_columns(
        core_ref[0], dot_pairs((nt_high[...], nt_low[...]), grad_pre), up_kept_ref, up_sent_ref
    )
    dnorm[...] += dot_pairs(grad_pre, up, NT)

    @pl.when(step == pl.num_programs(0) - 1)
    def _():
        hat, scale = normalized(middle_ref[...])
        kept = keep_ref[:, :1] * result[...]
        out_ref[...] = middle_ref[...] + scale_ref[...] * kept
        dscale_ref[...] = jnp.sum(cot_ref[...] * kept, axis=0, keepdims=True)
        dgain_ref[...] = jnp.sum(dnorm[...] * hat, axis=0, keepdims=True)
        dmiddle_ref[...] = cot_ref[...] + norm_backward(dnorm[...] * gain_ref[...], hat, scale)


def ffn(core, middle, cot, keep, gain, scale, weight_up, weight_down, count_ha, count_ba, chunk=512):
    cells, dim = middle.shape
    hidden = weight_up.shape[1]
    pair = [pltpu.VMEM((cells, dim), BF16)] * 2
    pair_turned = [pltpu.VMEM((dim, cells), BF16)] * 2
    up_wide, down_wide = hidden // count_ha, hidden // count_ba
    up = pl.BlockSpec((chunk // (2 * up_wide), count_ba, dim // count_ba, up_wide), lambda i: (i, 0, 0, 0))
    down = pl.BlockSpec((count_ha // 2, chunk // down_wide, dim // count_ha, down_wide), lambda i: (0, i, 0, 0))
    up_shape = shape_of(count_ha // 2, count_ba, dim // count_ba, up_wide)
    down_shape = shape_of(count_ha // 2, count_ba, dim // count_ha, down_wide)
    return pl.pallas_call(
        ffn_kernel,
        grid=(hidden // chunk,),
        in_specs=[
            pl.BlockSpec(memory_space=pltpu.SMEM),
            whole((cells, dim)),
            whole((cells, dim)),
            whole((cells, LANES)),
            whole((1, dim)),
            whole((1, dim)),
            pl.BlockSpec((dim, chunk), lambda i: (0, i)),
            pl.BlockSpec((chunk, dim), lambda i: (i, 0)),
        ],
        out_specs=[whole((cells, dim)), whole((cells, dim)), up, up, down, down, whole((1, dim)), whole((1, dim))],
        out_shape=[
            shape_of(cells, dim),
            shape_of(cells, dim),
            up_shape,
            up_shape,
            down_shape,
            down_shape,
            shape_of(1, dim),
            shape_of(1, dim),
        ],
        scratch_shapes=pair
        + pair_turned
        + pair
        + pair_turned
        + [pltpu.VMEM((cells, dim), F32), pltpu.VMEM((cells, dim), F32)],
        compiler_params=params(),
        cost_estimate=lasting(30),
    )(core, middle, cot, keep, gain, scale, weight_up, weight_down)


def head_grad_kernel(
    core_ref, canvas_ref, valid_ref, gain_ref, dmiddle_ref, djoined_ref, weight_ref,
    dcanvas_ref, kept_ref, sent_ref, dgain_ref, nt_high, nt_low, dnorm,
):
    step = pl.program_id(0)

    @pl.when(step == 0)
    def _():
        hat, _ = normalized(canvas_ref[...] * valid_ref[:, :1])
        nt_high[...], nt_low[...] = halves((hat * gain_ref[...]).T)
        dnorm[...] = jnp.zeros_like(dnorm)

    grad = halves(djoined_ref[...])
    share_columns(core_ref[0], dot_pairs((nt_high[...], nt_low[...]), grad), kept_ref, sent_ref)
    dnorm[...] += dot_pairs(grad, halves(weight_ref[...]), NT)

    @pl.when(step == pl.num_programs(0) - 1)
    def _():
        hat, scale = normalized(canvas_ref[...] * valid_ref[:, :1])
        dgain = jnp.sum(dnorm[...] * hat, axis=0, keepdims=True)
        dgain_ref[...] = jnp.zeros_like(dgain_ref)
        for k in range(dgain.shape[1] // LANES):
            dgain_ref[k : k + 1] = dgain[:, k * LANES : (k + 1) * LANES]
        inner = dmiddle_ref[...] + norm_backward(dnorm[...] * gain_ref[...], hat, scale)
        dcanvas_ref[...] = inner * valid_ref[:, :1]


def head_backward(core, canvas, valid, gain, dmiddle, djoined, weight, count_ha, count_ba, chunk=256):
    cells, dim = canvas.shape
    width = weight.shape[1]
    own = width // count_ha
    chunks = shape_of(count_ha // 2, count_ba, dim // count_ba, own)
    chunk_spec = pl.BlockSpec((chunk // (2 * own), count_ba, dim // count_ba, own), lambda i: (i, 0, 0, 0))
    return pl.pallas_call(
        head_grad_kernel,
        grid=(width // chunk,),
        in_specs=[
            pl.BlockSpec(memory_space=pltpu.SMEM),
            whole((cells, dim)),
            whole((cells, LANES)),
            whole((1, dim)),
            whole((cells, dim)),
            pl.BlockSpec((cells, chunk), lambda i: (0, i)),
            pl.BlockSpec((dim, chunk), lambda i: (0, i)),
        ],
        out_specs=[whole((cells, dim)), chunk_spec, chunk_spec, whole((16, LANES))],
        out_shape=[shape_of(cells, dim), chunks, chunks, shape_of(16, LANES)],
        scratch_shapes=[
            pltpu.VMEM((dim, cells), BF16),
            pltpu.VMEM((dim, cells), BF16),
            pltpu.VMEM((cells, dim), F32),
        ],
        compiler_params=params(),
        cost_estimate=lasting(9),
    )(core, canvas, valid, gain, dmiddle, djoined, weight)


def exchange(values, axis, bit):
    return lax.ppermute(values, axis, [(i, i ^ bit) for i in range(lax.axis_size(axis))])


def picked(parts, index, axis):
    return [lax.dynamic_index_in_dim(part, index, axis, keepdims=False) for part in parts]


def total(parts):
    result = parts[0]
    for part in parts[1:]:
        result = result + part
    return result


def reduce_chunks(parts, order):
    bits = len(order)
    z = lax.axis_index("ha") // 2
    ba = lax.axis_index("ba")
    parts = [part.reshape(part.shape[:1] + (2,) * bits + part.shape[2:]) for part in parts]
    left = list(reversed(range(bits)))
    for bit in order:
        axis = 1 + left.index(bit)
        left.remove(bit)
        mine = (ba >> bit) & 1
        got = exchange(total(picked(parts, 1 - mine, axis)), "ba", 1 << bit)
        parts = picked(parts, mine, axis) + [got]
    got = [
        exchange(total(picked(parts, z ^ step, 0)), "ha", 2 * step) for step in range(1, lax.axis_size("ha") // 2)
    ]
    return total(picked(parts, z, 0) + got)


def reduce_whole(rows):
    half = rows.shape[0] // 2
    core = lax.axis_index("ha") % 2
    halves_of = rows.reshape(2, half, rows.shape[1])
    mine = total(picked([halves_of], core, 0) + [exchange(picked([halves_of], 1 - core, 0)[0], "ha", 1)])
    for axis, first in (("ba", 1), ("ha", 2)):
        bit = first
        while bit < lax.axis_size(axis):
            mine = mine + exchange(mine, axis, bit)
            bit *= 2
    other = exchange(mine, "ha", 1)
    low = jnp.where(core == 0, mine, other)
    high = jnp.where(core == 0, other, mine)
    return jnp.concatenate([low, high], axis=0)


def from_blocks(rows, tall):
    return jnp.concatenate([rows[i : i + tall] for i in range(0, rows.shape[0], tall)], axis=1)


def neighbour_rows(rows, width, dim):
    count = lax.axis_size("ha")
    up = [(i, i + 1) for i in range(count - 1)]
    down = [(i + 1, i) for i in range(count - 1)]
    tail = lax.slice_in_dim(rows, rows.shape[dim] - width, rows.shape[dim], axis=dim)
    head = lax.slice_in_dim(rows, 0, width, axis=dim)
    return lax.ppermute(tail, "ha", up), lax.ppermute(head, "ha", down)


def shards(
    canvas,
    image_id,
    keep_first,
    keep_second,
    first_gain,
    weight_in,
    depth_kernel,
    gate_first,
    gate_second,
    gate_third,
    weight_out,
    scale_first,
    second_gain,
    weight_up,
    weight_down,
    scale_second,
    cotangent,
):
    _, rows, cols, dim = canvas.shape
    cells = rows * cols
    taps = KERN * KERN
    reach = REACH * cols
    split = weight_in.shape[1] - depth_kernel.shape[1]
    count_ha, count_ba = lax.axis_size("ha"), lax.axis_size("ba")
    core = (lax.axis_index("ha") % 2)[None]
    first_row = (lax.axis_index("ha") * rows)[None]
    own = canvas.reshape(cells, dim)
    above, below = neighbour_rows(own, reach, 0)
    valid_ext, keep_one, keep_two, row_mask, col_mask = masks(first_row, keep_first, keep_second, image_id[0], rows)
    valid_ext = valid_ext.reshape(-1, LANES)
    valid = valid_ext[reach : reach + cells]
    keep_one = keep_one.reshape(cells, LANES)
    keep_two = keep_two.reshape(cells, LANES)
    middle_tap = (jnp.arange(taps) == taps // 2).astype(F32) / SPREAD
    kern = jnp.concatenate([jnp.broadcast_to(middle_tap[:, None], (taps, split)), depth_kernel], axis=1)
    gates = (gate_first, gate_second, gate_third)
    widths = (split,) + tuple(gate.shape[1] for gate in gates)

    joined = head_forward(own, valid, first_gain[None], weight_in)
    joined_above = head_forward(above, valid_ext[:reach], first_gain[None], weight_in)
    joined_below = head_forward(below, valid_ext[reach + cells :], first_gain[None], weight_in)
    conv = conv_forward(row_mask, joined_above, joined, joined_below, kern, col_mask, rows, cols)
    middle, mixed, mapped = gates_forward(conv, own, valid, keep_one, scale_first[None], gates, weight_out)
    output, dmiddle, up_kept, up_sent, down_kept, down_sent, dgain_two, dscale_two = ffn(
        core, middle, cotangent.reshape(cells, dim), keep_two, second_gain[None], scale_second[None],
        weight_up, weight_down, count_ha, count_ba,
    )
    order = list(range(count_ba.bit_length() - 1))
    turned = order[len(order) // 2 :] + order[: len(order) // 2]
    dup = reduce_chunks([up_kept, exchange(up_sent, "ha", 1)], order)
    ddown = reduce_chunks([down_kept, exchange(down_sent, "ha", 1)], turned)
    dconv, dmapped = gates_backward(dmiddle, conv, mapped, keep_one, scale_first[None], gates, weight_out)
    above, below = neighbour_rows(dconv, reach, 1)
    out_kept, out_sent, packed = gates_weights(
        core, dmiddle, keep_one, scale_first[None], weight_out, mixed, dmapped, dgain_two, dscale_two,
        widths, count_ha, count_ba,
    )
    dout = reduce_chunks([out_kept, exchange(out_sent, "ha", 1)], order)
    packed = reduce_whole(packed)
    djoined, dkern = conv_backward(row_mask, above, dconv, below, joined, kern, col_mask, rows, cols)
    dkern = reduce_whole(dkern.reshape(-1, LANES)).reshape(dkern.shape)
    dcanvas, in_kept, in_sent, dgain_one = head_backward(
        core, own, valid, first_gain[None], dmiddle, djoined, weight_in, count_ha, count_ba
    )
    in_parts = [in_kept, exchange(in_sent, "ha", 1)]
    middle_row = in_kept.shape[2] // 2
    din = jnp.concatenate(
        [
            reduce_chunks([part[:, :, :middle_row] for part in in_parts], order),
            reduce_chunks([part[:, :, middle_row:] for part in in_parts], turned),
        ],
        axis=0,
    )
    dgain_one = reduce_whole(dgain_one)

    small = []
    row = 0
    for tall, width in zip(widths[:-1], widths[1:]):
        size = tall * width // LANES
        small.append(from_blocks(packed[row : row + size], tall))
        row += size
    for _ in range(3):
        small.append(packed[row : row + dim // LANES].reshape(dim))
        row += dim // LANES
    dkern = jnp.concatenate([dkern[k, :taps] for k in range(dkern.shape[0])], axis=1)[:, split:]
    return (
        output.reshape(canvas.shape),
        dcanvas.reshape(canvas.shape),
        dgain_one[: dim // LANES].reshape(dim),
        din,
        dkern,
        small[0],
        small[1],
        small[2],
        dout.T,
        small[3],
        small[4],
        dup,
        ddown.T,
        small[5],
    )


def solution(mesh):
    in_specs = (
        P("ba", "ha", None, None),
        P("ba", None, None),
        P("ba", None),
        P("ba", None),
    ) + (P(),) * 12 + (P("ba", "ha", None, None),)
    tiled = P("ba", "ha")
    out_specs = (
        P("ba", "ha", None, None),
        P("ba", "ha", None, None),
        P(),
        tiled,
        P(),
        P(),
        P(),
        P(),
        tiled,
        P(),
        P(),
        tiled,
        tiled,
        P(),
    )
    return jax.shard_map(shards, mesh=mesh, in_specs=in_specs, out_specs=out_specs, check_vma=False)
```

```python
import functools

import jax
import jax.numpy as jnp
from jax import lax
from jax.experimental import pallas as pl
from jax.experimental.pallas import tpu as pltpu
from jax.sharding import PartitionSpec as P

KERN = 7
TAPS = KERN * KERN
REACH = KERN // 2
KEEP_RATE = 0.8
SPREAD = 1.0 / 3.0
EPSILON = 1e-06
LANES = 128
EDGE = 8
F32 = jnp.float32
INV_SQRT_2 = 0.7071067811865476
INV_SQRT_2PI = 0.3989422804014327
NN = (((1,), (0,)), ((), ()))
NT = (((1,), (1,)), ((), ()))
TN = (((0,), (0,)), ((), ()))


def dot(left, right, dims=NN):
    return lax.dot_general(left, right, dims, precision=lax.Precision.HIGH, preferred_element_type=F32)


def normalized(values):
    centered = values - jnp.mean(values, axis=-1, keepdims=True)
    scale = lax.rsqrt(jnp.mean(centered * centered, axis=-1, keepdims=True) + EPSILON)
    return centered * scale, scale


def norm_backward(grad_hat, hat, scale):
    return scale * (
        grad_hat
        - jnp.mean(grad_hat, axis=-1, keepdims=True)
        - hat * jnp.mean(grad_hat * hat, axis=-1, keepdims=True)
    )


def params(mebibytes):
    return pltpu.CompilerParams(vmem_limit_bytes=mebibytes << 20)


def lasting(microseconds):
    return pl.CostEstimate(flops=int(microseconds * 1.1e9), bytes_accessed=0, transcendentals=0)


def whole(shape):
    return pl.BlockSpec(tuple(shape), lambda *_: (0,) * len(shape), pipeline_mode=pl.Buffered(1))


def in_smem():
    return pl.BlockSpec(memory_space=pltpu.SMEM)


def anywhere():
    return pl.BlockSpec(memory_space=pl.ANY)


def shape_of(*shape):
    return jax.ShapeDtypeStruct(shape, F32)


def lane_blocks(width):
    return -(-width // LANES)


def masks_kernel(
    place_ref, keep_one, keep_two, ids_ref, valid_ref, one_ref, two_ref, row_ref, col_ref, padded, *, rows
):
    height, cols = ids_ref.shape
    slots = keep_one.shape[1]
    rows_ext = rows + 2 * REACH
    padded[...] = jnp.full(padded.shape, -1, jnp.int32)
    padded[EDGE : EDGE + height, :] = ids_ref[...]
    first = place_ref[0] * rows
    ids = padded[pl.ds(first + (EDGE - REACH), rows_ext), :]
    turned = jnp.concatenate([ids, jnp.full((-rows_ext % 8, cols), -1, jnp.int32)], axis=0).T
    own = turned[:, REACH : REACH + rows]
    one = jnp.zeros(own.shape, F32)
    two = jnp.zeros(own.shape, F32)
    for slot in range(slots):
        hit = own == slot
        one = jnp.where(hit, keep_one[0, slot].astype(F32) / KEEP_RATE, one)
        two = jnp.where(hit, keep_two[0, slot].astype(F32) / KEEP_RATE, two)
    valid = (turned >= 0).astype(F32)
    for r in range(rows_ext):
        valid_ref[r * cols : (r + 1) * cols, :] = jnp.broadcast_to(valid[:, r : r + 1], (cols, LANES))
    for r in range(rows):
        one_ref[r * cols : (r + 1) * cols, :] = jnp.broadcast_to(one[:, r : r + 1], (cols, LANES))
        two_ref[r * cols : (r + 1) * cols, :] = jnp.broadcast_to(two[:, r : r + 1], (cols, LANES))
    wide_ids = jnp.broadcast_to(ids_ref[...].T[:, height // 2 : height // 2 + 1], (cols, LANES))
    column = lax.broadcasted_iota(jnp.int32, (cols, LANES), 0)
    for b in range(KERN):
        shift = b - REACH
        moved = pltpu.roll(wide_ids, (-shift) % cols, 0)
        inside = (column + shift >= 0) & (column + shift < cols)
        same = (moved == wide_ids) & inside
        col_ref[b] = same.astype(F32).reshape(cols // 8, 8, LANES)
    across = ids[:, cols // 2 : cols // 2 + 1]
    place = first - REACH + lax.broadcasted_iota(jnp.int32, across.shape, 0)
    across = jnp.where((place >= 0) & (place < height), across, -2)
    lane = lax.broadcasted_iota(jnp.int32, (rows, LANES), 1)
    mask = jnp.zeros((rows, LANES), F32)
    for a in range(KERN):
        same = (across[a : a + rows] == across[REACH : REACH + rows]).astype(F32)
        mask = jnp.where(lane == a + 1, same, mask)
    row_ref[...] = mask


def masks(place, keep_one, keep_two, ids, rows):
    height, cols = ids.shape
    return pl.pallas_call(
        functools.partial(masks_kernel, rows=rows),
        in_specs=[in_smem(), in_smem(), in_smem(), pl.BlockSpec(memory_space=pltpu.VMEM)],
        out_shape=[
            shape_of((rows + 2 * REACH) * cols, LANES),
            shape_of(rows * cols, LANES),
            shape_of(rows * cols, LANES),
            shape_of(rows, LANES),
            shape_of(KERN, cols // 8, 8, LANES),
        ],
        scratch_shapes=[pltpu.VMEM((height + 2 * EDGE, cols), jnp.int32)],
        compiler_params=params(16),
        cost_estimate=lasting(3),
    )(place, keep_one, keep_two, ids)


def lay_kernel(kern_ref, laid, split):
    tap = lax.broadcasted_iota(jnp.int32, (TAPS, split), 0)
    own = jnp.where(tap == TAPS // 2, 1.0 / SPREAD, 0.0).astype(F32)
    for k in range(laid.shape[0]):
        start = k * LANES - split
        left = own if k == 0 else kern_ref[:, start : start + split]
        laid[k] = jnp.concatenate([left, kern_ref[:, start + split : start + LANES]], axis=1) * SPREAD


def fill_shifted(flat, col_ref, shifted, rows_ext, cols):
    groups = cols // 8
    for b in range(KERN):
        mask = col_ref[b]

        def some(h, _, b=b, mask=mask):
            for k in range(2):
                r = 2 * h + k
                start = pl.multiple_of(r * cols, cols) + (EDGE + b - REACH)
                x = flat[pl.ds(start, cols), :].reshape(groups, 8, LANES)
                shifted[b, r] = x if b == REACH else x * mask
            return 0

        lax.fori_loop(0, rows_ext // 2, some, 0)


def conv_block(row_mask, kern, shifted, wide, out_ref, rows, cols):
    groups = cols // 8
    for t in range(KERN):
        wide[t] = jnp.zeros((8, LANES), F32)
        wide[KERN * (KERN + 1) + t] = jnp.zeros((8, LANES), F32)
    for t in range(TAPS):
        wide[KERN + t] = jnp.broadcast_to(kern[t : t + 1, :], (8, LANES))

    def pair(h, _):
        r = 2 * h

        def step(i, totals):
            first, second = totals
            mask_first = row_mask[r, i + 1]
            mask_second = row_mask[r + 1, i]
            for b in range(KERN):
                x = shifted[b, r + i]
                first = first + (wide[(i + 1) * KERN + b] * mask_first)[None] * x
                second = second + (wide[i * KERN + b] * mask_second)[None] * x
            return first, second

        zero = jnp.zeros((groups, 8, LANES), F32)
        first, second = lax.fori_loop(0, KERN + 1, step, (zero, zero))
        out_ref[pl.ds(pl.multiple_of(r * cols, cols), cols), :] = first.reshape(cols, LANES)
        out_ref[pl.ds(pl.multiple_of((r + 1) * cols, cols), cols), :] = second.reshape(cols, LANES)
        return 0

    lax.fori_loop(0, rows // 2, pair, 0)


def conv_grad_block(row_mask, kern, shifted, wide, dk, mix_ref, out_ref, dk_ref, rows, cols):
    groups = cols // 8
    for t in range(TAPS):
        wide[t] = jnp.broadcast_to(kern[TAPS - 1 - t : TAPS - t, :], (8, LANES))
        dk[t] = jnp.zeros((8, LANES), F32)

    def one(r, _):
        start = pl.ds(pl.multiple_of(r * cols, cols), cols)
        mix = mix_ref[start, :].reshape(groups, 8, LANES)

        def step(i, total):
            mask = row_mask[r, i + 1]
            for b in range(KERN):
                x = shifted[b, r + i]
                total = total + (wide[i * KERN + b] * mask)[None] * x
                dk[i * KERN + b] += jnp.sum(mix * x, axis=0) * mask
            return total

        total = lax.fori_loop(0, KERN, step, jnp.zeros((groups, 8, LANES), F32))
        out_ref[start, :] = total.reshape(cols, LANES)
        return 0

    lax.fori_loop(0, rows, one, 0)
    for t in range(TAPS):
        dk_ref[TAPS - 1 - t : TAPS - t, :] = jnp.sum(dk[t], axis=0, keepdims=True) * SPREAD
    dk_ref[TAPS:, :] = jnp.zeros((dk_ref.shape[0] - TAPS, LANES), F32)


def share(core, first, second, kept_ref, sent_ref, z, p):
    mine = core == 0
    tall, width = first.shape
    for ref, chunk in (
        (kept_ref, jnp.where(mine, first, second)),
        (sent_ref, jnp.where(mine, second, first)),
    ):
        for k in range(lane_blocks(width)):
            part = chunk[:, k * LANES : (k + 1) * LANES]
            if part.shape[1] < LANES:
                part = jnp.concatenate([part, jnp.zeros((tall, LANES - part.shape[1]), F32)], axis=1)
            ref[z, p, k * tall : (k + 1) * tall, :] = part


def share_columns(core, grad, kept_ref, sent_ref, width):
    groups, parts = kept_ref.shape[:2]
    tall = grad.shape[0] // parts
    for z in range(groups):
        for p in range(parts):
            rows = slice(p * tall, (p + 1) * tall)
            first = grad[rows, 2 * z * width : (2 * z + 1) * width]
            second = grad[rows, (2 * z + 1) * width : (2 * z + 2) * width]
            share(core, first, second, kept_ref, sent_ref, z, p)


def share_rows(core, grad, kept_ref, sent_ref, tall):
    groups, parts = kept_ref.shape[:2]
    width = grad.shape[1] // parts
    for z in range(groups):
        for p in range(parts):
            columns = slice(p * width, (p + 1) * width)
            first = grad[2 * z * tall : (2 * z + 1) * tall, columns]
            second = grad[(2 * z + 1) * tall : (2 * z + 2) * tall, columns]
            share(core, first, second, kept_ref, sent_ref, z, p)


def forward_kernel(
    place_ref, row_mask, above_ref, own_ref, below_ref, valid_ref, one_keep_ref, two_keep_ref, cot_ref,
    first_gain_ref, first_scale_ref, second_gain_ref, second_scale_ref,
    in_ref, kern_ref, col_ref, one_ref, two_ref, three_ref, out_ref, up_ref, down_ref,
    joined_ref, output_ref, dmiddle_ref, dconv_ref,
    up_kept_ref, up_sent_ref, down_kept_ref, down_sent_ref, out_kept_ref, out_sent_ref, packed_ref,
    normed, flat, shifted, laid, wide, conv, mixed_ref, mapped_ref, middle_ref, result, dnorm,
    *, rows, cols, count_ha, count_ba,
):
    step = pl.program_id(0)
    blocks = flat.shape[0]
    cells = rows * cols
    reach = REACH * cols
    cells_ext = cells + 2 * reach
    core = place_ref[0] % 2
    split = one_ref.shape[0]
    dim = own_ref.shape[1]
    head_steps = blocks // 2
    ffn_first = head_steps + blocks
    gate_refs = (one_ref, two_ref, three_ref)

    @pl.when(step == 0)
    def _():
        lay_kernel(kern_ref, laid, split)
        start = 0
        for ref in (above_ref, own_ref, below_ref):
            size = ref.shape[0]
            hat, _ = normalized(ref[...] * valid_ref[start : start + size, :1])
            normed[start : start + size] = hat * first_gain_ref[...]
            start += size

    @pl.when(step < head_steps)
    def _():
        joined = dot(normed[...], in_ref[...])
        for k in range(2):
            part = joined[:, k * LANES : (k + 1) * LANES]
            block = 2 * step + k
            flat[block, :EDGE] = jnp.zeros((EDGE, LANES), F32)
            flat[block, EDGE : EDGE + cells_ext] = part
            flat[block, EDGE + cells_ext :] = jnp.zeros((EDGE, LANES), F32)
            joined_ref[k] = part[reach : reach + cells]

    @pl.when((step >= head_steps) & (step < ffn_first))
    def _():
        block = step - head_steps
        fill_shifted(flat.at[block], col_ref, shifted, rows + 2 * REACH, cols)
        conv_block(row_mask, laid[block], shifted, wide, conv.at[block], rows, cols)

    def conv_part(start, width):
        return jnp.concatenate([conv[start // LANES + k] for k in range(width // LANES)], axis=1)

    @pl.when(step == ffn_first)
    def _():
        mixed = conv[0, :, :split] * conv[0, :, split:]
        mixed_ref[:, :split] = mixed
        start = 2 * split
        for ref in gate_refs:
            width = ref.shape[1]
            mapped = dot(mixed, ref[...])
            mapped_ref[:, start - 2 * split : start - 2 * split + width] = mapped
            mixed = mapped * conv_part(start, width)
            mixed_ref[:, start : start + width] = mixed
            start += width
        branch = dot(mixed, out_ref[...])
        masked = own_ref[...] * valid_ref[reach : reach + cells, :1]
        middle = masked + one_keep_ref[:, :1] * first_scale_ref[...] * branch
        middle_ref[...] = middle
        hat, _ = normalized(middle)
        normed[:cells] = hat * second_gain_ref[...]
        normed[cells : cells + reach] = jnp.zeros((reach, dim), F32)
        result[...] = jnp.zeros_like(result)
        dnorm[...] = jnp.zeros_like(dnorm)

    @pl.when(step >= ffn_first)
    def _():
        grad_result = two_keep_ref[:, :1] * second_scale_ref[...] * cot_ref[...]
        pre = dot(normed[:cells], up_ref[...])
        cdf = 0.5 + 0.5 * lax.erf(pre * INV_SQRT_2)
        slope = cdf + pre * (INV_SQRT_2PI * jnp.exp(-0.5 * pre * pre))
        hidden = pre * cdf
        result[...] += dot(hidden, down_ref[...])
        grad_pre = dot(grad_result, down_ref[...], NT) * slope
        share_rows(core, dot(grad_result, hidden, TN), down_kept_ref, down_sent_ref, dim // count_ha)
        width = down_ref.shape[0] // (2 * up_kept_ref.shape[0])
        share_columns(core, dot(normed[:cells], grad_pre, TN), up_kept_ref, up_sent_ref, width)
        dnorm[...] += dot(grad_pre, up_ref[...], NT)

    @pl.when(step == pl.num_programs(0) - 1)
    def _():
        hat, scale = normalized(middle_ref[...])
        kept = two_keep_ref[:, :1] * result[...]
        output_ref[...] = middle_ref[...] + second_scale_ref[...] * kept
        dscale_two = jnp.sum(cot_ref[...] * kept, axis=0, keepdims=True)
        dgain_two = jnp.sum(dnorm[...] * hat, axis=0, keepdims=True)
        dmiddle = cot_ref[...] + norm_backward(dnorm[...] * second_gain_ref[...], hat, scale)
        dmiddle_ref[...] = dmiddle
        kept = one_keep_ref[:, :1] * dmiddle
        start = mixed_ref.shape[1] - out_ref.shape[0]
        crossed = dot(mixed_ref[:, start:], kept, TN)
        dscale_one = jnp.sum(crossed * out_ref[...], axis=0, keepdims=True)
        share_rows(core, (crossed * first_scale_ref[...]).T, out_kept_ref, out_sent_ref, dim // count_ha)
        grad = dot(kept * first_scale_ref[...], out_ref[...], NT)
        row = packed_ref.shape[0]
        start = blocks * LANES
        for ref in reversed(gate_refs):
            tall, width = ref.shape
            start -= width
            source = start - tall if tall > split else 0
            columns = slice(start - 2 * split, start - 2 * split + width)
            dconv = grad * mapped_ref[:, columns]
            for k in range(width // LANES):
                dconv_ref[start // LANES + k] = dconv[:, k * LANES : (k + 1) * LANES]
            grad_mapped = grad * conv_part(start, width)
            part = dot(mixed_ref[:, source : source + tall], grad_mapped, TN)
            row -= tall * width // LANES
            for k in range(width // LANES):
                packed_ref[row + k * tall : row + (k + 1) * tall] = part[:, k * LANES : (k + 1) * LANES]
            grad = dot(grad_mapped, ref[...], NT)
        dconv_ref[0] = jnp.concatenate([grad * conv[0, :, split:], grad * conv[0, :, :split]], axis=1)
        packed_ref[:row] = jnp.zeros((row, LANES), F32)
        row = 0
        for vector in (dscale_one, dgain_two, dscale_two):
            for k in range(dim // LANES):
                packed_ref[row : row + 1] = vector[:, k * LANES : (k + 1) * LANES]
                row += 1


def packed_rows(gates, dim):
    rows = sum(gate.size for gate in gates) // LANES + 3 * dim // LANES
    return -(-rows // 16) * 16


def forward(
    place, row_mask, above, own, below, valid, one_keep, two_keep, cot, vectors, weight_in, kern, col_mask, gates,
    weight_out, weight_up, weight_down, rows, cols, count_ha, count_ba, chunk=512,
):
    cells, dim = own.shape
    reach = above.shape[0]
    blocks = weight_in.shape[1] // LANES
    hidden = weight_up.shape[1]
    split = gates[0].shape[0]
    wide = blocks * LANES
    head_steps = blocks // 2
    ffn_first = head_steps + blocks
    ffn_steps = hidden // chunk

    def ffn_step(i):
        return jnp.clip(i - ffn_first, 0, ffn_steps - 1)

    up_wide, down_wide = hidden // count_ha, hidden // count_ba
    up_rows = dim // count_ba * lane_blocks(up_wide)
    down_rows = dim // count_ha * lane_blocks(down_wide)
    out_rows = dim // count_ha * lane_blocks(dim // count_ba)
    half = count_ha // 2
    up_spec = pl.BlockSpec((chunk // (2 * up_wide), count_ba, up_rows, LANES), lambda i: (ffn_step(i), 0, 0, 0))
    down_spec = pl.BlockSpec((half, chunk // down_wide, down_rows, LANES), lambda i: (0, ffn_step(i), 0, 0))
    out_shape = (half, count_ba, out_rows, LANES)
    packed_shape = (packed_rows(gates, dim), LANES)
    cells_ext = cells + 2 * reach
    return pl.pallas_call(
        functools.partial(forward_kernel, rows=rows, cols=cols, count_ha=count_ha, count_ba=count_ba),
        grid=(ffn_first + ffn_steps,),
        in_specs=[in_smem(), in_smem()]
        + [whole(x.shape) for x in (above, own, below, valid, one_keep, two_keep, cot)]
        + [whole((1, dim))] * 4
        + [
            pl.BlockSpec((dim, 2 * LANES), lambda i: (0, jnp.minimum(i, head_steps - 1))),
            whole(kern.shape),
            whole(col_mask.shape),
        ]
        + [whole(gate.shape) for gate in gates]
        + [
            whole(weight_out.shape),
            pl.BlockSpec((dim, chunk), lambda i: (0, ffn_step(i))),
            pl.BlockSpec((chunk, dim), lambda i: (ffn_step(i), 0)),
        ],
        out_specs=[
            pl.BlockSpec((2, cells, LANES), lambda i: (jnp.minimum(i, head_steps - 1), 0, 0)),
            whole((cells, dim)),
            whole((cells, dim)),
            whole((blocks, cells, LANES)),
            up_spec,
            up_spec,
            down_spec,
            down_spec,
            whole(out_shape),
            whole(out_shape),
            whole(packed_shape),
        ],
        out_shape=[
            shape_of(blocks, cells, LANES),
            shape_of(cells, dim),
            shape_of(cells, dim),
            shape_of(blocks, cells, LANES),
            shape_of(half, count_ba, up_rows, LANES),
            shape_of(half, count_ba, up_rows, LANES),
            shape_of(half, count_ba, down_rows, LANES),
            shape_of(half, count_ba, down_rows, LANES),
            shape_of(*out_shape),
            shape_of(*out_shape),
            shape_of(*packed_shape),
        ],
        scratch_shapes=[
            pltpu.VMEM((cells_ext, dim), F32),
            pltpu.VMEM((blocks, cells_ext + 2 * EDGE, LANES), F32),
            pltpu.VMEM((KERN, rows + 2 * REACH, cols // 8, 8, LANES), F32),
            pltpu.VMEM((blocks, TAPS, LANES), F32),
            pltpu.VMEM((KERN * (KERN + 2), 8, LANES), F32),
            pltpu.VMEM((blocks, cells, LANES), F32),
            pltpu.VMEM((cells, wide), F32),
            pltpu.VMEM((cells, wide - 2 * split), F32),
            pltpu.VMEM((cells, dim), F32),
            pltpu.VMEM((cells, dim), F32),
            pltpu.VMEM((cells, dim), F32),
        ],
        compiler_params=params(60),
        cost_estimate=lasting(70),
    )(
        place, row_mask, above, own, below, valid, one_keep, two_keep, cot, *vectors,
        weight_in, kern, col_mask, *gates, weight_out, weight_up, weight_down,
    )


def backward_kernel(
    place_ref, row_mask, above_ref, own_ref, below_ref, mix_ref, kern_ref, col_ref, canvas_ref, valid_ref, gain_ref,
    dmiddle_ref, before_ref, in_ref, *rest, rows, cols, first_block, last, count_ties,
):
    rest = rest[count_ties:]
    if last:
        dcanvas_ref, kept_ref, sent_ref, dk_ref, dgain_ref = rest[:5]
    else:
        dnorm_ref, kept_ref, sent_ref, dk_ref = rest[:4]
    flat, shifted, laid, wide, dk, djoined, normed, dnorm = rest[-8:]
    step = pl.program_id(0)
    block = first_block + step
    cells = rows * cols
    reach = REACH * cols
    core = place_ref[0] % 2
    split = laid.shape[0] * LANES - kern_ref.shape[1]
    width = in_ref.shape[1] // (2 * kept_ref.shape[0])

    @pl.when(step == 0)
    def _():
        lay_kernel(kern_ref, laid, split)
        hat, _ = normalized(canvas_ref[...] * valid_ref[reach : reach + cells, :1])
        normed[...] = hat * gain_ref[...]
        dnorm[...] = before_ref[...] if first_block else jnp.zeros_like(dnorm)

    flat[:EDGE] = jnp.zeros((EDGE, LANES), F32)
    flat[EDGE : EDGE + reach] = above_ref[0]
    flat[EDGE + reach : EDGE + reach + cells] = own_ref[0]
    flat[EDGE + reach + cells : EDGE + 2 * reach + cells] = below_ref[0]
    flat[EDGE + 2 * reach + cells :] = jnp.zeros((EDGE, LANES), F32)
    fill_shifted(flat, col_ref, shifted, rows + 2 * REACH, cols)
    conv_grad_block(
        row_mask, laid[block], shifted, wide, dk, mix_ref.at[0], djoined.at[step % 2], dk_ref.at[0], rows, cols
    )

    @pl.when(step % 2 == 1)
    def _():
        grad = jnp.concatenate([djoined[0], djoined[1]], axis=1)
        share_columns(core, dot(normed[...], grad, TN), kept_ref, sent_ref, width)
        dnorm[...] += dot(grad, in_ref[...], NT)

    @pl.when(step == pl.num_programs(0) - 1)
    def _():
        if last:
            hat, scale = normalized(canvas_ref[...] * valid_ref[reach : reach + cells, :1])
            dgain = jnp.sum(dnorm[...] * hat, axis=0, keepdims=True)
            dgain_ref[...] = jnp.zeros_like(dgain_ref)
            for k in range(dgain.shape[1] // LANES):
                dgain_ref[k : k + 1] = dgain[:, k * LANES : (k + 1) * LANES]
            inner = dmiddle_ref[...] + norm_backward(dnorm[...] * gain_ref[...], hat, scale)
            dcanvas_ref[...] = inner * valid_ref[reach : reach + cells, :1]
        else:
            dnorm_ref[...] = dnorm[...]


def backward(
    place, row_mask, above, own, below, mix, kern, col_mask, canvas, valid, gain, dmiddle, before, weight_in,
    first_block, end_block, ties, rows, cols, count_ha, count_ba,
):
    cells, dim = canvas.shape
    blocks = own.shape[0]
    reach = above.shape[1]
    last = end_block == blocks
    steps = end_block - first_block
    own_wide = weight_in.shape[1] // count_ha
    chunk_rows = dim // count_ba * lane_blocks(own_wide)
    groups = 2 * LANES // (2 * own_wide)
    tall = -(-TAPS // 8) * 8

    def block_of(size):
        return pl.BlockSpec((1, size, LANES), lambda i: (first_block + i, 0, 0))

    chunk_spec = pl.BlockSpec((groups, count_ba, chunk_rows, LANES), lambda i: (i // 2, 0, 0, 0))
    chunks = shape_of(groups * steps // 2, count_ba, chunk_rows, LANES)
    dk_spec = pl.BlockSpec((1, tall, LANES), lambda i: (i, 0, 0))
    dk_shape = shape_of(steps, tall, LANES)
    gain_shape = (-(-dim // LANES // 16) * 16, LANES)
    return pl.pallas_call(
        functools.partial(
            backward_kernel, rows=rows, cols=cols, first_block=first_block, last=last, count_ties=len(ties)
        ),
        grid=(steps,),
        in_specs=[in_smem(), in_smem(), block_of(reach), block_of(cells), block_of(reach), block_of(cells)]
        + [whole(x.shape) for x in (kern, col_mask, canvas, valid)]
        + [whole((1, dim)), whole((cells, dim)), whole((cells, dim))]
        + [pl.BlockSpec((dim, 2 * LANES), lambda i: (0, first_block // 2 + i // 2))]
        + [anywhere()] * len(ties),
        out_specs=[whole((cells, dim)), chunk_spec, chunk_spec, dk_spec] + [whole(gain_shape)] * last,
        out_shape=[shape_of(cells, dim), chunks, chunks, dk_shape] + [shape_of(*gain_shape)] * last,
        scratch_shapes=[
            pltpu.VMEM((cells + 2 * reach + 2 * EDGE, LANES), F32),
            pltpu.VMEM((KERN, rows + 2 * REACH, cols // 8, 8, LANES), F32),
            pltpu.VMEM((blocks, TAPS, LANES), F32),
            pltpu.VMEM((TAPS, 8, LANES), F32),
            pltpu.VMEM((TAPS, 8, LANES), F32),
            pltpu.VMEM((2, cells, LANES), F32),
            pltpu.VMEM((cells, dim), F32),
            pltpu.VMEM((cells, dim), F32),
        ],
        compiler_params=params(32),
        cost_estimate=lasting(4 * steps),
    )(
        place, row_mask, above, own, below, mix, kern, col_mask, canvas, valid, gain, dmiddle, before, weight_in, *ties
    )


def unpack_kernel(packed_ref, dkern_ref, dgain_ref, *outs, dim):
    row = 0
    for ref in outs[:3]:
        for k in range(dim // LANES):
            ref[:, k * LANES : (k + 1) * LANES] = packed_ref[row : row + 1]
            row += 1
    row = packed_ref.shape[0]
    for ref in reversed(outs[3:6]):
        tall, width = ref.shape
        row -= tall * width // LANES
        for k in range(width // LANES):
            ref[:, k * LANES : (k + 1) * LANES] = packed_ref[row + k * tall : row + (k + 1) * tall]
    dk_ref, gain_ref = outs[6:]
    joined = jnp.concatenate([dkern_ref[k, :TAPS] for k in range(dkern_ref.shape[0])], axis=1)
    dk_ref[...] = joined[:, joined.shape[1] - dk_ref.shape[1] :]
    for k in range(dim // LANES):
        gain_ref[:, k * LANES : (k + 1) * LANES] = dgain_ref[k : k + 1]


def unpack(packed, dkern, dgain, gates, kern, dim):
    return pl.pallas_call(
        functools.partial(unpack_kernel, dim=dim),
        out_shape=[shape_of(1, dim)] * 3
        + [shape_of(*gate.shape) for gate in gates]
        + [shape_of(*kern.shape), shape_of(1, dim)],
        compiler_params=params(16),
        cost_estimate=lasting(2),
    )(packed, dkern, dgain)


def exchange(values, axis, bit):
    return lax.ppermute(values, axis, [(i, i ^ bit) for i in range(lax.axis_size(axis))])


def picked(parts, index, axis):
    return [lax.dynamic_index_in_dim(part, index, axis, keepdims=False) for part in parts]


def total(parts):
    result = parts[0]
    for part in parts[1:]:
        result = result + part
    return result


class Chunks:
    def __init__(self, parts, order):
        bits = len(order)
        self.parts = [part.reshape(part.shape[:1] + (2,) * bits + part.shape[2:]) for part in parts]
        self.order = list(order)
        self.left = list(reversed(range(bits)))

    def outgoing(self):
        bit = self.order[0]
        self.axis = 1 + self.left.index(bit)
        self.mine = (lax.axis_index("ba") >> bit) & 1
        self.leaving = total(picked(self.parts, 1 - self.mine, self.axis))
        return self.leaving

    def halve(self):
        bit = self.order.pop(0)
        self.left.remove(bit)
        got = exchange(self.leaving, "ba", 1 << bit)
        self.parts = picked(self.parts, self.mine, self.axis) + [got]

    def halve_rest(self):
        while self.order:
            self.outgoing()
            self.halve()


def finish(sums):
    z = lax.axis_index("ha") // 2
    stages = range(1, lax.axis_size("ha") // 2)
    got = []
    for step in stages:
        leaving = [total(picked(one.parts, z ^ step, 0)) for one in sums]
        got.append(exchange(jnp.concatenate(leaving, axis=0), "ha", 2 * step))
    results = []
    row = 0
    for one in sums:
        rows = one.parts[0].shape[1]
        results.append(total(picked(one.parts, z, 0) + [part[row : row + rows] for part in got]))
        row += rows
    return results


def reduce_whole(rows):
    half = rows.shape[0] // 2
    core = lax.axis_index("ha") % 2
    halves_of = rows.reshape(2, half, rows.shape[1])
    mine = total(picked([halves_of], core, 0) + [exchange(picked([halves_of], 1 - core, 0)[0], "ha", 1)])
    for axis, first in (("ba", 1), ("ha", 2)):
        bit = first
        while bit < lax.axis_size(axis):
            mine = mine + exchange(mine, axis, bit)
            bit *= 2
    other = exchange(mine, "ha", 1)
    low = jnp.where(core == 0, mine, other)
    high = jnp.where(core == 0, other, mine)
    return jnp.concatenate([low, high], axis=0)


def beside(rows, tall, width):
    parts = [rows[k * tall : (k + 1) * tall] for k in range(lane_blocks(width))]
    return jnp.concatenate(parts, axis=1)[:, :width]


def neighbour_rows(rows, width, dim):
    count = lax.axis_size("ha")
    up = [(i, i + 1) for i in range(count - 1)]
    down = [(i + 1, i) for i in range(count - 1)]
    tail = lax.slice_in_dim(rows, rows.shape[dim] - width, rows.shape[dim], axis=dim)
    head = lax.slice_in_dim(rows, 0, width, axis=dim)
    return lax.ppermute(tail, "ha", up), lax.ppermute(head, "ha", down)


def shards(
    canvas,
    image_id,
    keep_first,
    keep_second,
    first_gain,
    weight_in,
    depth_kernel,
    gate_first,
    gate_second,
    gate_third,
    weight_out,
    scale_first,
    second_gain,
    weight_up,
    weight_down,
    scale_second,
    cotangent,
):
    _, rows, cols, dim = canvas.shape
    cells = rows * cols
    reach = REACH * cols
    count_ha, count_ba = lax.axis_size("ha"), lax.axis_size("ba")
    hidden = weight_up.shape[1]
    blocks = weight_in.shape[1] // LANES
    place = lax.axis_index("ha")[None]
    own = canvas.reshape(cells, dim)
    gates = (gate_first, gate_second, gate_third)
    gain = first_gain[None]
    vectors = (gain, scale_first[None], second_gain[None], scale_second[None])
    order = list(range(count_ba.bit_length() - 1))
    turned = order[len(order) // 2 :] + order[: len(order) // 2]

    above, below = neighbour_rows(own, reach, 0)
    valid, one_keep, two_keep, row_mask, col_mask = masks(place, keep_first, keep_second, image_id[0], rows)
    (
        joined, output, dmiddle, dconv, up_kept, up_sent, down_kept, down_sent, out_kept, out_sent, packed
    ) = forward(
        place, row_mask, above, own, below, valid, one_keep, two_keep, cotangent.reshape(cells, dim), vectors,
        weight_in, depth_kernel, col_mask, gates, weight_out, weight_up, weight_down, rows, cols, count_ha, count_ba,
    )
    above, below = neighbour_rows(dconv, reach, 1)
    up = Chunks([up_kept, exchange(up_sent, "ha", 1)], order)
    down = Chunks([down_kept, exchange(down_sent, "ha", 1)], turned)
    out = Chunks([out_kept, exchange(out_sent, "ha", 1)], turned)
    packed = reduce_whole(packed)

    def back(first_block, end_block, before, ties):
        return backward(
            place, row_mask, above, dconv, below, joined, depth_kernel, col_mask, own, valid, gain, dmiddle, before,
            weight_in, first_block, end_block, ties, rows, cols, count_ha, count_ba,
        )

    ties = [up.outgoing(), down.outgoing()]
    up.halve()
    down.halve()
    cut = blocks * 3 // 4
    dnorm, first_kept, first_sent, first_dk = back(0, cut, dmiddle, ties)
    ties = [up.outgoing(), down.outgoing()]
    up.halve_rest()
    down.halve_rest()
    out.halve_rest()
    dcanvas, second_kept, second_sent, second_dk, dgain_one = back(cut, blocks, dnorm, ties)
    dkern = jnp.concatenate([first_dk, second_dk], axis=0)
    dkern = reduce_whole(dkern.reshape(-1, LANES)).reshape(dkern.shape)
    kept = jnp.concatenate([first_kept, second_kept], axis=0)
    sent = jnp.concatenate([first_sent, second_sent], axis=0)
    parts = [kept, exchange(sent, "ha", 1)]
    middle_row = kept.shape[2] // 2
    in_first = Chunks([part[:, :, :middle_row] for part in parts], order)
    in_second = Chunks([part[:, :, middle_row:] for part in parts], turned)
    in_first.halve_rest()
    in_second.halve_rest()
    dgain_one = reduce_whole(dgain_one)
    dup, ddown, dout = finish([up, down, out])
    din = jnp.concatenate(finish([in_first, in_second]), axis=0)
    dscale_one, dgain_two, dscale_two, dfirst, dsecond, dthird, dkern, dgain_one = unpack(
        packed, dkern, dgain_one, gates, depth_kernel, dim
    )
    return (
        output.reshape(canvas.shape),
        dcanvas.reshape(canvas.shape),
        dgain_one[0],
        beside(din, dim // count_ba, weight_in.shape[1] // count_ha),
        dkern,
        dfirst,
        dsecond,
        dthird,
        beside(dout, dim // count_ha, dim // count_ba).T,
        dscale_one[0],
        dgain_two[0],
        beside(dup, dim // count_ba, hidden // count_ha),
        beside(ddown, dim // count_ha, hidden // count_ba).T,
        dscale_two[0],
    )


def solution(mesh):
    in_specs = (
        P("ba", "ha", None, None),
        P("ba", None, None),
        P("ba", None),
        P("ba", None),
    ) + (P(),) * 12 + (P("ba", "ha", None, None),)
    tiled = P("ba", "ha")
    out_specs = (
        P("ba", "ha", None, None),
        P("ba", "ha", None, None),
        P(),
        tiled,
        P(),
        P(),
        P(),
        P(),
        tiled,
        P(),
        P(),
        tiled,
        tiled,
        P(),
    )
    return jax.shard_map(shards, mesh=mesh, in_specs=in_specs, out_specs=out_specs, check_vma=False)
```

```python
import functools

import jax
import jax.numpy as jnp
from jax import lax
from jax.experimental import pallas as pl
from jax.experimental.pallas import tpu as pltpu
from jax.sharding import PartitionSpec as P

KERN = 7
TAPS = KERN * KERN
REACH = KERN // 2
KEEP_RATE = 0.8
SPREAD = 1.0 / 3.0
EPSILON = 1e-06
LANES = 128
EDGE = 8
VMEM_BYTES = 62 << 20
F32 = jnp.float32
INV_SQRT_2 = 0.7071067811865476
INV_SQRT_2PI = 0.3989422804014327
NN = (((1,), (0,)), ((), ()))
NT = (((1,), (1,)), ((), ()))
TN = (((0,), (0,)), ((), ()))


def dot(left, right, dims=NN):
    return lax.dot_general(left, right, dims, precision=lax.Precision.HIGH, preferred_element_type=F32)


def normalized(values):
    centered = values - jnp.mean(values, axis=-1, keepdims=True)
    scale = lax.rsqrt(jnp.mean(centered * centered, axis=-1, keepdims=True) + EPSILON)
    return centered * scale, scale


def norm_backward(grad_hat, hat, scale):
    return scale * (
        grad_hat
        - jnp.mean(grad_hat, axis=-1, keepdims=True)
        - hat * jnp.mean(grad_hat * hat, axis=-1, keepdims=True)
    )


def params():
    return pltpu.CompilerParams(vmem_limit_bytes=VMEM_BYTES)


def lasting(microseconds):
    return pl.CostEstimate(flops=int(microseconds * 1.1e9), bytes_accessed=0, transcendentals=0)


def whole(shape):
    return pl.BlockSpec(tuple(shape), lambda *_: (0,) * len(shape), pipeline_mode=pl.Buffered(1))


def in_smem():
    return pl.BlockSpec(memory_space=pltpu.SMEM)


def anywhere():
    return pl.BlockSpec(memory_space=pl.ANY)


def shape_of(*shape):
    return jax.ShapeDtypeStruct(shape, F32)


def lane_blocks(width):
    return -(-width // LANES)


def image_ids(ids_ref, padded, place, rows):
    height, cols = ids_ref.shape
    padded[...] = jnp.full(padded.shape, -1, jnp.int32)
    padded[EDGE : EDGE + height, :] = ids_ref[...]
    ids = padded[pl.ds(place * rows + (EDGE - REACH), rows + 2 * REACH), :]
    return jnp.concatenate([ids, jnp.full((-ids.shape[0] % 8, cols), -1, jnp.int32)], axis=0).T


def spread_cells(factors, out_ref, first, rows):
    cols = factors.shape[0]
    for r in range(rows):
        column = factors[:, first + r : first + r + 1]
        out_ref[r * cols : (r + 1) * cols, :] = jnp.broadcast_to(column, (cols, LANES))


def keep_factors(turned, table_ref):
    result = jnp.zeros(turned.shape, F32)
    for slot in range(table_ref.shape[1]):
        result = jnp.where(turned == slot, table_ref[0, slot].astype(F32) / KEEP_RATE, result)
    return result


def conv_masks(ids_scalar, ids_ref, place, row_taps, col_mask, rows):
    height, cols = ids_ref.shape
    wide_ids = jnp.broadcast_to(ids_ref[...].T[:, height // 2 : height // 2 + 1], (cols, LANES))
    column = lax.broadcasted_iota(jnp.int32, (cols, LANES), 0)
    for b in range(KERN):
        shift = b - REACH
        moved = pltpu.roll(wide_ids, (-shift) % cols, 0)
        inside = (column + shift >= 0) & (column + shift < cols)
        same = (moved == wide_ids) & inside
        col_mask[b] = same.astype(F32).reshape(cols // 8, 8, LANES)

    def one(r, _):
        own = ids_scalar[place * rows + r, cols // 2]
        row_taps[r, 0] = KERN
        row_taps[r, KERN + 1] = KERN
        for a in range(KERN):
            other = place * rows + r + a - REACH
            inside = (other >= 0) & (other < height)
            same = ids_scalar[jnp.clip(other, 0, height - 1), cols // 2] == own
            row_taps[r, a + 1] = jnp.where(inside & same, a, KERN)
        return 0

    lax.fori_loop(0, rows, one, 0)


def lay_kernel(kern_ref, laid, split):
    tap = lax.broadcasted_iota(jnp.int32, (TAPS, split), 0)
    own = jnp.where(tap == TAPS // 2, 1.0 / SPREAD, 0.0).astype(F32)
    for k in range(laid.shape[0]):
        start = k * LANES - split
        left = own if k == 0 else kern_ref[:, start : start + split]
        laid[k] = jnp.concatenate([left, kern_ref[:, start + split : start + LANES]], axis=1) * SPREAD


def fill_shifted(flat, col_ref, shifted, rows_ext, cols):
    for b in range(KERN):
        for g in range(cols // 8):
            mask = None if b == REACH else col_ref[b, g]
            for r in range(rows_ext):
                x = flat[pl.ds(EDGE + r * cols + 8 * g + b - REACH, 8), :]
                shifted[b, r, g] = x if b == REACH else x * mask


def spread_taps(kern, wide, turned):
    for t in range(TAPS):
        source = TAPS - 1 - t if turned else t
        wide[t] = jnp.broadcast_to(kern[source : source + 1, :], (8, LANES))
    for t in range(KERN):
        wide[TAPS + t] = jnp.zeros((8, LANES), F32)


def conv_block(row_taps, kern, shifted, wide, out_ref, rows, cols):
    groups = cols // 8
    spread_taps(kern, wide, False)

    def pair(h, _):
        r = 2 * h

        def step(i, totals):
            first, second = totals
            taps_first = row_taps[r, i + 1] * KERN
            taps_second = row_taps[r + 1, i] * KERN
            for b in range(KERN):
                x = shifted[b, r + i]
                first = first + wide[taps_first + b][None] * x
                second = second + wide[taps_second + b][None] * x
            return first, second

        zero = jnp.zeros((groups, 8, LANES), F32)
        first, second = lax.fori_loop(0, KERN + 1, step, (zero, zero), unroll=4)
        out_ref[pl.ds(pl.multiple_of(r * cols, cols), cols), :] = first.reshape(cols, LANES)
        out_ref[pl.ds(pl.multiple_of((r + 1) * cols, cols), cols), :] = second.reshape(cols, LANES)
        return 0

    lax.fori_loop(0, rows // 2, pair, 0)


def conv_grad_block(row_taps, kern, shifted, wide, dk, mix_ref, out_ref, dk_ref, rows, cols):
    groups = cols // 8
    spread_taps(kern, wide, True)
    for t in range(TAPS):
        dk[t] = jnp.zeros((8, LANES), F32)

    def one(r, _):
        start = pl.ds(pl.multiple_of(r * cols, cols), cols)
        mix = mix_ref[start, :].reshape(groups, 8, LANES)
        total = jnp.zeros((groups, 8, LANES), F32)
        for i in range(KERN):
            row = row_taps[r, i + 1]
            same = jnp.where(row < KERN, 1.0, 0.0).astype(F32)
            for b in range(KERN):
                x = shifted[b, r + i]
                total = total + wide[row * KERN + b][None] * x
                dk[i * KERN + b] += jnp.sum(mix * x, axis=0) * same
        out_ref[start, :] = total.reshape(cols, LANES)
        return 0

    lax.fori_loop(0, rows, one, 0)
    for t in range(TAPS):
        dk_ref[TAPS - 1 - t : TAPS - t, :] = jnp.sum(dk[t], axis=0, keepdims=True) * SPREAD
    dk_ref[TAPS:, :] = jnp.zeros((dk_ref.shape[0] - TAPS, LANES), F32)


def share(core, first, second, kept_ref, sent_ref, z, p):
    mine = core == 0
    tall, width = first.shape
    for ref, chunk in (
        (kept_ref, jnp.where(mine, first, second)),
        (sent_ref, jnp.where(mine, second, first)),
    ):
        for k in range(lane_blocks(width)):
            part = chunk[:, k * LANES : (k + 1) * LANES]
            if part.shape[1] < LANES:
                part = jnp.concatenate([part, jnp.zeros((tall, LANES - part.shape[1]), F32)], axis=1)
            ref[z, p, k * tall : (k + 1) * tall, :] = part


def share_columns(core, grad, kept_ref, sent_ref, width):
    groups, parts = kept_ref.shape[:2]
    tall = grad.shape[0] // parts
    for z in range(groups):
        for p in range(parts):
            rows = slice(p * tall, (p + 1) * tall)
            first = grad[rows, 2 * z * width : (2 * z + 1) * width]
            second = grad[rows, (2 * z + 1) * width : (2 * z + 2) * width]
            share(core, first, second, kept_ref, sent_ref, z, p)


def share_rows(core, grad, kept_ref, sent_ref, tall):
    groups, parts = kept_ref.shape[:2]
    width = grad.shape[1] // parts
    for z in range(groups):
        for p in range(parts):
            columns = slice(p * width, (p + 1) * width)
            first = grad[2 * z * tall : (2 * z + 1) * tall, columns]
            second = grad[(2 * z + 1) * tall : (2 * z + 2) * tall, columns]
            share(core, first, second, kept_ref, sent_ref, z, p)


def forward_kernel(
    place_ref, ids_scalar, one_table, two_table, ids_ref, above_ref, own_ref, below_ref, cot_ref,
    first_gain_ref, first_scale_ref, second_gain_ref, second_scale_ref,
    in_ref, kern_ref, one_ref, two_ref, three_ref, out_ref, up_ref, down_ref,
    joined_ref, output_ref, dmiddle_ref, dconv_ref, dconv_top_ref, dconv_bottom_ref,
    up_kept_ref, up_sent_ref, down_kept_ref, down_sent_ref, out_kept_ref, out_sent_ref,
    packed_kept_ref, packed_sent_ref,
    row_taps, padded, valid_ref, one_keep_ref, two_keep_ref, col_ref, packed_ref, normed, flat, shifted, laid, wide, conv, mixed_ref, mapped_ref, middle_ref, result, dnorm,
    *, rows, cols, count_ha, count_ba,
):
    step = pl.program_id(0)
    blocks = flat.shape[0]
    cells = rows * cols
    reach = REACH * cols
    cells_ext = cells + 2 * reach
    core = place_ref[0] % 2
    split = one_ref.shape[0]
    dim = own_ref.shape[1]
    head_steps = blocks // 2
    ffn_first = head_steps + blocks
    gate_refs = (one_ref, two_ref, three_ref)

    @pl.when(step == 0)
    def _():
        lay_kernel(kern_ref, laid, split)
        turned = image_ids(ids_ref, padded, place_ref[0], rows)
        spread_cells((turned >= 0).astype(F32), valid_ref, 0, rows + 2 * REACH)
        spread_cells(keep_factors(turned, one_table), one_keep_ref, REACH, rows)
        spread_cells(keep_factors(turned, two_table), two_keep_ref, REACH, rows)
        conv_masks(ids_scalar, ids_ref, place_ref[0], row_taps, col_ref, rows)
        start = 0
        for ref in (above_ref, own_ref, below_ref):
            size = ref.shape[0]
            hat, _ = normalized(ref[...] * valid_ref[start : start + size, :1])
            normed[start : start + size] = hat * first_gain_ref[...]
            start += size

    @pl.when(step < head_steps)
    def _():
        joined = dot(normed[...], in_ref[...])
        for k in range(2):
            part = joined[:, k * LANES : (k + 1) * LANES]
            block = 2 * step + k
            flat[block, :EDGE] = jnp.zeros((EDGE, LANES), F32)
            flat[block, EDGE : EDGE + cells_ext] = part
            flat[block, EDGE + cells_ext :] = jnp.zeros((EDGE, LANES), F32)
            joined_ref[k] = part[reach : reach + cells]

    @pl.when((step >= head_steps) & (step < ffn_first))
    def _():
        block = step - head_steps
        fill_shifted(flat.at[block], col_ref, shifted, rows + 2 * REACH, cols)
        conv_block(row_taps, laid[block], shifted, wide, conv.at[block], rows, cols)

    def conv_part(start, width):
        return jnp.concatenate([conv[start // LANES + k] for k in range(width // LANES)], axis=1)

    @pl.when(step == ffn_first)
    def _():
        mixed = conv[0, :, :split] * conv[0, :, split:]
        mixed_ref[:, :split] = mixed
        start = 2 * split
        for ref in gate_refs:
            width = ref.shape[1]
            mapped = dot(mixed, ref[...])
            mapped_ref[:, start - 2 * split : start - 2 * split + width] = mapped
            mixed = mapped * conv_part(start, width)
            mixed_ref[:, start : start + width] = mixed
            start += width
        branch = dot(mixed, out_ref[...])
        masked = own_ref[...] * valid_ref[reach : reach + cells, :1]
        middle = masked + one_keep_ref[:, :1] * first_scale_ref[...] * branch
        middle_ref[...] = middle
        hat, _ = normalized(middle)
        normed[:cells] = hat * second_gain_ref[...]
        normed[cells : cells + reach] = jnp.zeros((reach, dim), F32)
        result[...] = jnp.zeros_like(result)
        dnorm[...] = jnp.zeros_like(dnorm)

    @pl.when(step >= ffn_first)
    def _():
        grad_result = two_keep_ref[:, :1] * second_scale_ref[...] * cot_ref[...]
        pre = dot(normed[:cells], up_ref[...])
        cdf = 0.5 + 0.5 * lax.erf(pre * INV_SQRT_2)
        slope = cdf + pre * (INV_SQRT_2PI * jnp.exp(-0.5 * pre * pre))
        hidden = pre * cdf
        result[...] += dot(hidden, down_ref[...])
        grad_pre = dot(grad_result, down_ref[...], NT) * slope
        share_rows(core, dot(grad_result, hidden, TN), down_kept_ref, down_sent_ref, dim // count_ha)
        width = down_ref.shape[0] // (2 * up_kept_ref.shape[0])
        share_columns(core, dot(normed[:cells], grad_pre, TN), up_kept_ref, up_sent_ref, width)
        dnorm[...] += dot(grad_pre, up_ref[...], NT)

    @pl.when(step == pl.num_programs(0) - 1)
    def _():
        hat, scale = normalized(middle_ref[...])
        kept = two_keep_ref[:, :1] * result[...]
        output_ref[...] = middle_ref[...] + second_scale_ref[...] * kept
        dscale_two = jnp.sum(cot_ref[...] * kept, axis=0, keepdims=True)
        dgain_two = jnp.sum(dnorm[...] * hat, axis=0, keepdims=True)
        dmiddle = cot_ref[...] + norm_backward(dnorm[...] * second_gain_ref[...], hat, scale)
        dmiddle_ref[...] = dmiddle
        kept = one_keep_ref[:, :1] * dmiddle
        start = mixed_ref.shape[1] - out_ref.shape[0]
        crossed = dot(mixed_ref[:, start:], kept, TN)
        dscale_one = jnp.sum(crossed * out_ref[...], axis=0, keepdims=True)
        share_rows(core, (crossed * first_scale_ref[...]).T, out_kept_ref, out_sent_ref, dim // count_ha)
        grad = dot(kept * first_scale_ref[...], out_ref[...], NT)
        row = packed_ref.shape[0]
        start = blocks * LANES
        for ref in reversed(gate_refs):
            tall, width = ref.shape
            start -= width
            source = start - tall if tall > split else 0
            columns = slice(start - 2 * split, start - 2 * split + width)
            dconv = grad * mapped_ref[:, columns]
            for k in range(width // LANES):
                dconv_ref[start // LANES + k] = dconv[:, k * LANES : (k + 1) * LANES]
            grad_mapped = grad * conv_part(start, width)
            part = dot(mixed_ref[:, source : source + tall], grad_mapped, TN)
            row -= tall * width // LANES
            for k in range(width // LANES):
                packed_ref[row + k * tall : row + (k + 1) * tall] = part[:, k * LANES : (k + 1) * LANES]
            grad = dot(grad_mapped, ref[...], NT)
        dconv_ref[0] = jnp.concatenate([grad * conv[0, :, split:], grad * conv[0, :, :split]], axis=1)
        packed_ref[:row] = jnp.zeros((row, LANES), F32)
        row = 0
        for vector in (dscale_one, dgain_two, dscale_two):
            for k in range(dim // LANES):
                packed_ref[row : row + 1] = vector[:, k * LANES : (k + 1) * LANES]
                row += 1
        half = packed_kept_ref.shape[0]
        packed_kept_ref[...] = packed_ref[pl.ds(pl.multiple_of(core * half, 8), half), :]
        packed_sent_ref[...] = packed_ref[pl.ds(pl.multiple_of((1 - core) * half, 8), half), :]
        dconv_top_ref[...] = dconv_ref[:, :reach, :]
        dconv_bottom_ref[...] = dconv_ref[:, cells - reach :, :]


def mask_scratch(ids, rows):
    height, cols = ids.shape
    return [
        pltpu.SMEM((rows, KERN + 2), jnp.int32),
        pltpu.VMEM((height + 2 * EDGE, cols), jnp.int32),
        pltpu.VMEM(((rows + 2 * REACH) * cols, LANES), F32),
    ]


def packed_rows(gates, dim):
    rows = sum(gate.size for gate in gates) // LANES + 3 * dim // LANES
    return -(-rows // 16) * 16


def forward(
    place, ids, keep_one, keep_two, above, own, below, cot, vectors, weight_in, kern, gates,
    weight_out, weight_up, weight_down, rows, cols, count_ha, count_ba, chunk=512,
):
    cells, dim = own.shape
    reach = above.shape[0]
    blocks = weight_in.shape[1] // LANES
    hidden = weight_up.shape[1]
    split = gates[0].shape[0]
    wide = blocks * LANES
    head_steps = blocks // 2
    ffn_first = head_steps + blocks
    ffn_steps = hidden // chunk

    def ffn_step(i):
        return jnp.clip(i - ffn_first, 0, ffn_steps - 1)

    up_wide, down_wide = hidden // count_ha, hidden // count_ba
    up_rows = dim // count_ba * lane_blocks(up_wide)
    down_rows = dim // count_ha * lane_blocks(down_wide)
    out_rows = dim // count_ha * lane_blocks(dim // count_ba)
    half = count_ha // 2
    up_spec = pl.BlockSpec((chunk // (2 * up_wide), count_ba, up_rows, LANES), lambda i: (ffn_step(i), 0, 0, 0))
    down_spec = pl.BlockSpec((half, chunk // down_wide, down_rows, LANES), lambda i: (0, ffn_step(i), 0, 0))
    out_shape = (half, count_ba, out_rows, LANES)
    packed_shape = (packed_rows(gates, dim), LANES)
    half_packed = (packed_shape[0] // 2, LANES)
    cells_ext = cells + 2 * reach
    return pl.pallas_call(
        functools.partial(forward_kernel, rows=rows, cols=cols, count_ha=count_ha, count_ba=count_ba),
        grid=(ffn_first + ffn_steps,),
        in_specs=[in_smem()] * 4
        + [whole(x.shape) for x in (ids, above, own, below, cot)]
        + [whole((1, dim))] * 4
        + [
            pl.BlockSpec((dim, 2 * LANES), lambda i: (0, jnp.minimum(i, head_steps - 1))),
            whole(kern.shape),
        ]
        + [whole(gate.shape) for gate in gates]
        + [
            whole(weight_out.shape),
            pl.BlockSpec((dim, chunk), lambda i: (0, ffn_step(i))),
            pl.BlockSpec((chunk, dim), lambda i: (ffn_step(i), 0)),
        ],
        out_specs=[
            pl.BlockSpec((2, cells, LANES), lambda i: (jnp.minimum(i, head_steps - 1), 0, 0)),
            whole((cells, dim)),
            whole((cells, dim)),
            whole((blocks, cells, LANES)),
            whole((blocks, reach, LANES)),
            whole((blocks, reach, LANES)),
            up_spec,
            up_spec,
            down_spec,
            down_spec,
            whole(out_shape),
            whole(out_shape),
            whole(half_packed),
            whole(half_packed),
        ],
        out_shape=[
            shape_of(blocks, cells, LANES),
            shape_of(cells, dim),
            shape_of(cells, dim),
            shape_of(blocks, cells, LANES),
            shape_of(blocks, reach, LANES),
            shape_of(blocks, reach, LANES),
            shape_of(half, count_ba, up_rows, LANES),
            shape_of(half, count_ba, up_rows, LANES),
            shape_of(half, count_ba, down_rows, LANES),
            shape_of(half, count_ba, down_rows, LANES),
            shape_of(*out_shape),
            shape_of(*out_shape),
            shape_of(*half_packed),
            shape_of(*half_packed),
        ],
        scratch_shapes=mask_scratch(ids, rows)
        + [
            pltpu.VMEM((cells, LANES), F32),
            pltpu.VMEM((cells, LANES), F32),
            pltpu.VMEM((KERN, cols // 8, 8, LANES), F32),
            pltpu.VMEM(packed_shape, F32),
            pltpu.VMEM((cells_ext, dim), F32),
            pltpu.VMEM((blocks, cells_ext + 2 * EDGE, LANES), F32),
            pltpu.VMEM((KERN, rows + 2 * REACH, cols // 8, 8, LANES), F32),
            pltpu.VMEM((blocks, TAPS, LANES), F32),
            pltpu.VMEM((TAPS + KERN, 8, LANES), F32),
            pltpu.VMEM((blocks, cells, LANES), F32),
            pltpu.VMEM((cells, wide), F32),
            pltpu.VMEM((cells, wide - 2 * split), F32),
            pltpu.VMEM((cells, dim), F32),
            pltpu.VMEM((cells, dim), F32),
            pltpu.VMEM((cells, dim), F32),
        ],
        compiler_params=params(),
        cost_estimate=lasting(55),
    )(
        place, ids, keep_one, keep_two, ids, above, own, below, cot, *vectors,
        weight_in, kern, *gates, weight_out, weight_up, weight_down,
    )


def backward_kernel(
    place_ref, ids_scalar, ids_ref, above_ref, own_ref, below_ref, mix_ref, kern_ref, canvas_ref, gain_ref,
    dmiddle_ref, before_ref, in_ref, *rest, rows, cols, first_block, last,
):
    total_ref, kept_ref, sent_ref, dk_ref = rest[-16:-12]
    row_taps, padded, valid_ref, col_ref, flat, shifted, laid, wide, dk, djoined, normed, dnorm = rest[-12:]
    step = pl.program_id(0)
    block = first_block + step
    cells = rows * cols
    reach = REACH * cols
    core = place_ref[0] % 2
    split = laid.shape[0] * LANES - kern_ref.shape[1]
    width = in_ref.shape[1] // (2 * kept_ref.shape[0])

    @pl.when(step == 0)
    def _():
        lay_kernel(kern_ref, laid, split)
        turned = image_ids(ids_ref, padded, place_ref[0], rows)
        spread_cells((turned >= 0).astype(F32), valid_ref, 0, rows + 2 * REACH)
        conv_masks(ids_scalar, ids_ref, place_ref[0], row_taps, col_ref, rows)
        hat, _ = normalized(canvas_ref[...] * valid_ref[reach : reach + cells, :1])
        normed[...] = hat * gain_ref[...]
        dnorm[...] = before_ref[...] if first_block else jnp.zeros_like(dnorm)

    flat[:EDGE] = jnp.zeros((EDGE, LANES), F32)
    flat[EDGE : EDGE + reach] = above_ref[0]
    flat[EDGE + reach : EDGE + reach + cells] = own_ref[0]
    flat[EDGE + reach + cells : EDGE + 2 * reach + cells] = below_ref[0]
    flat[EDGE + 2 * reach + cells :] = jnp.zeros((EDGE, LANES), F32)
    fill_shifted(flat, col_ref, shifted, rows + 2 * REACH, cols)
    conv_grad_block(
        row_taps, laid[block], shifted, wide, dk, mix_ref.at[0], djoined.at[step % 2], dk_ref.at[0], rows, cols
    )

    @pl.when(step % 2 == 1)
    def _():
        grad = jnp.concatenate([djoined[0], djoined[1]], axis=1)
        share_columns(core, dot(normed[...], grad, TN), kept_ref, sent_ref, width)
        dnorm[...] += dot(grad, in_ref[...], NT)

    @pl.when(step == pl.num_programs(0) - 1)
    def _():
        if not last:
            total_ref[...] = dnorm[...]
            return
        hat, scale = normalized(canvas_ref[...] * valid_ref[reach : reach + cells, :1])
        dgain = jnp.sum(dnorm[...] * hat, axis=0, keepdims=True)
        for k in range(dgain.shape[1] // LANES):
            dk_ref[0, TAPS + k : TAPS + k + 1] = dgain[:, k * LANES : (k + 1) * LANES]
        inner = dmiddle_ref[...] + norm_backward(dnorm[...] * gain_ref[...], hat, scale)
        total_ref[...] = inner * valid_ref[reach : reach + cells, :1]


def backward(
    place, ids, above, own, below, mix, kern, canvas, gain, dmiddle, before, weight_in,
    first_block, end_block, written, ties, rows, cols, count_ha, count_ba,
):
    cells, dim = canvas.shape
    blocks = own.shape[0]
    reach = above.shape[1]
    steps = end_block - first_block
    own_wide = weight_in.shape[1] // count_ha
    chunk_rows = dim // count_ba * lane_blocks(own_wide)
    groups = 2 * LANES // (2 * own_wide)
    tall = -(-(TAPS + dim // LANES) // 8) * 8

    def block_of(size):
        return pl.BlockSpec((1, size, LANES), lambda i: (first_block + i, 0, 0))

    chunk_spec = pl.BlockSpec((groups, count_ba, chunk_rows, LANES), lambda i: (first_block // 2 + i // 2, 0, 0, 0))
    chunks = shape_of(count_ha // 2, count_ba, chunk_rows, LANES)
    fixed = 13
    return pl.pallas_call(
        functools.partial(
            backward_kernel, rows=rows, cols=cols, first_block=first_block, last=end_block == blocks
        ),
        grid=(steps,),
        in_specs=[in_smem(), in_smem(), whole(ids.shape)]
        + [block_of(size) for size in (reach, cells, reach, cells)]
        + [whole(kern.shape), whole(canvas.shape)]
        + [whole((1, dim)), whole((cells, dim)), whole((cells, dim))]
        + [pl.BlockSpec((dim, 2 * LANES), lambda i: (0, first_block // 2 + i // 2))]
        + [anywhere()] * (len(written) + len(ties)),
        out_specs=[whole((cells, dim)), chunk_spec, chunk_spec, block_of(tall)],
        out_shape=[shape_of(cells, dim), chunks, chunks, shape_of(blocks, tall, LANES)],
        input_output_aliases={fixed + k: 1 + k for k in range(len(written))},
        scratch_shapes=mask_scratch(ids, rows)
        + [
            pltpu.VMEM((KERN, cols // 8, 8, LANES), F32),
            pltpu.VMEM((cells + 2 * reach + 2 * EDGE, LANES), F32),
            pltpu.VMEM((KERN, rows + 2 * REACH, cols // 8, 8, LANES), F32),
            pltpu.VMEM((blocks, TAPS, LANES), F32),
            pltpu.VMEM((TAPS + KERN, 8, LANES), F32),
            pltpu.VMEM((TAPS, 8, LANES), F32),
            pltpu.VMEM((2, cells, LANES), F32),
            pltpu.VMEM((cells, dim), F32),
            pltpu.VMEM((cells, dim), F32),
        ],
        compiler_params=params(),
        cost_estimate=lasting(4 * steps),
    )(
        place, ids, ids, above, own, below, mix, kern, canvas, gain, dmiddle, before, weight_in,
        *written, *ties,
    )


def unpack_kernel(packed_ref, dkern_ref, *outs, dim):
    row = 0
    for ref in outs[:3]:
        for k in range(dim // LANES):
            ref[:, k * LANES : (k + 1) * LANES] = packed_ref[row : row + 1]
            row += 1
    row = packed_ref.shape[0]
    for ref in reversed(outs[3:6]):
        tall, width = ref.shape
        row -= tall * width // LANES
        for k in range(width // LANES):
            ref[:, k * LANES : (k + 1) * LANES] = packed_ref[row + k * tall : row + (k + 1) * tall]
    dk_ref, gain_ref = outs[6:]
    joined = jnp.concatenate([dkern_ref[k, :TAPS] for k in range(dkern_ref.shape[0])], axis=1)
    dk_ref[...] = joined[:, joined.shape[1] - dk_ref.shape[1] :]
    for k in range(dim // LANES):
        gain_ref[:, k * LANES : (k + 1) * LANES] = dkern_ref[dkern_ref.shape[0] - 1, TAPS + k : TAPS + k + 1]


def unpack(packed, dkern, gates, kern, dim):
    return pl.pallas_call(
        functools.partial(unpack_kernel, dim=dim),
        out_shape=[shape_of(1, dim)] * 3
        + [shape_of(*gate.shape) for gate in gates]
        + [shape_of(*kern.shape), shape_of(1, dim)],
        compiler_params=params(),
        cost_estimate=lasting(2),
    )(packed, dkern)


def exchange(values, axis, bit):
    return lax.ppermute(values, axis, [(i, i ^ bit) for i in range(lax.axis_size(axis))])


def picked(parts, index, axis):
    return [lax.dynamic_index_in_dim(part, index, axis, keepdims=False) for part in parts]


def total(parts):
    result = parts[0]
    for part in parts[1:]:
        result = result + part
    return result


def along(way):
    return lax.axis_index("ha") // 2 if way == "z" else (lax.axis_index("ba") >> way) & 1


class Sum:
    def __init__(self, parts):
        bits = lax.axis_size("ba").bit_length() - 1
        self.parts = [part.reshape(part.shape[:1] + (2,) * bits + part.shape[2:]) for part in parts]
        self.ways = ["z"] + list(reversed(range(bits)))

    def leaving(self, way, step):
        return total(picked(self.parts, along(way) ^ step, self.ways.index(way)))

    def keep(self, way, got):
        self.parts = picked(self.parts, along(way), self.ways.index(way)) + got
        self.ways.remove(way)

    def result(self):
        return total(self.parts)


class Stage:
    def __init__(self, sums, way, riders=()):
        self.sums, self.way, self.riders = sums, way, list(riders)
        self.steps = range(1, lax.axis_size("ha") // 2) if way == "z" else [1]
        self.shapes, self.leaving = [], []
        for step in self.steps:
            leaving = [one.leaving(way, step) for one in sums]
            self.shapes = [part.shape for part in leaving]
            flat = [part.reshape(-1, LANES) for part in leaving] + self.riders
            self.leaving.append(flat[0] if len(flat) == 1 else jnp.concatenate(flat, axis=0))

    def go(self):
        axis, unit = ("ha", 2) if self.way == "z" else ("ba", 1 << self.way)
        arrived = [exchange(part, axis, unit * step) for step, part in zip(self.steps, self.leaving)]
        row = 0
        for one, shape in zip(self.sums, self.shapes):
            rows = 1
            for size in shape[:-1]:
                rows *= size
            one.keep(self.way, [part[row : row + rows].reshape(shape) for part in arrived])
            row += rows
        for k, rider in enumerate(self.riders):
            self.riders[k] = total([rider] + [part[row : row + rider.shape[0]] for part in arrived])
            row += rider.shape[0]
        return self.riders


def half_of(rows):
    core = lax.axis_index("ha") % 2
    both = rows.reshape(2, rows.shape[0] // 2, rows.shape[1])
    return total(picked([both], core, 0) + [exchange(picked([both], 1 - core, 0)[0], "ha", 1)])


def with_other_half(mine):
    core = lax.axis_index("ha") % 2
    other = exchange(mine, "ha", 1)
    return jnp.concatenate([jnp.where(core == 0, mine, other), jnp.where(core == 0, other, mine)], axis=0)


def beside(rows, tall, width):
    parts = [rows[k * tall : (k + 1) * tall] for k in range(lane_blocks(width))]
    return jnp.concatenate(parts, axis=1)[:, :width]


def neighbour_rows(top, bottom):
    count = lax.axis_size("ha")
    up = [(i, i + 1) for i in range(count - 1)]
    down = [(i + 1, i) for i in range(count - 1)]
    return lax.ppermute(bottom, "ha", up), lax.ppermute(top, "ha", down)


def after(values, token):
    return values + 0.0 * token[0, 0]


def shards(
    canvas,
    image_id,
    keep_first,
    keep_second,
    first_gain,
    weight_in,
    depth_kernel,
    gate_first,
    gate_second,
    gate_third,
    weight_out,
    scale_first,
    second_gain,
    weight_up,
    weight_down,
    scale_second,
    cotangent,
):
    _, rows, cols, dim = canvas.shape
    cells = rows * cols
    reach = REACH * cols
    count_ha, count_ba = lax.axis_size("ha"), lax.axis_size("ba")
    hidden = weight_up.shape[1]
    blocks = weight_in.shape[1] // LANES
    place = lax.axis_index("ha")[None]
    own = canvas.reshape(cells, dim)
    gates = (gate_first, gate_second, gate_third)
    gain = first_gain[None]
    vectors = (gain, scale_first[None], second_gain[None], scale_second[None])
    order = list(range(count_ba.bit_length() - 1))
    turned = order[len(order) // 2 :] + order[: len(order) // 2]

    ids = image_id[0]
    above, below = neighbour_rows(own[:reach], own[cells - reach :])
    (
        joined, output, dmiddle, dconv, dconv_top, dconv_bottom, up_kept, up_sent, down_kept, down_sent,
        out_kept, out_sent, packed_kept, packed_sent,
    ) = forward(
        place, ids, keep_first, keep_second, above, own, below, cotangent.reshape(cells, dim), vectors,
        weight_in, depth_kernel, gates, weight_out, weight_up, weight_down, rows, cols, count_ha, count_ba,
    )
    above, below = neighbour_rows(dconv_top, dconv_bottom)

    def back(first_block, end_block, before, written, ties):
        return backward(
            place, ids, above, dconv, below, joined, depth_kernel, own, gain, dmiddle, before,
            weight_in, first_block, end_block, written, ties, rows, cols, count_ha, count_ba,
        )

    up = Sum([up_kept, exchange(up_sent, "ha", 1)])
    down = Sum([down_kept, exchange(down_sent, "ha", 1)])
    out = Sum([out_kept, exchange(out_sent, "ha", 1)])
    packed = packed_kept + exchange(packed_sent, "ha", 1)
    stages = [Stage([up], order[0]), Stage([down, out], turned[0])]
    cut = blocks * 3 // 4
    dnorm, *written = back(0, cut, dmiddle, [], stages[0].leaving + stages[1].leaving)
    for stage in stages:
        stage.go()
    z_steps = [2 << k for k in range((count_ha // 2).bit_length() - 1)]
    packed = after(packed + exchange(packed, "ha", z_steps[0]), dnorm)
    stages = [Stage([up], order[1]), Stage([down, out], turned[1])]
    dcanvas, in_kept, in_sent, dkern = back(
        cut, blocks, dnorm, written, stages[0].leaving + stages[1].leaving + [packed]
    )
    for stage in stages:
        stage.go()
    for step in z_steps[1:]:
        packed = after(packed + exchange(packed, "ha", step), dcanvas)
    for first, second in zip(order[2:], turned[2:]):
        Stage([up], first).go()
        Stage([down, out], second).go()
    Stage([up, down, out], "z").go()
    parts = [in_kept, exchange(in_sent, "ha", 1)]
    middle_row = in_kept.shape[2] // 2
    in_first = Sum([part[:, :, :middle_row] for part in parts])
    in_second = Sum([part[:, :, middle_row:] for part in parts])
    small = half_of(dkern.reshape(-1, LANES))
    for first, second in zip(order, turned):
        (small,) = Stage([in_first], first, [small]).go()
        (packed,) = Stage([in_second], second, [packed]).go()
    sums = [after(one.result(), small) for one in (up, down, out)]
    (small,) = Stage([in_first, in_second], "z", [small]).go()
    din = jnp.concatenate([in_first.result(), in_second.result()], axis=0)
    dup, ddown, dout = sums
    dscale_one, dgain_two, dscale_two, dfirst, dsecond, dthird, dkern, dgain_one = unpack(
        with_other_half(packed), with_other_half(small).reshape(dkern.shape), gates, depth_kernel, dim
    )
    return (
        output.reshape(canvas.shape),
        dcanvas.reshape(canvas.shape),
        dgain_one[0],
        beside(din, dim // count_ba, weight_in.shape[1] // count_ha),
        dkern,
        dfirst,
        dsecond,
        dthird,
        beside(dout, dim // count_ha, dim // count_ba).T,
        dscale_one[0],
        dgain_two[0],
        beside(dup, dim // count_ba, hidden // count_ha),
        beside(ddown, dim // count_ha, hidden // count_ba).T,
        dscale_two[0],
    )


def solution(mesh):
    in_specs = (
        P("ba", "ha", None, None),
        P("ba", None, None),
        P("ba", None),
        P("ba", None),
    ) + (P(),) * 12 + (P("ba", "ha", None, None),)
    tiled = P("ba", "ha")
    out_specs = (
        P("ba", "ha", None, None),
        P("ba", "ha", None, None),
        P(),
        tiled,
        P(),
        P(),
        P(),
        P(),
        tiled,
        P(),
        P(),
        tiled,
        tiled,
        P(),
    )
    return jax.shard_map(shards, mesh=mesh, in_specs=in_specs, out_specs=out_specs, check_vma=False)
```

```python
import functools

import jax
import jax.numpy as jnp
from jax import lax
from jax.experimental import pallas as pl
from jax.experimental.pallas import tpu as pltpu
from jax.sharding import PartitionSpec as P

KERN = 7
TAPS = KERN * KERN
REACH = KERN // 2
KEEP_RATE = 0.8
SPREAD = 1.0 / 3.0
EPSILON = 1e-06
LANES = 128
EDGE = 8
VMEM_BYTES = 64 << 20
F32 = jnp.float32
INV_SQRT_2 = 0.7071067811865476
INV_SQRT_2PI = 0.3989422804014327
NN = (((1,), (0,)), ((), ()))
NT = (((1,), (1,)), ((), ()))
TN = (((0,), (0,)), ((), ()))


def dot(left, right, dims=NN):
    return lax.dot_general(left, right, dims, precision=lax.Precision.HIGH, preferred_element_type=F32)


def normalized(values):
    centered = values - jnp.mean(values, axis=-1, keepdims=True)
    scale = lax.rsqrt(jnp.mean(centered * centered, axis=-1, keepdims=True) + EPSILON)
    return centered * scale, scale


def norm_backward(grad_hat, hat, scale):
    return scale * (
        grad_hat
        - jnp.mean(grad_hat, axis=-1, keepdims=True)
        - hat * jnp.mean(grad_hat * hat, axis=-1, keepdims=True)
    )


def params():
    return pltpu.CompilerParams(vmem_limit_bytes=VMEM_BYTES)


def lasting(microseconds):
    return pl.CostEstimate(flops=int(microseconds * 1.1e9), bytes_accessed=0, transcendentals=0)


def whole(shape):
    return pl.BlockSpec(tuple(shape), lambda *_: (0,) * len(shape), pipeline_mode=pl.Buffered(1))


def in_smem():
    return pl.BlockSpec(memory_space=pltpu.SMEM)


def in_hbm():
    return pl.BlockSpec(memory_space=pltpu.HBM)


def shape_of(*shape):
    return jax.ShapeDtypeStruct(shape, F32)


def lane_blocks(width):
    return -(-width // LANES)


def image_ids(ids_ref, padded, place, rows):
    height, cols = ids_ref.shape
    padded[...] = jnp.full(padded.shape, -1, jnp.int32)
    padded[EDGE : EDGE + height, :] = ids_ref[...]
    ids = padded[pl.ds(place * rows + (EDGE - REACH), rows + 2 * REACH), :]
    return jnp.concatenate([ids, jnp.full((-ids.shape[0] % 8, cols), -1, jnp.int32)], axis=0).T


def spread_cells(factors, out_ref, first, rows):
    cols = factors.shape[0]
    for r in range(rows):
        column = factors[:, first + r : first + r + 1]
        out_ref[r * cols : (r + 1) * cols, :] = jnp.broadcast_to(column, (cols, LANES))


def keep_factors(turned, table_ref):
    result = jnp.zeros(turned.shape, F32)
    for slot in range(table_ref.shape[1]):
        result = jnp.where(turned == slot, table_ref[0, slot].astype(F32) / KEEP_RATE, result)
    return result


def conv_masks(ids_scalar, ids_ref, place, row_taps, col_mask, rows):
    height, cols = ids_ref.shape
    wide_ids = jnp.broadcast_to(ids_ref[...].T[:, height // 2 : height // 2 + 1], (cols, LANES))
    column = lax.broadcasted_iota(jnp.int32, (cols, LANES), 0)
    for b in range(KERN):
        shift = b - REACH
        moved = pltpu.roll(wide_ids, (-shift) % cols, 0)
        inside = (column + shift >= 0) & (column + shift < cols)
        same = (moved == wide_ids) & inside
        col_mask[b] = same.astype(F32).reshape(cols // 8, 8, LANES)

    def one(r, _):
        own = ids_scalar[place * rows + r, cols // 2]
        row_taps[r, 0] = KERN
        row_taps[r, KERN + 1] = KERN
        for a in range(KERN):
            other = place * rows + r + a - REACH
            inside = (other >= 0) & (other < height)
            same = ids_scalar[jnp.clip(other, 0, height - 1), cols // 2] == own
            row_taps[r, a + 1] = jnp.where(inside & same, a, KERN)
        return 0

    lax.fori_loop(0, rows, one, 0)


def lay_kernel(kern_ref, laid, split):
    tap = lax.broadcasted_iota(jnp.int32, (TAPS, split), 0)
    own = jnp.where(tap == TAPS // 2, 1.0 / SPREAD, 0.0).astype(F32)
    for k in range(laid.shape[0]):
        start = k * LANES - split
        left = own if k == 0 else kern_ref[:, start : start + split]
        laid[k] = jnp.concatenate([left, kern_ref[:, start + split : start + LANES]], axis=1) * SPREAD


def fill_shifted(flat, col_ref, shifted, rows_ext, cols):
    for b in range(KERN):
        for g in range(cols // 8):
            mask = None if b == REACH else col_ref[b, g]
            for r in range(rows_ext):
                x = flat[pl.ds(EDGE + r * cols + 8 * g + b - REACH, 8), :]
                shifted[b, r, g] = x if b == REACH else x * mask


def spread_taps(kern, wide, turned):
    for t in range(TAPS):
        source = TAPS - 1 - t if turned else t
        wide[t] = jnp.broadcast_to(kern[source : source + 1, :], (8, LANES))
    for t in range(KERN):
        wide[TAPS + t] = jnp.zeros((8, LANES), F32)


def conv_block(row_taps, kern, shifted, wide, out_ref, rows, cols, turned=False):
    groups = cols // 8
    spread_taps(kern, wide, turned)

    def pair(h, _):
        r = 2 * h

        def step(i, totals):
            first, second = totals
            taps_first = row_taps[r, i + 1] * KERN
            taps_second = row_taps[r + 1, i] * KERN
            for b in range(KERN):
                x = shifted[b, r + i]
                first = first + wide[taps_first + b][None] * x
                second = second + wide[taps_second + b][None] * x
            return first, second

        zero = jnp.zeros((groups, 8, LANES), F32)
        first, second = lax.fori_loop(0, KERN + 1, step, (zero, zero), unroll=4)
        out_ref[pl.ds(pl.multiple_of(r * cols, cols), cols), :] = first.reshape(cols, LANES)
        out_ref[pl.ds(pl.multiple_of((r + 1) * cols, cols), cols), :] = second.reshape(cols, LANES)
        return 0

    lax.fori_loop(0, rows // 2, pair, 0)


def kernel_grad_block(row_taps, shifted, dk, mix_ref, dk_ref, rows, cols):
    groups = cols // 8
    for t in range(TAPS):
        dk[t] = jnp.zeros((8, LANES), F32)

    def one(r, _):
        mix = mix_ref[pl.ds(pl.multiple_of(r * cols, cols), cols), :].reshape(groups, 8, LANES)
        for i in range(KERN):
            same = jnp.where(row_taps[r, i + 1] < KERN, 1.0, 0.0).astype(F32)
            for b in range(KERN):
                dk[i * KERN + b] += jnp.sum(mix * shifted[b, r + i], axis=0) * same
        return 0

    lax.fori_loop(0, rows, one, 0)
    for t in range(TAPS):
        dk_ref[TAPS - 1 - t : TAPS - t, :] = jnp.sum(dk[t], axis=0, keepdims=True) * SPREAD
    dk_ref[TAPS:, :] = jnp.zeros((dk_ref.shape[0] - TAPS, LANES), F32)


def share(core, first, second, kept_ref, sent_ref, z, p):
    mine = core == 0
    tall, width = first.shape
    for ref, chunk in (
        (kept_ref, jnp.where(mine, first, second)),
        (sent_ref, jnp.where(mine, second, first)),
    ):
        for k in range(lane_blocks(width)):
            part = chunk[:, k * LANES : (k + 1) * LANES]
            if part.shape[1] < LANES:
                part = jnp.concatenate([part, jnp.zeros((tall, LANES - part.shape[1]), F32)], axis=1)
            ref[z, p, k * tall : (k + 1) * tall, :] = part


def share_columns(core, grad, kept_ref, sent_ref, width):
    groups, parts = kept_ref.shape[:2]
    tall = grad.shape[0] // parts
    for z in range(groups):
        for p in range(parts):
            rows = slice(p * tall, (p + 1) * tall)
            first = grad[rows, 2 * z * width : (2 * z + 1) * width]
            second = grad[rows, (2 * z + 1) * width : (2 * z + 2) * width]
            share(core, first, second, kept_ref, sent_ref, z, p)


def share_rows(core, grad, kept_ref, sent_ref, tall):
    groups, parts = kept_ref.shape[:2]
    width = grad.shape[1] // parts
    for z in range(groups):
        for p in range(parts):
            columns = slice(p * width, (p + 1) * width)
            first = grad[2 * z * tall : (2 * z + 1) * tall, columns]
            second = grad[(2 * z + 1) * tall : (2 * z + 2) * tall, columns]
            share(core, first, second, kept_ref, sent_ref, z, p)


def forward_kernel(
    place_ref, ids_scalar, one_table, two_table, ids_ref, above_ref, own_ref, below_ref, cot_ref,
    first_gain_ref, first_scale_ref, second_gain_ref, second_scale_ref,
    in_ref, kern_ref, one_ref, two_ref, three_ref, out_ref, up_ref, down_ref,
    joined_ref, output_ref, dmiddle_ref, dconv_ref, dconv_top_ref, dconv_bottom_ref,
    up_kept_ref, up_sent_ref, down_kept_ref, down_sent_ref, out_kept_ref, out_sent_ref,
    packed_kept_ref, packed_sent_ref,
    row_taps, padded, valid_ref, one_keep_ref, two_keep_ref, col_ref, packed_ref, normed, flat, shifted, laid, wide, conv, mixed_ref, mapped_ref, middle_ref, result, dnorm,
    *, rows, cols, count_ha, count_ba,
):
    step = pl.program_id(0)
    blocks = flat.shape[0]
    cells = rows * cols
    reach = REACH * cols
    cells_ext = cells + 2 * reach
    core = place_ref[0] % 2
    split = one_ref.shape[0]
    dim = own_ref.shape[1]
    head_steps = blocks // 2
    ffn_first = head_steps + blocks
    gate_refs = (one_ref, two_ref, three_ref)

    @pl.when(step == 0)
    def _():
        lay_kernel(kern_ref, laid, split)
        turned = image_ids(ids_ref, padded, place_ref[0], rows)
        spread_cells((turned >= 0).astype(F32), valid_ref, 0, rows + 2 * REACH)
        spread_cells(keep_factors(turned, one_table), one_keep_ref, REACH, rows)
        spread_cells(keep_factors(turned, two_table), two_keep_ref, REACH, rows)
        conv_masks(ids_scalar, ids_ref, place_ref[0], row_taps, col_ref, rows)
        start = 0
        for ref in (above_ref, own_ref, below_ref):
            size = ref.shape[0]
            hat, _ = normalized(ref[...] * valid_ref[start : start + size, :1])
            normed[start : start + size] = hat * first_gain_ref[...]
            start += size

    @pl.when(step < head_steps)
    def _():
        joined = dot(normed[...], in_ref[...])
        for k in range(2):
            part = joined[:, k * LANES : (k + 1) * LANES]
            block = 2 * step + k
            flat[block, :EDGE] = jnp.zeros((EDGE, LANES), F32)
            flat[block, EDGE : EDGE + cells_ext] = part
            flat[block, EDGE + cells_ext :] = jnp.zeros((EDGE, LANES), F32)
            joined_ref[k] = part[reach : reach + cells]

    @pl.when((step >= head_steps) & (step < ffn_first))
    def _():
        block = step - head_steps
        fill_shifted(flat.at[block], col_ref, shifted, rows + 2 * REACH, cols)
        conv_block(row_taps, laid[block], shifted, wide, conv.at[block], rows, cols)

    def conv_part(start, width):
        return jnp.concatenate([conv[start // LANES + k] for k in range(width // LANES)], axis=1)

    @pl.when(step == ffn_first)
    def _():
        mixed = conv[0, :, :split] * conv[0, :, split:]
        mixed_ref[:, :split] = mixed
        start = 2 * split
        for ref in gate_refs:
            width = ref.shape[1]
            mapped = dot(mixed, ref[...])
            mapped_ref[:, start - 2 * split : start - 2 * split + width] = mapped
            mixed = mapped * conv_part(start, width)
            mixed_ref[:, start : start + width] = mixed
            start += width
        branch = dot(mixed, out_ref[...])
        masked = own_ref[...] * valid_ref[reach : reach + cells, :1]
        middle = masked + one_keep_ref[:, :1] * first_scale_ref[...] * branch
        middle_ref[...] = middle
        hat, _ = normalized(middle)
        normed[:cells] = hat * second_gain_ref[...]
        normed[cells : cells + reach] = jnp.zeros((reach, dim), F32)
        result[...] = jnp.zeros_like(result)
        dnorm[...] = jnp.zeros_like(dnorm)

    @pl.when(step >= ffn_first)
    def _():
        grad_result = two_keep_ref[:, :1] * second_scale_ref[...] * cot_ref[...]
        pre = dot(normed[:cells], up_ref[...])
        cdf = 0.5 + 0.5 * lax.erf(pre * INV_SQRT_2)
        slope = cdf + pre * (INV_SQRT_2PI * jnp.exp(-0.5 * pre * pre))
        hidden = pre * cdf
        result[...] += dot(hidden, down_ref[...])
        grad_pre = dot(grad_result, down_ref[...], NT) * slope
        share_rows(core, dot(grad_result, hidden, TN), down_kept_ref, down_sent_ref, dim // count_ha)
        width = down_ref.shape[0] // (2 * up_kept_ref.shape[0])
        share_columns(core, dot(normed[:cells], grad_pre, TN), up_kept_ref, up_sent_ref, width)
        dnorm[...] += dot(grad_pre, up_ref[...], NT)

    @pl.when(step == pl.num_programs(0) - 1)
    def _():
        hat, scale = normalized(middle_ref[...])
        kept = two_keep_ref[:, :1] * result[...]
        output_ref[...] = middle_ref[...] + second_scale_ref[...] * kept
        dscale_two = jnp.sum(cot_ref[...] * kept, axis=0, keepdims=True)
        dgain_two = jnp.sum(dnorm[...] * hat, axis=0, keepdims=True)
        dmiddle = cot_ref[...] + norm_backward(dnorm[...] * second_gain_ref[...], hat, scale)
        dmiddle_ref[...] = dmiddle
        kept = one_keep_ref[:, :1] * dmiddle
        start = mixed_ref.shape[1] - out_ref.shape[0]
        crossed = dot(mixed_ref[:, start:], kept, TN)
        dscale_one = jnp.sum(crossed * out_ref[...], axis=0, keepdims=True)
        share_rows(core, (crossed * first_scale_ref[...]).T, out_kept_ref, out_sent_ref, dim // count_ha)
        grad = dot(kept * first_scale_ref[...], out_ref[...], NT)
        row = packed_ref.shape[0]
        start = blocks * LANES
        for ref in reversed(gate_refs):
            tall, width = ref.shape
            start -= width
            source = start - tall if tall > split else 0
            columns = slice(start - 2 * split, start - 2 * split + width)
            dconv = grad * mapped_ref[:, columns]
            for k in range(width // LANES):
                dconv_ref[start // LANES + k] = dconv[:, k * LANES : (k + 1) * LANES]
            grad_mapped = grad * conv_part(start, width)
            part = dot(mixed_ref[:, source : source + tall], grad_mapped, TN)
            row -= tall * width // LANES
            for k in range(width // LANES):
                packed_ref[row + k * tall : row + (k + 1) * tall] = part[:, k * LANES : (k + 1) * LANES]
            grad = dot(grad_mapped, ref[...], NT)
        dconv_ref[0] = jnp.concatenate([grad * conv[0, :, split:], grad * conv[0, :, :split]], axis=1)
        packed_ref[:row] = jnp.zeros((row, LANES), F32)
        row = 0
        for vector in (dscale_one, dgain_two, dscale_two):
            for k in range(dim // LANES):
                packed_ref[row : row + 1] = vector[:, k * LANES : (k + 1) * LANES]
                row += 1
        half = packed_kept_ref.shape[0]
        packed_kept_ref[...] = packed_ref[pl.ds(pl.multiple_of(core * half, 8), half), :]
        packed_sent_ref[...] = packed_ref[pl.ds(pl.multiple_of((1 - core) * half, 8), half), :]
        dconv_top_ref[...] = dconv_ref[:, :reach, :]
        dconv_bottom_ref[...] = dconv_ref[:, cells - reach :, :]


def mask_scratch(ids, rows):
    height, cols = ids.shape
    return [
        pltpu.SMEM((rows, KERN + 2), jnp.int32),
        pltpu.VMEM((height + 2 * EDGE, cols), jnp.int32),
        pltpu.VMEM(((rows + 2 * REACH) * cols, LANES), F32),
    ]


def packed_rows(gates, dim):
    rows = sum(gate.size for gate in gates) // LANES + 3 * dim // LANES
    return -(-rows // 16) * 16


def forward(
    place, ids, keep_one, keep_two, above, own, below, cot, vectors, weight_in, kern, gates,
    weight_out, weight_up, weight_down, rows, cols, count_ha, count_ba, chunk=512,
):
    cells, dim = own.shape
    reach = above.shape[0]
    blocks = weight_in.shape[1] // LANES
    hidden = weight_up.shape[1]
    split = gates[0].shape[0]
    wide = blocks * LANES
    head_steps = blocks // 2
    ffn_first = head_steps + blocks
    ffn_steps = hidden // chunk

    def ffn_step(i):
        return jnp.clip(i - ffn_first, 0, ffn_steps - 1)

    up_wide, down_wide = hidden // count_ha, hidden // count_ba
    up_rows = dim // count_ba * lane_blocks(up_wide)
    down_rows = dim // count_ha * lane_blocks(down_wide)
    out_rows = dim // count_ha * lane_blocks(dim // count_ba)
    half = count_ha // 2
    up_spec = pl.BlockSpec((chunk // (2 * up_wide), count_ba, up_rows, LANES), lambda i: (ffn_step(i), 0, 0, 0))
    down_spec = pl.BlockSpec((half, chunk // down_wide, down_rows, LANES), lambda i: (0, ffn_step(i), 0, 0))
    out_shape = (half, count_ba, out_rows, LANES)
    packed_shape = (packed_rows(gates, dim), LANES)
    half_packed = (packed_shape[0] // 2, LANES)
    cells_ext = cells + 2 * reach
    return pl.pallas_call(
        functools.partial(forward_kernel, rows=rows, cols=cols, count_ha=count_ha, count_ba=count_ba),
        grid=(ffn_first + ffn_steps,),
        in_specs=[in_smem()] * 4
        + [whole(x.shape) for x in (ids, above, own, below, cot)]
        + [whole((1, dim))] * 4
        + [
            pl.BlockSpec((dim, 2 * LANES), lambda i: (0, jnp.minimum(i, head_steps - 1))),
            whole(kern.shape),
        ]
        + [whole(gate.shape) for gate in gates]
        + [
            whole(weight_out.shape),
            pl.BlockSpec((dim, chunk), lambda i: (0, ffn_step(i))),
            pl.BlockSpec((chunk, dim), lambda i: (ffn_step(i), 0)),
        ],
        out_specs=[
            pl.BlockSpec((2, cells, LANES), lambda i: (jnp.minimum(i, head_steps - 1), 0, 0)),
            whole((cells, dim)),
            whole((cells, dim)),
            whole((blocks, cells, LANES)),
            whole((blocks, reach, LANES)),
            whole((blocks, reach, LANES)),
            up_spec,
            up_spec,
            down_spec,
            down_spec,
            whole(out_shape),
            whole(out_shape),
            whole(half_packed),
            whole(half_packed),
        ],
        out_shape=[
            shape_of(blocks, cells, LANES),
            shape_of(cells, dim),
            shape_of(cells, dim),
            shape_of(blocks, cells, LANES),
            shape_of(blocks, reach, LANES),
            shape_of(blocks, reach, LANES),
            shape_of(half, count_ba, up_rows, LANES),
            shape_of(half, count_ba, up_rows, LANES),
            shape_of(half, count_ba, down_rows, LANES),
            shape_of(half, count_ba, down_rows, LANES),
            shape_of(*out_shape),
            shape_of(*out_shape),
            shape_of(*half_packed),
            shape_of(*half_packed),
        ],
        scratch_shapes=mask_scratch(ids, rows)
        + [
            pltpu.VMEM((cells, LANES), F32),
            pltpu.VMEM((cells, LANES), F32),
            pltpu.VMEM((KERN, cols // 8, 8, LANES), F32),
            pltpu.VMEM(packed_shape, F32),
            pltpu.VMEM((cells_ext, dim), F32),
            pltpu.VMEM((blocks, cells_ext + 2 * EDGE, LANES), F32),
            pltpu.VMEM((KERN, rows + 2 * REACH, cols // 8, 8, LANES), F32),
            pltpu.VMEM((blocks, TAPS, LANES), F32),
            pltpu.VMEM((TAPS + KERN, 8, LANES), F32),
            pltpu.VMEM((blocks, cells, LANES), F32),
            pltpu.VMEM((cells, wide), F32),
            pltpu.VMEM((cells, wide - 2 * split), F32),
            pltpu.VMEM((cells, dim), F32),
            pltpu.VMEM((cells, dim), F32),
            pltpu.VMEM((cells, dim), F32),
        ],
        compiler_params=params(),
        cost_estimate=lasting(55),
    )(
        place, ids, keep_one, keep_two, ids, above, own, below, cot, *vectors,
        weight_in, kern, *gates, weight_out, weight_up, weight_down,
    )


def lay_flat(above_ref, own_ref, below_ref, flat):
    reach, cells = above_ref.shape[1], own_ref.shape[1]
    flat[:EDGE] = jnp.zeros((EDGE, LANES), F32)
    flat[EDGE : EDGE + reach] = above_ref[0]
    flat[EDGE + reach : EDGE + reach + cells] = own_ref[0]
    flat[EDGE + reach + cells : EDGE + 2 * reach + cells] = below_ref[0]
    flat[EDGE + 2 * reach + cells :] = jnp.zeros((EDGE, LANES), F32)


def backward_kernel(
    place_ref, ids_scalar, ids_ref, above_ref, own_ref, below_ref, kern_ref, canvas_ref, gain_ref,
    dmiddle_ref, in_ref, *rest, rows, cols,
):
    dcanvas_ref, kept_ref, sent_ref, dgain_ref = rest[-15:-11]
    row_taps, padded, valid_ref, col_ref, flat, shifted, laid, wide, djoined, normed, dnorm = rest[-11:]
    step = pl.program_id(0)
    cells = rows * cols
    reach = REACH * cols
    core = place_ref[0] % 2
    split = laid.shape[0] * LANES - kern_ref.shape[1]
    width = in_ref.shape[1] // (2 * kept_ref.shape[0])

    @pl.when(step == 0)
    def _():
        lay_kernel(kern_ref, laid, split)
        turned = image_ids(ids_ref, padded, place_ref[0], rows)
        spread_cells((turned >= 0).astype(F32), valid_ref, 0, rows + 2 * REACH)
        conv_masks(ids_scalar, ids_ref, place_ref[0], row_taps, col_ref, rows)
        hat, _ = normalized(canvas_ref[...] * valid_ref[reach : reach + cells, :1])
        normed[...] = hat * gain_ref[...]
        dnorm[...] = jnp.zeros_like(dnorm)

    lay_flat(above_ref, own_ref, below_ref, flat)
    fill_shifted(flat, col_ref, shifted, rows + 2 * REACH, cols)
    conv_block(row_taps, laid[step], shifted, wide, djoined.at[step % 2], rows, cols, turned=True)

    @pl.when(step % 2 == 1)
    def _():
        grad = jnp.concatenate([djoined[0], djoined[1]], axis=1)
        share_columns(core, dot(normed[...], grad, TN), kept_ref, sent_ref, width)
        dnorm[...] += dot(grad, in_ref[...], NT)

    @pl.when(step == pl.num_programs(0) - 1)
    def _():
        hat, scale = normalized(canvas_ref[...] * valid_ref[reach : reach + cells, :1])
        dgain = jnp.sum(dnorm[...] * hat, axis=0, keepdims=True)
        dgain_ref[...] = jnp.zeros_like(dgain_ref)
        for k in range(dgain.shape[1] // LANES):
            dgain_ref[k : k + 1] = dgain[:, k * LANES : (k + 1) * LANES]
        inner = dmiddle_ref[...] + norm_backward(dnorm[...] * gain_ref[...], hat, scale)
        dcanvas_ref[...] = inner * valid_ref[reach : reach + cells, :1]


def block_of(size):
    return pl.BlockSpec((1, size, LANES), lambda i: (i, 0, 0))


def backward(
    place, ids, above, own, below, kern, canvas, gain, dmiddle, weight_in, ties, rows, cols, count_ha, count_ba
):
    cells, dim = canvas.shape
    blocks = own.shape[0]
    reach = above.shape[1]
    own_wide = weight_in.shape[1] // count_ha
    chunk_rows = dim // count_ba * lane_blocks(own_wide)
    groups = 2 * LANES // (2 * own_wide)
    chunk_spec = pl.BlockSpec((groups, count_ba, chunk_rows, LANES), lambda i: (i // 2, 0, 0, 0))
    chunks = shape_of(count_ha // 2, count_ba, chunk_rows, LANES)
    gain_shape = (-(-dim // LANES // 8) * 8, LANES)
    return pl.pallas_call(
        functools.partial(backward_kernel, rows=rows, cols=cols),
        grid=(blocks,),
        in_specs=[in_smem(), in_smem(), whole(ids.shape)]
        + [block_of(size) for size in (reach, cells, reach)]
        + [whole(kern.shape), whole(canvas.shape)]
        + [whole((1, dim)), whole((cells, dim))]
        + [pl.BlockSpec((dim, 2 * LANES), lambda i: (0, i // 2))]
        + [in_hbm()] * len(ties),
        out_specs=[whole((cells, dim)), chunk_spec, chunk_spec, whole(gain_shape)],
        out_shape=[shape_of(cells, dim), chunks, chunks, shape_of(*gain_shape)],
        scratch_shapes=mask_scratch(ids, rows)
        + [
            pltpu.VMEM((KERN, cols // 8, 8, LANES), F32),
            pltpu.VMEM((cells + 2 * reach + 2 * EDGE, LANES), F32),
            pltpu.VMEM((KERN, rows + 2 * REACH, cols // 8, 8, LANES), F32),
            pltpu.VMEM((blocks, TAPS, LANES), F32),
            pltpu.VMEM((TAPS + KERN, 8, LANES), F32),
            pltpu.VMEM((2, cells, LANES), F32),
            pltpu.VMEM((cells, dim), F32),
            pltpu.VMEM((cells, dim), F32),
        ],
        compiler_params=params(),
        cost_estimate=lasting(20),
    )(place, ids, ids, above, own, below, kern, canvas, gain, dmiddle, weight_in, *ties)


def kernel_grad_kernel(
    place_ref, ids_scalar, ids_ref, above_ref, own_ref, below_ref, mix_ref, dgain_ref, *rest, rows, cols
):
    kept_ref, sent_ref, row_taps, padded, valid_ref, col_ref, flat, shifted, dk, sums = rest[-10:]
    step = pl.program_id(0)

    @pl.when(step == 0)
    def _():
        conv_masks(ids_scalar, ids_ref, place_ref[0], row_taps, col_ref, rows)

    lay_flat(above_ref, own_ref, below_ref, flat)
    fill_shifted(flat, col_ref, shifted, rows + 2 * REACH, cols)
    kernel_grad_block(row_taps, shifted, dk, mix_ref.at[0], sums.at[step], rows, cols)

    @pl.when(step == pl.num_programs(0) - 1)
    def _():
        count = sums.shape[0]
        spare = sums.shape[1] - TAPS
        sums[count - 1, TAPS:] = dgain_ref[:spare]
        core = place_ref[0] % 2
        half = count // 2
        for ref, start in ((kept_ref, core * half), (sent_ref, (1 - core) * half)):
            ref[...] = sums[pl.ds(start, half)].reshape(ref.shape)


def kernel_grad(place, ids, above, own, below, mix, dgain, ties, rows, cols, dim):
    blocks, cells, _ = own.shape
    reach = above.shape[1]
    tall = -(-(TAPS + dim // LANES) // 8) * 8
    half = (blocks // 2 * tall, LANES)
    return pl.pallas_call(
        functools.partial(kernel_grad_kernel, rows=rows, cols=cols),
        grid=(blocks,),
        in_specs=[in_smem(), in_smem(), whole(ids.shape)]
        + [block_of(size) for size in (reach, cells, reach, cells)]
        + [whole(dgain.shape)]
        + [in_hbm()] * len(ties),
        out_specs=[whole(half), whole(half)],
        out_shape=[shape_of(*half), shape_of(*half)],
        scratch_shapes=mask_scratch(ids, rows)
        + [
            pltpu.VMEM((KERN, cols // 8, 8, LANES), F32),
            pltpu.VMEM((cells + 2 * reach + 2 * EDGE, LANES), F32),
            pltpu.VMEM((KERN, rows + 2 * REACH, cols // 8, 8, LANES), F32),
            pltpu.VMEM((TAPS, 8, LANES), F32),
            pltpu.VMEM((blocks, tall, LANES), F32),
        ],
        compiler_params=params(),
        cost_estimate=lasting(11),
    )(place, ids, ids, above, own, below, mix, dgain, *ties)


def exchange(values, axis, bit):
    return lax.ppermute(values, axis, [(i, i ^ bit) for i in range(lax.axis_size(axis))])


class View:
    def __init__(self, array, start, ways, fixed, rows):
        self.array, self.start, self.ways, self.fixed, self.rows = array, start, ways, fixed, rows

    def fix(self, way, step):
        left = [entry for entry in self.ways if entry[0] != way]
        (stride,) = [entry[2] for entry in self.ways if entry[0] == way]
        return View(self.array, self.start, left, self.fixed + [(way, step, stride)], self.rows)

    def size(self):
        count = self.rows
        for _, size, _ in self.ways:
            count *= size
        return count

    def runs(self, ha, ba):
        start = self.start
        for way, step, stride in self.fixed:
            place = ha // 2 if way == "z" else (ba >> way) & 1
            start = start + (place ^ step) * stride
        offsets = [0]
        for _, size, stride in self.ways:
            offsets = [offset + k * stride for offset in offsets for k in range(size)]
        return [pl.multiple_of(start + offset, 8) for offset in offsets]


def plain(array):
    rows = array.reshape(-1, LANES)
    return [View(rows, 0, [], [], rows.shape[0])]


def combine(place, groups, ties=(), epilogue=None, out_shape=None):
    pieces = [views for group in groups for views in group]
    arrays = []
    for views in pieces:
        for view in views:
            if not any(view.array is other for other in arrays):
                arrays.append(view.array)
    index_of = {id(array): k for k, array in enumerate(arrays)}
    sizes = [sum(views[0].size() for views in group) for group in groups]
    copies = sum(view.size() // view.rows for views in pieces for view in views)
    if epilogue is None:
        out_shape = [shape_of(size, LANES) for size in sizes]

    def kernel(place_ref, *refs):
        inputs = refs[: len(arrays)]
        refs = refs[len(arrays) + len(ties) :]
        outs, (buffers, sems) = refs[: len(out_shape)], (refs[len(out_shape) : -1], refs[-1])
        ha, ba = place_ref[0], place_ref[1]
        moves, count = [], 0
        for piece, views in enumerate(pieces):
            moves.append([])
            for term, view in enumerate(views):
                source = inputs[index_of[id(view.array)]]
                for k, start in enumerate(view.runs(ha, ba)):
                    target = buffers[piece].at[term, pl.ds(k * view.rows, view.rows), :]
                    moves[-1].append(
                        pltpu.make_async_copy(source.at[pl.ds(start, view.rows), :], target, sems.at[count])
                    )
                    moves[-1][-1].start()
                    count += 1
        piece = 0
        values = []
        for out, group in enumerate(groups):
            row = 0
            for views in group:
                for move in moves[piece]:
                    move.wait()
                value = buffers[piece][0]
                for term in range(1, len(views)):
                    value = value + buffers[piece][term]
                if epilogue is None:
                    outs[out][row : row + value.shape[0], :] = value
                values.append(value)
                row += value.shape[0]
                piece += 1
        if epilogue is not None:
            epilogue(ha, values, outs)

    moved = sum(view.size() for views in pieces for view in views) + sum(sizes)
    return pl.pallas_call(
        kernel,
        in_specs=[in_smem()] + [in_hbm()] * (len(arrays) + len(ties)),
        out_specs=[pl.BlockSpec(memory_space=pltpu.VMEM)] * len(out_shape),
        out_shape=out_shape,
        scratch_shapes=[pltpu.VMEM((len(views), views[0].size(), LANES), F32) for views in pieces]
        + [pltpu.SemaphoreType.DMA((copies,))],
        compiler_params=params(),
        cost_estimate=lasting(1 + moved * LANES * 4 / 3.0e6),
    )(place, *arrays, *ties)


class Sum:
    def __init__(self, arrays, first=0, last=None):
        self.views = []
        bits = lax.axis_size("ba").bit_length() - 1
        for array in arrays:
            groups, parts, rows, _ = array.shape
            ways = [("z", groups, parts * rows)] + [(bit, 2, rows << bit) for bit in reversed(range(bits))]
            end = rows if last is None else last
            self.views.append(View(array.reshape(-1, LANES), first, ways, [], end - first))

    def leaving(self, way, step):
        return [view.fix(way, step) for view in self.views]

    def keep(self, way, arrived):
        self.views = [view.fix(way, 0) for view in self.views]
        for array, start in arrived:
            stride, ways = self.views[0].rows, []
            for name, size, _ in reversed(self.views[0].ways):
                ways.insert(0, (name, size, stride))
                stride *= size
            self.views.append(View(array, start, ways, [], self.views[0].rows))


class Rider:
    def __init__(self, views):
        self.views = views

    def leaving(self, way, step):
        return self.views

    def keep(self, way, arrived):
        rows = self.views[0].size()
        self.views = self.views + [View(array, start, [], [], rows) for array, start in arrived]

    def settle(self, array, start=0):
        self.views = [View(array, start, [], [], self.views[0].size())]


class Stage:
    def __init__(self, sums, way):
        self.sums, self.way = sums, way
        self.steps = range(1, lax.axis_size("ha") // 2) if way == "z" else [1]

    def groups(self):
        return [[one.leaving(self.way, step) for one in self.sums] for step in self.steps]

    def go(self, payloads):
        axis, unit = ("ha", 2) if self.way == "z" else ("ba", 1 << self.way)
        arrived = [exchange(part, axis, unit * step) for step, part in zip(self.steps, payloads)]
        row = 0
        for one in self.sums:
            rows = sum(view.size() for view in one.leaving(self.way, 1)[:1])
            if isinstance(one, Rider):
                one.settle(payloads[0], row)
            one.keep(self.way, [(part, row) for part in arrived])
            row += rows
        return arrived


def run(place, stages, ties=(), extra=()):
    groups = [group for stage in stages for group in stage.groups()]
    made = combine(place, groups + list(extra), ties)
    rest, arrived = made, []
    for stage in stages:
        count = len(stage.steps)
        arrived += stage.go(rest[:count])
        rest = rest[count:]
    return made, rest, arrived


def neighbour_rows(top, bottom):
    count = lax.axis_size("ha")
    up = [(i, i + 1) for i in range(count - 1)]
    down = [(i + 1, i) for i in range(count - 1)]
    return lax.ppermute(bottom, "ha", up), lax.ppermute(top, "ha", down)


def lay_out(ha, values, outs, blocks):
    first, second, up, down, out, small, small_other, packed, packed_other = values
    din_ref, dup_ref, ddown_ref, dout_ref, dk_ref, gain_ref = outs[:6]
    whole_in = jnp.concatenate([first, second], axis=0)
    for value, ref in ((whole_in, din_ref), (up, dup_ref), (down, ddown_ref), (out, dout_ref)):
        tall, width = ref.shape
        for k in range(lane_blocks(width)):
            columns = slice(k * LANES, min(width, (k + 1) * LANES))
            ref[:, columns] = value[k * tall : (k + 1) * tall, : columns.stop - columns.start]
    mine = ha % 2 == 0
    dkern, packed = (
        jnp.concatenate([jnp.where(mine, own, other), jnp.where(mine, other, own)], axis=0)
        for own, other in ((small, small_other), (packed, packed_other))
    )
    tall = dkern.shape[0] // blocks
    joined = jnp.concatenate([dkern[k * tall : k * tall + TAPS] for k in range(blocks)], axis=1)
    dk_ref[...] = joined[:, joined.shape[1] - dk_ref.shape[1] :]
    dim = gain_ref.shape[1]
    vectors = [(gain_ref, dkern, (blocks - 1) * tall + TAPS)]
    vectors += [(ref, packed, k * dim // LANES) for k, ref in enumerate(outs[6:9])]
    for ref, rows, start in vectors:
        for k in range(dim // LANES):
            ref[:, k * LANES : (k + 1) * LANES] = rows[start + k : start + k + 1]
    row = packed.shape[0]
    for ref in reversed(outs[9:]):
        tall, width = ref.shape
        row -= tall * width // LANES
        for k in range(width // LANES):
            ref[:, k * LANES : (k + 1) * LANES] = packed[row + k * tall : row + (k + 1) * tall]


def shards(
    canvas,
    image_id,
    keep_first,
    keep_second,
    first_gain,
    weight_in,
    depth_kernel,
    gate_first,
    gate_second,
    gate_third,
    weight_out,
    scale_first,
    second_gain,
    weight_up,
    weight_down,
    scale_second,
    cotangent,
):
    _, rows, cols, dim = canvas.shape
    cells = rows * cols
    reach = REACH * cols
    count_ha, count_ba = lax.axis_size("ha"), lax.axis_size("ba")
    hidden = weight_up.shape[1]
    blocks = weight_in.shape[1] // LANES
    place = jnp.stack([lax.axis_index("ha"), lax.axis_index("ba")])
    own = canvas.reshape(cells, dim)
    gates = (gate_first, gate_second, gate_third)
    gain = first_gain[None]
    vectors = (gain, scale_first[None], second_gain[None], scale_second[None])
    order = list(range(count_ba.bit_length() - 1))
    turned = order[len(order) // 2 :] + order[: len(order) // 2]

    ids = image_id[0]
    above, below = neighbour_rows(own[:reach], own[cells - reach :])
    (
        joined, output, dmiddle, dconv, dconv_top, dconv_bottom, up_kept, up_sent, down_kept, down_sent,
        out_kept, out_sent, packed_kept, packed_sent,
    ) = forward(
        place, ids, keep_first, keep_second, above, own, below, cotangent.reshape(cells, dim), vectors,
        weight_in, depth_kernel, gates, weight_out, weight_up, weight_down, rows, cols, count_ha, count_ba,
    )
    above, below = neighbour_rows(dconv_top, dconv_bottom)

    up = Sum([up_kept, exchange(up_sent, "ha", 1)])
    down = Sum([down_kept, exchange(down_sent, "ha", 1)])
    out = Sum([out_kept, exchange(out_sent, "ha", 1)])
    packed = plain(packed_kept) + plain(exchange(packed_sent, "ha", 1))
    made, (packed,), _ = run(place, [Stage([up], order[0]), Stage([down, out], turned[0])], extra=[[packed]])
    ring = [[2 * z + core for z in range(count_ha // 2)] for core in range(2)]
    packed = lax.psum(packed, "ha", axis_index_groups=ring)
    dcanvas, in_kept, in_sent, dgain_one = backward(
        place, ids, above, dconv, below, depth_kernel, own, gain, dmiddle, weight_in, made,
        rows, cols, count_ha, count_ba,
    )
    in_got = exchange(in_sent, "ha", 1)
    made, _, _ = run(place, [Stage([up], order[1]), Stage([down, out], turned[1])], ties=[dcanvas])
    small_kept, small_sent = kernel_grad(place, ids, above, dconv, below, joined, dgain_one, made, rows, cols, dim)
    small = Rider(plain(small_kept) + plain(exchange(small_sent, "ha", 1)))
    for first, second in zip(order[2:], turned[2:]):
        run(place, [Stage([up], first), Stage([down, out], second)])
    ahead, _, arrived = run(place, [Stage([up, down, out], "z")], ties=[small_kept])
    middle_row = in_kept.shape[2] // 2
    in_first = Sum([in_kept, in_got], 0, middle_row)
    in_second = Sum([in_kept, in_got], middle_row)
    packed = Rider(plain(packed))
    for first, second in zip(order, turned):
        run(place, [Stage([in_first, small], first), Stage([in_second, packed], second)], ties=ahead)
        ahead = arrived[: len(arrived) * 2 // 3]
    _, (packed, up, down, out), _ = run(
        place,
        [Stage([in_first, in_second, small], "z")],
        extra=[[packed.views], [up.views], [down.views], [out.views]],
    )
    (small,) = combine(place, [[small.views]])
    din, dup, ddown, dout, dkern, dgain_one, dscale_one, dgain_two, dscale_two, dfirst, dsecond, dthird = combine(
        place,
        [
            [
                in_first.views,
                in_second.views,
                plain(up),
                plain(down),
                plain(out),
                plain(small),
                plain(exchange(small, "ha", 1)),
                plain(packed),
                plain(exchange(packed, "ha", 1)),
            ]
        ],
        epilogue=functools.partial(lay_out, blocks=blocks),
        out_shape=[
            shape_of(dim // count_ba, weight_in.shape[1] // count_ha),
            shape_of(dim // count_ba, hidden // count_ha),
            shape_of(dim // count_ha, hidden // count_ba),
            shape_of(dim // count_ha, dim // count_ba),
            shape_of(*depth_kernel.shape),
        ]
        + [shape_of(1, dim)] * 4
        + [shape_of(*gate.shape) for gate in gates],
    )
    return (
        output.reshape(canvas.shape),
        dcanvas.reshape(canvas.shape),
        dgain_one[0],
        din,
        dkern,
        dfirst,
        dsecond,
        dthird,
        dout.T,
        dscale_one[0],
        dgain_two[0],
        dup,
        ddown.T,
        dscale_two[0],
    )


def solution(mesh):
    in_specs = (
        P("ba", "ha", None, None),
        P("ba", None, None),
        P("ba", None),
        P("ba", None),
    ) + (P(),) * 12 + (P("ba", "ha", None, None),)
    tiled = P("ba", "ha")
    out_specs = (
        P("ba", "ha", None, None),
        P("ba", "ha", None, None),
        P(),
        tiled,
        P(),
        P(),
        P(),
        P(),
        tiled,
        P(),
        P(),
        tiled,
        tiled,
        P(),
    )
    return jax.shard_map(shards, mesh=mesh, in_specs=in_specs, out_specs=out_specs, check_vma=False)
```

```python
import functools

import jax
import jax.numpy as jnp
from jax import lax
from jax.experimental import pallas as pl
from jax.experimental.pallas import tpu as pltpu
from jax.sharding import PartitionSpec as P

KERN = 7
TAPS = KERN * KERN
REACH = KERN // 2
KEEP_RATE = 0.8
SPREAD = 1.0 / 3.0
EPSILON = 1e-06
LANES = 128
EDGE = 8
VMEM_BYTES = 64 << 20
F32 = jnp.float32
INV_SQRT_2 = 0.7071067811865476
INV_SQRT_2PI = 0.3989422804014327
NN = (((1,), (0,)), ((), ()))
NT = (((1,), (1,)), ((), ()))
TN = (((0,), (0,)), ((), ()))


def dot(left, right, dims=NN):
    return lax.dot_general(left, right, dims, precision=lax.Precision.HIGH, preferred_element_type=F32)


def normalized(values):
    centered = values - jnp.mean(values, axis=-1, keepdims=True)
    scale = lax.rsqrt(jnp.mean(centered * centered, axis=-1, keepdims=True) + EPSILON)
    return centered * scale, scale


def norm_backward(grad_hat, hat, scale):
    return scale * (
        grad_hat
        - jnp.mean(grad_hat, axis=-1, keepdims=True)
        - hat * jnp.mean(grad_hat * hat, axis=-1, keepdims=True)
    )


def params():
    return pltpu.CompilerParams(vmem_limit_bytes=VMEM_BYTES)


def lasting(microseconds):
    return pl.CostEstimate(flops=int(microseconds * 1.1e9), bytes_accessed=0, transcendentals=0)


def whole(shape):
    return pl.BlockSpec(tuple(shape), lambda *_: (0,) * len(shape), pipeline_mode=pl.Buffered(1))


def in_smem():
    return pl.BlockSpec(memory_space=pltpu.SMEM)


def in_hbm():
    return pl.BlockSpec(memory_space=pltpu.HBM)


def shape_of(*shape):
    return jax.ShapeDtypeStruct(shape, F32)


def lane_blocks(width):
    return -(-width // LANES)


def image_ids(ids_ref, padded, place, rows):
    height, cols = ids_ref.shape
    padded[...] = jnp.full(padded.shape, -1, jnp.int32)
    padded[EDGE : EDGE + height, :] = ids_ref[...]
    ids = padded[pl.ds(place * rows + (EDGE - REACH), rows + 2 * REACH), :]
    return jnp.concatenate([ids, jnp.full((-ids.shape[0] % 8, cols), -1, jnp.int32)], axis=0).T


def spread_cells(factors, out_ref, first, rows):
    cols = factors.shape[0]
    for r in range(rows):
        column = factors[:, first + r : first + r + 1]
        out_ref[r * cols : (r + 1) * cols, :] = jnp.broadcast_to(column, (cols, LANES))


def keep_factors(turned, table_ref):
    result = jnp.zeros(turned.shape, F32)
    for slot in range(table_ref.shape[1]):
        result = jnp.where(turned == slot, table_ref[0, slot].astype(F32) / KEEP_RATE, result)
    return result


def conv_masks(ids_scalar, ids_ref, place, row_taps, col_mask, rows):
    height, cols = ids_ref.shape
    wide_ids = jnp.broadcast_to(ids_ref[...].T[:, height // 2 : height // 2 + 1], (cols, LANES))
    column = lax.broadcasted_iota(jnp.int32, (cols, LANES), 0)
    for b in range(KERN):
        shift = b - REACH
        moved = pltpu.roll(wide_ids, (-shift) % cols, 0)
        inside = (column + shift >= 0) & (column + shift < cols)
        same = (moved == wide_ids) & inside
        col_mask[b] = same.astype(F32).reshape(cols // 8, 8, LANES)

    def one(r, _):
        own = ids_scalar[place * rows + r, cols // 2]
        row_taps[r, 0] = KERN
        row_taps[r, KERN + 1] = KERN
        for a in range(KERN):
            other = place * rows + r + a - REACH
            inside = (other >= 0) & (other < height)
            same = ids_scalar[jnp.clip(other, 0, height - 1), cols // 2] == own
            row_taps[r, a + 1] = jnp.where(inside & same, a, KERN)
        return 0

    lax.fori_loop(0, rows, one, 0)


def lay_kernel(kern_ref, laid, split):
    tap = lax.broadcasted_iota(jnp.int32, (TAPS, split), 0)
    own = jnp.where(tap == TAPS // 2, 1.0 / SPREAD, 0.0).astype(F32)
    for k in range(laid.shape[0]):
        start = k * LANES - split
        left = own if k == 0 else kern_ref[:, start : start + split]
        laid[k] = jnp.concatenate([left, kern_ref[:, start + split : start + LANES]], axis=1) * SPREAD


def fill_shifted(flat, col_ref, shifted, rows_ext, cols):
    for b in range(KERN):
        for g in range(cols // 8):
            mask = None if b == REACH else col_ref[b, g]
            for r in range(rows_ext):
                x = flat[pl.ds(EDGE + r * cols + 8 * g + b - REACH, 8), :]
                shifted[b, r, g] = x if b == REACH else x * mask


def spread_taps(kern, wide, turned):
    for t in range(TAPS):
        source = TAPS - 1 - t if turned else t
        wide[t] = jnp.broadcast_to(kern[source : source + 1, :], (8, LANES))
    for t in range(KERN):
        wide[TAPS + t] = jnp.zeros((8, LANES), F32)


def conv_block(row_taps, kern, shifted, wide, out_ref, rows, cols):
    groups = cols // 8
    spread_taps(kern, wide, False)

    def pair(h, _):
        r = 2 * h

        def step(i, totals):
            first, second = totals
            taps_first = row_taps[r, i + 1] * KERN
            taps_second = row_taps[r + 1, i] * KERN
            for b in range(KERN):
                x = shifted[b, r + i]
                first = first + wide[taps_first + b][None] * x
                second = second + wide[taps_second + b][None] * x
            return first, second

        zero = jnp.zeros((groups, 8, LANES), F32)
        first, second = lax.fori_loop(0, KERN + 1, step, (zero, zero), unroll=4)
        out_ref[pl.ds(pl.multiple_of(r * cols, cols), cols), :] = first.reshape(cols, LANES)
        out_ref[pl.ds(pl.multiple_of((r + 1) * cols, cols), cols), :] = second.reshape(cols, LANES)
        return 0

    lax.fori_loop(0, rows // 2, pair, 0)


def conv_grad_block(row_taps, kern, shifted, wide, dk, mix_ref, out_ref, dk_ref, rows, cols):
    groups = cols // 8
    spread_taps(kern, wide, True)
    for t in range(TAPS):
        dk[t] = jnp.zeros((8, LANES), F32)

    def one(r, _):
        start = pl.ds(pl.multiple_of(r * cols, cols), cols)
        mix = mix_ref[start, :].reshape(groups, 8, LANES)
        total = jnp.zeros((groups, 8, LANES), F32)
        for i in range(KERN):
            row = row_taps[r, i + 1]
            same = jnp.where(row < KERN, 1.0, 0.0).astype(F32)
            for b in range(KERN):
                x = shifted[b, r + i]
                total = total + wide[row * KERN + b][None] * x
                dk[i * KERN + b] += jnp.sum(mix * x, axis=0) * same
        out_ref[start, :] = total.reshape(cols, LANES)
        return 0

    lax.fori_loop(0, rows, one, 0)
    for t in range(TAPS):
        dk_ref[TAPS - 1 - t : TAPS - t, :] = jnp.sum(dk[t], axis=0, keepdims=True) * SPREAD
    dk_ref[TAPS:, :] = jnp.zeros((dk_ref.shape[0] - TAPS, LANES), F32)


def share(core, first, second, kept_ref, sent_ref, z, p):
    mine = core == 0
    tall, width = first.shape
    for ref, chunk in (
        (kept_ref, jnp.where(mine, first, second)),
        (sent_ref, jnp.where(mine, second, first)),
    ):
        for k in range(lane_blocks(width)):
            part = chunk[:, k * LANES : (k + 1) * LANES]
            if part.shape[1] < LANES:
                part = jnp.concatenate([part, jnp.zeros((tall, LANES - part.shape[1]), F32)], axis=1)
            ref[z, p, k * tall : (k + 1) * tall, :] = part


def share_columns(core, grad, kept_ref, sent_ref, width, plane_first=False):
    groups, parts = reversed(kept_ref.shape[:2]) if plane_first else kept_ref.shape[:2]
    tall = grad.shape[0] // parts
    for z in range(groups):
        for p in range(parts):
            rows = slice(p * tall, (p + 1) * tall)
            first = grad[rows, 2 * z * width : (2 * z + 1) * width]
            second = grad[rows, (2 * z + 1) * width : (2 * z + 2) * width]
            share(core, first, second, kept_ref, sent_ref, *((p, z) if plane_first else (z, p)))


def share_rows(core, grad, kept_ref, sent_ref, tall):
    groups, parts = kept_ref.shape[:2]
    width = grad.shape[1] // parts
    for z in range(groups):
        for p in range(parts):
            columns = slice(p * width, (p + 1) * width)
            first = grad[2 * z * tall : (2 * z + 1) * tall, columns]
            second = grad[(2 * z + 1) * tall : (2 * z + 2) * tall, columns]
            share(core, first, second, kept_ref, sent_ref, z, p)


def forward_kernel(
    place_ref, ids_scalar, one_table, two_table, ids_ref, above_ref, own_ref, below_ref, cot_ref,
    first_gain_ref, first_scale_ref, second_gain_ref, second_scale_ref,
    in_ref, kern_ref, one_ref, two_ref, three_ref, out_ref, up_ref, down_ref,
    joined_ref, output_ref, dmiddle_ref, dconv_ref, dconv_top_ref, dconv_bottom_ref,
    plane_kept_ref, plane_sent_ref, line_kept_ref, line_sent_ref, packed_kept_ref, packed_sent_ref,
    up_kept, up_sent, down_kept, down_sent, out_kept, out_sent, sems,
    row_taps, padded, valid_ref, one_keep_ref, two_keep_ref, col_ref, packed_ref, normed, flat, shifted, laid, wide, conv, mixed_ref, mapped_ref, middle_ref, result, dnorm,
    *, rows, cols, count_ha, count_ba,
):
    step = pl.program_id(0)
    blocks = flat.shape[0]
    cells = rows * cols
    reach = REACH * cols
    cells_ext = cells + 2 * reach
    core = place_ref[0] % 2
    split = one_ref.shape[0]
    dim = own_ref.shape[1]
    head_steps = blocks // 2
    ffn_first = head_steps + blocks
    gate_refs = (one_ref, two_ref, three_ref)
    ffn_steps = up_kept.shape[0]

    def chunk_copies(place):
        copies = []
        sides = ((up_kept, down_kept, plane_kept_ref, line_kept_ref), (up_sent, down_sent, plane_sent_ref, line_sent_ref))
        for up, down, plane, line in sides:
            cut = plane.shape[2] // 2
            rest = up.shape[3] - cut
            zs = pl.ds(place * up.shape[1], up.shape[1])
            bas = pl.ds(place * down.shape[2], down.shape[2])
            copies += [
                (up.at[place, :, ba, pl.ds(0, cut), :], plane.at[ba, zs, pl.ds(0, cut), :])
                for ba in range(plane.shape[0])
            ]
            copies += [
                (down.at[place, z, :, pl.ds(0, cut), :], plane.at[bas, z, pl.ds(cut, cut), :])
                for z in range(plane.shape[1])
            ]
            copies.append((up.at[place, :, :, pl.ds(cut, rest), :], line.at[zs, :, pl.ds(0, rest), :]))
            copies.append((down.at[place, :, :, pl.ds(cut, rest), :], line.at[:, bas, pl.ds(rest, rest), :]))
        return [
            pltpu.make_async_copy(source, target, sems.at[place, k]) for k, (source, target) in enumerate(copies)
        ]

    def out_copies():
        copies = []
        for k, (source, line) in enumerate(((out_kept, line_kept_ref), (out_sent, line_sent_ref))):
            rows_out = source.shape[2]
            target = line.at[:, :, pl.ds(line.shape[2] - rows_out, rows_out), :]
            copies.append(pltpu.make_async_copy(source, target, sems.at[ffn_steps, k]))
        return copies

    @pl.when(step == 0)
    def _():
        lay_kernel(kern_ref, laid, split)
        turned = image_ids(ids_ref, padded, place_ref[0], rows)
        spread_cells((turned >= 0).astype(F32), valid_ref, 0, rows + 2 * REACH)
        spread_cells(keep_factors(turned, one_table), one_keep_ref, REACH, rows)
        spread_cells(keep_factors(turned, two_table), two_keep_ref, REACH, rows)
        conv_masks(ids_scalar, ids_ref, place_ref[0], row_taps, col_ref, rows)
        start = 0
        for ref in (above_ref, own_ref, below_ref):
            size = ref.shape[0]
            hat, _ = normalized(ref[...] * valid_ref[start : start + size, :1])
            normed[start : start + size] = hat * first_gain_ref[...]
            start += size

    @pl.when(step < head_steps)
    def _():
        joined = dot(normed[...], in_ref[...])
        for k in range(2):
            part = joined[:, k * LANES : (k + 1) * LANES]
            block = 2 * step + k
            flat[block, :EDGE] = jnp.zeros((EDGE, LANES), F32)
            flat[block, EDGE : EDGE + cells_ext] = part
            flat[block, EDGE + cells_ext :] = jnp.zeros((EDGE, LANES), F32)
            joined_ref[k] = part[reach : reach + cells]

    @pl.when((step >= head_steps) & (step < ffn_first))
    def _():
        block = step - head_steps
        fill_shifted(flat.at[block], col_ref, shifted, rows + 2 * REACH, cols)
        conv_block(row_taps, laid[block], shifted, wide, conv.at[block], rows, cols)

    def conv_part(start, width):
        return jnp.concatenate([conv[start // LANES + k] for k in range(width // LANES)], axis=1)

    @pl.when(step == ffn_first)
    def _():
        mixed = conv[0, :, :split] * conv[0, :, split:]
        mixed_ref[:, :split] = mixed
        start = 2 * split
        for ref in gate_refs:
            width = ref.shape[1]
            mapped = dot(mixed, ref[...])
            mapped_ref[:, start - 2 * split : start - 2 * split + width] = mapped
            mixed = mapped * conv_part(start, width)
            mixed_ref[:, start : start + width] = mixed
            start += width
        branch = dot(mixed, out_ref[...])
        masked = own_ref[...] * valid_ref[reach : reach + cells, :1]
        middle = masked + one_keep_ref[:, :1] * first_scale_ref[...] * branch
        middle_ref[...] = middle
        hat, _ = normalized(middle)
        normed[:cells] = hat * second_gain_ref[...]
        normed[cells : cells + reach] = jnp.zeros((reach, dim), F32)
        result[...] = jnp.zeros_like(result)
        dnorm[...] = jnp.zeros_like(dnorm)

    @pl.when(step >= ffn_first)
    def _():
        grad_result = two_keep_ref[:, :1] * second_scale_ref[...] * cot_ref[...]
        pre = dot(normed[:cells], up_ref[...])
        cdf = 0.5 + 0.5 * lax.erf(pre * INV_SQRT_2)
        slope = cdf + pre * (INV_SQRT_2PI * jnp.exp(-0.5 * pre * pre))
        hidden = pre * cdf
        result[...] += dot(hidden, down_ref[...])
        grad_pre = dot(grad_result, down_ref[...], NT) * slope
        place = step - ffn_first
        for ref in (up_kept, up_sent, down_kept, down_sent):
            assert ref.shape[0] == ffn_steps
        share_rows(
            core, dot(grad_result, hidden, TN), down_kept.at[place], down_sent.at[place], dim // count_ha
        )
        width = down_ref.shape[0] // (2 * up_kept.shape[1])
        share_columns(core, dot(normed[:cells], grad_pre, TN), up_kept.at[place], up_sent.at[place], width)
        for copy in chunk_copies(place):
            copy.start()
        dnorm[...] += dot(grad_pre, up_ref[...], NT)

    @pl.when(step == pl.num_programs(0) - 1)
    def _():
        hat, scale = normalized(middle_ref[...])
        kept = two_keep_ref[:, :1] * result[...]
        output_ref[...] = middle_ref[...] + second_scale_ref[...] * kept
        dscale_two = jnp.sum(cot_ref[...] * kept, axis=0, keepdims=True)
        dgain_two = jnp.sum(dnorm[...] * hat, axis=0, keepdims=True)
        dmiddle = cot_ref[...] + norm_backward(dnorm[...] * second_gain_ref[...], hat, scale)
        dmiddle_ref[...] = dmiddle
        kept = one_keep_ref[:, :1] * dmiddle
        start = mixed_ref.shape[1] - out_ref.shape[0]
        crossed = dot(mixed_ref[:, start:], kept, TN)
        dscale_one = jnp.sum(crossed * out_ref[...], axis=0, keepdims=True)
        share_rows(core, (crossed * first_scale_ref[...]).T, out_kept, out_sent, dim // count_ha)
        for copy in out_copies():
            copy.start()
        grad = dot(kept * first_scale_ref[...], out_ref[...], NT)
        row = packed_ref.shape[0]
        start = blocks * LANES
        for ref in reversed(gate_refs):
            tall, width = ref.shape
            start -= width
            source = start - tall if tall > split else 0
            columns = slice(start - 2 * split, start - 2 * split + width)
            dconv = grad * mapped_ref[:, columns]
            for k in range(width // LANES):
                dconv_ref[start // LANES + k] = dconv[:, k * LANES : (k + 1) * LANES]
            grad_mapped = grad * conv_part(start, width)
            part = dot(mixed_ref[:, source : source + tall], grad_mapped, TN)
            row -= tall * width // LANES
            for k in range(width // LANES):
                packed_ref[row + k * tall : row + (k + 1) * tall] = part[:, k * LANES : (k + 1) * LANES]
            grad = dot(grad_mapped, ref[...], NT)
        dconv_ref[0] = jnp.concatenate([grad * conv[0, :, split:], grad * conv[0, :, :split]], axis=1)
        packed_ref[:row] = jnp.zeros((row, LANES), F32)
        row = 0
        for vector in (dscale_one, dgain_two, dscale_two):
            for k in range(dim // LANES):
                packed_ref[row : row + 1] = vector[:, k * LANES : (k + 1) * LANES]
                row += 1
        half = packed_kept_ref.shape[0]
        packed_kept_ref[...] = packed_ref[pl.ds(pl.multiple_of(core * half, 8), half), :]
        packed_sent_ref[...] = packed_ref[pl.ds(pl.multiple_of((1 - core) * half, 8), half), :]
        dconv_top_ref[...] = dconv_ref[:, :reach, :]
        dconv_bottom_ref[...] = dconv_ref[:, cells - reach :, :]
        for copy in out_copies():
            copy.wait()
        for place in range(ffn_steps):
            for copy in chunk_copies(place):
                copy.wait()


def mask_scratch(ids, rows):
    height, cols = ids.shape
    return [
        pltpu.SMEM((rows, KERN + 2), jnp.int32),
        pltpu.VMEM((height + 2 * EDGE, cols), jnp.int32),
        pltpu.VMEM(((rows + 2 * REACH) * cols, LANES), F32),
    ]


def packed_rows(gates, dim, parts):
    rows = sum(gate.size for gate in gates) // LANES + 3 * dim // LANES
    return -(-rows // (8 * parts)) * 8 * parts


def plane_share(rows):
    return max(rows * 13 // 16 // 8 * 8, 8)


def forward(
    place, ids, keep_one, keep_two, above, own, below, cot, vectors, weight_in, kern, gates,
    weight_out, weight_up, weight_down, rows, cols, count_ha, count_ba, chunk=512,
):
    cells, dim = own.shape
    reach = above.shape[0]
    blocks = weight_in.shape[1] // LANES
    hidden = weight_up.shape[1]
    split = gates[0].shape[0]
    wide = blocks * LANES
    head_steps = blocks // 2
    ffn_first = head_steps + blocks
    ffn_steps = hidden // chunk

    def ffn_step(i):
        return jnp.clip(i - ffn_first, 0, ffn_steps - 1)

    up_wide, down_wide = hidden // count_ha, hidden // count_ba
    up_rows = dim // count_ba * lane_blocks(up_wide)
    down_rows = dim // count_ha * lane_blocks(down_wide)
    out_rows = dim // count_ha * lane_blocks(dim // count_ba)
    half = count_ha // 2
    assert up_rows == down_rows
    cut = plane_share(up_rows)
    rest = up_rows - cut
    plane = (count_ba, half, 2 * cut, LANES)
    line = (half, count_ba, 2 * rest + out_rows, LANES)
    packed_shape = (packed_rows(gates, dim, count_ha), LANES)
    half_packed = (packed_shape[0] // 2, LANES)
    copies = 2 * (count_ba + half + 2)
    cells_ext = cells + 2 * reach
    return pl.pallas_call(
        functools.partial(forward_kernel, rows=rows, cols=cols, count_ha=count_ha, count_ba=count_ba),
        grid=(ffn_first + ffn_steps,),
        in_specs=[in_smem()] * 4
        + [whole(x.shape) for x in (ids, above, own, below, cot)]
        + [whole((1, dim))] * 4
        + [
            pl.BlockSpec((dim, 2 * LANES), lambda i: (0, jnp.minimum(i, head_steps - 1))),
            whole(kern.shape),
        ]
        + [whole(gate.shape) for gate in gates]
        + [
            whole(weight_out.shape),
            pl.BlockSpec((dim, chunk), lambda i: (0, ffn_step(i))),
            pl.BlockSpec((chunk, dim), lambda i: (ffn_step(i), 0)),
        ],
        out_specs=[
            pl.BlockSpec((2, cells, LANES), lambda i: (jnp.minimum(i, head_steps - 1), 0, 0)),
            whole((cells, dim)),
            whole((cells, dim)),
            whole((blocks, cells, LANES)),
            whole((blocks, reach, LANES)),
            whole((blocks, reach, LANES)),
            in_hbm(),
            in_hbm(),
            in_hbm(),
            in_hbm(),
            whole(half_packed),
            whole(half_packed),
        ],
        out_shape=[
            shape_of(blocks, cells, LANES),
            shape_of(cells, dim),
            shape_of(cells, dim),
            shape_of(blocks, cells, LANES),
            shape_of(blocks, reach, LANES),
            shape_of(blocks, reach, LANES),
            shape_of(*plane),
            shape_of(*plane),
            shape_of(*line),
            shape_of(*line),
            shape_of(*half_packed),
            shape_of(*half_packed),
        ],
        scratch_shapes=[
            pltpu.VMEM((ffn_steps, chunk // (2 * up_wide), count_ba, up_rows, LANES), F32),
            pltpu.VMEM((ffn_steps, chunk // (2 * up_wide), count_ba, up_rows, LANES), F32),
            pltpu.VMEM((ffn_steps, half, chunk // down_wide, down_rows, LANES), F32),
            pltpu.VMEM((ffn_steps, half, chunk // down_wide, down_rows, LANES), F32),
            pltpu.VMEM((half, count_ba, out_rows, LANES), F32),
            pltpu.VMEM((half, count_ba, out_rows, LANES), F32),
            pltpu.SemaphoreType.DMA((ffn_steps + 1, copies)),
        ]
        + mask_scratch(ids, rows)
        + [
            pltpu.VMEM((cells, LANES), F32),
            pltpu.VMEM((cells, LANES), F32),
            pltpu.VMEM((KERN, cols // 8, 8, LANES), F32),
            pltpu.VMEM(packed_shape, F32),
            pltpu.VMEM((cells_ext, dim), F32),
            pltpu.VMEM((blocks, cells_ext + 2 * EDGE, LANES), F32),
            pltpu.VMEM((KERN, rows + 2 * REACH, cols // 8, 8, LANES), F32),
            pltpu.VMEM((blocks, TAPS, LANES), F32),
            pltpu.VMEM((TAPS + KERN, 8, LANES), F32),
            pltpu.VMEM((blocks, cells, LANES), F32),
            pltpu.VMEM((cells, wide), F32),
            pltpu.VMEM((cells, wide - 2 * split), F32),
            pltpu.VMEM((cells, dim), F32),
            pltpu.VMEM((cells, dim), F32),
            pltpu.VMEM((cells, dim), F32),
        ],
        compiler_params=params(),
        cost_estimate=lasting(55),
    )(
        place, ids, keep_one, keep_two, ids, above, own, below, cot, *vectors,
        weight_in, kern, *gates, weight_out, weight_up, weight_down,
    )


def lay_flat(above_ref, own_ref, below_ref, flat):
    reach, cells = above_ref.shape[1], own_ref.shape[1]
    flat[:EDGE] = jnp.zeros((EDGE, LANES), F32)
    flat[EDGE : EDGE + reach] = above_ref[0]
    flat[EDGE + reach : EDGE + reach + cells] = own_ref[0]
    flat[EDGE + reach + cells : EDGE + 2 * reach + cells] = below_ref[0]
    flat[EDGE + 2 * reach + cells :] = jnp.zeros((EDGE, LANES), F32)


def backward_kernel(
    place_ref, ids_scalar, ids_ref, above_ref, own_ref, below_ref, mix_ref, kern_ref, canvas_ref, gain_ref,
    dmiddle_ref, in_ref, *rest, rows, cols,
):
    dcanvas_ref, kept_ref, sent_ref, small_kept_ref, small_sent_ref = rest[-18:-13]
    row_taps, padded, valid_ref, col_ref, flat, shifted, laid, wide, dk, sums, djoined, normed, dnorm = rest[-13:]
    step = pl.program_id(0)
    cells = rows * cols
    reach = REACH * cols
    core = place_ref[0] % 2
    split = laid.shape[0] * LANES - kern_ref.shape[1]
    width = in_ref.shape[1] // (2 * kept_ref.shape[1])

    @pl.when(step == 0)
    def _():
        lay_kernel(kern_ref, laid, split)
        turned = image_ids(ids_ref, padded, place_ref[0], rows)
        spread_cells((turned >= 0).astype(F32), valid_ref, 0, rows + 2 * REACH)
        conv_masks(ids_scalar, ids_ref, place_ref[0], row_taps, col_ref, rows)
        hat, _ = normalized(canvas_ref[...] * valid_ref[reach : reach + cells, :1])
        normed[...] = hat * gain_ref[...]
        dnorm[...] = jnp.zeros_like(dnorm)

    lay_flat(above_ref, own_ref, below_ref, flat)
    fill_shifted(flat, col_ref, shifted, rows + 2 * REACH, cols)
    conv_grad_block(
        row_taps, laid[step], shifted, wide, dk, mix_ref.at[0], djoined.at[step % 2], sums.at[step], rows, cols
    )

    @pl.when(step % 2 == 1)
    def _():
        grad = jnp.concatenate([djoined[0], djoined[1]], axis=1)
        share_columns(core, dot(normed[...], grad, TN), kept_ref, sent_ref, width, plane_first=True)
        dnorm[...] += dot(grad, in_ref[...], NT)

    @pl.when(step == pl.num_programs(0) - 1)
    def _():
        hat, scale = normalized(canvas_ref[...] * valid_ref[reach : reach + cells, :1])
        dgain = jnp.sum(dnorm[...] * hat, axis=0, keepdims=True)
        count = sums.shape[0]
        for k in range(dgain.shape[1] // LANES):
            sums[count - 1, TAPS + k : TAPS + k + 1] = dgain[:, k * LANES : (k + 1) * LANES]
        for ref, start in ((small_kept_ref, core * (count // 2)), (small_sent_ref, (1 - core) * (count // 2))):
            ref[...] = sums[pl.ds(start, count // 2)].reshape(ref.shape)
        inner = dmiddle_ref[...] + norm_backward(dnorm[...] * gain_ref[...], hat, scale)
        dcanvas_ref[...] = inner * valid_ref[reach : reach + cells, :1]


def block_of(size):
    return pl.BlockSpec((1, size, LANES), lambda i: (i, 0, 0))


def backward(
    place, ids, above, own, below, mix, kern, canvas, gain, dmiddle, weight_in, ties, rows, cols, count_ha, count_ba
):
    cells, dim = canvas.shape
    blocks = own.shape[0]
    reach = above.shape[1]
    own_wide = weight_in.shape[1] // count_ha
    chunk_rows = dim // count_ba * lane_blocks(own_wide)
    groups = 2 * LANES // (2 * own_wide)
    chunk_spec = pl.BlockSpec((count_ba, groups, chunk_rows, LANES), lambda i: (0, i // 2, 0, 0))
    chunks = shape_of(count_ba, count_ha // 2, chunk_rows, LANES)
    tall = -(-(TAPS + dim // LANES) // 8) * 8
    small = (blocks // 2 * tall, LANES)
    return pl.pallas_call(
        functools.partial(backward_kernel, rows=rows, cols=cols),
        grid=(blocks,),
        in_specs=[in_smem(), in_smem(), whole(ids.shape)]
        + [block_of(size) for size in (reach, cells, reach, cells)]
        + [whole(kern.shape), whole(canvas.shape)]
        + [whole((1, dim)), whole((cells, dim))]
        + [pl.BlockSpec((dim, 2 * LANES), lambda i: (0, i // 2))]
        + [in_hbm()] * len(ties),
        out_specs=[whole((cells, dim)), chunk_spec, chunk_spec, whole(small), whole(small)],
        out_shape=[shape_of(cells, dim), chunks, chunks, shape_of(*small), shape_of(*small)],
        scratch_shapes=mask_scratch(ids, rows)
        + [
            pltpu.VMEM((KERN, cols // 8, 8, LANES), F32),
            pltpu.VMEM((cells + 2 * reach + 2 * EDGE, LANES), F32),
            pltpu.VMEM((KERN, rows + 2 * REACH, cols // 8, 8, LANES), F32),
            pltpu.VMEM((blocks, TAPS, LANES), F32),
            pltpu.VMEM((TAPS + KERN, 8, LANES), F32),
            pltpu.VMEM((TAPS, 8, LANES), F32),
            pltpu.VMEM((blocks, tall, LANES), F32),
            pltpu.VMEM((2, cells, LANES), F32),
            pltpu.VMEM((cells, dim), F32),
            pltpu.VMEM((cells, dim), F32),
        ],
        compiler_params=params(),
        cost_estimate=lasting(25),
    )(place, ids, ids, above, own, below, mix, kern, canvas, gain, dmiddle, weight_in, *ties)


def exchange(values, axis, bit):
    return lax.ppermute(values, axis, [(i, i ^ bit) for i in range(lax.axis_size(axis))])


class View:
    def __init__(self, array, start, ways, fixed, rows):
        self.array, self.start, self.ways, self.fixed, self.rows = array, start, ways, fixed, rows

    def fix(self, way, step):
        left = [entry for entry in self.ways if entry[0] != way]
        (stride,) = [entry[2] for entry in self.ways if entry[0] == way]
        return View(self.array, self.start, left, self.fixed + [(way, step, stride)], self.rows)

    def size(self):
        count = self.rows
        for _, size, _ in self.ways:
            count *= size
        return count

    def runs(self, ha, ba):
        start = self.start
        for way, step, stride in self.fixed:
            place = ha // 2 if way == "line" else ba
            start = start + (place ^ step) * stride
        rows, ways = self.rows, list(self.ways)
        while ways and ways[-1][2] == rows:
            rows *= ways.pop()[1]
        offsets = [0]
        for _, size, stride in ways:
            offsets = [offset + k * stride for offset in offsets for k in range(size)]
        return [pl.multiple_of(start + offset, 8) for offset in offsets], rows


def flat_view(array, start=0, rows=None):
    flat = array.reshape(-1, LANES)
    return View(flat, start, [], [], flat.shape[0] if rows is None else rows)


def combine(place, groups, ties=(), epilogue=None, out_shape=None):
    pieces, arrays = [], []
    for group in groups:
        for views in group:
            if not any(views is other for other in pieces):
                pieces.append(views)
    for views in pieces:
        for view in views:
            if not any(view.array is other for other in arrays):
                arrays.append(view.array)
    index_of = {id(array): k for k, array in enumerate(arrays)}
    piece_of = {id(views): k for k, views in enumerate(pieces)}
    sizes = [sum(views[0].size() for views in group) for group in groups]
    copies = sum(len(view.runs(0, 0)[0]) for views in pieces for view in views)
    plain = epilogue is None
    if plain:
        out_shape = [shape_of(size, LANES) for size in sizes]

    def kernel(place_ref, *refs):
        inputs = refs[: len(arrays)]
        refs = refs[len(arrays) + len(ties) :]
        outs, refs = refs[: len(out_shape)], refs[len(out_shape) :]
        buffers, refs = refs[: len(pieces)], refs[len(pieces) :]
        sems, results, out_sems = refs[0], refs[1:-1], refs[-1]
        ha, ba = place_ref[0], place_ref[1]
        moves, count = [], 0
        for piece, views in enumerate(pieces):
            moves.append([])
            for term, view in enumerate(views):
                source = inputs[index_of[id(view.array)]]
                starts, rows = view.runs(ha, ba)
                for k, start in enumerate(starts):
                    target = buffers[piece].at[term, pl.ds(k * rows, rows), :]
                    move = pltpu.make_async_copy(source.at[pl.ds(start, rows), :], target, sems.at[count])
                    move.start()
                    moves[-1].append(move)
                    count += 1
        values, waited, leaving = [], set(), []
        for out, group in enumerate(groups):
            row = 0
            for views in group:
                piece = piece_of[id(views)]
                if piece not in waited:
                    waited.add(piece)
                    for move in moves[piece]:
                        move.wait()
                value = buffers[piece][0]
                for term in range(1, len(views)):
                    value = value + buffers[piece][term]
                if plain:
                    results[out][row : row + value.shape[0], :] = value
                values.append(value)
                row += value.shape[0]
            if plain:
                leaving.append(pltpu.make_async_copy(results[out], outs[out], out_sems.at[out]))
                leaving[-1].start()
        if not plain:
            epilogue(ha, values, outs)
        for move in leaving:
            move.wait()

    moved = sum(view.size() for views in pieces for view in views) + sum(sizes)
    scratch = [pltpu.VMEM((len(views), views[0].size(), LANES), F32) for views in pieces]
    scratch.append(pltpu.SemaphoreType.DMA((copies,)))
    if plain:
        scratch += [pltpu.VMEM((size, LANES), F32) for size in sizes]
    scratch.append(pltpu.SemaphoreType.DMA((len(groups),)))
    return pl.pallas_call(
        kernel,
        in_specs=[in_smem()] + [in_hbm()] * (len(arrays) + len(ties)),
        out_specs=[in_hbm() if plain else pl.BlockSpec(memory_space=pltpu.VMEM)] * len(out_shape),
        out_shape=out_shape,
        scratch_shapes=scratch,
        compiler_params=params(),
        cost_estimate=lasting(1 + moved * LANES * 4 / 3.0e6),
    )(place, *arrays, *ties)


def tied(arrays, ties):
    return pl.pallas_call(
        lambda *refs: None,
        in_specs=[pl.BlockSpec(memory_space=pl.ANY)] * (len(arrays) + len(ties)),
        out_specs=[pl.BlockSpec(memory_space=pl.ANY)] * len(arrays),
        out_shape=[shape_of(*array.shape) for array in arrays],
        input_output_aliases={k: k for k in range(len(arrays))},
        compiler_params=params(),
    )(*arrays, *ties)


class Sum:
    def __init__(self, arrays, names):
        self.views = []
        sizes = {"line": lax.axis_size("ha") // 2, "plane": lax.axis_size("ba")}
        for array in arrays:
            flat = array.reshape(-1, LANES)
            stride, ways = flat.shape[0], []
            for name in names:
                stride //= sizes[name]
                ways.append((name, sizes[name], stride))
            self.views.append(View(flat, 0, ways, [], stride))

    def leaving(self, way, step):
        return [view.fix(way, step) for view in self.views]

    def keep(self, way, sent, arrived):
        self.views = [view.fix(way, 0) for view in self.views]
        rows = self.views[0].rows
        ways = [(name, size, rows) for name, size, _ in self.views[0].ways]
        self.views += [View(array, start, ways, [], rows) for array, start in arrived]

    def part(self, first, rows):
        return [View(view.array, view.start + first, view.ways, view.fixed, rows) for view in self.views]


class Rider:
    def __init__(self, views):
        self.views = views

    def leaving(self, way, step):
        return self.views

    def keep(self, way, sent, arrived):
        rows = self.views[0].size()
        self.views = [View(array, start, [], [], rows) for array, start in [sent] + arrived]


class Gather(Rider):
    def keep(self, way, sent, arrived):
        rows = self.views[0].size()
        self.gathered = [[View(array, start, [], [], rows)] for array, start in [sent] + arrived]


class Stage:
    def __init__(self, sums, way):
        self.sums, self.way = sums, way
        self.steps = range(1, lax.axis_size("ha") // 2 if way == "line" else lax.axis_size("ba"))

    def groups(self):
        return [[one.leaving(self.way, step) for one in self.sums] for step in self.steps]

    def go(self, payloads):
        axis, unit = ("ha", 2) if self.way == "line" else ("ba", 1)
        arrived = [exchange(part, axis, unit * step) for step, part in zip(self.steps, payloads)]
        row = 0
        for one in self.sums:
            rows = one.leaving(self.way, 1)[0].size()
            one.keep(self.way, (payloads[0], row), [(part, row) for part in arrived])
            row += rows
        return arrived


def run(place, stages):
    groups = [group for stage in stages for group in stage.groups()]
    made = combine(place, groups)
    rest, arrived = made, []
    for stage in stages:
        arrived += stage.go(rest[: len(stage.steps)])
        rest = rest[len(stage.steps) :]
    return made, arrived


def neighbour_rows(top, bottom):
    count = lax.axis_size("ha")
    up = [(i, i + 1) for i in range(count - 1)]
    down = [(i + 1, i) for i in range(count - 1)]
    return lax.ppermute(bottom, "ha", up), lax.ppermute(top, "ha", down)


def lay_beside(value, ref):
    tall, width = ref.shape
    for k in range(lane_blocks(width)):
        columns = slice(k * LANES, min(width, (k + 1) * LANES))
        ref[:, columns] = value[k * tall : (k + 1) * tall, : columns.stop - columns.start]


def lay_large(ha, values, outs):
    up_first, up_second, down_first, down_second, out = values
    lay_beside(jnp.concatenate([up_first, up_second], axis=0), outs[0])
    lay_beside(jnp.concatenate([down_first, down_second], axis=0), outs[1])
    lay_beside(out, outs[2])


def lay_small(ha, values, outs, blocks):
    din_ref, dk_ref, gain_ref = outs[:3]
    scratch = outs[-1]
    lay_beside(values[0], din_ref)
    own, other = values[1], values[2]
    small_rows = blocks // 2 * (-(-(TAPS + gain_ref.shape[1] // LANES) // 8) * 8)
    mine = ha % 2 == 0
    first, second = jnp.where(mine, own, other), jnp.where(mine, other, own)
    dkern = jnp.concatenate([first[:small_rows], second[:small_rows]], axis=0)
    tall = dkern.shape[0] // blocks
    joined = jnp.concatenate([dkern[k * tall : k * tall + TAPS] for k in range(blocks)], axis=1)
    dk_ref[...] = joined[:, joined.shape[1] - dk_ref.shape[1] :]
    half = own.shape[0] - small_rows
    count = lax.axis_size("ha") // 2
    part = half // count
    for core, rows in ((0, first), (1, second)):
        for step in range(count):
            start = core * half + ((ha // 2) ^ step) * part
            source = small_rows + step * part
            scratch[pl.ds(pl.multiple_of(start, 8), part), :] = rows[source : source + part]
    dim = gain_ref.shape[1]
    for k in range(dim // LANES):
        columns = slice(k * LANES, (k + 1) * LANES)
        row = (blocks - 1) * tall + TAPS + k
        gain_ref[:, columns] = dkern[row : row + 1]
        for vector, ref in enumerate(outs[3:6]):
            ref[:, columns] = scratch[vector * dim // LANES + k : vector * dim // LANES + k + 1, :]
    row = scratch.shape[0]
    for ref in reversed(outs[6:-1]):
        tall, width = ref.shape
        row -= tall * width // LANES
        for k in range(width // LANES):
            ref[:, k * LANES : (k + 1) * LANES] = scratch[row + k * tall : row + (k + 1) * tall, :]


def shards(
    canvas,
    image_id,
    keep_first,
    keep_second,
    first_gain,
    weight_in,
    depth_kernel,
    gate_first,
    gate_second,
    gate_third,
    weight_out,
    scale_first,
    second_gain,
    weight_up,
    weight_down,
    scale_second,
    cotangent,
):
    _, rows, cols, dim = canvas.shape
    cells = rows * cols
    reach = REACH * cols
    count_ha, count_ba = lax.axis_size("ha"), lax.axis_size("ba")
    hidden = weight_up.shape[1]
    blocks = weight_in.shape[1] // LANES
    place = jnp.stack([lax.axis_index("ha"), lax.axis_index("ba")])
    own = canvas.reshape(cells, dim)
    gates = (gate_first, gate_second, gate_third)
    gain = first_gain[None]
    vectors = (gain, scale_first[None], second_gain[None], scale_second[None])
    ids = image_id[0]
    above, below = neighbour_rows(own[:reach], own[cells - reach :])
    (
        joined, output, dmiddle, dconv, dconv_top, dconv_bottom, plane_kept, plane_sent, line_kept, line_sent,
        packed_kept, packed_sent,
    ) = forward(
        place, ids, keep_first, keep_second, above, own, below, cotangent.reshape(cells, dim), vectors,
        weight_in, depth_kernel, gates, weight_out, weight_up, weight_down, rows, cols, count_ha, count_ba,
    )
    above, below = neighbour_rows(dconv_top, dconv_bottom)

    plane_sum = Sum([plane_kept, exchange(plane_sent, "ha", 1)], ["plane", "line"])
    line_sum = Sum([line_kept, exchange(line_sent, "ha", 1)], ["line", "plane"])
    packed = Sum([packed_kept, exchange(packed_sent, "ha", 1)], ["line"])
    made, arrived = run(place, [Stage([line_sum, packed], "line"), Stage([plane_sum], "plane")])
    dcanvas, in_kept, in_sent, small_kept, small_sent = backward(
        place, ids, above, dconv, below, joined, depth_kernel, own, gain, dmiddle, weight_in, made,
        rows, cols, count_ha, count_ba,
    )
    in_sent, small_sent = tied([in_sent, small_sent], arrived[1:])
    in_sum = Sum([in_kept, exchange(in_sent, "ha", 1)], ["plane", "line"])
    small = Rider([flat_view(small_kept), flat_view(exchange(small_sent, "ha", 1))])
    packed = Rider(packed.views)
    run(place, [Stage([plane_sum, small], "line"), Stage([line_sum, in_sum, packed], "plane")])
    packed = Gather(packed.views)
    run(place, [Stage([in_sum, packed], "line"), Stage([small], "plane")])
    cut = plane_sum.views[0].rows // 2
    rest = (line_sum.views[0].rows - dim // count_ha * lane_blocks(dim // count_ba)) // 2
    dup, ddown, dout = combine(
        place,
        [
            [
                plane_sum.part(0, cut),
                line_sum.part(0, rest),
                plane_sum.part(cut, cut),
                line_sum.part(rest, rest),
                line_sum.part(2 * rest, line_sum.views[0].rows - 2 * rest),
            ]
        ],
        epilogue=lay_large,
        out_shape=[
            shape_of(dim // count_ba, hidden // count_ha),
            shape_of(dim // count_ha, hidden // count_ba),
            shape_of(dim // count_ha, dim // count_ba),
        ],
    )
    (halves_of,) = combine(place, [[small.views] + packed.gathered])
    din, dkern, dgain_one, dscale_one, dgain_two, dscale_two, dfirst, dsecond, dthird, _ = combine(
        place,
        [[in_sum.views, [flat_view(halves_of)], [flat_view(exchange(halves_of, "ha", 1))]]],
        epilogue=functools.partial(lay_small, blocks=blocks),
        out_shape=[shape_of(dim // count_ba, weight_in.shape[1] // count_ha), shape_of(*depth_kernel.shape)]
        + [shape_of(1, dim)] * 4
        + [shape_of(*gate.shape) for gate in gates]
        + [shape_of(packed_rows(gates, dim, count_ha), LANES)],
    )
    return (
        output.reshape(canvas.shape),
        dcanvas.reshape(canvas.shape),
        dgain_one[0],
        din,
        dkern,
        dfirst,
        dsecond,
        dthird,
        dout.T,
        dscale_one[0],
        dgain_two[0],
        dup,
        ddown.T,
        dscale_two[0],
    )


def solution(mesh):
    in_specs = (
        P("ba", "ha", None, None),
        P("ba", None, None),
        P("ba", None),
        P("ba", None),
    ) + (P(),) * 12 + (P("ba", "ha", None, None),)
    tiled = P("ba", "ha")
    out_specs = (
        P("ba", "ha", None, None),
        P("ba", "ha", None, None),
        P(),
        tiled,
        P(),
        P(),
        P(),
        P(),
        tiled,
        P(),
        P(),
        tiled,
        tiled,
        P(),
    )
    return jax.shard_map(shards, mesh=mesh, in_specs=in_specs, out_specs=out_specs, check_vma=False)
```

```python
import functools

import jax
import jax.numpy as jnp
from jax import lax
from jax.experimental import pallas as pl
from jax.experimental.pallas import tpu as pltpu
from jax.sharding import PartitionSpec as P

KERN = 7
TAPS = KERN * KERN
REACH = KERN // 2
KEEP_RATE = 0.8
SPREAD = 1.0 / 3.0
EPSILON = 1e-06
LANES = 128
EDGE = 8
VMEM_BYTES = 64 << 20
F32 = jnp.float32
INV_SQRT_2 = 0.7071067811865476
INV_SQRT_2PI = 0.3989422804014327
NN = (((1,), (0,)), ((), ()))
NT = (((1,), (1,)), ((), ()))
TN = (((0,), (0,)), ((), ()))


def dot(left, right, dims=NN):
    return lax.dot_general(left, right, dims, precision=lax.Precision.HIGH, preferred_element_type=F32)


def normalized(values):
    centered = values - jnp.mean(values, axis=-1, keepdims=True)
    scale = lax.rsqrt(jnp.mean(centered * centered, axis=-1, keepdims=True) + EPSILON)
    return centered * scale, scale


def norm_backward(grad_hat, hat, scale):
    return scale * (
        grad_hat
        - jnp.mean(grad_hat, axis=-1, keepdims=True)
        - hat * jnp.mean(grad_hat * hat, axis=-1, keepdims=True)
    )


def params():
    return pltpu.CompilerParams(vmem_limit_bytes=VMEM_BYTES)


def lasting(microseconds):
    return pl.CostEstimate(flops=int(microseconds * 1.1e9), bytes_accessed=0, transcendentals=0)


def whole(shape):
    return pl.BlockSpec(tuple(shape), lambda *_: (0,) * len(shape), pipeline_mode=pl.Buffered(1))


def in_smem():
    return pl.BlockSpec(memory_space=pltpu.SMEM)


def in_hbm():
    return pl.BlockSpec(memory_space=pltpu.HBM)


def shape_of(*shape):
    return jax.ShapeDtypeStruct(shape, F32)


def lane_blocks(width):
    return -(-width // LANES)


def image_ids(ids_ref, padded, place, rows):
    height, cols = ids_ref.shape
    padded[...] = jnp.full(padded.shape, -1, jnp.int32)
    padded[EDGE : EDGE + height, :] = ids_ref[...]
    ids = padded[pl.ds(place * rows + (EDGE - REACH), rows + 2 * REACH), :]
    return jnp.concatenate([ids, jnp.full((-ids.shape[0] % 8, cols), -1, jnp.int32)], axis=0).T


def spread_cells(factors, out_ref, first, rows):
    cols = factors.shape[0]
    for r in range(rows):
        column = factors[:, first + r : first + r + 1]
        out_ref[r * cols : (r + 1) * cols, :] = jnp.broadcast_to(column, (cols, LANES))


def keep_factors(turned, table_ref):
    result = jnp.zeros(turned.shape, F32)
    for slot in range(table_ref.shape[1]):
        result = jnp.where(turned == slot, table_ref[0, slot].astype(F32) / KEEP_RATE, result)
    return result


def conv_masks(ids_scalar, ids_ref, place, row_taps, col_mask, rows):
    height, cols = ids_ref.shape
    wide_ids = jnp.broadcast_to(ids_ref[...].T[:, height // 2 : height // 2 + 1], (cols, LANES))
    column = lax.broadcasted_iota(jnp.int32, (cols, LANES), 0)
    for b in range(KERN):
        shift = b - REACH
        moved = pltpu.roll(wide_ids, (-shift) % cols, 0)
        inside = (column + shift >= 0) & (column + shift < cols)
        same = (moved == wide_ids) & inside
        col_mask[b] = same.astype(F32).reshape(cols // 8, 8, LANES)

    def one(r, _):
        own = ids_scalar[place * rows + r, cols // 2]
        row_taps[r, 0] = KERN
        row_taps[r, KERN + 1] = KERN
        for a in range(KERN):
            other = place * rows + r + a - REACH
            inside = (other >= 0) & (other < height)
            same = ids_scalar[jnp.clip(other, 0, height - 1), cols // 2] == own
            row_taps[r, a + 1] = jnp.where(inside & same, a, KERN)
        return 0

    lax.fori_loop(0, rows, one, 0)


def lay_kernel(kern_ref, laid, split):
    tap = lax.broadcasted_iota(jnp.int32, (TAPS, split), 0)
    own = jnp.where(tap == TAPS // 2, 1.0 / SPREAD, 0.0).astype(F32)
    for k in range(laid.shape[0]):
        start = k * LANES - split
        left = own if k == 0 else kern_ref[:, start : start + split]
        laid[k] = jnp.concatenate([left, kern_ref[:, start + split : start + LANES]], axis=1) * SPREAD


def fill_shifted(flat, col_ref, shifted, rows_ext, cols):
    for b in range(KERN):
        for g in range(cols // 8):
            mask = None if b == REACH else col_ref[b, g]
            for r in range(rows_ext):
                x = flat[pl.ds(EDGE + r * cols + 8 * g + b - REACH, 8), :]
                shifted[b, r, g] = x if b == REACH else x * mask


def spread_taps(kern, wide, turned):
    for t in range(TAPS):
        source = TAPS - 1 - t if turned else t
        wide[t] = jnp.broadcast_to(kern[source : source + 1, :], (8, LANES))
    for t in range(KERN):
        wide[TAPS + t] = jnp.zeros((8, LANES), F32)


def conv_block(row_taps, kern, shifted, wide, out_ref, rows, cols):
    groups = cols // 8
    spread_taps(kern, wide, False)

    def pair(h, _):
        r = 2 * h

        def step(i, totals):
            first, second = totals
            taps_first = row_taps[r, i + 1] * KERN
            taps_second = row_taps[r + 1, i] * KERN
            for b in range(KERN):
                x = shifted[b, r + i]
                first = first + wide[taps_first + b][None] * x
                second = second + wide[taps_second + b][None] * x
            return first, second

        zero = jnp.zeros((groups, 8, LANES), F32)
        first, second = lax.fori_loop(0, KERN + 1, step, (zero, zero), unroll=4)
        out_ref[pl.ds(pl.multiple_of(r * cols, cols), cols), :] = first.reshape(cols, LANES)
        out_ref[pl.ds(pl.multiple_of((r + 1) * cols, cols), cols), :] = second.reshape(cols, LANES)
        return 0

    lax.fori_loop(0, rows // 2, pair, 0)


def conv_grad_block(row_taps, kern, shifted, wide, dk, mix_ref, out_ref, dk_ref, rows, cols):
    groups = cols // 8
    spread_taps(kern, wide, True)
    for t in range(TAPS):
        dk[t] = jnp.zeros((8, LANES), F32)

    def one(r, _):
        start = pl.ds(pl.multiple_of(r * cols, cols), cols)
        mix = mix_ref[start, :].reshape(groups, 8, LANES)
        total = jnp.zeros((groups, 8, LANES), F32)
        for i in range(KERN):
            row = row_taps[r, i + 1]
            same = jnp.where(row < KERN, 1.0, 0.0).astype(F32)
            for b in range(KERN):
                x = shifted[b, r + i]
                total = total + wide[row * KERN + b][None] * x
                dk[i * KERN + b] += jnp.sum(mix * x, axis=0) * same
        out_ref[start, :] = total.reshape(cols, LANES)
        return 0

    lax.fori_loop(0, rows, one, 0)
    for t in range(TAPS):
        dk_ref[TAPS - 1 - t : TAPS - t, :] = jnp.sum(dk[t], axis=0, keepdims=True) * SPREAD
    dk_ref[TAPS:, :] = jnp.zeros((dk_ref.shape[0] - TAPS, LANES), F32)


def share(core, first, second, kept_ref, sent_ref, z, p):
    mine = core == 0
    tall, width = first.shape
    for ref, chunk in (
        (kept_ref, jnp.where(mine, first, second)),
        (sent_ref, jnp.where(mine, second, first)),
    ):
        for k in range(lane_blocks(width)):
            part = chunk[:, k * LANES : (k + 1) * LANES]
            if part.shape[1] < LANES:
                part = jnp.concatenate([part, jnp.zeros((tall, LANES - part.shape[1]), F32)], axis=1)
            ref[z, p, k * tall : (k + 1) * tall, :] = part


def share_columns(core, grad, kept_ref, sent_ref, width, plane_first=False):
    groups, parts = reversed(kept_ref.shape[:2]) if plane_first else kept_ref.shape[:2]
    tall = grad.shape[0] // parts
    for z in range(groups):
        for p in range(parts):
            rows = slice(p * tall, (p + 1) * tall)
            first = grad[rows, 2 * z * width : (2 * z + 1) * width]
            second = grad[rows, (2 * z + 1) * width : (2 * z + 2) * width]
            share(core, first, second, kept_ref, sent_ref, *((p, z) if plane_first else (z, p)))


def share_rows(core, grad, kept_ref, sent_ref, tall):
    groups, parts = kept_ref.shape[:2]
    width = grad.shape[1] // parts
    for z in range(groups):
        for p in range(parts):
            columns = slice(p * width, (p + 1) * width)
            first = grad[2 * z * tall : (2 * z + 1) * tall, columns]
            second = grad[(2 * z + 1) * tall : (2 * z + 2) * tall, columns]
            share(core, first, second, kept_ref, sent_ref, z, p)


def forward_kernel(
    place_ref, ids_scalar, one_table, two_table, ids_ref, above_ref, own_ref, below_ref, cot_ref,
    first_gain_ref, first_scale_ref, second_gain_ref, second_scale_ref,
    in_ref, kern_ref, one_ref, two_ref, three_ref, out_ref, up_ref, down_ref,
    joined_ref, output_ref, dmiddle_ref, dconv_ref, dconv_top_ref, dconv_bottom_ref,
    plane_kept_ref, plane_sent_ref, line_kept_ref, line_sent_ref, packed_kept_ref, packed_sent_ref,
    up_kept, up_sent, down_kept, down_sent, out_kept, out_sent, sems,
    row_taps, padded, valid_ref, one_keep_ref, two_keep_ref, col_ref, packed_ref, normed, flat, shifted, laid, wide, conv, mixed_ref, mapped_ref, middle_ref, result, dnorm,
    *, rows, cols, count_ha, count_ba,
):
    step = pl.program_id(0)
    blocks = flat.shape[0]
    cells = rows * cols
    reach = REACH * cols
    cells_ext = cells + 2 * reach
    core = place_ref[0] % 2
    split = one_ref.shape[0]
    dim = own_ref.shape[1]
    head_steps = blocks // 2
    ffn_first = head_steps + blocks
    gate_refs = (one_ref, two_ref, three_ref)
    ffn_steps = up_kept.shape[0]

    def chunk_copies(place):
        copies = []
        sides = ((up_kept, down_kept, plane_kept_ref, line_kept_ref), (up_sent, down_sent, plane_sent_ref, line_sent_ref))
        for up, down, plane, line in sides:
            cut = plane.shape[2] // 2
            rest = up.shape[3] - cut
            zs = pl.ds(place * up.shape[1], up.shape[1])
            bas = pl.ds(place * down.shape[2], down.shape[2])
            copies += [
                (up.at[place, :, ba, pl.ds(0, cut), :], plane.at[ba, zs, pl.ds(0, cut), :])
                for ba in range(plane.shape[0])
            ]
            copies += [
                (down.at[place, z, :, pl.ds(0, cut), :], plane.at[bas, z, pl.ds(cut, cut), :])
                for z in range(plane.shape[1])
            ]
            copies.append((up.at[place, :, :, pl.ds(cut, rest), :], line.at[zs, :, pl.ds(0, rest), :]))
            copies.append((down.at[place, :, :, pl.ds(cut, rest), :], line.at[:, bas, pl.ds(rest, rest), :]))
        return [
            pltpu.make_async_copy(source, target, sems.at[place, k]) for k, (source, target) in enumerate(copies)
        ]

    def out_copies():
        copies = []
        for k, (source, line) in enumerate(((out_kept, line_kept_ref), (out_sent, line_sent_ref))):
            rows_out = source.shape[2]
            target = line.at[:, :, pl.ds(line.shape[2] - rows_out, rows_out), :]
            copies.append(pltpu.make_async_copy(source, target, sems.at[ffn_steps, k]))
        return copies

    @pl.when(step == 0)
    def _():
        lay_kernel(kern_ref, laid, split)
        turned = image_ids(ids_ref, padded, place_ref[0], rows)
        spread_cells((turned >= 0).astype(F32), valid_ref, 0, rows + 2 * REACH)
        spread_cells(keep_factors(turned, one_table), one_keep_ref, REACH, rows)
        spread_cells(keep_factors(turned, two_table), two_keep_ref, REACH, rows)
        conv_masks(ids_scalar, ids_ref, place_ref[0], row_taps, col_ref, rows)
        start = 0
        for ref in (above_ref, own_ref, below_ref):
            size = ref.shape[0]
            hat, _ = normalized(ref[...] * valid_ref[start : start + size, :1])
            normed[start : start + size] = hat * first_gain_ref[...]
            start += size

    @pl.when(step < head_steps)
    def _():
        joined = dot(normed[...], in_ref[...])
        for k in range(2):
            part = joined[:, k * LANES : (k + 1) * LANES]
            block = 2 * step + k
            flat[block, :EDGE] = jnp.zeros((EDGE, LANES), F32)
            flat[block, EDGE : EDGE + cells_ext] = part
            flat[block, EDGE + cells_ext :] = jnp.zeros((EDGE, LANES), F32)
            joined_ref[k] = part[reach : reach + cells]

    @pl.when((step >= head_steps) & (step < ffn_first))
    def _():
        block = step - head_steps
        fill_shifted(flat.at[block], col_ref, shifted, rows + 2 * REACH, cols)
        conv_block(row_taps, laid[block], shifted, wide, conv.at[block], rows, cols)

    def conv_part(start, width):
        return jnp.concatenate([conv[start // LANES + k] for k in range(width // LANES)], axis=1)

    @pl.when(step == ffn_first)
    def _():
        mixed = conv[0, :, :split] * conv[0, :, split:]
        mixed_ref[:, :split] = mixed
        start = 2 * split
        for ref in gate_refs:
            width = ref.shape[1]
            mapped = dot(mixed, ref[...])
            mapped_ref[:, start - 2 * split : start - 2 * split + width] = mapped
            mixed = mapped * conv_part(start, width)
            mixed_ref[:, start : start + width] = mixed
            start += width
        branch = dot(mixed, out_ref[...])
        masked = own_ref[...] * valid_ref[reach : reach + cells, :1]
        middle = masked + one_keep_ref[:, :1] * first_scale_ref[...] * branch
        middle_ref[...] = middle
        hat, _ = normalized(middle)
        normed[:cells] = hat * second_gain_ref[...]
        normed[cells : cells + reach] = jnp.zeros((reach, dim), F32)
        result[...] = jnp.zeros_like(result)
        dnorm[...] = jnp.zeros_like(dnorm)

    @pl.when(step >= ffn_first)
    def _():
        grad_result = two_keep_ref[:, :1] * second_scale_ref[...] * cot_ref[...]
        pre = dot(normed[:cells], up_ref[...])
        cdf = 0.5 + 0.5 * lax.erf(pre * INV_SQRT_2)
        slope = cdf + pre * (INV_SQRT_2PI * jnp.exp(-0.5 * pre * pre))
        hidden = pre * cdf
        result[...] += dot(hidden, down_ref[...])
        grad_pre = dot(grad_result, down_ref[...], NT) * slope
        place = step - ffn_first
        for ref in (up_kept, up_sent, down_kept, down_sent):
            assert ref.shape[0] == ffn_steps
        share_rows(
            core, dot(grad_result, hidden, TN), down_kept.at[place], down_sent.at[place], dim // count_ha
        )
        width = down_ref.shape[0] // (2 * up_kept.shape[1])
        share_columns(core, dot(normed[:cells], grad_pre, TN), up_kept.at[place], up_sent.at[place], width)
        for copy in chunk_copies(place):
            copy.start()
        dnorm[...] += dot(grad_pre, up_ref[...], NT)

    @pl.when(step == pl.num_programs(0) - 1)
    def _():
        hat, scale = normalized(middle_ref[...])
        kept = two_keep_ref[:, :1] * result[...]
        output_ref[...] = middle_ref[...] + second_scale_ref[...] * kept
        dscale_two = jnp.sum(cot_ref[...] * kept, axis=0, keepdims=True)
        dgain_two = jnp.sum(dnorm[...] * hat, axis=0, keepdims=True)
        dmiddle = cot_ref[...] + norm_backward(dnorm[...] * second_gain_ref[...], hat, scale)
        dmiddle_ref[...] = dmiddle
        kept = one_keep_ref[:, :1] * dmiddle
        start = mixed_ref.shape[1] - out_ref.shape[0]
        crossed = dot(mixed_ref[:, start:], kept, TN)
        dscale_one = jnp.sum(crossed * out_ref[...], axis=0, keepdims=True)
        share_rows(core, (crossed * first_scale_ref[...]).T, out_kept, out_sent, dim // count_ha)
        for copy in out_copies():
            copy.start()
        grad = dot(kept * first_scale_ref[...], out_ref[...], NT)
        row = packed_ref.shape[0]
        start = blocks * LANES
        for ref in reversed(gate_refs):
            tall, width = ref.shape
            start -= width
            source = start - tall if tall > split else 0
            columns = slice(start - 2 * split, start - 2 * split + width)
            dconv = grad * mapped_ref[:, columns]
            for k in range(width // LANES):
                dconv_ref[start // LANES + k] = dconv[:, k * LANES : (k + 1) * LANES]
            grad_mapped = grad * conv_part(start, width)
            part = dot(mixed_ref[:, source : source + tall], grad_mapped, TN)
            row -= tall * width // LANES
            for k in range(width // LANES):
                packed_ref[row + k * tall : row + (k + 1) * tall] = part[:, k * LANES : (k + 1) * LANES]
            grad = dot(grad_mapped, ref[...], NT)
        dconv_ref[0] = jnp.concatenate([grad * conv[0, :, split:], grad * conv[0, :, :split]], axis=1)
        packed_ref[:row] = jnp.zeros((row, LANES), F32)
        row = 0
        for vector in (dscale_one, dgain_two, dscale_two):
            for k in range(dim // LANES):
                packed_ref[row : row + 1] = vector[:, k * LANES : (k + 1) * LANES]
                row += 1
        half = packed_kept_ref.shape[0]
        packed_kept_ref[...] = packed_ref[pl.ds(pl.multiple_of(core * half, 8), half), :]
        packed_sent_ref[...] = packed_ref[pl.ds(pl.multiple_of((1 - core) * half, 8), half), :]
        dconv_top_ref[...] = dconv_ref[:, :reach, :]
        dconv_bottom_ref[...] = dconv_ref[:, cells - reach :, :]
        for copy in out_copies():
            copy.wait()
        for place in range(ffn_steps):
            for copy in chunk_copies(place):
                copy.wait()


def mask_scratch(ids, rows):
    height, cols = ids.shape
    return [
        pltpu.SMEM((rows, KERN + 2), jnp.int32),
        pltpu.VMEM((height + 2 * EDGE, cols), jnp.int32),
        pltpu.VMEM(((rows + 2 * REACH) * cols, LANES), F32),
    ]


def packed_rows(gates, dim, parts):
    rows = sum(gate.size for gate in gates) // LANES + 3 * dim // LANES
    return -(-rows // (16 * parts)) * 16 * parts


def plane_share(rows):
    return max(rows * 3 // 4 // 8 * 8, 8)


def forward(
    place, ids, keep_one, keep_two, above, own, below, cot, vectors, weight_in, kern, gates,
    weight_out, weight_up, weight_down, rows, cols, count_ha, count_ba, chunk=512,
):
    cells, dim = own.shape
    reach = above.shape[0]
    blocks = weight_in.shape[1] // LANES
    hidden = weight_up.shape[1]
    split = gates[0].shape[0]
    wide = blocks * LANES
    head_steps = blocks // 2
    ffn_first = head_steps + blocks
    ffn_steps = hidden // chunk

    def ffn_step(i):
        return jnp.clip(i - ffn_first, 0, ffn_steps - 1)

    up_wide, down_wide = hidden // count_ha, hidden // count_ba
    up_rows = dim // count_ba * lane_blocks(up_wide)
    down_rows = dim // count_ha * lane_blocks(down_wide)
    out_rows = dim // count_ha * lane_blocks(dim // count_ba)
    half = count_ha // 2
    assert up_rows == down_rows
    cut = plane_share(up_rows)
    rest = up_rows - cut
    plane = (count_ba, half, 2 * cut, LANES)
    line = (half, count_ba, 2 * rest + out_rows, LANES)
    packed_shape = (packed_rows(gates, dim, count_ba), LANES)
    half_packed = (packed_shape[0] // 2, LANES)
    copies = 2 * (count_ba + half + 2)
    cells_ext = cells + 2 * reach
    return pl.pallas_call(
        functools.partial(forward_kernel, rows=rows, cols=cols, count_ha=count_ha, count_ba=count_ba),
        grid=(ffn_first + ffn_steps,),
        in_specs=[in_smem()] * 4
        + [whole(x.shape) for x in (ids, above, own, below, cot)]
        + [whole((1, dim))] * 4
        + [
            pl.BlockSpec((dim, 2 * LANES), lambda i: (0, jnp.minimum(i, head_steps - 1))),
            whole(kern.shape),
        ]
        + [whole(gate.shape) for gate in gates]
        + [
            whole(weight_out.shape),
            pl.BlockSpec((dim, chunk), lambda i: (0, ffn_step(i))),
            pl.BlockSpec((chunk, dim), lambda i: (ffn_step(i), 0)),
        ],
        out_specs=[
            pl.BlockSpec((2, cells, LANES), lambda i: (jnp.minimum(i, head_steps - 1), 0, 0)),
            whole((cells, dim)),
            whole((cells, dim)),
            whole((blocks, cells, LANES)),
            whole((blocks, reach, LANES)),
            whole((blocks, reach, LANES)),
            in_hbm(),
            in_hbm(),
            in_hbm(),
            in_hbm(),
            whole(half_packed),
            whole(half_packed),
        ],
        out_shape=[
            shape_of(blocks, cells, LANES),
            shape_of(cells, dim),
            shape_of(cells, dim),
            shape_of(blocks, cells, LANES),
            shape_of(blocks, reach, LANES),
            shape_of(blocks, reach, LANES),
            shape_of(*plane),
            shape_of(*plane),
            shape_of(*line),
            shape_of(*line),
            shape_of(*half_packed),
            shape_of(*half_packed),
        ],
        scratch_shapes=[
            pltpu.VMEM((ffn_steps, chunk // (2 * up_wide), count_ba, up_rows, LANES), F32),
            pltpu.VMEM((ffn_steps, chunk // (2 * up_wide), count_ba, up_rows, LANES), F32),
            pltpu.VMEM((ffn_steps, half, chunk // down_wide, down_rows, LANES), F32),
            pltpu.VMEM((ffn_steps, half, chunk // down_wide, down_rows, LANES), F32),
            pltpu.VMEM((half, count_ba, out_rows, LANES), F32),
            pltpu.VMEM((half, count_ba, out_rows, LANES), F32),
            pltpu.SemaphoreType.DMA((ffn_steps + 1, copies)),
        ]
        + mask_scratch(ids, rows)
        + [
            pltpu.VMEM((cells, LANES), F32),
            pltpu.VMEM((cells, LANES), F32),
            pltpu.VMEM((KERN, cols // 8, 8, LANES), F32),
            pltpu.VMEM(packed_shape, F32),
            pltpu.VMEM((cells_ext, dim), F32),
            pltpu.VMEM((blocks, cells_ext + 2 * EDGE, LANES), F32),
            pltpu.VMEM((KERN, rows + 2 * REACH, cols // 8, 8, LANES), F32),
            pltpu.VMEM((blocks, TAPS, LANES), F32),
            pltpu.VMEM((TAPS + KERN, 8, LANES), F32),
            pltpu.VMEM((blocks, cells, LANES), F32),
            pltpu.VMEM((cells, wide), F32),
            pltpu.VMEM((cells, wide - 2 * split), F32),
            pltpu.VMEM((cells, dim), F32),
            pltpu.VMEM((cells, dim), F32),
            pltpu.VMEM((cells, dim), F32),
        ],
        compiler_params=params(),
        cost_estimate=lasting(55),
    )(
        place, ids, keep_one, keep_two, ids, above, own, below, cot, *vectors,
        weight_in, kern, *gates, weight_out, weight_up, weight_down,
    )


def lay_flat(above_ref, own_ref, below_ref, flat):
    reach, cells = above_ref.shape[1], own_ref.shape[1]
    flat[:EDGE] = jnp.zeros((EDGE, LANES), F32)
    flat[EDGE : EDGE + reach] = above_ref[0]
    flat[EDGE + reach : EDGE + reach + cells] = own_ref[0]
    flat[EDGE + reach + cells : EDGE + 2 * reach + cells] = below_ref[0]
    flat[EDGE + 2 * reach + cells :] = jnp.zeros((EDGE, LANES), F32)


def backward_kernel(
    place_ref, ids_scalar, ids_ref, above_ref, own_ref, below_ref, mix_ref, kern_ref, canvas_ref, gain_ref,
    dmiddle_ref, in_ref, *rest, rows, cols,
):
    dcanvas_ref, kept_ref, sent_ref, small_kept_ref, small_sent_ref = rest[-18:-13]
    row_taps, padded, valid_ref, col_ref, flat, shifted, laid, wide, dk, sums, djoined, normed, dnorm = rest[-13:]
    step = pl.program_id(0)
    cells = rows * cols
    reach = REACH * cols
    core = place_ref[0] % 2
    split = laid.shape[0] * LANES - kern_ref.shape[1]
    width = in_ref.shape[1] // (2 * kept_ref.shape[1])

    @pl.when(step == 0)
    def _():
        lay_kernel(kern_ref, laid, split)
        turned = image_ids(ids_ref, padded, place_ref[0], rows)
        spread_cells((turned >= 0).astype(F32), valid_ref, 0, rows + 2 * REACH)
        conv_masks(ids_scalar, ids_ref, place_ref[0], row_taps, col_ref, rows)
        hat, _ = normalized(canvas_ref[...] * valid_ref[reach : reach + cells, :1])
        normed[...] = hat * gain_ref[...]
        dnorm[...] = jnp.zeros_like(dnorm)

    lay_flat(above_ref, own_ref, below_ref, flat)
    fill_shifted(flat, col_ref, shifted, rows + 2 * REACH, cols)
    conv_grad_block(
        row_taps, laid[step], shifted, wide, dk, mix_ref.at[0], djoined.at[step % 2], sums.at[step], rows, cols
    )

    @pl.when(step % 2 == 1)
    def _():
        grad = jnp.concatenate([djoined[0], djoined[1]], axis=1)
        share_columns(core, dot(normed[...], grad, TN), kept_ref, sent_ref, width, plane_first=True)
        dnorm[...] += dot(grad, in_ref[...], NT)

    @pl.when(step == pl.num_programs(0) - 1)
    def _():
        hat, scale = normalized(canvas_ref[...] * valid_ref[reach : reach + cells, :1])
        dgain = jnp.sum(dnorm[...] * hat, axis=0, keepdims=True)
        count = sums.shape[0]
        for k in range(dgain.shape[1] // LANES):
            sums[count - 1, TAPS + k : TAPS + k + 1] = dgain[:, k * LANES : (k + 1) * LANES]
        for ref, start in ((small_kept_ref, core * (count // 2)), (small_sent_ref, (1 - core) * (count // 2))):
            ref[...] = sums[pl.ds(start, count // 2)].reshape(ref.shape)
        inner = dmiddle_ref[...] + norm_backward(dnorm[...] * gain_ref[...], hat, scale)
        dcanvas_ref[...] = inner * valid_ref[reach : reach + cells, :1]


def block_of(size):
    return pl.BlockSpec((1, size, LANES), lambda i: (i, 0, 0))


def backward(
    place, ids, above, own, below, mix, kern, canvas, gain, dmiddle, weight_in, ties, rows, cols, count_ha, count_ba
):
    cells, dim = canvas.shape
    blocks = own.shape[0]
    reach = above.shape[1]
    own_wide = weight_in.shape[1] // count_ha
    chunk_rows = dim // count_ba * lane_blocks(own_wide)
    groups = 2 * LANES // (2 * own_wide)
    chunk_spec = pl.BlockSpec((count_ba, groups, chunk_rows, LANES), lambda i: (0, i // 2, 0, 0))
    chunks = shape_of(count_ba, count_ha // 2, chunk_rows, LANES)
    tall = -(-(TAPS + dim // LANES) // 8) * 8
    small = (blocks // 2 * tall, LANES)
    return pl.pallas_call(
        functools.partial(backward_kernel, rows=rows, cols=cols),
        grid=(blocks,),
        in_specs=[in_smem(), in_smem(), whole(ids.shape)]
        + [block_of(size) for size in (reach, cells, reach, cells)]
        + [whole(kern.shape), whole(canvas.shape)]
        + [whole((1, dim)), whole((cells, dim))]
        + [pl.BlockSpec((dim, 2 * LANES), lambda i: (0, i // 2))]
        + [in_hbm()] * len(ties),
        out_specs=[whole((cells, dim)), chunk_spec, chunk_spec, whole(small), whole(small)],
        out_shape=[shape_of(cells, dim), chunks, chunks, shape_of(*small), shape_of(*small)],
        scratch_shapes=mask_scratch(ids, rows)
        + [
            pltpu.VMEM((KERN, cols // 8, 8, LANES), F32),
            pltpu.VMEM((cells + 2 * reach + 2 * EDGE, LANES), F32),
            pltpu.VMEM((KERN, rows + 2 * REACH, cols // 8, 8, LANES), F32),
            pltpu.VMEM((blocks, TAPS, LANES), F32),
            pltpu.VMEM((TAPS + KERN, 8, LANES), F32),
            pltpu.VMEM((TAPS, 8, LANES), F32),
            pltpu.VMEM((blocks, tall, LANES), F32),
            pltpu.VMEM((2, cells, LANES), F32),
            pltpu.VMEM((cells, dim), F32),
            pltpu.VMEM((cells, dim), F32),
        ],
        compiler_params=params(),
        cost_estimate=lasting(25),
    )(place, ids, ids, above, own, below, mix, kern, canvas, gain, dmiddle, weight_in, *ties)


def exchange(values, axis, bit):
    return lax.ppermute(values, axis, [(i, i ^ bit) for i in range(lax.axis_size(axis))])


class View:
    def __init__(self, array, start, ways, fixed, rows):
        self.array, self.start, self.ways, self.fixed, self.rows = array, start, ways, fixed, rows

    def fix(self, way, step):
        if way == "line":
            near = lax.axis_size("ha") // 4
            return self.fix("far", step // near).fix("near", step % near)
        left = [entry for entry in self.ways if entry[0] != way]
        (stride,) = [entry[2] for entry in self.ways if entry[0] == way]
        return View(self.array, self.start, left, self.fixed + [(way, step, stride)], self.rows)

    def size(self):
        count = self.rows
        for _, size, _ in self.ways:
            count *= size
        return count

    def runs(self, ha, ba):
        start = self.start
        near = lax.axis_size("ha") // 4
        places = {"plane": ba, "far": ha // 2 // near, "near": ha // 2 % near}
        for way, step, stride in self.fixed:
            start = start + (places[way] ^ step) * stride
        rows, ways = self.rows, list(self.ways)
        while ways and ways[-1][2] == rows:
            rows *= ways.pop()[1]
        offsets = [0]
        for _, size, stride in ways:
            offsets = [offset + k * stride for offset in offsets for k in range(size)]
        return [pl.multiple_of(start + offset, 8) for offset in offsets], rows


def flat_view(array, start=0, rows=None):
    flat = array.reshape(-1, LANES)
    return View(flat, start, [], [], flat.shape[0] if rows is None else rows)


def combine(place, groups, ties=(), epilogue=None, out_shape=None):
    pieces, arrays = [], []
    for group in groups:
        for views in group:
            if not any(views is other for other in pieces):
                pieces.append(views)
    for views in pieces:
        for view in views:
            if not any(view.array is other for other in arrays):
                arrays.append(view.array)
    index_of = {id(array): k for k, array in enumerate(arrays)}
    piece_of = {id(views): k for k, views in enumerate(pieces)}
    sizes = [sum(views[0].size() for views in group) for group in groups]
    copies = sum(len(view.runs(0, 0)[0]) for views in pieces for view in views)
    plain = epilogue is None
    if plain:
        out_shape = [shape_of(size, LANES) for size in sizes]

    def kernel(place_ref, *refs):
        inputs = refs[: len(arrays)]
        refs = refs[len(arrays) + len(ties) :]
        outs, refs = refs[: len(out_shape)], refs[len(out_shape) :]
        buffers, refs = refs[: len(pieces)], refs[len(pieces) :]
        sems, results, out_sems = refs[0], refs[1:-1], refs[-1]
        ha, ba = place_ref[0], place_ref[1]
        moves, count = [], 0
        for piece, views in enumerate(pieces):
            moves.append([])
            for term, view in enumerate(views):
                source = inputs[index_of[id(view.array)]]
                starts, rows = view.runs(ha, ba)
                for k, start in enumerate(starts):
                    target = buffers[piece].at[term, pl.ds(k * rows, rows), :]
                    move = pltpu.make_async_copy(source.at[pl.ds(start, rows), :], target, sems.at[count])
                    move.start()
                    moves[-1].append(move)
                    count += 1
        values, waited, leaving = [], set(), []
        for out, group in enumerate(groups):
            row = 0
            for views in group:
                piece = piece_of[id(views)]
                if piece not in waited:
                    waited.add(piece)
                    for move in moves[piece]:
                        move.wait()
                value = buffers[piece][0]
                for term in range(1, len(views)):
                    value = value + buffers[piece][term]
                if plain:
                    results[out][row : row + value.shape[0], :] = value
                values.append(value)
                row += value.shape[0]
            if plain:
                leaving.append(pltpu.make_async_copy(results[out], outs[out], out_sems.at[out]))
                leaving[-1].start()
        if not plain:
            epilogue(ha, ba, values, outs)
        for move in leaving:
            move.wait()

    moved = sum(view.size() for views in pieces for view in views) + sum(sizes)
    scratch = [pltpu.VMEM((len(views), views[0].size(), LANES), F32) for views in pieces]
    scratch.append(pltpu.SemaphoreType.DMA((copies,)))
    if plain:
        scratch += [pltpu.VMEM((size, LANES), F32) for size in sizes]
    scratch.append(pltpu.SemaphoreType.DMA((len(groups),)))
    return pl.pallas_call(
        kernel,
        in_specs=[in_smem()] + [in_hbm()] * (len(arrays) + len(ties)),
        out_specs=[in_hbm() if plain else pl.BlockSpec(memory_space=pltpu.VMEM)] * len(out_shape),
        out_shape=out_shape,
        scratch_shapes=scratch,
        compiler_params=params(),
        cost_estimate=lasting(1 + moved * LANES * 4 / 3.0e6),
    )(place, *arrays, *ties)


def tied(arrays, ties):
    return pl.pallas_call(
        lambda *refs: None,
        in_specs=[pl.BlockSpec(memory_space=pl.ANY)] * (len(arrays) + len(ties)),
        out_specs=[pl.BlockSpec(memory_space=pl.ANY)] * len(arrays),
        out_shape=[shape_of(*array.shape) for array in arrays],
        input_output_aliases={k: k for k in range(len(arrays))},
        compiler_params=params(),
    )(*arrays, *ties)


class Sum:
    def __init__(self, arrays, names):
        self.views = []
        near = lax.axis_size("ha") // 4
        sizes = {"plane": lax.axis_size("ba"), "far": 2, "near": near}
        for array in arrays:
            flat = array.reshape(-1, LANES)
            stride, ways = flat.shape[0], []
            for name in names:
                stride //= sizes[name]
                ways.append((name, sizes[name], stride))
            self.views.append(View(flat, 0, ways, [], stride))

    def leaving(self, way, step):
        return [view.fix(way, step) for view in self.views]

    def keep(self, way, sent, arrived):
        self.views = [view.fix(way, 0) for view in self.views]
        rows = self.views[0].rows
        stride, ways = rows, []
        for name, size, _ in reversed(self.views[0].ways):
            ways.insert(0, (name, size, stride))
            stride *= size
        self.views += [View(array, start, ways, [], rows) for array, start in arrived]

    def part(self, first, rows):
        return [View(view.array, view.start + first, view.ways, view.fixed, rows) for view in self.views]


class Rider:
    def __init__(self, views):
        self.views = views

    def leaving(self, way, step):
        return self.views

    def keep(self, way, sent, arrived):
        rows = self.views[0].size()
        self.views = [View(array, start, [], [], rows) for array, start in [sent] + arrived]


class Gather(Rider):
    def keep(self, way, sent, arrived):
        rows = self.views[0].size()
        self.gathered = [[View(array, start, [], [], rows)] for array, start in [sent] + arrived]


class Stage:
    def __init__(self, members, way):
        self.members, self.way = members, way
        line, near = lax.axis_size("ha") // 2, lax.axis_size("ha") // 4
        self.steps = {"plane": range(1, lax.axis_size("ba")), "line": range(1, line), "far": [near]}[way]
        self.near = near

    def taking(self, step):
        return [(one, way) for one, way in self.members if way != "near" or step < self.near]

    def groups(self):
        return [
            [one.leaving(way, step // self.near if way == "far" else step) for one, way in self.taking(step)]
            for step in self.steps
        ]

    def go(self, payloads):
        axis, unit = ("ba", 1) if self.way == "plane" else ("ha", 2)
        arrived = [exchange(part, axis, unit * step) for step, part in zip(self.steps, payloads)]
        places = {}
        for step, sent, part in zip(self.steps, payloads, arrived):
            row = 0
            for one, way in self.taking(step):
                places.setdefault(id(one), []).append(((sent, row), (part, row)))
                row += one.leaving(way, 1)[0].size()
        for one, way in self.members:
            mine = places.get(id(one), [])
            one.keep(way, mine[0][0] if mine else None, [part for _, part in mine])
        return arrived


def run(place, stages):
    groups = [group for stage in stages for group in stage.groups()]
    made = combine(place, groups)
    rest, arrived = made, []
    for stage in stages:
        arrived += stage.go(rest[: len(stage.steps)])
        rest = rest[len(stage.steps) :]
    return made, arrived


def neighbour_rows(top, bottom):
    count = lax.axis_size("ha")
    up = [(i, i + 1) for i in range(count - 1)]
    down = [(i + 1, i) for i in range(count - 1)]
    return lax.ppermute(bottom, "ha", up), lax.ppermute(top, "ha", down)


def lay_beside(value, ref):
    tall, width = ref.shape
    for k in range(lane_blocks(width)):
        columns = slice(k * LANES, min(width, (k + 1) * LANES))
        ref[:, columns] = value[k * tall : (k + 1) * tall, : columns.stop - columns.start]


def lay_large(ha, ba, values, outs):
    up_first, up_second, down_first, down_second, out = values
    lay_beside(jnp.concatenate([up_first, up_second], axis=0), outs[0])
    lay_beside(jnp.concatenate([down_first, down_second], axis=0), outs[1])
    lay_beside(out, outs[2])


def lay_small(ha, ba, values, outs, blocks):
    din_ref, dk_ref, gain_ref = outs[:3]
    scratch = outs[-1]
    lay_beside(values[0], din_ref)
    own, other = values[1], values[2]
    small_rows = blocks // 2 * (-(-(TAPS + gain_ref.shape[1] // LANES) // 8) * 8)
    mine = ha % 2 == 0
    first, second = jnp.where(mine, own, other), jnp.where(mine, other, own)
    dkern = jnp.concatenate([first[:small_rows], second[:small_rows]], axis=0)
    tall = dkern.shape[0] // blocks
    joined = jnp.concatenate([dkern[k * tall : k * tall + TAPS] for k in range(blocks)], axis=1)
    dk_ref[...] = joined[:, joined.shape[1] - dk_ref.shape[1] :]
    half = own.shape[0] - small_rows
    count = lax.axis_size("ba")
    part = half // count
    for core, rows in ((0, first), (1, second)):
        for step in range(count):
            start = core * half + (ba ^ step) * part
            source = small_rows + step * part
            scratch[pl.ds(pl.multiple_of(start, 8), part), :] = rows[source : source + part]
    dim = gain_ref.shape[1]
    for k in range(dim // LANES):
        columns = slice(k * LANES, (k + 1) * LANES)
        row = (blocks - 1) * tall + TAPS + k
        gain_ref[:, columns] = dkern[row : row + 1]
        for vector, ref in enumerate(outs[3:6]):
            ref[:, columns] = scratch[vector * dim // LANES + k : vector * dim // LANES + k + 1, :]
    row = scratch.shape[0]
    for ref in reversed(outs[6:-1]):
        tall, width = ref.shape
        row -= tall * width // LANES
        for k in range(width // LANES):
            ref[:, k * LANES : (k + 1) * LANES] = scratch[row + k * tall : row + (k + 1) * tall, :]


def shards(
    canvas,
    image_id,
    keep_first,
    keep_second,
    first_gain,
    weight_in,
    depth_kernel,
    gate_first,
    gate_second,
    gate_third,
    weight_out,
    scale_first,
    second_gain,
    weight_up,
    weight_down,
    scale_second,
    cotangent,
):
    _, rows, cols, dim = canvas.shape
    cells = rows * cols
    reach = REACH * cols
    count_ha, count_ba = lax.axis_size("ha"), lax.axis_size("ba")
    hidden = weight_up.shape[1]
    blocks = weight_in.shape[1] // LANES
    place = jnp.stack([lax.axis_index("ha"), lax.axis_index("ba")])
    own = canvas.reshape(cells, dim)
    gates = (gate_first, gate_second, gate_third)
    gain = first_gain[None]
    vectors = (gain, scale_first[None], second_gain[None], scale_second[None])
    ids = image_id[0]
    above, below = neighbour_rows(own[:reach], own[cells - reach :])
    (
        joined, output, dmiddle, dconv, dconv_top, dconv_bottom, plane_kept, plane_sent, line_kept, line_sent,
        packed_kept, packed_sent,
    ) = forward(
        place, ids, keep_first, keep_second, above, own, below, cotangent.reshape(cells, dim), vectors,
        weight_in, depth_kernel, gates, weight_out, weight_up, weight_down, rows, cols, count_ha, count_ba,
    )
    above, below = neighbour_rows(dconv_top, dconv_bottom)

    plane_sum = Sum([plane_kept, exchange(plane_sent, "ha", 1)], ["plane", "far", "near"])
    line_sum = Sum([line_kept, exchange(line_sent, "ha", 1)], ["far", "near", "plane"])
    packed = Sum([packed_kept, exchange(packed_sent, "ha", 1)], ["plane"])
    made, arrived = run(
        place, [Stage([(line_sum, "far")], "far"), Stage([(plane_sum, "plane"), (packed, "plane")], "plane")]
    )
    dcanvas, in_kept, in_sent, small_kept, small_sent = backward(
        place, ids, above, dconv, below, joined, depth_kernel, own, gain, dmiddle, weight_in, made,
        rows, cols, count_ha, count_ba,
    )
    in_sent, small_sent = tied([in_sent, small_sent], arrived)
    in_sum = Sum([in_kept, exchange(in_sent, "ha", 1)], ["plane", "far", "near"])
    small = Rider([flat_view(small_kept), flat_view(exchange(small_sent, "ha", 1))])
    packed = Rider(packed.views)
    run(
        place,
        [
            Stage([(plane_sum, "line"), (packed, "line"), (line_sum, "near")], "line"),
            Stage([(in_sum, "plane"), (small, "plane")], "plane"),
        ],
    )
    packed = Gather(packed.views)
    run(
        place,
        [
            Stage([(in_sum, "line"), (small, "line")], "line"),
            Stage([(line_sum, "plane"), (packed, "plane")], "plane"),
        ],
    )
    cut = plane_sum.views[0].rows // 2
    rest = (line_sum.views[0].rows - dim // count_ha * lane_blocks(dim // count_ba)) // 2
    dup, ddown, dout = combine(
        place,
        [
            [
                plane_sum.part(0, cut),
                line_sum.part(0, rest),
                plane_sum.part(cut, cut),
                line_sum.part(rest, rest),
                line_sum.part(2 * rest, line_sum.views[0].rows - 2 * rest),
            ]
        ],
        epilogue=lay_large,
        out_shape=[
            shape_of(dim // count_ba, hidden // count_ha),
            shape_of(dim // count_ha, hidden // count_ba),
            shape_of(dim // count_ha, dim // count_ba),
        ],
    )
    (halves_of,) = combine(place, [[small.views] + packed.gathered])
    din, dkern, dgain_one, dscale_one, dgain_two, dscale_two, dfirst, dsecond, dthird, _ = combine(
        place,
        [[in_sum.views, [flat_view(halves_of)], [flat_view(exchange(halves_of, "ha", 1))]]],
        epilogue=functools.partial(lay_small, blocks=blocks),
        out_shape=[shape_of(dim // count_ba, weight_in.shape[1] // count_ha), shape_of(*depth_kernel.shape)]
        + [shape_of(1, dim)] * 4
        + [shape_of(*gate.shape) for gate in gates]
        + [shape_of(packed_rows(gates, dim, count_ba), LANES)],
    )
    return (
        output.reshape(canvas.shape),
        dcanvas.reshape(canvas.shape),
        dgain_one[0],
        din,
        dkern,
        dfirst,
        dsecond,
        dthird,
        dout.T,
        dscale_one[0],
        dgain_two[0],
        dup,
        ddown.T,
        dscale_two[0],
    )


def solution(mesh):
    in_specs = (
        P("ba", "ha", None, None),
        P("ba", None, None),
        P("ba", None),
        P("ba", None),
    ) + (P(),) * 12 + (P("ba", "ha", None, None),)
    tiled = P("ba", "ha")
    out_specs = (
        P("ba", "ha", None, None),
        P("ba", "ha", None, None),
        P(),
        tiled,
        P(),
        P(),
        P(),
        P(),
        tiled,
        P(),
        P(),
        tiled,
        tiled,
        P(),
    )
    return jax.shard_map(shards, mesh=mesh, in_specs=in_specs, out_specs=out_specs, check_vma=False)
```

```python
import functools

import jax
import jax.numpy as jnp
from jax import lax
from jax.experimental import pallas as pl
from jax.experimental.pallas import tpu as pltpu
from jax.sharding import PartitionSpec as P

KERN = 7
TAPS = KERN * KERN
REACH = KERN // 2
KEEP_RATE = 0.8
SPREAD = 1.0 / 3.0
EPSILON = 1e-06
LANES = 128
EDGE = 8
VMEM_BYTES = 64 << 20
F32 = jnp.float32
INV_SQRT_2 = 0.7071067811865476
INV_SQRT_2PI = 0.3989422804014327
NN = (((1,), (0,)), ((), ()))
NT = (((1,), (1,)), ((), ()))
TN = (((0,), (0,)), ((), ()))


def dot(left, right, dims=NN):
    return lax.dot_general(left, right, dims, precision=lax.Precision.HIGH, preferred_element_type=F32)


def normalized(values):
    centered = values - jnp.mean(values, axis=-1, keepdims=True)
    scale = lax.rsqrt(jnp.mean(centered * centered, axis=-1, keepdims=True) + EPSILON)
    return centered * scale, scale


def norm_backward(grad_hat, hat, scale):
    return scale * (
        grad_hat
        - jnp.mean(grad_hat, axis=-1, keepdims=True)
        - hat * jnp.mean(grad_hat * hat, axis=-1, keepdims=True)
    )


def params():
    return pltpu.CompilerParams(vmem_limit_bytes=VMEM_BYTES)


def lasting(microseconds):
    return pl.CostEstimate(flops=int(microseconds * 1.1e9), bytes_accessed=0, transcendentals=0)


def whole(shape):
    return pl.BlockSpec(tuple(shape), lambda *_: (0,) * len(shape), pipeline_mode=pl.Buffered(1))


def in_smem():
    return pl.BlockSpec(memory_space=pltpu.SMEM)


def in_hbm():
    return pl.BlockSpec(memory_space=pltpu.HBM)


def shape_of(*shape):
    return jax.ShapeDtypeStruct(shape, F32)


def lane_blocks(width):
    return -(-width // LANES)


def image_ids(ids_ref, padded, place, rows):
    height, cols = ids_ref.shape
    padded[...] = jnp.full(padded.shape, -1, jnp.int32)
    padded[EDGE : EDGE + height, :] = ids_ref[...]
    ids = padded[pl.ds(place * rows + (EDGE - REACH), rows + 2 * REACH), :]
    return jnp.concatenate([ids, jnp.full((-ids.shape[0] % 8, cols), -1, jnp.int32)], axis=0).T


def spread_cells(factors, out_ref, first, rows):
    cols = factors.shape[0]
    for r in range(rows):
        column = factors[:, first + r : first + r + 1]
        out_ref[r * cols : (r + 1) * cols, :] = jnp.broadcast_to(column, (cols, LANES))


def keep_factors(turned, table_ref):
    result = jnp.zeros(turned.shape, F32)
    for slot in range(table_ref.shape[1]):
        result = jnp.where(turned == slot, table_ref[0, slot].astype(F32) / KEEP_RATE, result)
    return result


def conv_masks(ids_scalar, ids_ref, place, row_taps, col_mask, rows):
    height, cols = ids_ref.shape
    wide_ids = jnp.broadcast_to(ids_ref[...].T[:, height // 2 : height // 2 + 1], (cols, LANES))
    column = lax.broadcasted_iota(jnp.int32, (cols, LANES), 0)
    for b in range(KERN):
        shift = b - REACH
        moved = pltpu.roll(wide_ids, (-shift) % cols, 0)
        inside = (column + shift >= 0) & (column + shift < cols)
        same = (moved == wide_ids) & inside
        col_mask[b] = same.astype(F32).reshape(cols // 8, 8, LANES)

    def one(r, _):
        own = ids_scalar[place * rows + r, cols // 2]
        row_taps[r, 0] = KERN
        row_taps[r, KERN + 1] = KERN
        for a in range(KERN):
            other = place * rows + r + a - REACH
            inside = (other >= 0) & (other < height)
            same = ids_scalar[jnp.clip(other, 0, height - 1), cols // 2] == own
            row_taps[r, a + 1] = jnp.where(inside & same, a, KERN)
        return 0

    lax.fori_loop(0, rows, one, 0)


def lay_kernel(kern_ref, laid, split):
    tap = lax.broadcasted_iota(jnp.int32, (TAPS, split), 0)
    own = jnp.where(tap == TAPS // 2, 1.0 / SPREAD, 0.0).astype(F32)
    for k in range(laid.shape[0]):
        start = k * LANES - split
        left = own if k == 0 else kern_ref[:, start : start + split]
        laid[k] = jnp.concatenate([left, kern_ref[:, start + split : start + LANES]], axis=1) * SPREAD


def fill_shifted(flat, col_ref, shifted, rows_ext, cols):
    for b in range(KERN):
        for g in range(cols // 8):
            mask = None if b == REACH else col_ref[b, g]
            for r in range(rows_ext):
                x = flat[pl.ds(EDGE + r * cols + 8 * g + b - REACH, 8), :]
                shifted[b, r, g] = x if b == REACH else x * mask


def spread_taps(kern, wide, turned):
    for t in range(TAPS):
        source = TAPS - 1 - t if turned else t
        wide[t] = jnp.broadcast_to(kern[source : source + 1, :], (8, LANES))
    for t in range(KERN):
        wide[TAPS + t] = jnp.zeros((8, LANES), F32)


def conv_block(row_taps, kern, shifted, wide, out_ref, rows, cols):
    groups = cols // 8
    spread_taps(kern, wide, False)

    def pair(h, _):
        r = 2 * h

        def step(i, totals):
            first, second = totals
            taps_first = row_taps[r, i + 1] * KERN
            taps_second = row_taps[r + 1, i] * KERN
            for b in range(KERN):
                x = shifted[b, r + i]
                first = first + wide[taps_first + b][None] * x
                second = second + wide[taps_second + b][None] * x
            return first, second

        zero = jnp.zeros((groups, 8, LANES), F32)
        first, second = lax.fori_loop(0, KERN + 1, step, (zero, zero), unroll=4)
        out_ref[pl.ds(pl.multiple_of(r * cols, cols), cols), :] = first.reshape(cols, LANES)
        out_ref[pl.ds(pl.multiple_of((r + 1) * cols, cols), cols), :] = second.reshape(cols, LANES)
        return 0

    lax.fori_loop(0, rows // 2, pair, 0)


def conv_grad_block(row_taps, kern, shifted, wide, dk, mix_ref, out_ref, dk_ref, rows, cols):
    groups = cols // 8
    spread_taps(kern, wide, True)
    for t in range(TAPS):
        dk[t] = jnp.zeros((8, LANES), F32)

    def one(r, _):
        start = pl.ds(pl.multiple_of(r * cols, cols), cols)
        mix = mix_ref[start, :].reshape(groups, 8, LANES)
        total = jnp.zeros((groups, 8, LANES), F32)
        for i in range(KERN):
            row = row_taps[r, i + 1]
            same = jnp.where(row < KERN, 1.0, 0.0).astype(F32)
            for b in range(KERN):
                x = shifted[b, r + i]
                total = total + wide[row * KERN + b][None] * x
                dk[i * KERN + b] += jnp.sum(mix * x, axis=0) * same
        out_ref[start, :] = total.reshape(cols, LANES)
        return 0

    lax.fori_loop(0, rows, one, 0)
    for t in range(TAPS):
        dk_ref[TAPS - 1 - t : TAPS - t, :] = jnp.sum(dk[t], axis=0, keepdims=True) * SPREAD
    dk_ref[TAPS:, :] = jnp.zeros((dk_ref.shape[0] - TAPS, LANES), F32)


def share(core, first, second, kept_ref, sent_ref, z, p):
    mine = core == 0
    tall, width = first.shape
    for ref, chunk in (
        (kept_ref, jnp.where(mine, first, second)),
        (sent_ref, jnp.where(mine, second, first)),
    ):
        for k in range(lane_blocks(width)):
            part = chunk[:, k * LANES : (k + 1) * LANES]
            if part.shape[1] < LANES:
                part = jnp.concatenate([part, jnp.zeros((tall, LANES - part.shape[1]), F32)], axis=1)
            ref[z, p, k * tall : (k + 1) * tall, :] = part


def share_columns(core, grad, kept_ref, sent_ref, width, plane_first=False):
    groups, parts = reversed(kept_ref.shape[:2]) if plane_first else kept_ref.shape[:2]
    tall = grad.shape[0] // parts
    for z in range(groups):
        for p in range(parts):
            rows = slice(p * tall, (p + 1) * tall)
            first = grad[rows, 2 * z * width : (2 * z + 1) * width]
            second = grad[rows, (2 * z + 1) * width : (2 * z + 2) * width]
            share(core, first, second, kept_ref, sent_ref, *((p, z) if plane_first else (z, p)))


def share_rows(core, grad, kept_ref, sent_ref, tall):
    groups, parts = kept_ref.shape[:2]
    width = grad.shape[1] // parts
    for z in range(groups):
        for p in range(parts):
            columns = slice(p * width, (p + 1) * width)
            first = grad[2 * z * tall : (2 * z + 1) * tall, columns]
            second = grad[(2 * z + 1) * tall : (2 * z + 2) * tall, columns]
            share(core, first, second, kept_ref, sent_ref, z, p)


class Copies:
    def __init__(self, sems):
        self.sems, self.count, self.pending = sems, 0, {}

    def start(self, name, source, target):
        copy = pltpu.make_async_copy(source, target, self.sems.at[self.count])
        self.count += 1
        copy.start()
        self.pending.setdefault(name, []).append(copy)

    def wait(self, *names):
        for name in names:
            for copy in self.pending.pop(name):
                copy.wait()

    def wait_all(self):
        self.wait(*list(self.pending))


def forward_kernel(
    place_ref, ids_scalar, one_table, two_table, ids_hbm, above_hbm, own_hbm, below_hbm, cot_hbm,
    first_gain_hbm, first_scale_hbm, second_gain_hbm, second_scale_hbm,
    in_hbm_ref, kern_hbm, one_hbm, two_hbm, three_hbm, out_hbm, up_hbm, down_hbm,
    joined_hbm, output_hbm, dmiddle_hbm, dconv_hbm, dconv_top_hbm, dconv_bottom_hbm,
    plane_kept_ref, plane_sent_ref, line_kept_ref, line_sent_ref, packed_kept_hbm, packed_sent_hbm,
    ids_ref, rows_ref, cot_ref, first_gain_ref, first_scale_ref, second_gain_ref, second_scale_ref,
    in_ref, kern_ref, one_ref, two_ref, three_ref, out_ref, up_ref, down_ref, dconv_ref, sems, chunk_sems,
    up_kept, up_sent, down_kept, down_sent, out_kept, out_sent,
    row_taps, padded, valid_ref, one_keep_ref, two_keep_ref, col_ref, packed_ref, normed, flat, shifted, laid, wide, conv,
    mixed_ref, mapped_ref, middle_ref, result, dnorm,
    *, rows, cols, count_ha, count_ba,
):
    blocks = flat.shape[0]
    cells = rows * cols
    reach = REACH * cols
    cells_ext = cells + 2 * reach
    core = place_ref[0] % 2
    split = one_ref.shape[0]
    dim = rows_ref.shape[1]
    head_steps = blocks // 2
    ffn_steps = up_kept.shape[0]
    chunk = down_ref.shape[1]
    gate_refs = (one_ref, two_ref, three_ref)

    copies = Copies(sems)
    copies.start("ids", ids_hbm, ids_ref)
    copies.start("above", above_hbm, rows_ref.at[pl.ds(0, reach)])
    copies.start("own", own_hbm, rows_ref.at[pl.ds(reach, cells)])
    copies.start("below", below_hbm, rows_ref.at[pl.ds(reach + cells, reach)])
    copies.start("vectors", first_gain_hbm, first_gain_ref)
    for k in range(head_steps):
        copies.start(("in", k), in_hbm_ref.at[:, pl.ds(2 * LANES * k, 2 * LANES)], in_ref.at[k])
    copies.start("kern", kern_hbm, kern_ref)
    def weights(k):
        ends = pl.ds(pl.multiple_of(k * chunk, chunk), chunk)
        return [
            pltpu.make_async_copy(up_hbm.at[:, ends], up_ref.at[k], chunk_sems.at[k, 0]),
            pltpu.make_async_copy(down_hbm.at[ends, :], down_ref.at[k], chunk_sems.at[k, 1]),
        ]

    def chunk_copies(place):
        moves = []
        sides = ((up_kept, down_kept, plane_kept_ref, line_kept_ref), (up_sent, down_sent, plane_sent_ref, line_sent_ref))
        for up, down, plane, line in sides:
            cut = plane.shape[2] // 2
            rest = up.shape[3] - cut
            zs = pl.ds(place * up.shape[1], up.shape[1])
            bas = pl.ds(place * down.shape[2], down.shape[2])
            moves += [
                (up.at[place, :, ba, pl.ds(0, cut), :], plane.at[ba, zs, pl.ds(0, cut), :])
                for ba in range(plane.shape[0])
            ]
            moves += [
                (down.at[place, z, :, pl.ds(0, cut), :], plane.at[bas, z, pl.ds(cut, cut), :])
                for z in range(plane.shape[1])
            ]
            moves.append((up.at[place, :, :, pl.ds(cut, rest), :], line.at[zs, :, pl.ds(0, rest), :]))
            moves.append((down.at[place, :, :, pl.ds(cut, rest), :], line.at[:, bas, pl.ds(rest, rest), :]))
        return [
            pltpu.make_async_copy(source, target, chunk_sems.at[place, 2 + k])
            for k, (source, target) in enumerate(moves)
        ]

    copies.wait("ids")
    turned = image_ids(ids_ref, padded, place_ref[0], rows)
    spread_cells((turned >= 0).astype(F32), valid_ref, 0, rows + 2 * REACH)
    spread_cells(keep_factors(turned, one_table), one_keep_ref, REACH, rows)
    spread_cells(keep_factors(turned, two_table), two_keep_ref, REACH, rows)
    conv_masks(ids_scalar, ids_ref, place_ref[0], row_taps, col_ref, rows)
    copies.wait("vectors")
    start = 0
    for name, size in (("above", reach), ("own", cells), ("below", reach)):
        copies.wait(name)
        hat, _ = normalized(rows_ref[start : start + size, :] * valid_ref[start : start + size, :1])
        normed[start : start + size] = hat * first_gain_ref[...]
        start += size

    for k in range(blocks):
        flat[k, :EDGE] = jnp.zeros((EDGE, LANES), F32)
        flat[k, EDGE + cells_ext :] = jnp.zeros((EDGE, LANES), F32)
    for step in range(head_steps):
        copies.wait(("in", step))
        joined = dot(normed[...], in_ref[step])
        for k in range(2):
            flat[2 * step + k, EDGE : EDGE + cells_ext] = joined[:, k * LANES : (k + 1) * LANES]
        if step == 0:
            copies.start("gates", first_scale_hbm, first_scale_ref)
            copies.start("gates", second_gain_hbm, second_gain_ref)
            copies.start("gates", second_scale_hbm, second_scale_ref)
            for source, target in zip((one_hbm, two_hbm, three_hbm, out_hbm, cot_hbm), gate_refs + (out_ref, cot_ref)):
                copies.start("gates", source, target)
            for k in range(ffn_steps):
                for copy in weights(k):
                    copy.start()
        pair = pl.ds(2 * step, 2)
        copies.start("outs", flat.at[pair, pl.ds(EDGE + reach, cells), :], joined_hbm.at[pair])

    copies.wait("kern")
    lay_kernel(kern_ref, laid, split)

    def conv_step(block, _):
        fill_shifted(flat.at[block], col_ref, shifted, rows + 2 * REACH, cols)
        conv_block(row_taps, laid[block], shifted, wide, conv.at[block], rows, cols)
        return 0

    lax.fori_loop(0, blocks, conv_step, 0)

    def conv_part(start, width):
        return jnp.concatenate([conv[start // LANES + k] for k in range(width // LANES)], axis=1)

    copies.wait("gates")
    mixed = conv[0, :, :split] * conv[0, :, split:]
    mixed_ref[:, :split] = mixed
    start = 2 * split
    for ref in gate_refs:
        width = ref.shape[1]
        mapped = dot(mixed, ref[...])
        mapped_ref[:, start - 2 * split : start - 2 * split + width] = mapped
        mixed = mapped * conv_part(start, width)
        mixed_ref[:, start : start + width] = mixed
        start += width
    branch = dot(mixed, out_ref[...])
    masked = rows_ref[reach : reach + cells, :] * valid_ref[reach : reach + cells, :1]
    middle = masked + one_keep_ref[:, :1] * first_scale_ref[...] * branch
    middle_ref[...] = middle
    hat, _ = normalized(middle)
    normed[:cells] = hat * second_gain_ref[...]
    result[...] = jnp.zeros_like(result)
    dnorm[...] = jnp.zeros_like(dnorm)

    def ffn_step(place, _):
        for copy in weights(place):
            copy.wait()
        grad_result = two_keep_ref[:, :1] * second_scale_ref[...] * cot_ref[...]
        pre = dot(normed[:cells], up_ref[place])
        cdf = 0.5 + 0.5 * lax.erf(pre * INV_SQRT_2)
        slope = cdf + pre * (INV_SQRT_2PI * jnp.exp(-0.5 * pre * pre))
        hidden = pre * cdf
        result[...] += dot(hidden, down_ref[place])
        grad_pre = dot(grad_result, down_ref[place], NT) * slope
        share_rows(
            core, dot(grad_result, hidden, TN), down_kept.at[place], down_sent.at[place], dim // count_ha
        )
        width = chunk // (2 * up_kept.shape[1])
        share_columns(core, dot(normed[:cells], grad_pre, TN), up_kept.at[place], up_sent.at[place], width)
        for copy in chunk_copies(place):
            copy.start()
        dnorm[...] += dot(grad_pre, up_ref[place], NT)
        return 0

    lax.fori_loop(0, ffn_steps, ffn_step, 0)

    hat, scale = normalized(middle_ref[...])
    kept = two_keep_ref[:, :1] * result[...]
    dscale_two = jnp.sum(cot_ref[...] * kept, axis=0, keepdims=True)
    result[...] = middle_ref[...] + second_scale_ref[...] * kept
    copies.start("outs", result, output_hbm)
    dgain_two = jnp.sum(dnorm[...] * hat, axis=0, keepdims=True)
    dmiddle = cot_ref[...] + norm_backward(dnorm[...] * second_gain_ref[...], hat, scale)
    dnorm[...] = dmiddle
    copies.start("outs", dnorm, dmiddle_hbm)
    kept = one_keep_ref[:, :1] * dmiddle
    grad = dot(kept * first_scale_ref[...], out_ref[...], NT)
    row = packed_ref.shape[0]
    start = blocks * LANES
    for ref in reversed(gate_refs):
        tall, width = ref.shape
        start -= width
        source = start - tall if tall > split else 0
        columns = slice(start - 2 * split, start - 2 * split + width)
        dconv = grad * mapped_ref[:, columns]
        for k in range(width // LANES):
            dconv_ref[start // LANES + k] = dconv[:, k * LANES : (k + 1) * LANES]
        grad_mapped = grad * conv_part(start, width)
        part = dot(mixed_ref[:, source : source + tall], grad_mapped, TN)
        row -= tall * width // LANES
        for k in range(width // LANES):
            packed_ref[row + k * tall : row + (k + 1) * tall] = part[:, k * LANES : (k + 1) * LANES]
        grad = dot(grad_mapped, ref[...], NT)
    dconv_ref[0] = jnp.concatenate([grad * conv[0, :, split:], grad * conv[0, :, :split]], axis=1)
    copies.start("outs", dconv_ref.at[:, pl.ds(0, reach), :], dconv_top_hbm)
    copies.start("outs", dconv_ref.at[:, pl.ds(cells - reach, reach), :], dconv_bottom_hbm)
    copies.start("outs", dconv_ref, dconv_hbm)
    start = mixed_ref.shape[1] - out_ref.shape[0]
    crossed = dot(mixed_ref[:, start:], kept, TN)
    dscale_one = jnp.sum(crossed * out_ref[...], axis=0, keepdims=True)
    packed_ref[:row] = jnp.zeros((row, LANES), F32)
    row = 0
    for vector in (dscale_one, dgain_two, dscale_two):
        for k in range(dim // LANES):
            packed_ref[row : row + 1] = vector[:, k * LANES : (k + 1) * LANES]
            row += 1
    half = packed_kept_hbm.shape[0]
    for place, target in ((core, packed_kept_hbm), (1 - core, packed_sent_hbm)):
        copies.start("outs", packed_ref.at[pl.ds(pl.multiple_of(place * half, 8), half), :], target)
    share_rows(core, (crossed * first_scale_ref[...]).T, out_kept, out_sent, dim // count_ha)
    for source, line in ((out_kept, line_kept_ref), (out_sent, line_sent_ref)):
        tall = source.shape[2]
        copies.start("outs", source, line.at[:, :, pl.ds(line.shape[2] - tall, tall), :])
    for place in range(ffn_steps):
        for copy in chunk_copies(place):
            copy.wait()
    copies.wait_all()


def mask_scratch(ids, rows):
    height, cols = ids.shape
    return [
        pltpu.SMEM((rows, KERN + 2), jnp.int32),
        pltpu.VMEM((height + 2 * EDGE, cols), jnp.int32),
        pltpu.VMEM(((rows + 2 * REACH) * cols, LANES), F32),
    ]


def packed_rows(gates, dim, parts):
    rows = sum(gate.size for gate in gates) // LANES + 3 * dim // LANES
    return -(-rows // (16 * parts)) * 16 * parts


def plane_share(rows):
    return max(rows * 3 // 4 // 8 * 8, 8)


def forward(
    place, ids, keep_one, keep_two, above, own, below, cot, vectors, weight_in, kern, gates,
    weight_out, weight_up, weight_down, rows, cols, count_ha, count_ba, chunk=512,
):
    cells, dim = own.shape
    reach = above.shape[0]
    blocks = weight_in.shape[1] // LANES
    hidden = weight_up.shape[1]
    split = gates[0].shape[0]
    wide = blocks * LANES
    head_steps = blocks // 2
    ffn_steps = hidden // chunk

    up_wide, down_wide = hidden // count_ha, hidden // count_ba
    up_rows = dim // count_ba * lane_blocks(up_wide)
    down_rows = dim // count_ha * lane_blocks(down_wide)
    out_rows = dim // count_ha * lane_blocks(dim // count_ba)
    half = count_ha // 2
    assert up_rows == down_rows
    cut = plane_share(up_rows)
    rest = up_rows - cut
    plane = (count_ba, half, 2 * cut, LANES)
    line = (half, count_ba, 2 * rest + out_rows, LANES)
    packed_shape = (packed_rows(gates, dim, count_ba), LANES)
    half_packed = (packed_shape[0] // 2, LANES)
    cells_ext = cells + 2 * reach
    vmem = functools.partial(pltpu.VMEM, dtype=F32)
    operands = (
        place, ids, keep_one, keep_two, ids, above, own, below, cot, *vectors,
        weight_in, kern, *gates, weight_out, weight_up, weight_down,
    )
    out_shape = [
        shape_of(blocks, cells, LANES),
        shape_of(cells, dim),
        shape_of(cells, dim),
        shape_of(blocks, cells, LANES),
        shape_of(blocks, reach, LANES),
        shape_of(blocks, reach, LANES),
        shape_of(*plane),
        shape_of(*plane),
        shape_of(*line),
        shape_of(*line),
        shape_of(*half_packed),
        shape_of(*half_packed),
    ]
    return pl.pallas_call(
        functools.partial(forward_kernel, rows=rows, cols=cols, count_ha=count_ha, count_ba=count_ba),
        in_specs=[in_smem()] * 4 + [in_hbm()] * (len(operands) - 4),
        out_specs=[in_hbm()] * len(out_shape),
        out_shape=out_shape,
        scratch_shapes=[pltpu.VMEM(ids.shape, jnp.int32), vmem((cells_ext, dim)), vmem((cells, dim))]
        + [vmem((1, dim))] * 4
        + [vmem((head_steps, dim, 2 * LANES)), vmem(kern.shape)]
        + [vmem(gate.shape) for gate in gates]
        + [
            vmem(weight_out.shape),
            vmem((ffn_steps, dim, chunk)),
            vmem((ffn_steps, chunk, dim)),
            vmem((blocks, cells, LANES)),
            pltpu.SemaphoreType.DMA((40 + head_steps,)),
            pltpu.SemaphoreType.DMA((ffn_steps, 2 + 2 * (count_ba + half + 2))),
        ]
        + [vmem((ffn_steps, chunk // (2 * up_wide), count_ba, up_rows, LANES))] * 2
        + [vmem((ffn_steps, half, chunk // down_wide, down_rows, LANES))] * 2
        + [vmem((half, count_ba, out_rows, LANES))] * 2
        + mask_scratch(ids, rows)
        + [
            vmem((cells, LANES)),
            vmem((cells, LANES)),
            vmem((KERN, cols // 8, 8, LANES)),
            vmem(packed_shape),
            vmem((cells_ext, dim)),
            vmem((blocks, cells_ext + 2 * EDGE, LANES)),
            vmem((KERN, rows + 2 * REACH, cols // 8, 8, LANES)),
            vmem((blocks, TAPS, LANES)),
            vmem((TAPS + KERN, 8, LANES)),
            vmem((blocks, cells, LANES)),
            vmem((cells, wide)),
            vmem((cells, wide - 2 * split)),
            vmem((cells, dim)),
            vmem((cells, dim)),
            vmem((cells, dim)),
        ],
        compiler_params=params(),
        cost_estimate=lasting(45),
    )(*operands)


def lay_flat(above_ref, own_ref, below_ref, flat):
    reach, cells = above_ref.shape[1], own_ref.shape[1]
    flat[:EDGE] = jnp.zeros((EDGE, LANES), F32)
    flat[EDGE : EDGE + reach] = above_ref[0]
    flat[EDGE + reach : EDGE + reach + cells] = own_ref[0]
    flat[EDGE + reach + cells : EDGE + 2 * reach + cells] = below_ref[0]
    flat[EDGE + 2 * reach + cells :] = jnp.zeros((EDGE, LANES), F32)


def backward_kernel(
    place_ref, ids_scalar, ids_ref, above_ref, own_ref, below_ref, mix_ref, kern_ref, canvas_ref, gain_ref,
    dmiddle_ref, in_ref, *rest, rows, cols,
):
    dcanvas_ref, kept_ref, sent_ref, small_kept_ref, small_sent_ref = rest[-18:-13]
    row_taps, padded, valid_ref, col_ref, flat, shifted, laid, wide, dk, sums, djoined, normed, dnorm = rest[-13:]
    step = pl.program_id(0)
    cells = rows * cols
    reach = REACH * cols
    core = place_ref[0] % 2
    split = laid.shape[0] * LANES - kern_ref.shape[1]
    width = in_ref.shape[1] // (2 * kept_ref.shape[1])

    @pl.when(step == 0)
    def _():
        lay_kernel(kern_ref, laid, split)
        turned = image_ids(ids_ref, padded, place_ref[0], rows)
        spread_cells((turned >= 0).astype(F32), valid_ref, 0, rows + 2 * REACH)
        conv_masks(ids_scalar, ids_ref, place_ref[0], row_taps, col_ref, rows)
        hat, _ = normalized(canvas_ref[...] * valid_ref[reach : reach + cells, :1])
        normed[...] = hat * gain_ref[...]
        dnorm[...] = jnp.zeros_like(dnorm)

    lay_flat(above_ref, own_ref, below_ref, flat)
    fill_shifted(flat, col_ref, shifted, rows + 2 * REACH, cols)
    conv_grad_block(
        row_taps, laid[step], shifted, wide, dk, mix_ref.at[0], djoined.at[step % 2], sums.at[step], rows, cols
    )

    @pl.when(step % 2 == 1)
    def _():
        grad = jnp.concatenate([djoined[0], djoined[1]], axis=1)
        share_columns(core, dot(normed[...], grad, TN), kept_ref, sent_ref, width, plane_first=True)
        dnorm[...] += dot(grad, in_ref[...], NT)

    @pl.when(step == pl.num_programs(0) - 1)
    def _():
        hat, scale = normalized(canvas_ref[...] * valid_ref[reach : reach + cells, :1])
        dgain = jnp.sum(dnorm[...] * hat, axis=0, keepdims=True)
        count = sums.shape[0]
        for k in range(dgain.shape[1] // LANES):
            sums[count - 1, TAPS + k : TAPS + k + 1] = dgain[:, k * LANES : (k + 1) * LANES]
        for ref, start in ((small_kept_ref, core * (count // 2)), (small_sent_ref, (1 - core) * (count // 2))):
            ref[...] = sums[pl.ds(start, count // 2)].reshape(ref.shape)
        inner = dmiddle_ref[...] + norm_backward(dnorm[...] * gain_ref[...], hat, scale)
        dcanvas_ref[...] = inner * valid_ref[reach : reach + cells, :1]


def block_of(size):
    return pl.BlockSpec((1, size, LANES), lambda i: (i, 0, 0))


def backward(
    place, ids, above, own, below, mix, kern, canvas, gain, dmiddle, weight_in, ties, rows, cols, count_ha, count_ba
):
    cells, dim = canvas.shape
    blocks = own.shape[0]
    reach = above.shape[1]
    own_wide = weight_in.shape[1] // count_ha
    chunk_rows = dim // count_ba * lane_blocks(own_wide)
    groups = 2 * LANES // (2 * own_wide)
    chunk_spec = pl.BlockSpec((count_ba, groups, chunk_rows, LANES), lambda i: (0, i // 2, 0, 0))
    chunks = shape_of(count_ba, count_ha // 2, chunk_rows, LANES)
    tall = -(-(TAPS + dim // LANES) // 8) * 8
    small = (blocks // 2 * tall, LANES)
    return pl.pallas_call(
        functools.partial(backward_kernel, rows=rows, cols=cols),
        grid=(blocks,),
        in_specs=[in_smem(), in_smem(), whole(ids.shape)]
        + [block_of(size) for size in (reach, cells, reach, cells)]
        + [whole(kern.shape), whole(canvas.shape)]
        + [whole((1, dim)), whole((cells, dim))]
        + [pl.BlockSpec((dim, 2 * LANES), lambda i: (0, i // 2))]
        + [in_hbm()] * len(ties),
        out_specs=[whole((cells, dim)), chunk_spec, chunk_spec, whole(small), whole(small)],
        out_shape=[shape_of(cells, dim), chunks, chunks, shape_of(*small), shape_of(*small)],
        scratch_shapes=mask_scratch(ids, rows)
        + [
            pltpu.VMEM((KERN, cols // 8, 8, LANES), F32),
            pltpu.VMEM((cells + 2 * reach + 2 * EDGE, LANES), F32),
            pltpu.VMEM((KERN, rows + 2 * REACH, cols // 8, 8, LANES), F32),
            pltpu.VMEM((blocks, TAPS, LANES), F32),
            pltpu.VMEM((TAPS + KERN, 8, LANES), F32),
            pltpu.VMEM((TAPS, 8, LANES), F32),
            pltpu.VMEM((blocks, tall, LANES), F32),
            pltpu.VMEM((2, cells, LANES), F32),
            pltpu.VMEM((cells, dim), F32),
            pltpu.VMEM((cells, dim), F32),
        ],
        compiler_params=params(),
        cost_estimate=lasting(25),
    )(place, ids, ids, above, own, below, mix, kern, canvas, gain, dmiddle, weight_in, *ties)


def exchange(values, axis, bit):
    return lax.ppermute(values, axis, [(i, i ^ bit) for i in range(lax.axis_size(axis))])


class View:
    def __init__(self, array, start, ways, fixed, rows):
        self.array, self.start, self.ways, self.fixed, self.rows = array, start, ways, fixed, rows

    def fix(self, way, step):
        if way == "line":
            near = lax.axis_size("ha") // 4
            return self.fix("far", step // near).fix("near", step % near)
        left = [entry for entry in self.ways if entry[0] != way]
        (stride,) = [entry[2] for entry in self.ways if entry[0] == way]
        return View(self.array, self.start, left, self.fixed + [(way, step, stride)], self.rows)

    def size(self):
        count = self.rows
        for _, size, _ in self.ways:
            count *= size
        return count

    def runs(self, ha, ba):
        start = self.start
        near = lax.axis_size("ha") // 4
        places = {"plane": ba, "far": ha // 2 // near, "near": ha // 2 % near}
        for way, step, stride in self.fixed:
            start = start + (places[way] ^ step) * stride
        rows, ways = self.rows, list(self.ways)
        while ways and ways[-1][2] == rows:
            rows *= ways.pop()[1]
        offsets = [0]
        for _, size, stride in ways:
            offsets = [offset + k * stride for offset in offsets for k in range(size)]
        return [pl.multiple_of(start + offset, 8) for offset in offsets], rows


def flat_view(array, start=0, rows=None):
    flat = array.reshape(-1, LANES)
    return View(flat, start, [], [], flat.shape[0] if rows is None else rows)


def combine(place, groups, ties=(), epilogue=None, out_shape=None):
    pieces, arrays = [], []
    for group in groups:
        for views in group:
            if not any(views is other for other in pieces):
                pieces.append(views)
    for views in pieces:
        for view in views:
            if not any(view.array is other for other in arrays):
                arrays.append(view.array)
    index_of = {id(array): k for k, array in enumerate(arrays)}
    piece_of = {id(views): k for k, views in enumerate(pieces)}
    sizes = [sum(views[0].size() for views in group) for group in groups]
    copies = sum(len(view.runs(0, 0)[0]) for views in pieces for view in views)
    plain = epilogue is None
    if plain:
        out_shape = [shape_of(size, LANES) for size in sizes]

    def kernel(place_ref, *refs):
        inputs = refs[: len(arrays)]
        refs = refs[len(arrays) + len(ties) :]
        outs, refs = refs[: len(out_shape)], refs[len(out_shape) :]
        buffers, refs = refs[: len(pieces)], refs[len(pieces) :]
        sems, results, out_sems = refs[0], refs[1:-1], refs[-1]
        ha, ba = place_ref[0], place_ref[1]
        moves, count = [], 0
        for piece, views in enumerate(pieces):
            moves.append([])
            for term, view in enumerate(views):
                source = inputs[index_of[id(view.array)]]
                starts, rows = view.runs(ha, ba)
                for k, start in enumerate(starts):
                    target = buffers[piece].at[term, pl.ds(k * rows, rows), :]
                    move = pltpu.make_async_copy(source.at[pl.ds(start, rows), :], target, sems.at[count])
                    move.start()
                    moves[-1].append(move)
                    count += 1
        values, waited, leaving = [], set(), []
        for out, group in enumerate(groups):
            row = 0
            for views in group:
                piece = piece_of[id(views)]
                if piece not in waited:
                    waited.add(piece)
                    for move in moves[piece]:
                        move.wait()
                value = buffers[piece][0]
                for term in range(1, len(views)):
                    value = value + buffers[piece][term]
                if plain:
                    results[out][row : row + value.shape[0], :] = value
                values.append(value)
                row += value.shape[0]
            if plain:
                leaving.append(pltpu.make_async_copy(results[out], outs[out], out_sems.at[out]))
                leaving[-1].start()
        if not plain:
            epilogue(ha, ba, values, outs)
        for move in leaving:
            move.wait()

    moved = sum(view.size() for views in pieces for view in views) + sum(sizes)
    scratch = [pltpu.VMEM((len(views), views[0].size(), LANES), F32) for views in pieces]
    scratch.append(pltpu.SemaphoreType.DMA((copies,)))
    if plain:
        scratch += [pltpu.VMEM((size, LANES), F32) for size in sizes]
    scratch.append(pltpu.SemaphoreType.DMA((len(groups),)))
    return pl.pallas_call(
        kernel,
        in_specs=[in_smem()] + [in_hbm()] * (len(arrays) + len(ties)),
        out_specs=[in_hbm() if plain else pl.BlockSpec(memory_space=pltpu.VMEM)] * len(out_shape),
        out_shape=out_shape,
        scratch_shapes=scratch,
        compiler_params=params(),
        cost_estimate=lasting(1 + moved * LANES * 4 / 3.0e6),
    )(place, *arrays, *ties)


def tied(arrays, ties):
    return pl.pallas_call(
        lambda *refs: None,
        in_specs=[pl.BlockSpec(memory_space=pl.ANY)] * (len(arrays) + len(ties)),
        out_specs=[pl.BlockSpec(memory_space=pl.ANY)] * len(arrays),
        out_shape=[shape_of(*array.shape) for array in arrays],
        input_output_aliases={k: k for k in range(len(arrays))},
        compiler_params=params(),
    )(*arrays, *ties)


class Sum:
    def __init__(self, arrays, names):
        self.views = []
        near = lax.axis_size("ha") // 4
        sizes = {"plane": lax.axis_size("ba"), "far": 2, "near": near}
        for array in arrays:
            flat = array.reshape(-1, LANES)
            stride, ways = flat.shape[0], []
            for name in names:
                stride //= sizes[name]
                ways.append((name, sizes[name], stride))
            self.views.append(View(flat, 0, ways, [], stride))

    def leaving(self, way, step):
        return [view.fix(way, step) for view in self.views]

    def keep(self, way, sent, arrived):
        self.views = [view.fix(way, 0) for view in self.views]
        rows = self.views[0].rows
        stride, ways = rows, []
        for name, size, _ in reversed(self.views[0].ways):
            ways.insert(0, (name, size, stride))
            stride *= size
        self.views += [View(array, start, ways, [], rows) for array, start in arrived]

    def part(self, first, rows):
        return [View(view.array, view.start + first, view.ways, view.fixed, rows) for view in self.views]


class Rider:
    def __init__(self, views):
        self.views = views

    def leaving(self, way, step):
        return self.views

    def keep(self, way, sent, arrived):
        rows = self.views[0].size()
        self.views = [View(array, start, [], [], rows) for array, start in [sent] + arrived]


class Gather(Rider):
    def keep(self, way, sent, arrived):
        rows = self.views[0].size()
        self.gathered = [[View(array, start, [], [], rows)] for array, start in [sent] + arrived]


class Stage:
    def __init__(self, members, way):
        self.members, self.way = members, way
        line, near = lax.axis_size("ha") // 2, lax.axis_size("ha") // 4
        self.steps = {"plane": range(1, lax.axis_size("ba")), "line": range(1, line), "far": [near]}[way]
        self.near = near

    def taking(self, step):
        return [(one, way) for one, way in self.members if way != "near" or step < self.near]

    def groups(self):
        return [
            [one.leaving(way, step // self.near if way == "far" else step) for one, way in self.taking(step)]
            for step in self.steps
        ]

    def go(self, payloads, in_turn=False):
        axis, unit = ("ba", 1) if self.way == "plane" else ("ha", 2)
        arrived = []
        for step, part in zip(self.steps, payloads):
            if in_turn and step == len(self.steps) and step > 2:
                (part,) = tied([part], arrived[1:2])
            arrived.append(exchange(part, axis, unit * step))
        places = {}
        for step, sent, part in zip(self.steps, payloads, arrived):
            row = 0
            for one, way in self.taking(step):
                places.setdefault(id(one), []).append(((sent, row), (part, row)))
                row += one.leaving(way, 1)[0].size()
        for one, way in self.members:
            mine = places.get(id(one), [])
            one.keep(way, mine[0][0] if mine else None, [part for _, part in mine])
        return arrived


def run(place, stage, ties=(), in_turn=False):
    made = list(combine(place, stage.groups(), ties))
    return made, stage.go(made, in_turn)


def neighbour_rows(top, bottom):
    count = lax.axis_size("ha")
    up = [(i, i + 1) for i in range(count - 1)]
    down = [(i + 1, i) for i in range(count - 1)]
    return lax.ppermute(bottom, "ha", up), lax.ppermute(top, "ha", down)


def lay_beside(value, ref):
    tall, width = ref.shape
    for k in range(lane_blocks(width)):
        columns = slice(k * LANES, min(width, (k + 1) * LANES))
        ref[:, columns] = value[k * tall : (k + 1) * tall, : columns.stop - columns.start]


def lay_large(ha, ba, values, outs):
    up_first, up_second, down_first, down_second, out = values
    lay_beside(jnp.concatenate([up_first, up_second], axis=0), outs[0])
    lay_beside(jnp.concatenate([down_first, down_second], axis=0), outs[1])
    lay_beside(out, outs[2])


def lay_small(ha, ba, values, outs, blocks):
    din_ref, dk_ref, gain_ref = outs[:3]
    scratch = outs[-1]
    lay_beside(values[0], din_ref)
    own, other = values[1], values[2]
    small_rows = blocks // 2 * (-(-(TAPS + gain_ref.shape[1] // LANES) // 8) * 8)
    mine = ha % 2 == 0
    first, second = jnp.where(mine, own, other), jnp.where(mine, other, own)
    dkern = jnp.concatenate([first[:small_rows], second[:small_rows]], axis=0)
    tall = dkern.shape[0] // blocks
    joined = jnp.concatenate([dkern[k * tall : k * tall + TAPS] for k in range(blocks)], axis=1)
    dk_ref[...] = joined[:, joined.shape[1] - dk_ref.shape[1] :]
    half = own.shape[0] - small_rows
    count = lax.axis_size("ba")
    part = half // count
    for core, rows in ((0, first), (1, second)):
        for step in range(count):
            start = core * half + (ba ^ step) * part
            source = small_rows + step * part
            scratch[pl.ds(pl.multiple_of(start, 8), part), :] = rows[source : source + part]
    dim = gain_ref.shape[1]
    for k in range(dim // LANES):
        columns = slice(k * LANES, (k + 1) * LANES)
        row = (blocks - 1) * tall + TAPS + k
        gain_ref[:, columns] = dkern[row : row + 1]
        for vector, ref in enumerate(outs[3:6]):
            ref[:, columns] = scratch[vector * dim // LANES + k : vector * dim // LANES + k + 1, :]
    row = scratch.shape[0]
    for ref in reversed(outs[6:-1]):
        tall, width = ref.shape
        row -= tall * width // LANES
        for k in range(width // LANES):
            ref[:, k * LANES : (k + 1) * LANES] = scratch[row + k * tall : row + (k + 1) * tall, :]


def shards(
    canvas,
    image_id,
    keep_first,
    keep_second,
    first_gain,
    weight_in,
    depth_kernel,
    gate_first,
    gate_second,
    gate_third,
    weight_out,
    scale_first,
    second_gain,
    weight_up,
    weight_down,
    scale_second,
    cotangent,
):
    _, rows, cols, dim = canvas.shape
    cells = rows * cols
    reach = REACH * cols
    count_ha, count_ba = lax.axis_size("ha"), lax.axis_size("ba")
    hidden = weight_up.shape[1]
    blocks = weight_in.shape[1] // LANES
    place = jnp.stack([lax.axis_index("ha"), lax.axis_index("ba")])
    own = canvas.reshape(cells, dim)
    gates = (gate_first, gate_second, gate_third)
    gain = first_gain[None]
    vectors = (gain, scale_first[None], second_gain[None], scale_second[None])
    ids = image_id[0]
    above, below = neighbour_rows(own[:reach], own[cells - reach :])
    (
        joined, output, dmiddle, dconv, dconv_top, dconv_bottom, plane_kept, plane_sent, line_kept, line_sent,
        packed_kept, packed_sent,
    ) = forward(
        place, ids, keep_first, keep_second, above, own, below, cotangent.reshape(cells, dim), vectors,
        weight_in, depth_kernel, gates, weight_out, weight_up, weight_down, rows, cols, count_ha, count_ba,
    )
    above, below = neighbour_rows(dconv_top, dconv_bottom)

    plane_sum = Sum([plane_kept, exchange(plane_sent, "ha", 1)], ["plane", "far", "near"])
    line_sum = Sum([line_kept, exchange(line_sent, "ha", 1)], ["far", "near", "plane"])
    packed = Sum([packed_kept, exchange(packed_sent, "ha", 1)], ["plane"])
    made, arrived = run(place, Stage([(plane_sum, "plane"), (packed, "plane")], "plane"))
    more, far = run(place, Stage([(line_sum, "far")], "far"), ties=made + [above, below])
    made, arrived = made + more, arrived + far
    dcanvas, in_kept, in_sent, small_kept, small_sent = backward(
        place, ids, above, dconv, below, joined, depth_kernel, own, gain, dmiddle, weight_in, made,
        rows, cols, count_ha, count_ba,
    )
    in_sent, small_sent = tied([in_sent, small_sent], arrived)
    in_sum = Sum([in_kept, exchange(in_sent, "ha", 1)], ["plane", "far", "near"])
    small = Rider([flat_view(small_kept), flat_view(exchange(small_sent, "ha", 1))])
    packed = Rider(packed.views)
    made, arrived = run(
        place, Stage([(plane_sum, "line"), (packed, "line"), (line_sum, "near")], "line"), in_turn=True
    )
    run(place, Stage([(in_sum, "plane"), (small, "plane")], "plane"), ties=made)
    made, _ = run(place, Stage([(in_sum, "line"), (small, "line")], "line"), ties=arrived, in_turn=True)
    packed = Gather(packed.views)
    run(place, Stage([(line_sum, "plane"), (packed, "plane")], "plane"), ties=made)
    cut = plane_sum.views[0].rows // 2
    rest = (line_sum.views[0].rows - dim // count_ha * lane_blocks(dim // count_ba)) // 2
    dup, ddown, dout = combine(
        place,
        [
            [
                plane_sum.part(0, cut),
                line_sum.part(0, rest),
                plane_sum.part(cut, cut),
                line_sum.part(rest, rest),
                line_sum.part(2 * rest, line_sum.views[0].rows - 2 * rest),
            ]
        ],
        epilogue=lay_large,
        out_shape=[
            shape_of(dim // count_ba, hidden // count_ha),
            shape_of(dim // count_ha, hidden // count_ba),
            shape_of(dim // count_ha, dim // count_ba),
        ],
    )
    (halves_of,) = combine(place, [[small.views] + packed.gathered])
    din, dkern, dgain_one, dscale_one, dgain_two, dscale_two, dfirst, dsecond, dthird, _ = combine(
        place,
        [[in_sum.views, [flat_view(halves_of)], [flat_view(exchange(halves_of, "ha", 1))]]],
        epilogue=functools.partial(lay_small, blocks=blocks),
        out_shape=[shape_of(dim // count_ba, weight_in.shape[1] // count_ha), shape_of(*depth_kernel.shape)]
        + [shape_of(1, dim)] * 4
        + [shape_of(*gate.shape) for gate in gates]
        + [shape_of(packed_rows(gates, dim, count_ba), LANES)],
    )
    return (
        output.reshape(canvas.shape),
        dcanvas.reshape(canvas.shape),
        dgain_one[0],
        din,
        dkern,
        dfirst,
        dsecond,
        dthird,
        dout.T,
        dscale_one[0],
        dgain_two[0],
        dup,
        ddown.T,
        dscale_two[0],
    )


def solution(mesh):
    in_specs = (
        P("ba", "ha", None, None),
        P("ba", None, None),
        P("ba", None),
        P("ba", None),
    ) + (P(),) * 12 + (P("ba", "ha", None, None),)
    tiled = P("ba", "ha")
    out_specs = (
        P("ba", "ha", None, None),
        P("ba", "ha", None, None),
        P(),
        tiled,
        P(),
        P(),
        P(),
        P(),
        tiled,
        P(),
        P(),
        tiled,
        tiled,
        P(),
    )
    return jax.shard_map(shards, mesh=mesh, in_specs=in_specs, out_specs=out_specs, check_vma=False)
```

```python
import functools

import jax
import jax.numpy as jnp
from jax import lax
from jax.experimental import pallas as pl
from jax.experimental.pallas import tpu as pltpu
from jax.sharding import PartitionSpec as P

KERN = 7
TAPS = KERN * KERN
REACH = KERN // 2
KEEP_RATE = 0.8
SPREAD = 1.0 / 3.0
EPSILON = 1e-06
LANES = 128
EDGE = 8
VMEM_BYTES = 64 << 20
F32 = jnp.float32
INV_SQRT_2 = 0.7071067811865476
INV_SQRT_2PI = 0.3989422804014327
NN = (((1,), (0,)), ((), ()))
NT = (((1,), (1,)), ((), ()))
TN = (((0,), (0,)), ((), ()))


def dot(left, right, dims=NN):
    return lax.dot_general(left, right, dims, precision=lax.Precision.HIGH, preferred_element_type=F32)


def normalized(values):
    centered = values - jnp.mean(values, axis=-1, keepdims=True)
    scale = lax.rsqrt(jnp.mean(centered * centered, axis=-1, keepdims=True) + EPSILON)
    return centered * scale, scale


def norm_backward(grad_hat, hat, scale):
    return scale * (
        grad_hat
        - jnp.mean(grad_hat, axis=-1, keepdims=True)
        - hat * jnp.mean(grad_hat * hat, axis=-1, keepdims=True)
    )


def params():
    return pltpu.CompilerParams(vmem_limit_bytes=VMEM_BYTES)


def lasting(microseconds):
    return pl.CostEstimate(flops=int(microseconds * 1.1e9), bytes_accessed=0, transcendentals=0)


def whole(shape):
    return pl.BlockSpec(tuple(shape), lambda *_: (0,) * len(shape), pipeline_mode=pl.Buffered(1))


def in_smem():
    return pl.BlockSpec(memory_space=pltpu.SMEM)


def in_hbm():
    return pl.BlockSpec(memory_space=pltpu.HBM)


def shape_of(*shape):
    return jax.ShapeDtypeStruct(shape, F32)


def lane_blocks(width):
    return -(-width // LANES)


def image_ids(ids_ref, padded, place, rows):
    height, cols = ids_ref.shape
    padded[...] = jnp.full(padded.shape, -1, jnp.int32)
    padded[EDGE : EDGE + height, :] = ids_ref[...]
    ids = padded[pl.ds(place * rows + (EDGE - REACH), rows + 2 * REACH), :]
    return jnp.concatenate([ids, jnp.full((-ids.shape[0] % 8, cols), -1, jnp.int32)], axis=0).T


def spread_cells(factors, out_ref, first, rows):
    cols = factors.shape[0]
    for r in range(rows):
        column = factors[:, first + r : first + r + 1]
        out_ref[r * cols : (r + 1) * cols, :] = jnp.broadcast_to(column, (cols, LANES))


def keep_factors(turned, table_ref):
    result = jnp.zeros(turned.shape, F32)
    for slot in range(table_ref.shape[1]):
        result = jnp.where(turned == slot, table_ref[0, slot].astype(F32) / KEEP_RATE, result)
    return result


def conv_masks(ids_scalar, ids_ref, place, row_taps, col_mask, rows):
    height, cols = ids_ref.shape
    wide_ids = jnp.broadcast_to(ids_ref[...].T[:, height // 2 : height // 2 + 1], (cols, LANES))
    column = lax.broadcasted_iota(jnp.int32, (cols, LANES), 0)
    for b in range(KERN):
        shift = b - REACH
        moved = pltpu.roll(wide_ids, (-shift) % cols, 0)
        inside = (column + shift >= 0) & (column + shift < cols)
        same = (moved == wide_ids) & inside
        col_mask[b] = same.astype(F32).reshape(cols // 8, 8, LANES)

    def one(r, _):
        own = ids_scalar[place * rows + r, cols // 2]
        row_taps[r, 0] = KERN
        row_taps[r, KERN + 1] = KERN
        for a in range(KERN):
            other = place * rows + r + a - REACH
            inside = (other >= 0) & (other < height)
            same = ids_scalar[jnp.clip(other, 0, height - 1), cols // 2] == own
            row_taps[r, a + 1] = jnp.where(inside & same, a, KERN)
        return 0

    lax.fori_loop(0, rows, one, 0)


def lay_kernel(kern_ref, laid, split):
    tap = lax.broadcasted_iota(jnp.int32, (TAPS, split), 0)
    own = jnp.where(tap == TAPS // 2, 1.0 / SPREAD, 0.0).astype(F32)
    for k in range(laid.shape[0]):
        start = k * LANES - split
        left = own if k == 0 else kern_ref[:, start : start + split]
        laid[k] = jnp.concatenate([left, kern_ref[:, start + split : start + LANES]], axis=1) * SPREAD


def fill_shifted(flat, col_ref, shifted, rows_ext, cols):
    for b in range(KERN):
        for g in range(cols // 8):
            mask = None if b == REACH else col_ref[b, g]
            for r in range(rows_ext):
                x = flat[pl.ds(EDGE + r * cols + 8 * g + b - REACH, 8), :]
                shifted[b, r, g] = x if b == REACH else x * mask


def spread_taps(kern, wide, turned):
    for t in range(TAPS):
        source = TAPS - 1 - t if turned else t
        wide[t] = jnp.broadcast_to(kern[source : source + 1, :], (8, LANES))
    for t in range(KERN):
        wide[TAPS + t] = jnp.zeros((8, LANES), F32)


def conv_block(row_taps, kern, shifted, wide, out_ref, rows, cols):
    groups = cols // 8
    spread_taps(kern, wide, False)

    def pair(h, _):
        r = 2 * h

        def step(i, totals):
            first, second = totals
            taps_first = row_taps[r, i + 1] * KERN
            taps_second = row_taps[r + 1, i] * KERN
            for b in range(KERN):
                x = shifted[b, r + i]
                first = first + wide[taps_first + b][None] * x
                second = second + wide[taps_second + b][None] * x
            return first, second

        zero = jnp.zeros((groups, 8, LANES), F32)
        first, second = lax.fori_loop(0, KERN + 1, step, (zero, zero), unroll=4)
        out_ref[pl.ds(pl.multiple_of(r * cols, cols), cols), :] = first.reshape(cols, LANES)
        out_ref[pl.ds(pl.multiple_of((r + 1) * cols, cols), cols), :] = second.reshape(cols, LANES)
        return 0

    lax.fori_loop(0, rows // 2, pair, 0)


def conv_grad_block(row_taps, kern, shifted, wide, dk, mix_ref, out_ref, dk_ref, rows, cols):
    groups = cols // 8
    spread_taps(kern, wide, True)
    for t in range(TAPS):
        dk[t] = jnp.zeros((8, LANES), F32)

    def one(r, _):
        start = pl.ds(pl.multiple_of(r * cols, cols), cols)
        mix = mix_ref[start, :].reshape(groups, 8, LANES)
        total = jnp.zeros((groups, 8, LANES), F32)
        for i in range(KERN):
            row = row_taps[r, i + 1]
            same = jnp.where(row < KERN, 1.0, 0.0).astype(F32)
            for b in range(KERN):
                x = shifted[b, r + i]
                total = total + wide[row * KERN + b][None] * x
                dk[i * KERN + b] += jnp.sum(mix * x, axis=0) * same
        out_ref[start, :] = total.reshape(cols, LANES)
        return 0

    lax.fori_loop(0, rows, one, 0)
    for t in range(TAPS):
        dk_ref[TAPS - 1 - t : TAPS - t, :] = jnp.sum(dk[t], axis=0, keepdims=True) * SPREAD
    dk_ref[TAPS:, :] = jnp.zeros((dk_ref.shape[0] - TAPS, LANES), F32)


def share(core, first, second, kept_ref, sent_ref, z, p):
    mine = core == 0
    tall, width = first.shape
    for ref, chunk in (
        (kept_ref, jnp.where(mine, first, second)),
        (sent_ref, jnp.where(mine, second, first)),
    ):
        for k in range(lane_blocks(width)):
            part = chunk[:, k * LANES : (k + 1) * LANES]
            if part.shape[1] < LANES:
                part = jnp.concatenate([part, jnp.zeros((tall, LANES - part.shape[1]), F32)], axis=1)
            ref[z, p, k * tall : (k + 1) * tall, :] = part


def share_columns(core, grad, kept_ref, sent_ref, width, plane_first=False):
    groups, parts = reversed(kept_ref.shape[:2]) if plane_first else kept_ref.shape[:2]
    tall = grad.shape[0] // parts
    for z in range(groups):
        for p in range(parts):
            rows = slice(p * tall, (p + 1) * tall)
            first = grad[rows, 2 * z * width : (2 * z + 1) * width]
            second = grad[rows, (2 * z + 1) * width : (2 * z + 2) * width]
            share(core, first, second, kept_ref, sent_ref, *((p, z) if plane_first else (z, p)))


def share_rows(core, grad, kept_ref, sent_ref, tall):
    groups, parts = kept_ref.shape[:2]
    width = grad.shape[1] // parts
    for z in range(groups):
        for p in range(parts):
            columns = slice(p * width, (p + 1) * width)
            first = grad[2 * z * tall : (2 * z + 1) * tall, columns]
            second = grad[(2 * z + 1) * tall : (2 * z + 2) * tall, columns]
            share(core, first, second, kept_ref, sent_ref, z, p)


class Copies:
    def __init__(self, sems):
        self.sems, self.count, self.pending = sems, 0, {}

    def start(self, name, source, target):
        copy = pltpu.make_async_copy(source, target, self.sems.at[self.count])
        self.count += 1
        copy.start()
        self.pending.setdefault(name, []).append(copy)

    def wait(self, *names):
        for name in names:
            for copy in self.pending.pop(name):
                copy.wait()

    def wait_all(self):
        self.wait(*list(self.pending))


def forward_kernel(
    place_ref, ids_scalar, one_table, two_table, ids_hbm, above_hbm, own_hbm, below_hbm, cot_hbm,
    first_gain_hbm, first_scale_hbm, second_gain_hbm, second_scale_hbm,
    in_hbm_ref, kern_hbm, one_hbm, two_hbm, three_hbm, out_hbm, up_hbm, down_hbm,
    joined_hbm, output_hbm, dmiddle_hbm, dconv_hbm, dconv_top_hbm, dconv_bottom_hbm,
    plane_kept_ref, plane_sent_ref, line_kept_ref, line_sent_ref, packed_kept_hbm, packed_sent_hbm,
    ids_ref, rows_ref, cot_ref, first_gain_ref, first_scale_ref, second_gain_ref, second_scale_ref,
    in_ref, kern_ref, one_ref, two_ref, three_ref, out_ref, up_ref, down_ref, dconv_ref, sems, chunk_sems,
    up_kept, up_sent, down_kept, down_sent, out_kept, out_sent,
    row_taps, padded, valid_ref, one_keep_ref, two_keep_ref, col_ref, packed_ref, normed, flat, shifted, laid, wide, conv,
    mixed_ref, mapped_ref, middle_ref, result, dnorm,
    *, rows, cols, count_ha, count_ba,
):
    blocks = flat.shape[0]
    cells = rows * cols
    reach = REACH * cols
    cells_ext = cells + 2 * reach
    core = place_ref[0] % 2
    split = one_ref.shape[0]
    dim = rows_ref.shape[1]
    head_steps = blocks // 2
    ffn_steps = up_kept.shape[0]
    chunk = down_ref.shape[1]
    gate_refs = (one_ref, two_ref, three_ref)

    copies = Copies(sems)
    copies.start("ids", ids_hbm, ids_ref)
    copies.start("above", above_hbm, rows_ref.at[pl.ds(0, reach)])
    copies.start("own", own_hbm, rows_ref.at[pl.ds(reach, cells)])
    copies.start("below", below_hbm, rows_ref.at[pl.ds(reach + cells, reach)])
    copies.start("vectors", first_gain_hbm, first_gain_ref)
    for k in range(head_steps):
        copies.start(("in", k), in_hbm_ref.at[:, pl.ds(2 * LANES * k, 2 * LANES)], in_ref.at[k])
    copies.start("kern", kern_hbm, kern_ref)
    def weights(k):
        ends = pl.ds(pl.multiple_of(k * chunk, chunk), chunk)
        return [
            pltpu.make_async_copy(up_hbm.at[:, ends], up_ref.at[k], chunk_sems.at[k, 0]),
            pltpu.make_async_copy(down_hbm.at[ends, :], down_ref.at[k], chunk_sems.at[k, 1]),
        ]

    def chunk_copies(place):
        moves = []
        sides = ((up_kept, down_kept, plane_kept_ref, line_kept_ref), (up_sent, down_sent, plane_sent_ref, line_sent_ref))
        for up, down, plane, line in sides:
            cut = plane.shape[2] // 2
            rest = up.shape[3] - cut
            zs = pl.ds(place * up.shape[1], up.shape[1])
            bas = pl.ds(place * down.shape[2], down.shape[2])
            moves += [
                (up.at[place, :, ba, pl.ds(0, cut), :], plane.at[ba, zs, pl.ds(0, cut), :])
                for ba in range(plane.shape[0])
            ]
            moves += [
                (down.at[place, z, :, pl.ds(0, cut), :], plane.at[bas, z, pl.ds(cut, cut), :])
                for z in range(plane.shape[1])
            ]
            moves.append((up.at[place, :, :, pl.ds(cut, rest), :], line.at[zs, :, pl.ds(0, rest), :]))
            moves.append((down.at[place, :, :, pl.ds(cut, rest), :], line.at[:, bas, pl.ds(rest, rest), :]))
        return [
            pltpu.make_async_copy(source, target, chunk_sems.at[place, 2 + k])
            for k, (source, target) in enumerate(moves)
        ]

    copies.wait("ids")
    turned = image_ids(ids_ref, padded, place_ref[0], rows)
    spread_cells((turned >= 0).astype(F32), valid_ref, 0, rows + 2 * REACH)
    spread_cells(keep_factors(turned, one_table), one_keep_ref, REACH, rows)
    spread_cells(keep_factors(turned, two_table), two_keep_ref, REACH, rows)
    conv_masks(ids_scalar, ids_ref, place_ref[0], row_taps, col_ref, rows)
    copies.wait("vectors")
    start = 0
    for name, size in (("above", reach), ("own", cells), ("below", reach)):
        copies.wait(name)
        hat, _ = normalized(rows_ref[start : start + size, :] * valid_ref[start : start + size, :1])
        normed[start : start + size] = hat * first_gain_ref[...]
        start += size

    for k in range(blocks):
        flat[k, :EDGE] = jnp.zeros((EDGE, LANES), F32)
        flat[k, EDGE + cells_ext :] = jnp.zeros((EDGE, LANES), F32)
    for step in range(head_steps):
        copies.wait(("in", step))
        joined = dot(normed[...], in_ref[step])
        for k in range(2):
            flat[2 * step + k, EDGE : EDGE + cells_ext] = joined[:, k * LANES : (k + 1) * LANES]
        if step == 0:
            copies.start("gates", first_scale_hbm, first_scale_ref)
            copies.start("gates", second_gain_hbm, second_gain_ref)
            copies.start("gates", second_scale_hbm, second_scale_ref)
            for source, target in zip((one_hbm, two_hbm, three_hbm, out_hbm, cot_hbm), gate_refs + (out_ref, cot_ref)):
                copies.start("gates", source, target)
            for k in range(ffn_steps):
                for copy in weights(k):
                    copy.start()
        pair = pl.ds(2 * step, 2)
        copies.start("outs", flat.at[pair, pl.ds(EDGE + reach, cells), :], joined_hbm.at[pair])

    copies.wait("kern")
    lay_kernel(kern_ref, laid, split)

    def conv_step(block, _):
        fill_shifted(flat.at[block], col_ref, shifted, rows + 2 * REACH, cols)
        conv_block(row_taps, laid[block], shifted, wide, conv.at[block], rows, cols)
        return 0

    lax.fori_loop(0, blocks, conv_step, 0)

    def conv_part(start, width):
        return jnp.concatenate([conv[start // LANES + k] for k in range(width // LANES)], axis=1)

    copies.wait("gates")
    mixed = conv[0, :, :split] * conv[0, :, split:]
    mixed_ref[:, :split] = mixed
    start = 2 * split
    for ref in gate_refs:
        width = ref.shape[1]
        mapped = dot(mixed, ref[...])
        mapped_ref[:, start - 2 * split : start - 2 * split + width] = mapped
        mixed = mapped * conv_part(start, width)
        mixed_ref[:, start : start + width] = mixed
        start += width
    branch = dot(mixed, out_ref[...])
    masked = rows_ref[reach : reach + cells, :] * valid_ref[reach : reach + cells, :1]
    middle = masked + one_keep_ref[:, :1] * first_scale_ref[...] * branch
    middle_ref[...] = middle
    hat, _ = normalized(middle)
    normed[:cells] = hat * second_gain_ref[...]
    result[...] = jnp.zeros_like(result)
    dnorm[...] = jnp.zeros_like(dnorm)

    def ffn_step(place, _):
        for copy in weights(place):
            copy.wait()
        grad_result = two_keep_ref[:, :1] * second_scale_ref[...] * cot_ref[...]
        pre = dot(normed[:cells], up_ref[place])
        cdf = 0.5 + 0.5 * lax.erf(pre * INV_SQRT_2)
        slope = cdf + pre * (INV_SQRT_2PI * jnp.exp(-0.5 * pre * pre))
        hidden = pre * cdf
        result[...] += dot(hidden, down_ref[place])
        grad_pre = dot(grad_result, down_ref[place], NT) * slope
        share_rows(
            core, dot(grad_result, hidden, TN), down_kept.at[place], down_sent.at[place], dim // count_ha
        )
        width = chunk // (2 * up_kept.shape[1])
        share_columns(core, dot(normed[:cells], grad_pre, TN), up_kept.at[place], up_sent.at[place], width)
        for copy in chunk_copies(place):
            copy.start()
        dnorm[...] += dot(grad_pre, up_ref[place], NT)
        return 0

    lax.fori_loop(0, ffn_steps, ffn_step, 0)

    hat, scale = normalized(middle_ref[...])
    kept = two_keep_ref[:, :1] * result[...]
    dscale_two = jnp.sum(cot_ref[...] * kept, axis=0, keepdims=True)
    result[...] = middle_ref[...] + second_scale_ref[...] * kept
    copies.start("outs", result, output_hbm)
    dgain_two = jnp.sum(dnorm[...] * hat, axis=0, keepdims=True)
    dmiddle = cot_ref[...] + norm_backward(dnorm[...] * second_gain_ref[...], hat, scale)
    dnorm[...] = dmiddle
    copies.start("outs", dnorm, dmiddle_hbm)
    kept = one_keep_ref[:, :1] * dmiddle
    grad = dot(kept * first_scale_ref[...], out_ref[...], NT)
    row = packed_ref.shape[0]
    start = blocks * LANES
    for ref in reversed(gate_refs):
        tall, width = ref.shape
        start -= width
        source = start - tall if tall > split else 0
        columns = slice(start - 2 * split, start - 2 * split + width)
        dconv = grad * mapped_ref[:, columns]
        for k in range(width // LANES):
            dconv_ref[start // LANES + k] = dconv[:, k * LANES : (k + 1) * LANES]
        grad_mapped = grad * conv_part(start, width)
        part = dot(mixed_ref[:, source : source + tall], grad_mapped, TN)
        row -= tall * width // LANES
        for k in range(width // LANES):
            packed_ref[row + k * tall : row + (k + 1) * tall] = part[:, k * LANES : (k + 1) * LANES]
        grad = dot(grad_mapped, ref[...], NT)
    dconv_ref[0] = jnp.concatenate([grad * conv[0, :, split:], grad * conv[0, :, :split]], axis=1)
    copies.start("outs", dconv_ref.at[:, pl.ds(0, reach), :], dconv_top_hbm)
    copies.start("outs", dconv_ref.at[:, pl.ds(cells - reach, reach), :], dconv_bottom_hbm)
    copies.start("outs", dconv_ref, dconv_hbm)
    start = mixed_ref.shape[1] - out_ref.shape[0]
    crossed = dot(mixed_ref[:, start:], kept, TN)
    dscale_one = jnp.sum(crossed * out_ref[...], axis=0, keepdims=True)
    packed_ref[:row] = jnp.zeros((row, LANES), F32)
    row = 0
    for vector in (dscale_one, dgain_two, dscale_two):
        for k in range(dim // LANES):
            packed_ref[row : row + 1] = vector[:, k * LANES : (k + 1) * LANES]
            row += 1
    half = packed_kept_hbm.shape[0]
    for place, target in ((core, packed_kept_hbm), (1 - core, packed_sent_hbm)):
        copies.start("outs", packed_ref.at[pl.ds(pl.multiple_of(place * half, 8), half), :], target)
    share_rows(core, (crossed * first_scale_ref[...]).T, out_kept, out_sent, dim // count_ha)
    for source, line in ((out_kept, line_kept_ref), (out_sent, line_sent_ref)):
        tall = source.shape[2]
        copies.start("outs", source, line.at[:, :, pl.ds(line.shape[2] - tall, tall), :])
    for place in range(ffn_steps):
        for copy in chunk_copies(place):
            copy.wait()
    copies.wait_all()


def mask_scratch(ids, rows):
    height, cols = ids.shape
    return [
        pltpu.SMEM((rows, KERN + 2), jnp.int32),
        pltpu.VMEM((height + 2 * EDGE, cols), jnp.int32),
        pltpu.VMEM(((rows + 2 * REACH) * cols, LANES), F32),
    ]


def packed_rows(gates, dim, parts):
    rows = sum(gate.size for gate in gates) // LANES + 3 * dim // LANES
    return -(-rows // (16 * parts)) * 16 * parts


def plane_share(rows):
    return max(rows * 3 // 4 // 8 * 8, 8)


def forward(
    place, ids, keep_one, keep_two, above, own, below, cot, vectors, weight_in, kern, gates,
    weight_out, weight_up, weight_down, rows, cols, count_ha, count_ba, chunk=512,
):
    cells, dim = own.shape
    reach = above.shape[0]
    blocks = weight_in.shape[1] // LANES
    hidden = weight_up.shape[1]
    split = gates[0].shape[0]
    wide = blocks * LANES
    head_steps = blocks // 2
    ffn_steps = hidden // chunk

    up_wide, down_wide = hidden // count_ha, hidden // count_ba
    up_rows = dim // count_ba * lane_blocks(up_wide)
    down_rows = dim // count_ha * lane_blocks(down_wide)
    out_rows = dim // count_ha * lane_blocks(dim // count_ba)
    half = count_ha // 2
    assert up_rows == down_rows
    cut = plane_share(up_rows)
    rest = up_rows - cut
    plane = (count_ba, half, 2 * cut, LANES)
    line = (half, count_ba, 2 * rest + out_rows, LANES)
    packed_shape = (packed_rows(gates, dim, count_ba), LANES)
    half_packed = (packed_shape[0] // 2, LANES)
    cells_ext = cells + 2 * reach
    vmem = functools.partial(pltpu.VMEM, dtype=F32)
    operands = (
        place, ids, keep_one, keep_two, ids, above, own, below, cot, *vectors,
        weight_in, kern, *gates, weight_out, weight_up, weight_down,
    )
    out_shape = [
        shape_of(blocks, cells, LANES),
        shape_of(cells, dim),
        shape_of(cells, dim),
        shape_of(blocks, cells, LANES),
        shape_of(blocks, reach, LANES),
        shape_of(blocks, reach, LANES),
        shape_of(*plane),
        shape_of(*plane),
        shape_of(*line),
        shape_of(*line),
        shape_of(*half_packed),
        shape_of(*half_packed),
    ]
    return pl.pallas_call(
        functools.partial(forward_kernel, rows=rows, cols=cols, count_ha=count_ha, count_ba=count_ba),
        in_specs=[in_smem()] * 4 + [in_hbm()] * (len(operands) - 4),
        out_specs=[in_hbm()] * len(out_shape),
        out_shape=out_shape,
        scratch_shapes=[pltpu.VMEM(ids.shape, jnp.int32), vmem((cells_ext, dim)), vmem((cells, dim))]
        + [vmem((1, dim))] * 4
        + [vmem((head_steps, dim, 2 * LANES)), vmem(kern.shape)]
        + [vmem(gate.shape) for gate in gates]
        + [
            vmem(weight_out.shape),
            vmem((ffn_steps, dim, chunk)),
            vmem((ffn_steps, chunk, dim)),
            vmem((blocks, cells, LANES)),
            pltpu.SemaphoreType.DMA((40 + head_steps,)),
            pltpu.SemaphoreType.DMA((ffn_steps, 2 + 2 * (count_ba + half + 2))),
        ]
        + [vmem((ffn_steps, chunk // (2 * up_wide), count_ba, up_rows, LANES))] * 2
        + [vmem((ffn_steps, half, chunk // down_wide, down_rows, LANES))] * 2
        + [vmem((half, count_ba, out_rows, LANES))] * 2
        + mask_scratch(ids, rows)
        + [
            vmem((cells, LANES)),
            vmem((cells, LANES)),
            vmem((KERN, cols // 8, 8, LANES)),
            vmem(packed_shape),
            vmem((cells_ext, dim)),
            vmem((blocks, cells_ext + 2 * EDGE, LANES)),
            vmem((KERN, rows + 2 * REACH, cols // 8, 8, LANES)),
            vmem((blocks, TAPS, LANES)),
            vmem((TAPS + KERN, 8, LANES)),
            vmem((blocks, cells, LANES)),
            vmem((cells, wide)),
            vmem((cells, wide - 2 * split)),
            vmem((cells, dim)),
            vmem((cells, dim)),
            vmem((cells, dim)),
        ],
        compiler_params=params(),
        cost_estimate=lasting(45),
    )(*operands)


def lay_flat(above_ref, own_ref, below_ref, flat):
    reach, cells = above_ref.shape[1], own_ref.shape[1]
    flat[:EDGE] = jnp.zeros((EDGE, LANES), F32)
    flat[EDGE : EDGE + reach] = above_ref[0]
    flat[EDGE + reach : EDGE + reach + cells] = own_ref[0]
    flat[EDGE + reach + cells : EDGE + 2 * reach + cells] = below_ref[0]
    flat[EDGE + 2 * reach + cells :] = jnp.zeros((EDGE, LANES), F32)


def backward_kernel(
    place_ref, ids_scalar, ids_ref, above_ref, own_ref, below_ref, mix_ref, kern_ref, canvas_ref, gain_ref,
    dmiddle_ref, in_ref, *rest, rows, cols,
):
    dcanvas_ref, kept_ref, sent_ref, small_kept_ref, small_sent_ref = rest[-18:-13]
    row_taps, padded, valid_ref, col_ref, flat, shifted, laid, wide, dk, sums, djoined, normed, dnorm = rest[-13:]
    step = pl.program_id(0)
    cells = rows * cols
    reach = REACH * cols
    core = place_ref[0] % 2
    split = laid.shape[0] * LANES - kern_ref.shape[1]
    width = in_ref.shape[1] // (2 * kept_ref.shape[1])

    @pl.when(step == 0)
    def _():
        lay_kernel(kern_ref, laid, split)
        turned = image_ids(ids_ref, padded, place_ref[0], rows)
        spread_cells((turned >= 0).astype(F32), valid_ref, 0, rows + 2 * REACH)
        conv_masks(ids_scalar, ids_ref, place_ref[0], row_taps, col_ref, rows)
        hat, _ = normalized(canvas_ref[...] * valid_ref[reach : reach + cells, :1])
        normed[...] = hat * gain_ref[...]
        dnorm[...] = jnp.zeros_like(dnorm)

    lay_flat(above_ref, own_ref, below_ref, flat)
    fill_shifted(flat, col_ref, shifted, rows + 2 * REACH, cols)
    conv_grad_block(
        row_taps, laid[step], shifted, wide, dk, mix_ref.at[0], djoined.at[step % 2], sums.at[step], rows, cols
    )

    @pl.when(step % 2 == 1)
    def _():
        grad = jnp.concatenate([djoined[0], djoined[1]], axis=1)
        share_columns(core, dot(normed[...], grad, TN), kept_ref, sent_ref, width, plane_first=True)
        dnorm[...] += dot(grad, in_ref[...], NT)

    @pl.when(step == pl.num_programs(0) - 1)
    def _():
        hat, scale = normalized(canvas_ref[...] * valid_ref[reach : reach + cells, :1])
        dgain = jnp.sum(dnorm[...] * hat, axis=0, keepdims=True)
        count = sums.shape[0]
        for k in range(dgain.shape[1] // LANES):
            sums[count - 1, TAPS + k : TAPS + k + 1] = dgain[:, k * LANES : (k + 1) * LANES]
        for ref, start in ((small_kept_ref, core * (count // 2)), (small_sent_ref, (1 - core) * (count // 2))):
            ref[...] = sums[pl.ds(start, count // 2)].reshape(ref.shape)
        inner = dmiddle_ref[...] + norm_backward(dnorm[...] * gain_ref[...], hat, scale)
        dcanvas_ref[...] = inner * valid_ref[reach : reach + cells, :1]


def block_of(size):
    return pl.BlockSpec((1, size, LANES), lambda i: (i, 0, 0))


def backward(
    place, ids, above, own, below, mix, kern, canvas, gain, dmiddle, weight_in, ties, rows, cols, count_ha, count_ba
):
    cells, dim = canvas.shape
    blocks = own.shape[0]
    reach = above.shape[1]
    own_wide = weight_in.shape[1] // count_ha
    chunk_rows = dim // count_ba * lane_blocks(own_wide)
    groups = 2 * LANES // (2 * own_wide)
    chunk_spec = pl.BlockSpec((count_ba, groups, chunk_rows, LANES), lambda i: (0, i // 2, 0, 0))
    chunks = shape_of(count_ba, count_ha // 2, chunk_rows, LANES)
    tall = -(-(TAPS + dim // LANES) // 8) * 8
    small = (blocks // 2 * tall, LANES)
    return pl.pallas_call(
        functools.partial(backward_kernel, rows=rows, cols=cols),
        grid=(blocks,),
        in_specs=[in_smem(), in_smem(), whole(ids.shape)]
        + [block_of(size) for size in (reach, cells, reach, cells)]
        + [whole(kern.shape), whole(canvas.shape)]
        + [whole((1, dim)), whole((cells, dim))]
        + [pl.BlockSpec((dim, 2 * LANES), lambda i: (0, i // 2))]
        + [in_hbm()] * len(ties),
        out_specs=[whole((cells, dim)), chunk_spec, chunk_spec, whole(small), whole(small)],
        out_shape=[shape_of(cells, dim), chunks, chunks, shape_of(*small), shape_of(*small)],
        scratch_shapes=mask_scratch(ids, rows)
        + [
            pltpu.VMEM((KERN, cols // 8, 8, LANES), F32),
            pltpu.VMEM((cells + 2 * reach + 2 * EDGE, LANES), F32),
            pltpu.VMEM((KERN, rows + 2 * REACH, cols // 8, 8, LANES), F32),
            pltpu.VMEM((blocks, TAPS, LANES), F32),
            pltpu.VMEM((TAPS + KERN, 8, LANES), F32),
            pltpu.VMEM((TAPS, 8, LANES), F32),
            pltpu.VMEM((blocks, tall, LANES), F32),
            pltpu.VMEM((2, cells, LANES), F32),
            pltpu.VMEM((cells, dim), F32),
            pltpu.VMEM((cells, dim), F32),
        ],
        compiler_params=params(),
        cost_estimate=lasting(25),
    )(place, ids, ids, above, own, below, mix, kern, canvas, gain, dmiddle, weight_in, *ties)


def exchange(values, axis, bit):
    return lax.ppermute(values, axis, [(i, i ^ bit) for i in range(lax.axis_size(axis))])


class View:
    def __init__(self, array, start, ways, fixed, rows):
        self.array, self.start, self.ways, self.fixed, self.rows = array, start, ways, fixed, rows

    def fix(self, way, step):
        if way == "line":
            near = lax.axis_size("ha") // 4
            return self.fix("far", step // near).fix("near", step % near)
        left = [entry for entry in self.ways if entry[0] != way]
        (stride,) = [entry[2] for entry in self.ways if entry[0] == way]
        return View(self.array, self.start, left, self.fixed + [(way, step, stride)], self.rows)

    def size(self):
        count = self.rows
        for _, size, _ in self.ways:
            count *= size
        return count

    def runs(self, ha, ba):
        start = self.start
        near = lax.axis_size("ha") // 4
        places = {"plane": ba, "far": ha // 2 // near, "near": ha // 2 % near}
        for way, step, stride in self.fixed:
            start = start + (places[way] ^ step) * stride
        rows, ways = self.rows, list(self.ways)
        while ways and ways[-1][2] == rows:
            rows *= ways.pop()[1]
        offsets = [0]
        for _, size, stride in ways:
            offsets = [offset + k * stride for offset in offsets for k in range(size)]
        return [pl.multiple_of(start + offset, 8) for offset in offsets], rows


def flat_view(array, start=0, rows=None):
    flat = array.reshape(-1, LANES)
    return View(flat, start, [], [], flat.shape[0] if rows is None else rows)


def combine(place, groups, ties=(), epilogue=None, out_shape=None):
    pieces, arrays = [], []
    for group in groups:
        for views in group:
            if not any(views is other for other in pieces):
                pieces.append(views)
    for views in pieces:
        for view in views:
            if not any(view.array is other for other in arrays):
                arrays.append(view.array)
    index_of = {id(array): k for k, array in enumerate(arrays)}
    piece_of = {id(views): k for k, views in enumerate(pieces)}
    sizes = [sum(views[0].size() for views in group) for group in groups]
    copies = sum(len(view.runs(0, 0)[0]) for views in pieces for view in views)
    plain = epilogue is None
    if plain:
        out_shape = [shape_of(size, LANES) for size in sizes]

    def kernel(place_ref, *refs):
        inputs = refs[: len(arrays)]
        refs = refs[len(arrays) + len(ties) :]
        outs, refs = refs[: len(out_shape)], refs[len(out_shape) :]
        buffers, refs = refs[: len(pieces)], refs[len(pieces) :]
        sems, results, out_sems = refs[0], refs[1:-1], refs[-1]
        ha, ba = place_ref[0], place_ref[1]
        moves, count = [], 0
        for piece, views in enumerate(pieces):
            moves.append([])
            for term, view in enumerate(views):
                source = inputs[index_of[id(view.array)]]
                starts, rows = view.runs(ha, ba)
                for k, start in enumerate(starts):
                    target = buffers[piece].at[term, pl.ds(k * rows, rows), :]
                    move = pltpu.make_async_copy(source.at[pl.ds(start, rows), :], target, sems.at[count])
                    move.start()
                    moves[-1].append(move)
                    count += 1
        values, waited, leaving = [], set(), []
        for out, group in enumerate(groups):
            row = 0
            for views in group:
                piece = piece_of[id(views)]
                if piece not in waited:
                    waited.add(piece)
                    for move in moves[piece]:
                        move.wait()
                value = buffers[piece][0]
                for term in range(1, len(views)):
                    value = value + buffers[piece][term]
                if plain:
                    results[out][row : row + value.shape[0], :] = value
                values.append(value)
                row += value.shape[0]
            if plain:
                leaving.append(pltpu.make_async_copy(results[out], outs[out], out_sems.at[out]))
                leaving[-1].start()
        if not plain:
            epilogue(ha, ba, values, outs)
        for move in leaving:
            move.wait()

    moved = sum(view.size() for views in pieces for view in views) + sum(sizes)
    scratch = [pltpu.VMEM((len(views), views[0].size(), LANES), F32) for views in pieces]
    scratch.append(pltpu.SemaphoreType.DMA((copies,)))
    if plain:
        scratch += [pltpu.VMEM((size, LANES), F32) for size in sizes]
    scratch.append(pltpu.SemaphoreType.DMA((len(groups),)))
    return pl.pallas_call(
        kernel,
        in_specs=[in_smem()] + [in_hbm()] * (len(arrays) + len(ties)),
        out_specs=[in_hbm() if plain else pl.BlockSpec(memory_space=pltpu.VMEM)] * len(out_shape),
        out_shape=out_shape,
        scratch_shapes=scratch,
        compiler_params=params(),
        cost_estimate=lasting(1 + moved * LANES * 4 / 3.0e6),
    )(place, *arrays, *ties)


def tied(arrays, ties):
    return pl.pallas_call(
        lambda *refs: None,
        in_specs=[pl.BlockSpec(memory_space=pl.ANY)] * (len(arrays) + len(ties)),
        out_specs=[pl.BlockSpec(memory_space=pl.ANY)] * len(arrays),
        out_shape=[shape_of(*array.shape) for array in arrays],
        input_output_aliases={k: k for k in range(len(arrays))},
        compiler_params=params(),
        cost_estimate=lasting(0.5),
    )(*arrays, *ties)


class Sum:
    def __init__(self, arrays, names):
        self.views = []
        near = lax.axis_size("ha") // 4
        sizes = {"plane": lax.axis_size("ba"), "far": 2, "near": near}
        for array in arrays:
            flat = array.reshape(-1, LANES)
            stride, ways = flat.shape[0], []
            for name in names:
                stride //= sizes[name]
                ways.append((name, sizes[name], stride))
            self.views.append(View(flat, 0, ways, [], stride))

    def leaving(self, way, step):
        return [view.fix(way, step) for view in self.views]

    def keep(self, way, sent, arrived):
        self.views = [view.fix(way, 0) for view in self.views]
        rows = self.views[0].rows
        stride, ways = rows, []
        for name, size, _ in reversed(self.views[0].ways):
            ways.insert(0, (name, size, stride))
            stride *= size
        self.views += [View(array, start, ways, [], rows) for array, start in arrived]

    def part(self, first, rows):
        return [View(view.array, view.start + first, view.ways, view.fixed, rows) for view in self.views]


class Rider:
    def __init__(self, views):
        self.views = views

    def leaving(self, way, step):
        return self.views

    def keep(self, way, sent, arrived):
        rows = self.views[0].size()
        self.views = [View(array, start, [], [], rows) for array, start in [sent] + arrived]


class Gather(Rider):
    def keep(self, way, sent, arrived):
        rows = self.views[0].size()
        self.gathered = [[View(array, start, [], [], rows)] for array, start in [sent] + arrived]


class Stage:
    def __init__(self, members, way):
        self.members, self.way = members, way
        line, near = lax.axis_size("ha") // 2, lax.axis_size("ha") // 4
        self.steps = {
            "plane": range(1, lax.axis_size("ba")),
            "line": range(1, line),
            "far": [near],
            "halves": range(1, near + 1),
        }[way]
        self.near = near

    def taking(self, step):
        return [
            (one, way)
            for one, way in self.members
            if way not in ("near", "far") or (way == "near") == (step < self.near)
        ]

    def groups(self):
        return [
            [one.leaving(way, step // self.near if way == "far" else step) for one, way in self.taking(step)]
            for step in self.steps
        ]

    def go(self, payloads, in_turn=False):
        axis, unit = ("ba", 1) if self.way == "plane" else ("ha", 2)
        arrived = []
        for step, part in zip(self.steps, payloads):
            if in_turn and step == len(self.steps) and step > 2:
                (part,) = tied([part], arrived[1:2])
            arrived.append(exchange(part, axis, unit * step))
        places = {}
        for step, sent, part in zip(self.steps, payloads, arrived):
            row = 0
            for one, way in self.taking(step):
                places.setdefault(id(one), []).append(((sent, row), (part, row)))
                row += one.leaving(way, 1)[0].size()
        for one, way in self.members:
            mine = places.get(id(one), [])
            one.keep(way, mine[0][0] if mine else None, [part for _, part in mine])
        return arrived


def run(place, stage, ties=(), in_turn=False, late_ties=()):
    made = list(combine(place, stage.groups(), ties))
    if late_ties:
        made = list(tied(made, late_ties))
    return made, stage.go(made, in_turn)


def neighbour_rows(top, bottom):
    count = lax.axis_size("ha")
    up = [(i, i + 1) for i in range(count - 1)]
    down = [(i + 1, i) for i in range(count - 1)]
    return lax.ppermute(bottom, "ha", up), lax.ppermute(top, "ha", down)


def lay_beside(value, ref):
    tall, width = ref.shape
    for k in range(lane_blocks(width)):
        columns = slice(k * LANES, min(width, (k + 1) * LANES))
        ref[:, columns] = value[k * tall : (k + 1) * tall, : columns.stop - columns.start]


def lay_large(ha, ba, values, outs):
    up_first, up_second, down_first, down_second, out = values
    lay_beside(jnp.concatenate([up_first, up_second], axis=0), outs[0])
    lay_beside(jnp.concatenate([down_first, down_second], axis=0), outs[1])
    lay_beside(out, outs[2])


def lay_small(ha, ba, values, outs, blocks):
    din_ref, dk_ref, gain_ref = outs[:3]
    scratch = outs[-1]
    lay_beside(values[0], din_ref)
    own, other = values[1], values[2]
    small_rows = blocks // 2 * (-(-(TAPS + gain_ref.shape[1] // LANES) // 8) * 8)
    mine = ha % 2 == 0
    first, second = jnp.where(mine, own, other), jnp.where(mine, other, own)
    dkern = jnp.concatenate([first[:small_rows], second[:small_rows]], axis=0)
    tall = dkern.shape[0] // blocks
    joined = jnp.concatenate([dkern[k * tall : k * tall + TAPS] for k in range(blocks)], axis=1)
    dk_ref[...] = joined[:, joined.shape[1] - dk_ref.shape[1] :]
    half = own.shape[0] - small_rows
    count = lax.axis_size("ba")
    part = half // count
    for core, rows in ((0, first), (1, second)):
        for step in range(count):
            start = core * half + (ba ^ step) * part
            source = small_rows + step * part
            scratch[pl.ds(pl.multiple_of(start, 8), part), :] = rows[source : source + part]
    dim = gain_ref.shape[1]
    for k in range(dim // LANES):
        columns = slice(k * LANES, (k + 1) * LANES)
        row = (blocks - 1) * tall + TAPS + k
        gain_ref[:, columns] = dkern[row : row + 1]
        for vector, ref in enumerate(outs[3:6]):
            ref[:, columns] = scratch[vector * dim // LANES + k : vector * dim // LANES + k + 1, :]
    row = scratch.shape[0]
    for ref in reversed(outs[6:-1]):
        tall, width = ref.shape
        row -= tall * width // LANES
        for k in range(width // LANES):
            ref[:, k * LANES : (k + 1) * LANES] = scratch[row + k * tall : row + (k + 1) * tall, :]


def shards(
    canvas,
    image_id,
    keep_first,
    keep_second,
    first_gain,
    weight_in,
    depth_kernel,
    gate_first,
    gate_second,
    gate_third,
    weight_out,
    scale_first,
    second_gain,
    weight_up,
    weight_down,
    scale_second,
    cotangent,
):
    _, rows, cols, dim = canvas.shape
    cells = rows * cols
    reach = REACH * cols
    count_ha, count_ba = lax.axis_size("ha"), lax.axis_size("ba")
    hidden = weight_up.shape[1]
    blocks = weight_in.shape[1] // LANES
    place = jnp.stack([lax.axis_index("ha"), lax.axis_index("ba")])
    own = canvas.reshape(cells, dim)
    gates = (gate_first, gate_second, gate_third)
    gain = first_gain[None]
    vectors = (gain, scale_first[None], second_gain[None], scale_second[None])
    ids = image_id[0]
    above, below = neighbour_rows(own[:reach], own[cells - reach :])
    (
        joined, output, dmiddle, dconv, dconv_top, dconv_bottom, plane_kept, plane_sent, line_kept, line_sent,
        packed_kept, packed_sent,
    ) = forward(
        place, ids, keep_first, keep_second, above, own, below, cotangent.reshape(cells, dim), vectors,
        weight_in, depth_kernel, gates, weight_out, weight_up, weight_down, rows, cols, count_ha, count_ba,
    )
    above, below = neighbour_rows(dconv_top, dconv_bottom)

    packed = Sum([packed_kept, exchange(packed_sent, "ha", 1)], ["plane"])
    plane_sum = Sum([plane_kept, exchange(plane_sent, "ha", 1)], ["plane", "far", "near"])
    line_sum = Sum([line_kept, exchange(line_sent, "ha", 1)], ["far", "near", "plane"])
    first, _ = run(place, Stage([(packed, "plane")], "plane"))
    packed = Rider(packed.views)
    made, arrived = run(place, Stage([(plane_sum, "plane")], "plane"), ties=first)
    more, far = run(
        place, Stage([(line_sum, "far"), (packed, "far")], "far"), ties=made, late_ties=[above, below]
    )
    made, arrived = made + more, arrived + far
    dcanvas, in_kept, in_sent, small_kept, small_sent = backward(
        place, ids, above, dconv, below, joined, depth_kernel, own, gain, dmiddle, weight_in, made,
        rows, cols, count_ha, count_ba,
    )
    in_sent, small_sent = tied([in_sent, small_sent], arrived)
    in_sum = Sum([in_kept, exchange(in_sent, "ha", 1)], ["plane", "far", "near"])
    small = Rider([flat_view(small_kept), flat_view(exchange(small_sent, "ha", 1))])
    packed = Rider(packed.views)
    made, arrived = run(
        place, Stage([(plane_sum, "far"), (line_sum, "near"), (packed, "near")], "halves")
    )
    run(place, Stage([(in_sum, "plane"), (small, "plane")], "plane"), ties=made)
    made, _ = run(
        place, Stage([(plane_sum, "near"), (in_sum, "line"), (small, "line")], "line"), ties=arrived, in_turn=True
    )
    packed = Gather(packed.views)
    run(place, Stage([(line_sum, "plane"), (packed, "plane")], "plane"), ties=made)
    cut = plane_sum.views[0].rows // 2
    rest = (line_sum.views[0].rows - dim // count_ha * lane_blocks(dim // count_ba)) // 2
    dup, ddown, dout = combine(
        place,
        [
            [
                plane_sum.part(0, cut),
                line_sum.part(0, rest),
                plane_sum.part(cut, cut),
                line_sum.part(rest, rest),
                line_sum.part(2 * rest, line_sum.views[0].rows - 2 * rest),
            ]
        ],
        epilogue=lay_large,
        out_shape=[
            shape_of(dim // count_ba, hidden // count_ha),
            shape_of(dim // count_ha, hidden // count_ba),
            shape_of(dim // count_ha, dim // count_ba),
        ],
    )
    (halves_of,) = combine(place, [[small.views] + packed.gathered], ties=[dup])
    din, dkern, dgain_one, dscale_one, dgain_two, dscale_two, dfirst, dsecond, dthird, _ = combine(
        place,
        [[in_sum.views, [flat_view(halves_of)], [flat_view(exchange(halves_of, "ha", 1))]]],
        epilogue=functools.partial(lay_small, blocks=blocks),
        out_shape=[shape_of(dim // count_ba, weight_in.shape[1] // count_ha), shape_of(*depth_kernel.shape)]
        + [shape_of(1, dim)] * 4
        + [shape_of(*gate.shape) for gate in gates]
        + [shape_of(packed_rows(gates, dim, count_ba), LANES)],
    )
    return (
        output.reshape(canvas.shape),
        dcanvas.reshape(canvas.shape),
        dgain_one[0],
        din,
        dkern,
        dfirst,
        dsecond,
        dthird,
        dout.T,
        dscale_one[0],
        dgain_two[0],
        dup,
        ddown.T,
        dscale_two[0],
    )


def solution(mesh):
    in_specs = (
        P("ba", "ha", None, None),
        P("ba", None, None),
        P("ba", None),
        P("ba", None),
    ) + (P(),) * 12 + (P("ba", "ha", None, None),)
    tiled = P("ba", "ha")
    out_specs = (
        P("ba", "ha", None, None),
        P("ba", "ha", None, None),
        P(),
        tiled,
        P(),
        P(),
        P(),
        P(),
        tiled,
        P(),
        P(),
        tiled,
        tiled,
        P(),
    )
    return jax.shard_map(shards, mesh=mesh, in_specs=in_specs, out_specs=out_specs, check_vma=False)
```

```python
import functools

import jax
import jax.numpy as jnp
from jax import lax
from jax.experimental import pallas as pl
from jax.experimental.pallas import tpu as pltpu
from jax.sharding import PartitionSpec as P

KERN = 7
TAPS = KERN * KERN
REACH = KERN // 2
KEEP_RATE = 0.8
SPREAD = 1.0 / 3.0
EPSILON = 1e-06
LANES = 128
EDGE = 8
VMEM_BYTES = 64 << 20
F32 = jnp.float32
INV_SQRT_2 = 0.7071067811865476
INV_SQRT_2PI = 0.3989422804014327
NN = (((1,), (0,)), ((), ()))
NT = (((1,), (1,)), ((), ()))
TN = (((0,), (0,)), ((), ()))


def dot(left, right, dims=NN):
    return lax.dot_general(left, right, dims, precision=lax.Precision.HIGH, preferred_element_type=F32)


def normalized(values):
    centered = values - jnp.mean(values, axis=-1, keepdims=True)
    scale = lax.rsqrt(jnp.mean(centered * centered, axis=-1, keepdims=True) + EPSILON)
    return centered * scale, scale


def norm_backward(grad_hat, hat, scale):
    return scale * (
        grad_hat
        - jnp.mean(grad_hat, axis=-1, keepdims=True)
        - hat * jnp.mean(grad_hat * hat, axis=-1, keepdims=True)
    )


def params():
    return pltpu.CompilerParams(vmem_limit_bytes=VMEM_BYTES)


def lasting(microseconds):
    return pl.CostEstimate(flops=int(microseconds * 1.1e9), bytes_accessed=0, transcendentals=0)


def whole(shape):
    return pl.BlockSpec(tuple(shape), lambda *_: (0,) * len(shape), pipeline_mode=pl.Buffered(1))


def in_smem():
    return pl.BlockSpec(memory_space=pltpu.SMEM)


def in_hbm():
    return pl.BlockSpec(memory_space=pltpu.HBM)


def shape_of(*shape):
    return jax.ShapeDtypeStruct(shape, F32)


def lane_blocks(width):
    return -(-width // LANES)


def image_ids(ids_ref, padded, place, rows):
    height, cols = ids_ref.shape
    padded[...] = jnp.full(padded.shape, -1, jnp.int32)
    padded[EDGE : EDGE + height, :] = ids_ref[...]
    ids = padded[pl.ds(place * rows + (EDGE - REACH), rows + 2 * REACH), :]
    return jnp.concatenate([ids, jnp.full((-ids.shape[0] % 8, cols), -1, jnp.int32)], axis=0).T


def spread_cells(factors, out_ref, first, rows):
    cols = factors.shape[0]
    for r in range(rows):
        column = factors[:, first + r : first + r + 1]
        out_ref[r * cols : (r + 1) * cols, :] = jnp.broadcast_to(column, (cols, LANES))


def keep_factors(turned, table_ref):
    result = jnp.zeros(turned.shape, F32)
    for slot in range(table_ref.shape[1]):
        result = jnp.where(turned == slot, table_ref[0, slot].astype(F32) / KEEP_RATE, result)
    return result


def conv_masks(ids_scalar, ids_ref, place, row_taps, col_mask, rows):
    height, cols = ids_ref.shape
    wide_ids = jnp.broadcast_to(ids_ref[...].T[:, height // 2 : height // 2 + 1], (cols, LANES))
    column = lax.broadcasted_iota(jnp.int32, (cols, LANES), 0)
    for b in range(KERN):
        shift = b - REACH
        moved = pltpu.roll(wide_ids, (-shift) % cols, 0)
        inside = (column + shift >= 0) & (column + shift < cols)
        same = (moved == wide_ids) & inside
        col_mask[b] = same.astype(F32).reshape(cols // 8, 8, LANES)

    def one(r, _):
        own = ids_scalar[place * rows + r, cols // 2]
        row_taps[r, 0] = KERN
        row_taps[r, KERN + 1] = KERN
        for a in range(KERN):
            other = place * rows + r + a - REACH
            inside = (other >= 0) & (other < height)
            same = ids_scalar[jnp.clip(other, 0, height - 1), cols // 2] == own
            row_taps[r, a + 1] = jnp.where(inside & same, a, KERN)
        return 0

    lax.fori_loop(0, rows, one, 0)


def lay_kernel(kern_ref, laid, split):
    tap = lax.broadcasted_iota(jnp.int32, (TAPS, split), 0)
    own = jnp.where(tap == TAPS // 2, 1.0 / SPREAD, 0.0).astype(F32)
    for k in range(laid.shape[0]):
        start = k * LANES - split
        left = own if k == 0 else kern_ref[:, start : start + split]
        laid[k] = jnp.concatenate([left, kern_ref[:, start + split : start + LANES]], axis=1) * SPREAD


def fill_shifted(flat, col_ref, shifted, rows_ext, cols):
    for b in range(KERN):
        for g in range(cols // 8):
            mask = None if b == REACH else col_ref[b, g]
            for r in range(rows_ext):
                x = flat[pl.ds(EDGE + r * cols + 8 * g + b - REACH, 8), :]
                shifted[b, r, g] = x if b == REACH else x * mask


def spread_taps(kern, wide, turned):
    for t in range(TAPS):
        source = TAPS - 1 - t if turned else t
        wide[t] = jnp.broadcast_to(kern[source : source + 1, :], (8, LANES))
    for t in range(KERN):
        wide[TAPS + t] = jnp.zeros((8, LANES), F32)


def conv_block(row_taps, kern, shifted, wide, out_ref, rows, cols):
    groups = cols // 8
    spread_taps(kern, wide, False)

    def pair(h, _):
        r = 2 * h

        def step(i, totals):
            first, second = totals
            taps_first = row_taps[r, i + 1] * KERN
            taps_second = row_taps[r + 1, i] * KERN
            for b in range(KERN):
                x = shifted[b, r + i]
                first = first + wide[taps_first + b][None] * x
                second = second + wide[taps_second + b][None] * x
            return first, second

        zero = jnp.zeros((groups, 8, LANES), F32)
        first, second = lax.fori_loop(0, KERN + 1, step, (zero, zero), unroll=4)
        out_ref[pl.ds(pl.multiple_of(r * cols, cols), cols), :] = first.reshape(cols, LANES)
        out_ref[pl.ds(pl.multiple_of((r + 1) * cols, cols), cols), :] = second.reshape(cols, LANES)
        return 0

    lax.fori_loop(0, rows // 2, pair, 0)


def conv_grad_block(row_taps, kern, shifted, wide, dk, mix_ref, out_ref, dk_ref, rows, cols):
    groups = cols // 8
    spread_taps(kern, wide, True)
    for t in range(TAPS):
        dk[t] = jnp.zeros((8, LANES), F32)

    def one(r, _):
        start = pl.ds(pl.multiple_of(r * cols, cols), cols)
        mix = mix_ref[start, :].reshape(groups, 8, LANES)
        total = jnp.zeros((groups, 8, LANES), F32)
        for i in range(KERN):
            row = row_taps[r, i + 1]
            same = jnp.where(row < KERN, 1.0, 0.0).astype(F32)
            for b in range(KERN):
                x = shifted[b, r + i]
                total = total + wide[row * KERN + b][None] * x
                dk[i * KERN + b] += jnp.sum(mix * x, axis=0) * same
        out_ref[start, :] = total.reshape(cols, LANES)
        return 0

    lax.fori_loop(0, rows, one, 0)
    for t in range(TAPS):
        dk_ref[TAPS - 1 - t : TAPS - t, :] = jnp.sum(dk[t], axis=0, keepdims=True) * SPREAD
    dk_ref[TAPS:, :] = jnp.zeros((dk_ref.shape[0] - TAPS, LANES), F32)


def share(core, first, second, kept_ref, sent_ref, z, p):
    mine = core == 0
    tall, width = first.shape
    for ref, chunk in (
        (kept_ref, jnp.where(mine, first, second)),
        (sent_ref, jnp.where(mine, second, first)),
    ):
        for k in range(lane_blocks(width)):
            part = chunk[:, k * LANES : (k + 1) * LANES]
            if part.shape[1] < LANES:
                part = jnp.concatenate([part, jnp.zeros((tall, LANES - part.shape[1]), F32)], axis=1)
            ref[z, p, k * tall : (k + 1) * tall, :] = part


def share_columns(core, grad, kept_ref, sent_ref, width, plane_first=False):
    groups, parts = reversed(kept_ref.shape[:2]) if plane_first else kept_ref.shape[:2]
    tall = grad.shape[0] // parts
    for z in range(groups):
        for p in range(parts):
            rows = slice(p * tall, (p + 1) * tall)
            first = grad[rows, 2 * z * width : (2 * z + 1) * width]
            second = grad[rows, (2 * z + 1) * width : (2 * z + 2) * width]
            share(core, first, second, kept_ref, sent_ref, *((p, z) if plane_first else (z, p)))


def share_rows(core, grad, kept_ref, sent_ref, tall):
    groups, parts = kept_ref.shape[:2]
    width = grad.shape[1] // parts
    for z in range(groups):
        for p in range(parts):
            columns = slice(p * width, (p + 1) * width)
            first = grad[2 * z * tall : (2 * z + 1) * tall, columns]
            second = grad[(2 * z + 1) * tall : (2 * z + 2) * tall, columns]
            share(core, first, second, kept_ref, sent_ref, z, p)


class Copies:
    def __init__(self, sems):
        self.sems, self.count, self.pending = sems, 0, {}

    def start(self, name, source, target):
        copy = pltpu.make_async_copy(source, target, self.sems.at[self.count])
        self.count += 1
        copy.start()
        self.pending.setdefault(name, []).append(copy)

    def wait(self, *names):
        for name in names:
            for copy in self.pending.pop(name):
                copy.wait()

    def wait_all(self):
        self.wait(*list(self.pending))


def forward_kernel(
    place_ref, ids_scalar, one_table, two_table, ids_hbm, above_hbm, own_hbm, below_hbm, cot_hbm,
    first_gain_hbm, first_scale_hbm, second_gain_hbm, second_scale_hbm,
    in_hbm_ref, kern_hbm, one_hbm, two_hbm, three_hbm, out_hbm, up_hbm, down_hbm,
    joined_hbm, output_hbm, dmiddle_hbm, dconv_hbm, dconv_top_hbm, dconv_bottom_hbm,
    plane_kept_ref, plane_sent_ref, line_kept_ref, line_sent_ref, packed_kept_hbm, packed_sent_hbm,
    ids_ref, rows_ref, cot_ref, first_gain_ref, first_scale_ref, second_gain_ref, second_scale_ref,
    in_ref, kern_ref, one_ref, two_ref, three_ref, out_ref, up_ref, down_ref, dconv_ref, sems, chunk_sems,
    up_kept, up_sent, down_kept, down_sent, out_kept, out_sent,
    row_taps, padded, valid_ref, one_keep_ref, two_keep_ref, col_ref, packed_ref, normed, flat, shifted, laid, wide, conv,
    mixed_ref, mapped_ref, middle_ref, result, dnorm,
    *, rows, cols, count_ha, count_ba,
):
    blocks = flat.shape[0]
    cells = rows * cols
    reach = REACH * cols
    cells_ext = cells + 2 * reach
    core = place_ref[0] % 2
    split = one_ref.shape[0]
    dim = rows_ref.shape[1]
    head_steps = blocks // 2
    ffn_steps = up_kept.shape[0]
    chunk = down_ref.shape[1]
    gate_refs = (one_ref, two_ref, three_ref)

    copies = Copies(sems)
    copies.start("ids", ids_hbm, ids_ref)
    copies.start("above", above_hbm, rows_ref.at[pl.ds(0, reach)])
    copies.start("own", own_hbm, rows_ref.at[pl.ds(reach, cells)])
    copies.start("below", below_hbm, rows_ref.at[pl.ds(reach + cells, reach)])
    copies.start("vectors", first_gain_hbm, first_gain_ref)
    for k in range(head_steps):
        copies.start(("in", k), in_hbm_ref.at[:, pl.ds(2 * LANES * k, 2 * LANES)], in_ref.at[k])
    copies.start("kern", kern_hbm, kern_ref)
    def weights(k):
        ends = pl.ds(pl.multiple_of(k * chunk, chunk), chunk)
        return [
            pltpu.make_async_copy(up_hbm.at[:, ends], up_ref.at[k], chunk_sems.at[k, 0]),
            pltpu.make_async_copy(down_hbm.at[ends, :], down_ref.at[k], chunk_sems.at[k, 1]),
        ]

    def chunk_copies(place):
        moves = []
        sides = ((up_kept, down_kept, plane_kept_ref, line_kept_ref), (up_sent, down_sent, plane_sent_ref, line_sent_ref))
        for up, down, plane, line in sides:
            cut = plane.shape[2] // 2
            rest = up.shape[3] - cut
            zs = pl.ds(place * up.shape[1], up.shape[1])
            bas = pl.ds(place * down.shape[2], down.shape[2])
            moves += [
                (up.at[place, :, ba, pl.ds(0, cut), :], plane.at[ba, zs, pl.ds(0, cut), :])
                for ba in range(plane.shape[0])
            ]
            moves += [
                (down.at[place, z, :, pl.ds(0, cut), :], plane.at[bas, z, pl.ds(cut, cut), :])
                for z in range(plane.shape[1])
            ]
            moves.append((up.at[place, :, :, pl.ds(cut, rest), :], line.at[zs, :, pl.ds(0, rest), :]))
            moves.append((down.at[place, :, :, pl.ds(cut, rest), :], line.at[:, bas, pl.ds(rest, rest), :]))
        return [
            pltpu.make_async_copy(source, target, chunk_sems.at[place, 2 + k])
            for k, (source, target) in enumerate(moves)
        ]

    copies.wait("ids")
    turned = image_ids(ids_ref, padded, place_ref[0], rows)
    spread_cells((turned >= 0).astype(F32), valid_ref, 0, rows + 2 * REACH)
    spread_cells(keep_factors(turned, one_table), one_keep_ref, REACH, rows)
    spread_cells(keep_factors(turned, two_table), two_keep_ref, REACH, rows)
    conv_masks(ids_scalar, ids_ref, place_ref[0], row_taps, col_ref, rows)
    copies.wait("vectors")
    start = 0
    for name, size in (("above", reach), ("own", cells), ("below", reach)):
        copies.wait(name)
        hat, _ = normalized(rows_ref[start : start + size, :] * valid_ref[start : start + size, :1])
        normed[start : start + size] = hat * first_gain_ref[...]
        start += size

    for k in range(blocks):
        flat[k, :EDGE] = jnp.zeros((EDGE, LANES), F32)
        flat[k, EDGE + cells_ext :] = jnp.zeros((EDGE, LANES), F32)
    for step in range(head_steps):
        copies.wait(("in", step))
        joined = dot(normed[...], in_ref[step])
        for k in range(2):
            flat[2 * step + k, EDGE : EDGE + cells_ext] = joined[:, k * LANES : (k + 1) * LANES]
        if step == 0:
            copies.start("gates", first_scale_hbm, first_scale_ref)
            copies.start("gates", second_gain_hbm, second_gain_ref)
            copies.start("gates", second_scale_hbm, second_scale_ref)
            for source, target in zip((one_hbm, two_hbm, three_hbm, out_hbm, cot_hbm), gate_refs + (out_ref, cot_ref)):
                copies.start("gates", source, target)
            for k in range(ffn_steps):
                for copy in weights(k):
                    copy.start()
        pair = pl.ds(2 * step, 2)
        copies.start("outs", flat.at[pair, pl.ds(EDGE + reach, cells), :], joined_hbm.at[pair])

    copies.wait("kern")
    lay_kernel(kern_ref, laid, split)

    def conv_step(block, _):
        fill_shifted(flat.at[block], col_ref, shifted, rows + 2 * REACH, cols)
        conv_block(row_taps, laid[block], shifted, wide, conv.at[block], rows, cols)
        return 0

    lax.fori_loop(0, blocks, conv_step, 0)

    def conv_part(start, width):
        return jnp.concatenate([conv[start // LANES + k] for k in range(width // LANES)], axis=1)

    copies.wait("gates")
    mixed = conv[0, :, :split] * conv[0, :, split:]
    mixed_ref[:, :split] = mixed
    start = 2 * split
    for ref in gate_refs:
        width = ref.shape[1]
        mapped = dot(mixed, ref[...])
        mapped_ref[:, start - 2 * split : start - 2 * split + width] = mapped
        mixed = mapped * conv_part(start, width)
        mixed_ref[:, start : start + width] = mixed
        start += width
    branch = dot(mixed, out_ref[...])
    masked = rows_ref[reach : reach + cells, :] * valid_ref[reach : reach + cells, :1]
    middle = masked + one_keep_ref[:, :1] * first_scale_ref[...] * branch
    middle_ref[...] = middle
    hat, _ = normalized(middle)
    normed[:cells] = hat * second_gain_ref[...]
    result[...] = jnp.zeros_like(result)
    dnorm[...] = jnp.zeros_like(dnorm)

    def ffn_step(place, _):
        for copy in weights(place):
            copy.wait()
        grad_result = two_keep_ref[:, :1] * second_scale_ref[...] * cot_ref[...]
        pre = dot(normed[:cells], up_ref[place])
        cdf = 0.5 + 0.5 * lax.erf(pre * INV_SQRT_2)
        slope = cdf + pre * (INV_SQRT_2PI * jnp.exp(-0.5 * pre * pre))
        hidden = pre * cdf
        result[...] += dot(hidden, down_ref[place])
        grad_pre = dot(grad_result, down_ref[place], NT) * slope
        share_rows(
            core, dot(grad_result, hidden, TN), down_kept.at[place], down_sent.at[place], dim // count_ha
        )
        width = chunk // (2 * up_kept.shape[1])
        share_columns(core, dot(normed[:cells], grad_pre, TN), up_kept.at[place], up_sent.at[place], width)
        for copy in chunk_copies(place):
            copy.start()
        dnorm[...] += dot(grad_pre, up_ref[place], NT)
        return 0

    lax.fori_loop(0, ffn_steps, ffn_step, 0)

    hat, scale = normalized(middle_ref[...])
    kept = two_keep_ref[:, :1] * result[...]
    dscale_two = jnp.sum(cot_ref[...] * kept, axis=0, keepdims=True)
    result[...] = middle_ref[...] + second_scale_ref[...] * kept
    copies.start("outs", result, output_hbm)
    dgain_two = jnp.sum(dnorm[...] * hat, axis=0, keepdims=True)
    dmiddle = cot_ref[...] + norm_backward(dnorm[...] * second_gain_ref[...], hat, scale)
    dnorm[...] = dmiddle
    copies.start("outs", dnorm, dmiddle_hbm)
    kept = one_keep_ref[:, :1] * dmiddle
    grad = dot(kept * first_scale_ref[...], out_ref[...], NT)
    row = packed_ref.shape[0]
    start = blocks * LANES
    for ref in reversed(gate_refs):
        tall, width = ref.shape
        start -= width
        source = start - tall if tall > split else 0
        columns = slice(start - 2 * split, start - 2 * split + width)
        dconv = grad * mapped_ref[:, columns]
        for k in range(width // LANES):
            dconv_ref[start // LANES + k] = dconv[:, k * LANES : (k + 1) * LANES]
        grad_mapped = grad * conv_part(start, width)
        part = dot(mixed_ref[:, source : source + tall], grad_mapped, TN)
        row -= tall * width // LANES
        for k in range(width // LANES):
            packed_ref[row + k * tall : row + (k + 1) * tall] = part[:, k * LANES : (k + 1) * LANES]
        grad = dot(grad_mapped, ref[...], NT)
    dconv_ref[0] = jnp.concatenate([grad * conv[0, :, split:], grad * conv[0, :, :split]], axis=1)
    copies.start("outs", dconv_ref.at[:, pl.ds(0, reach), :], dconv_top_hbm)
    copies.start("outs", dconv_ref.at[:, pl.ds(cells - reach, reach), :], dconv_bottom_hbm)
    copies.start("outs", dconv_ref, dconv_hbm)
    start = mixed_ref.shape[1] - out_ref.shape[0]
    crossed = dot(mixed_ref[:, start:], kept, TN)
    dscale_one = jnp.sum(crossed * out_ref[...], axis=0, keepdims=True)
    packed_ref[:row] = jnp.zeros((row, LANES), F32)
    row = 0
    for vector in (dscale_one, dgain_two, dscale_two):
        for k in range(dim // LANES):
            packed_ref[row : row + 1] = vector[:, k * LANES : (k + 1) * LANES]
            row += 1
    half = packed_kept_hbm.shape[0]
    for place, target in ((core, packed_kept_hbm), (1 - core, packed_sent_hbm)):
        copies.start("outs", packed_ref.at[pl.ds(pl.multiple_of(place * half, 8), half), :], target)
    share_rows(core, (crossed * first_scale_ref[...]).T, out_kept, out_sent, dim // count_ha)
    for source, line in ((out_kept, line_kept_ref), (out_sent, line_sent_ref)):
        tall = source.shape[2]
        copies.start("outs", source, line.at[:, :, pl.ds(line.shape[2] - tall, tall), :])
    for place in range(ffn_steps):
        for copy in chunk_copies(place):
            copy.wait()
    copies.wait_all()


def mask_scratch(ids, rows):
    height, cols = ids.shape
    return [
        pltpu.SMEM((rows, KERN + 2), jnp.int32),
        pltpu.VMEM((height + 2 * EDGE, cols), jnp.int32),
        pltpu.VMEM(((rows + 2 * REACH) * cols, LANES), F32),
    ]


def packed_rows(gates, dim, parts):
    rows = sum(gate.size for gate in gates) // LANES + 3 * dim // LANES
    return -(-rows // (16 * parts)) * 16 * parts


def plane_share(rows):
    return max(rows * 3 // 4 // 8 * 8, 8)


def forward(
    place, ids, keep_one, keep_two, above, own, below, cot, vectors, weight_in, kern, gates,
    weight_out, weight_up, weight_down, rows, cols, count_ha, count_ba, chunk=512,
):
    cells, dim = own.shape
    reach = above.shape[0]
    blocks = weight_in.shape[1] // LANES
    hidden = weight_up.shape[1]
    split = gates[0].shape[0]
    wide = blocks * LANES
    head_steps = blocks // 2
    ffn_steps = hidden // chunk

    up_wide, down_wide = hidden // count_ha, hidden // count_ba
    up_rows = dim // count_ba * lane_blocks(up_wide)
    down_rows = dim // count_ha * lane_blocks(down_wide)
    out_rows = dim // count_ha * lane_blocks(dim // count_ba)
    half = count_ha // 2
    assert up_rows == down_rows
    cut = plane_share(up_rows)
    rest = up_rows - cut
    plane = (count_ba, half, 2 * cut, LANES)
    line = (half, count_ba, 2 * rest + out_rows, LANES)
    packed_shape = (packed_rows(gates, dim, count_ba), LANES)
    half_packed = (packed_shape[0] // 2, LANES)
    cells_ext = cells + 2 * reach
    vmem = functools.partial(pltpu.VMEM, dtype=F32)
    operands = (
        place, ids, keep_one, keep_two, ids, above, own, below, cot, *vectors,
        weight_in, kern, *gates, weight_out, weight_up, weight_down,
    )
    out_shape = [
        shape_of(blocks, cells, LANES),
        shape_of(cells, dim),
        shape_of(cells, dim),
        shape_of(blocks, cells, LANES),
        shape_of(blocks, reach, LANES),
        shape_of(blocks, reach, LANES),
        shape_of(*plane),
        shape_of(*plane),
        shape_of(*line),
        shape_of(*line),
        shape_of(*half_packed),
        shape_of(*half_packed),
    ]
    return pl.pallas_call(
        functools.partial(forward_kernel, rows=rows, cols=cols, count_ha=count_ha, count_ba=count_ba),
        in_specs=[in_smem()] * 4 + [in_hbm()] * (len(operands) - 4),
        out_specs=[in_hbm()] * len(out_shape),
        out_shape=out_shape,
        scratch_shapes=[pltpu.VMEM(ids.shape, jnp.int32), vmem((cells_ext, dim)), vmem((cells, dim))]
        + [vmem((1, dim))] * 4
        + [vmem((head_steps, dim, 2 * LANES)), vmem(kern.shape)]
        + [vmem(gate.shape) for gate in gates]
        + [
            vmem(weight_out.shape),
            vmem((ffn_steps, dim, chunk)),
            vmem((ffn_steps, chunk, dim)),
            vmem((blocks, cells, LANES)),
            pltpu.SemaphoreType.DMA((40 + head_steps,)),
            pltpu.SemaphoreType.DMA((ffn_steps, 2 + 2 * (count_ba + half + 2))),
        ]
        + [vmem((ffn_steps, chunk // (2 * up_wide), count_ba, up_rows, LANES))] * 2
        + [vmem((ffn_steps, half, chunk // down_wide, down_rows, LANES))] * 2
        + [vmem((half, count_ba, out_rows, LANES))] * 2
        + mask_scratch(ids, rows)
        + [
            vmem((cells, LANES)),
            vmem((cells, LANES)),
            vmem((KERN, cols // 8, 8, LANES)),
            vmem(packed_shape),
            vmem((cells_ext, dim)),
            vmem((blocks, cells_ext + 2 * EDGE, LANES)),
            vmem((KERN, rows + 2 * REACH, cols // 8, 8, LANES)),
            vmem((blocks, TAPS, LANES)),
            vmem((TAPS + KERN, 8, LANES)),
            vmem((blocks, cells, LANES)),
            vmem((cells, wide)),
            vmem((cells, wide - 2 * split)),
            vmem((cells, dim)),
            vmem((cells, dim)),
            vmem((cells, dim)),
        ],
        compiler_params=params(),
        cost_estimate=lasting(45),
    )(*operands)


def lay_flat(above_ref, own_ref, below_ref, flat):
    reach, cells = above_ref.shape[1], own_ref.shape[1]
    flat[:EDGE] = jnp.zeros((EDGE, LANES), F32)
    flat[EDGE : EDGE + reach] = above_ref[0]
    flat[EDGE + reach : EDGE + reach + cells] = own_ref[0]
    flat[EDGE + reach + cells : EDGE + 2 * reach + cells] = below_ref[0]
    flat[EDGE + 2 * reach + cells :] = jnp.zeros((EDGE, LANES), F32)


def backward_kernel(
    place_ref, ids_scalar, ids_ref, above_ref, own_ref, below_ref, mix_ref, kern_ref, canvas_ref, gain_ref,
    dmiddle_ref, in_ref, *rest, rows, cols,
):
    dcanvas_ref, kept_ref, sent_ref, small_kept_ref, small_sent_ref = rest[-18:-13]
    row_taps, padded, valid_ref, col_ref, flat, shifted, laid, wide, dk, sums, djoined, normed, dnorm = rest[-13:]
    step = pl.program_id(0)
    cells = rows * cols
    reach = REACH * cols
    core = place_ref[0] % 2
    split = laid.shape[0] * LANES - kern_ref.shape[1]
    width = in_ref.shape[1] // (2 * kept_ref.shape[1])

    @pl.when(step == 0)
    def _():
        lay_kernel(kern_ref, laid, split)
        turned = image_ids(ids_ref, padded, place_ref[0], rows)
        spread_cells((turned >= 0).astype(F32), valid_ref, 0, rows + 2 * REACH)
        conv_masks(ids_scalar, ids_ref, place_ref[0], row_taps, col_ref, rows)
        hat, _ = normalized(canvas_ref[...] * valid_ref[reach : reach + cells, :1])
        normed[...] = hat * gain_ref[...]
        dnorm[...] = jnp.zeros_like(dnorm)

    lay_flat(above_ref, own_ref, below_ref, flat)
    fill_shifted(flat, col_ref, shifted, rows + 2 * REACH, cols)
    conv_grad_block(
        row_taps, laid[step], shifted, wide, dk, mix_ref.at[0], djoined.at[step % 2], sums.at[step], rows, cols
    )

    @pl.when(step % 2 == 1)
    def _():
        grad = jnp.concatenate([djoined[0], djoined[1]], axis=1)
        share_columns(core, dot(normed[...], grad, TN), kept_ref, sent_ref, width, plane_first=True)
        dnorm[...] += dot(grad, in_ref[...], NT)

    @pl.when(step == pl.num_programs(0) - 1)
    def _():
        hat, scale = normalized(canvas_ref[...] * valid_ref[reach : reach + cells, :1])
        dgain = jnp.sum(dnorm[...] * hat, axis=0, keepdims=True)
        count = sums.shape[0]
        for k in range(dgain.shape[1] // LANES):
            sums[count - 1, TAPS + k : TAPS + k + 1] = dgain[:, k * LANES : (k + 1) * LANES]
        for ref, start in ((small_kept_ref, core * (count // 2)), (small_sent_ref, (1 - core) * (count // 2))):
            ref[...] = sums[pl.ds(start, count // 2)].reshape(ref.shape)
        inner = dmiddle_ref[...] + norm_backward(dnorm[...] * gain_ref[...], hat, scale)
        dcanvas_ref[...] = inner * valid_ref[reach : reach + cells, :1]


def block_of(size):
    return pl.BlockSpec((1, size, LANES), lambda i: (i, 0, 0))


def backward(
    place, ids, above, own, below, mix, kern, canvas, gain, dmiddle, weight_in, ties, rows, cols, count_ha, count_ba
):
    cells, dim = canvas.shape
    blocks = own.shape[0]
    reach = above.shape[1]
    own_wide = weight_in.shape[1] // count_ha
    chunk_rows = dim // count_ba * lane_blocks(own_wide)
    groups = 2 * LANES // (2 * own_wide)
    chunk_spec = pl.BlockSpec((count_ba, groups, chunk_rows, LANES), lambda i: (0, i // 2, 0, 0))
    chunks = shape_of(count_ba, count_ha // 2, chunk_rows, LANES)
    tall = -(-(TAPS + dim // LANES) // 8) * 8
    small = (blocks // 2 * tall, LANES)
    return pl.pallas_call(
        functools.partial(backward_kernel, rows=rows, cols=cols),
        grid=(blocks,),
        in_specs=[in_smem(), in_smem(), whole(ids.shape)]
        + [block_of(size) for size in (reach, cells, reach, cells)]
        + [whole(kern.shape), whole(canvas.shape)]
        + [whole((1, dim)), whole((cells, dim))]
        + [pl.BlockSpec((dim, 2 * LANES), lambda i: (0, i // 2))]
        + [in_hbm()] * len(ties),
        out_specs=[whole((cells, dim)), chunk_spec, chunk_spec, whole(small), whole(small)],
        out_shape=[shape_of(cells, dim), chunks, chunks, shape_of(*small), shape_of(*small)],
        scratch_shapes=mask_scratch(ids, rows)
        + [
            pltpu.VMEM((KERN, cols // 8, 8, LANES), F32),
            pltpu.VMEM((cells + 2 * reach + 2 * EDGE, LANES), F32),
            pltpu.VMEM((KERN, rows + 2 * REACH, cols // 8, 8, LANES), F32),
            pltpu.VMEM((blocks, TAPS, LANES), F32),
            pltpu.VMEM((TAPS + KERN, 8, LANES), F32),
            pltpu.VMEM((TAPS, 8, LANES), F32),
            pltpu.VMEM((blocks, tall, LANES), F32),
            pltpu.VMEM((2, cells, LANES), F32),
            pltpu.VMEM((cells, dim), F32),
            pltpu.VMEM((cells, dim), F32),
        ],
        compiler_params=params(),
        cost_estimate=lasting(25),
    )(place, ids, ids, above, own, below, mix, kern, canvas, gain, dmiddle, weight_in, *ties)


def exchange(values, axis, bit):
    return lax.ppermute(values, axis, [(i, i ^ bit) for i in range(lax.axis_size(axis))])


class View:
    def __init__(self, array, start, ways, fixed, rows):
        self.array, self.start, self.ways, self.fixed, self.rows = array, start, ways, fixed, rows

    def fix(self, way, step):
        if way == "line":
            near = lax.axis_size("ha") // 4
            return self.fix("far", step // near).fix("near", step % near)
        left = [entry for entry in self.ways if entry[0] != way]
        (stride,) = [entry[2] for entry in self.ways if entry[0] == way]
        return View(self.array, self.start, left, self.fixed + [(way, step, stride)], self.rows)

    def size(self):
        count = self.rows
        for _, size, _ in self.ways:
            count *= size
        return count

    def runs(self, ha, ba):
        start = self.start
        near = lax.axis_size("ha") // 4
        places = {"plane": ba, "far": ha // 2 // near, "near": ha // 2 % near}
        for way, step, stride in self.fixed:
            start = start + (places[way] ^ step) * stride
        rows, ways = self.rows, list(self.ways)
        while ways and ways[-1][2] == rows:
            rows *= ways.pop()[1]
        offsets = [0]
        for _, size, stride in ways:
            offsets = [offset + k * stride for offset in offsets for k in range(size)]
        return [pl.multiple_of(start + offset, 8) for offset in offsets], rows


def flat_view(array, start=0, rows=None):
    flat = array.reshape(-1, LANES)
    return View(flat, start, [], [], flat.shape[0] if rows is None else rows)


def combine(place, groups, ties=(), epilogue=None, out_shape=None):
    pieces, arrays = [], []
    for group in groups:
        for views in group:
            if not any(views is other for other in pieces):
                pieces.append(views)
    for views in pieces:
        for view in views:
            if not any(view.array is other for other in arrays):
                arrays.append(view.array)
    index_of = {id(array): k for k, array in enumerate(arrays)}
    piece_of = {id(views): k for k, views in enumerate(pieces)}
    sizes = [sum(views[0].size() for views in group) for group in groups]
    copies = sum(len(view.runs(0, 0)[0]) for views in pieces for view in views)
    plain = epilogue is None
    if plain:
        out_shape = [shape_of(size, LANES) for size in sizes]

    def kernel(place_ref, *refs):
        inputs = refs[: len(arrays)]
        refs = refs[len(arrays) + len(ties) :]
        outs, refs = refs[: len(out_shape)], refs[len(out_shape) :]
        buffers, refs = refs[: len(pieces)], refs[len(pieces) :]
        sems, results, out_sems = refs[0], refs[1:-1], refs[-1]
        ha, ba = place_ref[0], place_ref[1]
        moves, count = [], 0
        for piece, views in enumerate(pieces):
            moves.append([])
            for term, view in enumerate(views):
                source = inputs[index_of[id(view.array)]]
                starts, rows = view.runs(ha, ba)
                for k, start in enumerate(starts):
                    target = buffers[piece].at[term, pl.ds(k * rows, rows), :]
                    move = pltpu.make_async_copy(source.at[pl.ds(start, rows), :], target, sems.at[count])
                    move.start()
                    moves[-1].append(move)
                    count += 1
        values, waited, leaving = [], set(), []
        for out, group in enumerate(groups):
            row = 0
            for views in group:
                piece = piece_of[id(views)]
                if piece not in waited:
                    waited.add(piece)
                    for move in moves[piece]:
                        move.wait()
                value = buffers[piece][0]
                for term in range(1, len(views)):
                    value = value + buffers[piece][term]
                if plain:
                    results[out][row : row + value.shape[0], :] = value
                values.append(value)
                row += value.shape[0]
            if plain:
                leaving.append(pltpu.make_async_copy(results[out], outs[out], out_sems.at[out]))
                leaving[-1].start()
        if not plain:
            epilogue(ha, ba, values, outs)
        for move in leaving:
            move.wait()

    moved = sum(view.size() for views in pieces for view in views) + sum(sizes)
    scratch = [pltpu.VMEM((len(views), views[0].size(), LANES), F32) for views in pieces]
    scratch.append(pltpu.SemaphoreType.DMA((copies,)))
    if plain:
        scratch += [pltpu.VMEM((size, LANES), F32) for size in sizes]
    scratch.append(pltpu.SemaphoreType.DMA((len(groups),)))
    return pl.pallas_call(
        kernel,
        in_specs=[in_smem()] + [in_hbm()] * (len(arrays) + len(ties)),
        out_specs=[in_hbm() if plain else pl.BlockSpec(memory_space=pltpu.VMEM)] * len(out_shape),
        out_shape=out_shape,
        scratch_shapes=scratch,
        compiler_params=params(),
        cost_estimate=lasting(1 + moved * LANES * 4 / 3.0e6),
    )(place, *arrays, *ties)


def tied(arrays, ties):
    return pl.pallas_call(
        lambda *refs: None,
        in_specs=[pl.BlockSpec(memory_space=pl.ANY)] * (len(arrays) + len(ties)),
        out_specs=[pl.BlockSpec(memory_space=pl.ANY)] * len(arrays),
        out_shape=[shape_of(*array.shape) for array in arrays],
        input_output_aliases={k: k for k in range(len(arrays))},
        compiler_params=params(),
        cost_estimate=lasting(0.5),
    )(*arrays, *ties)


class Sum:
    def __init__(self, arrays, names):
        self.views = []
        near = lax.axis_size("ha") // 4
        sizes = {"plane": lax.axis_size("ba"), "far": 2, "near": near}
        for array in arrays:
            flat = array.reshape(-1, LANES)
            stride, ways = flat.shape[0], []
            for name in names:
                stride //= sizes[name]
                ways.append((name, sizes[name], stride))
            self.views.append(View(flat, 0, ways, [], stride))

    def leaving(self, way, step):
        return [view.fix(way, step) for view in self.views]

    def keep(self, way, sent, arrived):
        self.views = [view.fix(way, 0) for view in self.views]
        rows = self.views[0].rows
        stride, ways = rows, []
        for name, size, _ in reversed(self.views[0].ways):
            ways.insert(0, (name, size, stride))
            stride *= size
        self.views += [View(array, start, ways, [], rows) for array, start in arrived]

    def part(self, first, rows):
        return [View(view.array, view.start + first, view.ways, view.fixed, rows) for view in self.views]


class Rider:
    def __init__(self, views):
        self.views = views

    def leaving(self, way, step):
        return self.views

    def keep(self, way, sent, arrived):
        rows = self.views[0].size()
        self.views = [View(array, start, [], [], rows) for array, start in [sent] + arrived]


class Gather(Rider):
    def keep(self, way, sent, arrived):
        rows = self.views[0].size()
        self.gathered = [[View(array, start, [], [], rows)] for array, start in [sent] + arrived]


class Stage:
    def __init__(self, members, way):
        self.members, self.way = members, way
        line, near = lax.axis_size("ha") // 2, lax.axis_size("ha") // 4
        self.steps = {
            "plane": list(range(1, lax.axis_size("ba"))),
            "line": list(range(1, line)),
            "near last": list(range(near, line)) + list(range(1, near)),
            "far": [near],
        }[way]
        self.near = near

    def taking(self, step):
        takes = {"plane": True, "line": True, "near": step < self.near, "far": step == self.near}
        return [(one, way) for one, way in self.members if takes[way]]

    def groups(self):
        return [
            [one.leaving(way, step // self.near if way == "far" else step) for one, way in self.taking(step)]
            for step in self.steps
        ]

    def go(self, payloads, in_turn=False):
        axis, unit = ("ba", 1) if self.way == "plane" else ("ha", 2)
        arrived = []
        for step, part in zip(self.steps, payloads):
            if in_turn and len(arrived) == 2:
                (part,) = tied([part], arrived[1:])
            arrived.append(exchange(part, axis, unit * step))
        places = {}
        for step, sent, part in zip(self.steps, payloads, arrived):
            row = 0
            for one, way in self.taking(step):
                places.setdefault(id(one), []).append(((sent, row), (part, row)))
                row += one.leaving(way, 1)[0].size()
        for one, way in self.members:
            mine = places.get(id(one), [])
            one.keep(way, mine[0][0] if mine else None, [part for _, part in mine])
        return arrived


def run(place, stage, ties=(), in_turn=False, late_ties=()):
    made = list(combine(place, stage.groups(), ties))
    if late_ties:
        made = list(tied(made, late_ties))
    return made, stage.go(made, in_turn)


def neighbour_rows(top, bottom):
    count = lax.axis_size("ha")
    up = [(i, i + 1) for i in range(count - 1)]
    down = [(i + 1, i) for i in range(count - 1)]
    return lax.ppermute(bottom, "ha", up), lax.ppermute(top, "ha", down)


def lay_beside(value, ref):
    tall, width = ref.shape
    for k in range(lane_blocks(width)):
        columns = slice(k * LANES, min(width, (k + 1) * LANES))
        ref[:, columns] = value[k * tall : (k + 1) * tall, : columns.stop - columns.start]


def lay_large(ha, ba, values, outs):
    up_first, up_second, down_first, down_second, out = values
    lay_beside(jnp.concatenate([up_first, up_second], axis=0), outs[0])
    lay_beside(jnp.concatenate([down_first, down_second], axis=0), outs[1])
    lay_beside(out, outs[2])


def lay_small(ha, ba, values, outs, blocks):
    din_ref, dk_ref, gain_ref = outs[:3]
    scratch = outs[-1]
    lay_beside(values[0], din_ref)
    own, other = values[1], values[2]
    small_rows = blocks // 2 * (-(-(TAPS + gain_ref.shape[1] // LANES) // 8) * 8)
    mine = ha % 2 == 0
    first, second = jnp.where(mine, own, other), jnp.where(mine, other, own)
    dkern = jnp.concatenate([first[:small_rows], second[:small_rows]], axis=0)
    tall = dkern.shape[0] // blocks
    joined = jnp.concatenate([dkern[k * tall : k * tall + TAPS] for k in range(blocks)], axis=1)
    dk_ref[...] = joined[:, joined.shape[1] - dk_ref.shape[1] :]
    half = own.shape[0] - small_rows
    count = lax.axis_size("ba")
    part = half // count
    for core, rows in ((0, first), (1, second)):
        for step in range(count):
            start = core * half + (ba ^ step) * part
            source = small_rows + step * part
            scratch[pl.ds(pl.multiple_of(start, 8), part), :] = rows[source : source + part]
    dim = gain_ref.shape[1]
    for k in range(dim // LANES):
        columns = slice(k * LANES, (k + 1) * LANES)
        row = (blocks - 1) * tall + TAPS + k
        gain_ref[:, columns] = dkern[row : row + 1]
        for vector, ref in enumerate(outs[3:6]):
            ref[:, columns] = scratch[vector * dim // LANES + k : vector * dim // LANES + k + 1, :]
    row = scratch.shape[0]
    for ref in reversed(outs[6:-1]):
        tall, width = ref.shape
        row -= tall * width // LANES
        for k in range(width // LANES):
            ref[:, k * LANES : (k + 1) * LANES] = scratch[row + k * tall : row + (k + 1) * tall, :]


def shards(
    canvas,
    image_id,
    keep_first,
    keep_second,
    first_gain,
    weight_in,
    depth_kernel,
    gate_first,
    gate_second,
    gate_third,
    weight_out,
    scale_first,
    second_gain,
    weight_up,
    weight_down,
    scale_second,
    cotangent,
):
    _, rows, cols, dim = canvas.shape
    cells = rows * cols
    reach = REACH * cols
    count_ha, count_ba = lax.axis_size("ha"), lax.axis_size("ba")
    hidden = weight_up.shape[1]
    blocks = weight_in.shape[1] // LANES
    place = jnp.stack([lax.axis_index("ha"), lax.axis_index("ba")])
    own = canvas.reshape(cells, dim)
    gates = (gate_first, gate_second, gate_third)
    gain = first_gain[None]
    vectors = (gain, scale_first[None], second_gain[None], scale_second[None])
    ids = image_id[0]
    above, below = neighbour_rows(own[:reach], own[cells - reach :])
    (
        joined, output, dmiddle, dconv, dconv_top, dconv_bottom, plane_kept, plane_sent, line_kept, line_sent,
        packed_kept, packed_sent,
    ) = forward(
        place, ids, keep_first, keep_second, above, own, below, cotangent.reshape(cells, dim), vectors,
        weight_in, depth_kernel, gates, weight_out, weight_up, weight_down, rows, cols, count_ha, count_ba,
    )
    above, below = neighbour_rows(dconv_top, dconv_bottom)

    plane_sum = Sum([plane_kept, exchange(plane_sent, "ha", 1)], ["plane", "far", "near"])
    line_sum = Sum([line_kept, exchange(line_sent, "ha", 1)], ["far", "near", "plane"])
    packed = Sum([packed_kept, exchange(packed_sent, "ha", 1)], ["plane"])
    made, arrived = run(place, Stage([(plane_sum, "plane"), (packed, "plane")], "plane"))
    more, far = run(place, Stage([(line_sum, "far")], "far"), ties=made, late_ties=[above, below])
    made, arrived = made + more, arrived + far
    dcanvas, in_kept, in_sent, small_kept, small_sent = backward(
        place, ids, above, dconv, below, joined, depth_kernel, own, gain, dmiddle, weight_in, made,
        rows, cols, count_ha, count_ba,
    )
    in_sent, small_sent = tied([in_sent, small_sent], arrived)
    in_sum = Sum([in_kept, exchange(in_sent, "ha", 1)], ["plane", "far", "near"])
    small = Rider([flat_view(small_kept), flat_view(exchange(small_sent, "ha", 1))])
    packed = Rider(packed.views)
    packed = Rider(packed.views)
    made, arrived = run(
        place, Stage([(plane_sum, "far"), (line_sum, "near"), (packed, "line")], "near last"), in_turn=True
    )
    run(place, Stage([(in_sum, "plane"), (small, "plane")], "plane"), ties=made)
    made, _ = run(
        place, Stage([(plane_sum, "near"), (in_sum, "line"), (small, "line")], "line"), ties=arrived, in_turn=True
    )
    packed = Gather(packed.views)
    run(place, Stage([(line_sum, "plane"), (packed, "plane")], "plane"), ties=made)
    cut = plane_sum.views[0].rows // 2
    rest = (line_sum.views[0].rows - dim // count_ha * lane_blocks(dim // count_ba)) // 2
    dup, ddown, dout = combine(
        place,
        [
            [
                plane_sum.part(0, cut),
                line_sum.part(0, rest),
                plane_sum.part(cut, cut),
                line_sum.part(rest, rest),
                line_sum.part(2 * rest, line_sum.views[0].rows - 2 * rest),
            ]
        ],
        epilogue=lay_large,
        out_shape=[
            shape_of(dim // count_ba, hidden // count_ha),
            shape_of(dim // count_ha, hidden // count_ba),
            shape_of(dim // count_ha, dim // count_ba),
        ],
    )
    (halves_of,) = combine(place, [[small.views] + packed.gathered], ties=[dup])
    din, dkern, dgain_one, dscale_one, dgain_two, dscale_two, dfirst, dsecond, dthird, _ = combine(
        place,
        [[in_sum.views, [flat_view(halves_of)], [flat_view(exchange(halves_of, "ha", 1))]]],
        epilogue=functools.partial(lay_small, blocks=blocks),
        out_shape=[shape_of(dim // count_ba, weight_in.shape[1] // count_ha), shape_of(*depth_kernel.shape)]
        + [shape_of(1, dim)] * 4
        + [shape_of(*gate.shape) for gate in gates]
        + [shape_of(packed_rows(gates, dim, count_ba), LANES)],
    )
    return (
        output.reshape(canvas.shape),
        dcanvas.reshape(canvas.shape),
        dgain_one[0],
        din,
        dkern,
        dfirst,
        dsecond,
        dthird,
        dout.T,
        dscale_one[0],
        dgain_two[0],
        dup,
        ddown.T,
        dscale_two[0],
    )


def solution(mesh):
    in_specs = (
        P("ba", "ha", None, None),
        P("ba", None, None),
        P("ba", None),
        P("ba", None),
    ) + (P(),) * 12 + (P("ba", "ha", None, None),)
    tiled = P("ba", "ha")
    out_specs = (
        P("ba", "ha", None, None),
        P("ba", "ha", None, None),
        P(),
        tiled,
        P(),
        P(),
        P(),
        P(),
        tiled,
        P(),
        P(),
        tiled,
        tiled,
        P(),
    )
    return jax.shard_map(shards, mesh=mesh, in_specs=in_specs, out_specs=out_specs, check_vma=False)
```

```python
import functools

import jax
import jax.numpy as jnp
from jax import lax
from jax.experimental import pallas as pl
from jax.experimental.pallas import tpu as pltpu
from jax.sharding import PartitionSpec as P

KERN = 7
TAPS = KERN * KERN
REACH = KERN // 2
KEEP_RATE = 0.8
SPREAD = 1.0 / 3.0
EPSILON = 1e-06
LANES = 128
EDGE = 8
VMEM_BYTES = 64 << 20
F32 = jnp.float32
INV_SQRT_2 = 0.7071067811865476
INV_SQRT_2PI = 0.3989422804014327
NN = (((1,), (0,)), ((), ()))
NT = (((1,), (1,)), ((), ()))
TN = (((0,), (0,)), ((), ()))


def dot(left, right, dims=NN):
    return lax.dot_general(left, right, dims, precision=lax.Precision.HIGH, preferred_element_type=F32)


def normalized(values):
    centered = values - jnp.mean(values, axis=-1, keepdims=True)
    scale = lax.rsqrt(jnp.mean(centered * centered, axis=-1, keepdims=True) + EPSILON)
    return centered * scale, scale


def norm_backward(grad_hat, hat, scale):
    return scale * (
        grad_hat
        - jnp.mean(grad_hat, axis=-1, keepdims=True)
        - hat * jnp.mean(grad_hat * hat, axis=-1, keepdims=True)
    )


def params():
    return pltpu.CompilerParams(vmem_limit_bytes=VMEM_BYTES)


def lasting(microseconds):
    return pl.CostEstimate(flops=int(microseconds * 1.1e9), bytes_accessed=0, transcendentals=0)


def whole(shape):
    return pl.BlockSpec(tuple(shape), lambda *_: (0,) * len(shape), pipeline_mode=pl.Buffered(1))


def in_smem():
    return pl.BlockSpec(memory_space=pltpu.SMEM)


def in_hbm():
    return pl.BlockSpec(memory_space=pltpu.HBM)


def shape_of(*shape):
    return jax.ShapeDtypeStruct(shape, F32)


def lane_blocks(width):
    return -(-width // LANES)


def image_ids(ids_ref, padded, place, rows):
    height, cols = ids_ref.shape
    padded[...] = jnp.full(padded.shape, -1, jnp.int32)
    padded[EDGE : EDGE + height, :] = ids_ref[...]
    ids = padded[pl.ds(place * rows + (EDGE - REACH), rows + 2 * REACH), :]
    return jnp.concatenate([ids, jnp.full((-ids.shape[0] % 8, cols), -1, jnp.int32)], axis=0).T


def spread_cells(factors, out_ref, first, rows):
    cols = factors.shape[0]
    for r in range(rows):
        column = factors[:, first + r : first + r + 1]
        out_ref[r * cols : (r + 1) * cols, :] = jnp.broadcast_to(column, (cols, LANES))


def keep_factors(turned, table_ref):
    result = jnp.zeros(turned.shape, F32)
    for slot in range(table_ref.shape[1]):
        result = jnp.where(turned == slot, table_ref[0, slot].astype(F32) / KEEP_RATE, result)
    return result


def conv_masks(ids_scalar, ids_ref, place, row_taps, col_mask, rows):
    height, cols = ids_ref.shape
    column_masks(ids_ref, col_mask)
    row_masks(ids_scalar, place, row_taps, rows, height, cols)


def column_masks(ids_ref, col_mask):
    height, cols = ids_ref.shape
    wide_ids = jnp.broadcast_to(ids_ref[...].T[:, height // 2 : height // 2 + 1], (cols, LANES))
    column = lax.broadcasted_iota(jnp.int32, (cols, LANES), 0)
    for b in range(KERN):
        shift = b - REACH
        moved = pltpu.roll(wide_ids, (-shift) % cols, 0)
        inside = (column + shift >= 0) & (column + shift < cols)
        same = (moved == wide_ids) & inside
        col_mask[b] = same.astype(F32).reshape(cols // 8, 8, LANES)


def row_masks(ids_scalar, place, row_taps, rows, height, cols):
    def one(r, _):
        own = ids_scalar[place * rows + r, cols // 2]
        row_taps[r, 0] = KERN
        row_taps[r, KERN + 1] = KERN
        for a in range(KERN):
            other = place * rows + r + a - REACH
            inside = (other >= 0) & (other < height)
            same = ids_scalar[jnp.clip(other, 0, height - 1), cols // 2] == own
            row_taps[r, a + 1] = jnp.where(inside & same, a, KERN)
        return 0

    lax.fori_loop(0, rows, one, 0)


def lay_kernel(kern_ref, laid, split):
    tap = lax.broadcasted_iota(jnp.int32, (TAPS, split), 0)
    own = jnp.where(tap == TAPS // 2, 1.0 / SPREAD, 0.0).astype(F32)
    for k in range(laid.shape[0]):
        start = k * LANES - split
        left = own if k == 0 else kern_ref[:, start : start + split]
        laid[k] = jnp.concatenate([left, kern_ref[:, start + split : start + LANES]], axis=1) * SPREAD


def fill_shifted(flat, col_ref, shifted, rows_ext, cols):
    for b in range(KERN):
        for g in range(cols // 8):
            mask = None if b == REACH else col_ref[b, g]
            for r in range(rows_ext):
                x = flat[pl.ds(EDGE + r * cols + 8 * g + b - REACH, 8), :]
                shifted[b, r, g] = x if b == REACH else x * mask


def spread_taps(kern, wide, turned):
    for t in range(TAPS):
        source = TAPS - 1 - t if turned else t
        wide[t] = jnp.broadcast_to(kern[source : source + 1, :], (8, LANES))
    for t in range(KERN):
        wide[TAPS + t] = jnp.zeros((8, LANES), F32)


def conv_block(row_taps, kern, shifted, wide, out_ref, rows, cols):
    groups = cols // 8
    spread_taps(kern, wide, False)

    def pair(h, _):
        r = 2 * h

        def step(i, totals):
            first, second = totals
            taps_first = row_taps[r, i + 1] * KERN
            taps_second = row_taps[r + 1, i] * KERN
            for b in range(KERN):
                x = shifted[b, r + i]
                first = first + wide[taps_first + b][None] * x
                second = second + wide[taps_second + b][None] * x
            return first, second

        zero = jnp.zeros((groups, 8, LANES), F32)
        first, second = lax.fori_loop(0, KERN + 1, step, (zero, zero), unroll=4)
        out_ref[pl.ds(pl.multiple_of(r * cols, cols), cols), :] = first.reshape(cols, LANES)
        out_ref[pl.ds(pl.multiple_of((r + 1) * cols, cols), cols), :] = second.reshape(cols, LANES)
        return 0

    lax.fori_loop(0, rows // 2, pair, 0)


def conv_grad_block(row_taps, kern, shifted, wide, dk, mix_ref, out_ref, dk_ref, rows, cols):
    groups = cols // 8
    spread_taps(kern, wide, True)
    for t in range(TAPS):
        dk[t] = jnp.zeros((8, LANES), F32)

    def one(r, _):
        start = pl.ds(pl.multiple_of(r * cols, cols), cols)
        mix = mix_ref[start, :].reshape(groups, 8, LANES)
        total = jnp.zeros((groups, 8, LANES), F32)
        for i in range(KERN):
            row = row_taps[r, i + 1]
            same = jnp.where(row < KERN, 1.0, 0.0).astype(F32)
            for b in range(KERN):
                x = shifted[b, r + i]
                total = total + wide[row * KERN + b][None] * x
                dk[i * KERN + b] += jnp.sum(mix * x, axis=0) * same
        out_ref[start, :] = total.reshape(cols, LANES)
        return 0

    lax.fori_loop(0, rows, one, 0)
    for t in range(TAPS):
        dk_ref[TAPS - 1 - t : TAPS - t, :] = jnp.sum(dk[t], axis=0, keepdims=True) * SPREAD
    dk_ref[TAPS:, :] = jnp.zeros((dk_ref.shape[0] - TAPS, LANES), F32)


def share(core, first, second, kept_ref, sent_ref, z, p):
    mine = core == 0
    tall, width = first.shape
    for ref, chunk in (
        (kept_ref, jnp.where(mine, first, second)),
        (sent_ref, jnp.where(mine, second, first)),
    ):
        for k in range(lane_blocks(width)):
            part = chunk[:, k * LANES : (k + 1) * LANES]
            if part.shape[1] < LANES:
                part = jnp.concatenate([part, jnp.zeros((tall, LANES - part.shape[1]), F32)], axis=1)
            ref[z, p, k * tall : (k + 1) * tall, :] = part


def share_columns(core, grad, kept_ref, sent_ref, width, plane_first=False):
    groups, parts = reversed(kept_ref.shape[:2]) if plane_first else kept_ref.shape[:2]
    tall = grad.shape[0] // parts
    for z in range(groups):
        for p in range(parts):
            rows = slice(p * tall, (p + 1) * tall)
            first = grad[rows, 2 * z * width : (2 * z + 1) * width]
            second = grad[rows, (2 * z + 1) * width : (2 * z + 2) * width]
            share(core, first, second, kept_ref, sent_ref, *((p, z) if plane_first else (z, p)))


def share_rows(core, grad, kept_ref, sent_ref, tall):
    groups, parts = kept_ref.shape[:2]
    width = grad.shape[1] // parts
    for z in range(groups):
        for p in range(parts):
            columns = slice(p * width, (p + 1) * width)
            first = grad[2 * z * tall : (2 * z + 1) * tall, columns]
            second = grad[(2 * z + 1) * tall : (2 * z + 2) * tall, columns]
            share(core, first, second, kept_ref, sent_ref, z, p)


class Copies:
    def __init__(self, sems):
        self.sems, self.count, self.pending = sems, 0, {}

    def start(self, name, source, target):
        copy = pltpu.make_async_copy(source, target, self.sems.at[self.count])
        self.count += 1
        copy.start()
        self.pending.setdefault(name, []).append(copy)

    def wait(self, *names):
        for name in names:
            for copy in self.pending.pop(name):
                copy.wait()

    def wait_all(self):
        self.wait(*list(self.pending))


def head_kernel(
    place_ref, ids_scalar, one_table, two_table, ids_hbm, own_hbm, gain_hbm, in_hbm_ref,
    joined_hbm, valid_hbm, one_keep_hbm, two_keep_hbm, col_hbm,
    ids_ref, rows_ref, gain_ref, in_ref, padded, valid_ref, one_keep_ref, two_keep_ref, col_ref, normed, joined, sems,
    *, rows, cols,
):
    cells = rows * cols
    reach = REACH * cols
    steps = in_ref.shape[0]
    copies = Copies(sems)
    copies.start("ids", ids_hbm, ids_ref)
    copies.start("own", own_hbm, rows_ref)
    copies.start("own", gain_hbm, gain_ref)
    for k in range(steps):
        copies.start(("in", k), in_hbm_ref.at[:, pl.ds(2 * LANES * k, 2 * LANES)], in_ref.at[k])
    copies.wait("ids")
    turned = image_ids(ids_ref, padded, place_ref[0], rows)
    spread_cells((turned >= 0).astype(F32), valid_ref, 0, rows + 2 * REACH)
    spread_cells(keep_factors(turned, one_table), one_keep_ref, REACH, rows)
    spread_cells(keep_factors(turned, two_table), two_keep_ref, REACH, rows)
    column_masks(ids_ref, col_ref)
    for source, target in (
        (valid_ref, valid_hbm), (one_keep_ref, one_keep_hbm), (two_keep_ref, two_keep_hbm), (col_ref, col_hbm)
    ):
        copies.start("outs", source, target)
    copies.wait("own")
    hat, _ = normalized(rows_ref[...] * valid_ref[reach : reach + cells, :1])
    normed[...] = hat * gain_ref[...]
    for step in range(steps):
        copies.wait(("in", step))
        part = dot(normed[...], in_ref[step])
        for k in range(2):
            joined[2 * step + k] = part[:, k * LANES : (k + 1) * LANES]
        pair = pl.ds(2 * step, 2)
        copies.start("outs", joined.at[pair], joined_hbm.at[pair])
    copies.wait_all()


def head(place, ids, keep_one, keep_two, own, gain, weight_in, rows, cols):
    cells, dim = own.shape
    cells_ext = cells + 2 * REACH * cols
    blocks = weight_in.shape[1] // LANES
    vmem = functools.partial(pltpu.VMEM, dtype=F32)
    shapes = [
        (blocks, cells, LANES), (cells_ext, LANES), (cells, LANES), (cells, LANES), (KERN, cols // 8, 8, LANES)
    ]
    return pl.pallas_call(
        functools.partial(head_kernel, rows=rows, cols=cols),
        in_specs=[in_smem()] * 4 + [in_hbm()] * 4,
        out_specs=[in_hbm()] * len(shapes),
        out_shape=[shape_of(*shape) for shape in shapes],
        scratch_shapes=[
            pltpu.VMEM(ids.shape, jnp.int32),
            vmem((cells, dim)),
            vmem((1, dim)),
            vmem((blocks // 2, dim, 2 * LANES)),
            pltpu.VMEM((ids.shape[0] + 2 * EDGE, ids.shape[1]), jnp.int32),
        ]
        + [vmem(shape) for shape in shapes[1:]]
        + [vmem((cells, dim)), vmem(shapes[0]), pltpu.SemaphoreType.DMA((7 + blocks,))],
        compiler_params=params(),
        cost_estimate=lasting(7),
    )(place, ids, keep_one, keep_two, ids, own, gain, weight_in)


def forward_kernel(
    place_ref, ids_scalar, joined_hbm, valid_hbm, one_keep_hbm, two_keep_hbm, col_hbm, above_hbm, own_hbm, below_hbm, cot_hbm,
    first_gain_hbm, first_scale_hbm, second_gain_hbm, second_scale_hbm,
    in_hbm_ref, kern_hbm, one_hbm, two_hbm, three_hbm, out_hbm, up_hbm, down_hbm,
    output_hbm, dmiddle_hbm, dconv_hbm, dconv_top_hbm, dconv_bottom_hbm,
    plane_kept_ref, plane_sent_ref, line_kept_ref, line_sent_ref, packed_kept_hbm, packed_sent_hbm,
    rows_ref, cot_ref, first_gain_ref, first_scale_ref, second_gain_ref, second_scale_ref,
    in_ref, kern_ref, one_ref, two_ref, three_ref, out_ref, up_ref, down_ref, dconv_ref, sems, chunk_sems,
    up_kept, up_sent, down_kept, down_sent, out_kept, out_sent,
    row_taps, valid_ref, one_keep_ref, two_keep_ref, col_ref, packed_ref, normed, flat, shifted, laid, wide, conv,
    mixed_ref, mapped_ref, middle_ref, result, dnorm,
    *, rows, cols, count_ha, count_ba,
):
    blocks = flat.shape[0]
    cells = rows * cols
    reach = REACH * cols
    cells_ext = cells + 2 * reach
    core = place_ref[0] % 2
    split = one_ref.shape[0]
    dim = rows_ref.shape[1]
    head_steps = blocks // 2
    ffn_steps = up_kept.shape[0]
    chunk = down_ref.shape[1]
    gate_refs = (one_ref, two_ref, three_ref)

    copies = Copies(sems)
    copies.start("rows", valid_hbm, valid_ref)
    copies.start("rows", first_gain_hbm, first_gain_ref)
    copies.start("above", above_hbm, rows_ref.at[pl.ds(0, reach)])
    copies.start("below", below_hbm, rows_ref.at[pl.ds(reach + cells, reach)])
    for k in range(head_steps):
        copies.start(("in", k), in_hbm_ref.at[:, pl.ds(2 * LANES * k, 2 * LANES)], in_ref.at[k])
    copies.start("conv", joined_hbm, flat.at[:, pl.ds(EDGE + reach, cells), :])
    copies.start("conv", col_hbm, col_ref)
    copies.start("gates", own_hbm, rows_ref.at[pl.ds(reach, cells)])
    copies.start("gates", one_keep_hbm, one_keep_ref)
    copies.start("gates", two_keep_hbm, two_keep_ref)
    copies.start("kern", kern_hbm, kern_ref)
    def weights(k):
        ends = pl.ds(pl.multiple_of(k * chunk, chunk), chunk)
        return [
            pltpu.make_async_copy(up_hbm.at[:, ends], up_ref.at[k], chunk_sems.at[k, 0]),
            pltpu.make_async_copy(down_hbm.at[ends, :], down_ref.at[k], chunk_sems.at[k, 1]),
        ]

    def chunk_copies(place):
        moves = []
        sides = ((up_kept, down_kept, plane_kept_ref, line_kept_ref), (up_sent, down_sent, plane_sent_ref, line_sent_ref))
        for up, down, plane, line in sides:
            cut = plane.shape[2] // 2
            rest = up.shape[3] - cut
            zs = pl.ds(place * up.shape[1], up.shape[1])
            bas = pl.ds(place * down.shape[2], down.shape[2])
            moves += [
                (up.at[place, :, ba, pl.ds(0, cut), :], plane.at[ba, zs, pl.ds(0, cut), :])
                for ba in range(plane.shape[0])
            ]
            moves += [
                (down.at[place, z, :, pl.ds(0, cut), :], plane.at[bas, z, pl.ds(cut, cut), :])
                for z in range(plane.shape[1])
            ]
            moves.append((up.at[place, :, :, pl.ds(cut, rest), :], line.at[zs, :, pl.ds(0, rest), :]))
            moves.append((down.at[place, :, :, pl.ds(cut, rest), :], line.at[:, bas, pl.ds(rest, rest), :]))
        return [
            pltpu.make_async_copy(source, target, chunk_sems.at[place, 2 + k])
            for k, (source, target) in enumerate(moves)
        ]

    row_masks(ids_scalar, place_ref[0], row_taps, rows, ids_scalar.shape[0], cols)
    copies.wait("rows")
    for name, start, place in (("above", 0, 0), ("below", reach + cells, reach)):
        copies.wait(name)
        hat, _ = normalized(rows_ref[start : start + reach, :] * valid_ref[start : start + reach, :1])
        normed[place : place + reach] = hat * first_gain_ref[...]

    for k in range(blocks):
        flat[k, :EDGE] = jnp.zeros((EDGE, LANES), F32)
        flat[k, EDGE + cells_ext :] = jnp.zeros((EDGE, LANES), F32)
    for step in range(head_steps):
        copies.wait(("in", step))
        joined = dot(normed[: 2 * reach], in_ref[step])
        for k in range(2):
            part = joined[:, k * LANES : (k + 1) * LANES]
            flat[2 * step + k, EDGE : EDGE + reach] = part[:reach]
            flat[2 * step + k, EDGE + reach + cells : EDGE + cells_ext] = part[reach:]
        if step == 0:
            copies.start("gates", first_scale_hbm, first_scale_ref)
            copies.start("gates", second_gain_hbm, second_gain_ref)
            copies.start("gates", second_scale_hbm, second_scale_ref)
            for source, target in zip((one_hbm, two_hbm, three_hbm, out_hbm, cot_hbm), gate_refs + (out_ref, cot_ref)):
                copies.start("gates", source, target)
            for k in range(ffn_steps):
                for copy in weights(k):
                    copy.start()

    copies.wait("conv")
    copies.wait("kern")
    lay_kernel(kern_ref, laid, split)

    def conv_step(block, _):
        fill_shifted(flat.at[block], col_ref, shifted, rows + 2 * REACH, cols)
        conv_block(row_taps, laid[block], shifted, wide, conv.at[block], rows, cols)
        return 0

    lax.fori_loop(0, blocks, conv_step, 0)

    def conv_part(start, width):
        return jnp.concatenate([conv[start // LANES + k] for k in range(width // LANES)], axis=1)

    copies.wait("gates")
    mixed = conv[0, :, :split] * conv[0, :, split:]
    mixed_ref[:, :split] = mixed
    start = 2 * split
    for ref in gate_refs:
        width = ref.shape[1]
        mapped = dot(mixed, ref[...])
        mapped_ref[:, start - 2 * split : start - 2 * split + width] = mapped
        mixed = mapped * conv_part(start, width)
        mixed_ref[:, start : start + width] = mixed
        start += width
    branch = dot(mixed, out_ref[...])
    masked = rows_ref[reach : reach + cells, :] * valid_ref[reach : reach + cells, :1]
    middle = masked + one_keep_ref[:, :1] * first_scale_ref[...] * branch
    middle_ref[...] = middle
    hat, _ = normalized(middle)
    normed[:cells] = hat * second_gain_ref[...]
    result[...] = jnp.zeros_like(result)
    dnorm[...] = jnp.zeros_like(dnorm)

    def ffn_step(place, _):
        for copy in weights(place):
            copy.wait()
        grad_result = two_keep_ref[:, :1] * second_scale_ref[...] * cot_ref[...]
        pre = dot(normed[:cells], up_ref[place])
        cdf = 0.5 + 0.5 * lax.erf(pre * INV_SQRT_2)
        slope = cdf + pre * (INV_SQRT_2PI * jnp.exp(-0.5 * pre * pre))
        hidden = pre * cdf
        result[...] += dot(hidden, down_ref[place])
        grad_pre = dot(grad_result, down_ref[place], NT) * slope
        share_rows(
            core, dot(grad_result, hidden, TN), down_kept.at[place], down_sent.at[place], dim // count_ha
        )
        width = chunk // (2 * up_kept.shape[1])
        share_columns(core, dot(normed[:cells], grad_pre, TN), up_kept.at[place], up_sent.at[place], width)
        for copy in chunk_copies(place):
            copy.start()
        dnorm[...] += dot(grad_pre, up_ref[place], NT)
        return 0

    lax.fori_loop(0, ffn_steps, ffn_step, 0)

    hat, scale = normalized(middle_ref[...])
    kept = two_keep_ref[:, :1] * result[...]
    dscale_two = jnp.sum(cot_ref[...] * kept, axis=0, keepdims=True)
    result[...] = middle_ref[...] + second_scale_ref[...] * kept
    copies.start("outs", result, output_hbm)
    dgain_two = jnp.sum(dnorm[...] * hat, axis=0, keepdims=True)
    dmiddle = cot_ref[...] + norm_backward(dnorm[...] * second_gain_ref[...], hat, scale)
    dnorm[...] = dmiddle
    copies.start("outs", dnorm, dmiddle_hbm)
    kept = one_keep_ref[:, :1] * dmiddle
    grad = dot(kept * first_scale_ref[...], out_ref[...], NT)
    row = packed_ref.shape[0]
    start = blocks * LANES
    for ref in reversed(gate_refs):
        tall, width = ref.shape
        start -= width
        source = start - tall if tall > split else 0
        columns = slice(start - 2 * split, start - 2 * split + width)
        dconv = grad * mapped_ref[:, columns]
        for k in range(width // LANES):
            dconv_ref[start // LANES + k] = dconv[:, k * LANES : (k + 1) * LANES]
        grad_mapped = grad * conv_part(start, width)
        part = dot(mixed_ref[:, source : source + tall], grad_mapped, TN)
        row -= tall * width // LANES
        for k in range(width // LANES):
            packed_ref[row + k * tall : row + (k + 1) * tall] = part[:, k * LANES : (k + 1) * LANES]
        grad = dot(grad_mapped, ref[...], NT)
    dconv_ref[0] = jnp.concatenate([grad * conv[0, :, split:], grad * conv[0, :, :split]], axis=1)
    copies.start("outs", dconv_ref.at[:, pl.ds(0, reach), :], dconv_top_hbm)
    copies.start("outs", dconv_ref.at[:, pl.ds(cells - reach, reach), :], dconv_bottom_hbm)
    copies.start("outs", dconv_ref, dconv_hbm)
    start = mixed_ref.shape[1] - out_ref.shape[0]
    crossed = dot(mixed_ref[:, start:], kept, TN)
    dscale_one = jnp.sum(crossed * out_ref[...], axis=0, keepdims=True)
    packed_ref[:row] = jnp.zeros((row, LANES), F32)
    row = 0
    for vector in (dscale_one, dgain_two, dscale_two):
        for k in range(dim // LANES):
            packed_ref[row : row + 1] = vector[:, k * LANES : (k + 1) * LANES]
            row += 1
    half = packed_kept_hbm.shape[0]
    for place, target in ((core, packed_kept_hbm), (1 - core, packed_sent_hbm)):
        copies.start("outs", packed_ref.at[pl.ds(pl.multiple_of(place * half, 8), half), :], target)
    share_rows(core, (crossed * first_scale_ref[...]).T, out_kept, out_sent, dim // count_ha)
    for source, line in ((out_kept, line_kept_ref), (out_sent, line_sent_ref)):
        tall = source.shape[2]
        copies.start("outs", source, line.at[:, :, pl.ds(line.shape[2] - tall, tall), :])
    for place in range(ffn_steps):
        for copy in chunk_copies(place):
            copy.wait()
    copies.wait_all()


def mask_scratch(ids, rows):
    height, cols = ids.shape
    return [
        pltpu.SMEM((rows, KERN + 2), jnp.int32),
        pltpu.VMEM((height + 2 * EDGE, cols), jnp.int32),
        pltpu.VMEM(((rows + 2 * REACH) * cols, LANES), F32),
    ]


def packed_rows(gates, dim, parts):
    rows = sum(gate.size for gate in gates) // LANES + 3 * dim // LANES
    return -(-rows // (16 * parts)) * 16 * parts


def plane_share(rows):
    return max(rows * 3 // 4 // 8 * 8, 8)


def forward(
    place, ids, ahead, above, own, below, cot, vectors, weight_in, kern, gates,
    weight_out, weight_up, weight_down, rows, cols, count_ha, count_ba, chunk=512,
):
    cells, dim = own.shape
    reach = above.shape[0]
    blocks = weight_in.shape[1] // LANES
    hidden = weight_up.shape[1]
    split = gates[0].shape[0]
    wide = blocks * LANES
    head_steps = blocks // 2
    ffn_steps = hidden // chunk

    up_wide, down_wide = hidden // count_ha, hidden // count_ba
    up_rows = dim // count_ba * lane_blocks(up_wide)
    down_rows = dim // count_ha * lane_blocks(down_wide)
    out_rows = dim // count_ha * lane_blocks(dim // count_ba)
    half = count_ha // 2
    assert up_rows == down_rows
    cut = plane_share(up_rows)
    rest = up_rows - cut
    plane = (count_ba, half, 2 * cut, LANES)
    line = (half, count_ba, 2 * rest + out_rows, LANES)
    packed_shape = (packed_rows(gates, dim, count_ba), LANES)
    half_packed = (packed_shape[0] // 2, LANES)
    cells_ext = cells + 2 * reach
    vmem = functools.partial(pltpu.VMEM, dtype=F32)
    operands = (
        place, ids, *ahead, above, own, below, cot, *vectors,
        weight_in, kern, *gates, weight_out, weight_up, weight_down,
    )
    out_shape = [
        shape_of(cells, dim),
        shape_of(cells, dim),
        shape_of(blocks, cells, LANES),
        shape_of(blocks, reach, LANES),
        shape_of(blocks, reach, LANES),
        shape_of(*plane),
        shape_of(*plane),
        shape_of(*line),
        shape_of(*line),
        shape_of(*half_packed),
        shape_of(*half_packed),
    ]
    return pl.pallas_call(
        functools.partial(forward_kernel, rows=rows, cols=cols, count_ha=count_ha, count_ba=count_ba),
        in_specs=[in_smem()] * 2 + [in_hbm()] * (len(operands) - 2),
        out_specs=[in_hbm()] * len(out_shape),
        out_shape=out_shape,
        scratch_shapes=[vmem((cells_ext, dim)), vmem((cells, dim))]
        + [vmem((1, dim))] * 4
        + [vmem((head_steps, dim, 2 * LANES)), vmem(kern.shape)]
        + [vmem(gate.shape) for gate in gates]
        + [
            vmem(weight_out.shape),
            vmem((ffn_steps, dim, chunk)),
            vmem((ffn_steps, chunk, dim)),
            vmem((blocks, cells, LANES)),
            pltpu.SemaphoreType.DMA((40 + head_steps,)),
            pltpu.SemaphoreType.DMA((ffn_steps, 2 + 2 * (count_ba + half + 2))),
        ]
        + [vmem((ffn_steps, chunk // (2 * up_wide), count_ba, up_rows, LANES))] * 2
        + [vmem((ffn_steps, half, chunk // down_wide, down_rows, LANES))] * 2
        + [vmem((half, count_ba, out_rows, LANES))] * 2
        + [
            pltpu.SMEM((rows, KERN + 2), jnp.int32),
            vmem((cells_ext, LANES)),
            vmem((cells, LANES)),
            vmem((cells, LANES)),
            vmem((KERN, cols // 8, 8, LANES)),
            vmem(packed_shape),
            vmem((max(cells, 2 * reach), dim)),
            vmem((blocks, cells_ext + 2 * EDGE, LANES)),
            vmem((KERN, rows + 2 * REACH, cols // 8, 8, LANES)),
            vmem((blocks, TAPS, LANES)),
            vmem((TAPS + KERN, 8, LANES)),
            vmem((blocks, cells, LANES)),
            vmem((cells, wide)),
            vmem((cells, wide - 2 * split)),
            vmem((cells, dim)),
            vmem((cells, dim)),
            vmem((cells, dim)),
        ],
        compiler_params=params(),
        cost_estimate=lasting(48),
    )(*operands)


def lay_flat(above_ref, own_ref, below_ref, flat):
    reach, cells = above_ref.shape[1], own_ref.shape[1]
    flat[:EDGE] = jnp.zeros((EDGE, LANES), F32)
    flat[EDGE : EDGE + reach] = above_ref[0]
    flat[EDGE + reach : EDGE + reach + cells] = own_ref[0]
    flat[EDGE + reach + cells : EDGE + 2 * reach + cells] = below_ref[0]
    flat[EDGE + 2 * reach + cells :] = jnp.zeros((EDGE, LANES), F32)


def backward_kernel(
    place_ref, ids_scalar, ids_ref, above_ref, own_ref, below_ref, mix_ref, kern_ref, canvas_ref, gain_ref,
    dmiddle_ref, in_ref, *rest, rows, cols,
):
    dcanvas_ref, kept_ref, sent_ref, small_kept_ref, small_sent_ref = rest[-19:-14]
    row_taps, padded, valid_ref, col_ref, flat, shifted, laid, wide, dk, sums, small, djoined, normed, dnorm = rest[-14:]
    step = pl.program_id(0)
    cells = rows * cols
    reach = REACH * cols
    core = place_ref[0] % 2
    split = laid.shape[0] * LANES - kern_ref.shape[1]
    width = in_ref.shape[1] // (2 * kept_ref.shape[1])

    @pl.when(step == 0)
    def _():
        lay_kernel(kern_ref, laid, split)
        turned = image_ids(ids_ref, padded, place_ref[0], rows)
        spread_cells((turned >= 0).astype(F32), valid_ref, 0, rows + 2 * REACH)
        conv_masks(ids_scalar, ids_ref, place_ref[0], row_taps, col_ref, rows)
        hat, _ = normalized(canvas_ref[...] * valid_ref[reach : reach + cells, :1])
        normed[...] = hat * gain_ref[...]
        dnorm[...] = jnp.zeros_like(dnorm)

    lay_flat(above_ref, own_ref, below_ref, flat)
    fill_shifted(flat, col_ref, shifted, rows + 2 * REACH, cols)
    conv_grad_block(
        row_taps, laid[step], shifted, wide, dk, mix_ref.at[0], djoined.at[step % 2], sums.at[step], rows, cols
    )

    @pl.when(step % 2 == 1)
    def _():
        grad = jnp.concatenate([djoined[0], djoined[1]], axis=1)
        share_columns(core, dot(normed[...], grad, TN), kept_ref, sent_ref, width, plane_first=True)
        dnorm[...] += dot(grad, in_ref[...], NT)

    @pl.when(step == pl.num_programs(0) - 1)
    def _():
        hat, scale = normalized(canvas_ref[...] * valid_ref[reach : reach + cells, :1])
        dgain = jnp.sum(dnorm[...] * hat, axis=0, keepdims=True)
        row = sums.shape[0] * TAPS
        for k in range(sums.shape[0]):
            small[k * TAPS : (k + 1) * TAPS, :] = sums[k, :TAPS]
        small[row:, :] = jnp.zeros((small.shape[0] - row, LANES), F32)
        for k in range(dgain.shape[1] // LANES):
            small[row + k : row + k + 1, :] = dgain[:, k * LANES : (k + 1) * LANES]
        half = small.shape[0] // 2
        for ref, start in ((small_kept_ref, core * half), (small_sent_ref, (1 - core) * half)):
            ref[...] = small[pl.ds(pl.multiple_of(start, 8), half), :]
        inner = dmiddle_ref[...] + norm_backward(dnorm[...] * gain_ref[...], hat, scale)
        dcanvas_ref[...] = inner * valid_ref[reach : reach + cells, :1]


def block_of(size):
    return pl.BlockSpec((1, size, LANES), lambda i: (i, 0, 0))


def small_rows(blocks, dim):
    return -(-(blocks * TAPS + dim // LANES) // 16) * 16


def backward(
    place, ids, above, own, below, mix, kern, canvas, gain, dmiddle, weight_in, ties, rows, cols, count_ha, count_ba
):
    cells, dim = canvas.shape
    blocks = own.shape[0]
    reach = above.shape[1]
    own_wide = weight_in.shape[1] // count_ha
    chunk_rows = dim // count_ba * lane_blocks(own_wide)
    groups = 2 * LANES // (2 * own_wide)
    chunk_spec = pl.BlockSpec((count_ba, groups, chunk_rows, LANES), lambda i: (0, i // 2, 0, 0))
    chunks = shape_of(count_ba, count_ha // 2, chunk_rows, LANES)
    tall = -(-TAPS // 8) * 8
    small = (small_rows(blocks, dim) // 2, LANES)
    return pl.pallas_call(
        functools.partial(backward_kernel, rows=rows, cols=cols),
        grid=(blocks,),
        in_specs=[in_smem(), in_smem(), whole(ids.shape)]
        + [block_of(size) for size in (reach, cells, reach, cells)]
        + [whole(kern.shape), whole(canvas.shape)]
        + [whole((1, dim)), whole((cells, dim))]
        + [pl.BlockSpec((dim, 2 * LANES), lambda i: (0, i // 2))]
        + [in_hbm()] * len(ties),
        out_specs=[whole((cells, dim)), chunk_spec, chunk_spec, whole(small), whole(small)],
        out_shape=[shape_of(cells, dim), chunks, chunks, shape_of(*small), shape_of(*small)],
        scratch_shapes=mask_scratch(ids, rows)
        + [
            pltpu.VMEM((KERN, cols // 8, 8, LANES), F32),
            pltpu.VMEM((cells + 2 * reach + 2 * EDGE, LANES), F32),
            pltpu.VMEM((KERN, rows + 2 * REACH, cols // 8, 8, LANES), F32),
            pltpu.VMEM((blocks, TAPS, LANES), F32),
            pltpu.VMEM((TAPS + KERN, 8, LANES), F32),
            pltpu.VMEM((TAPS, 8, LANES), F32),
            pltpu.VMEM((blocks, tall, LANES), F32),
            pltpu.VMEM((small_rows(blocks, dim), LANES), F32),
            pltpu.VMEM((2, cells, LANES), F32),
            pltpu.VMEM((cells, dim), F32),
            pltpu.VMEM((cells, dim), F32),
        ],
        compiler_params=params(),
        cost_estimate=lasting(25),
    )(place, ids, ids, above, own, below, mix, kern, canvas, gain, dmiddle, weight_in, *ties)


def exchange(values, axis, bit):
    return lax.ppermute(values, axis, [(i, i ^ bit) for i in range(lax.axis_size(axis))])


class View:
    def __init__(self, array, start, ways, fixed, rows):
        self.array, self.start, self.ways, self.fixed, self.rows = array, start, ways, fixed, rows

    def fix(self, way, step):
        if way == "line":
            near = lax.axis_size("ha") // 4
            return self.fix("far", step // near).fix("near", step % near)
        left = [entry for entry in self.ways if entry[0] != way]
        (stride,) = [entry[2] for entry in self.ways if entry[0] == way]
        return View(self.array, self.start, left, self.fixed + [(way, step, stride)], self.rows)

    def size(self):
        count = self.rows
        for _, size, _ in self.ways:
            count *= size
        return count

    def runs(self, ha, ba):
        start = self.start
        near = lax.axis_size("ha") // 4
        places = {"plane": ba, "far": ha // 2 // near, "near": ha // 2 % near}
        for way, step, stride in self.fixed:
            start = start + (places[way] ^ step) * stride
        rows, ways = self.rows, list(self.ways)
        while ways and ways[-1][2] == rows:
            rows *= ways.pop()[1]
        offsets = [0]
        for _, size, stride in ways:
            offsets = [offset + k * stride for offset in offsets for k in range(size)]
        return [pl.multiple_of(start + offset, 8) for offset in offsets], rows


def flat_view(array, start=0, rows=None):
    flat = array.reshape(-1, LANES)
    return View(flat, start, [], [], flat.shape[0] if rows is None else rows)


def combine(place, groups, ties=(), epilogue=None, out_shape=None):
    pieces, arrays = [], []
    for group in groups:
        for views in group:
            if not any(views is other for other in pieces):
                pieces.append(views)
    for views in pieces:
        for view in views:
            if not any(view.array is other for other in arrays):
                arrays.append(view.array)
    index_of = {id(array): k for k, array in enumerate(arrays)}
    piece_of = {id(views): k for k, views in enumerate(pieces)}
    sizes = [sum(views[0].size() for views in group) for group in groups]
    copies = sum(len(view.runs(0, 0)[0]) for views in pieces for view in views)
    plain = epilogue is None
    if plain:
        out_shape = [shape_of(size, LANES) for size in sizes]

    def kernel(place_ref, *refs):
        inputs = refs[: len(arrays)]
        refs = refs[len(arrays) + len(ties) :]
        outs, refs = refs[: len(out_shape)], refs[len(out_shape) :]
        buffers, refs = refs[: len(pieces)], refs[len(pieces) :]
        sems, results, out_sems = refs[0], refs[1:-1], refs[-1]
        ha, ba = place_ref[0], place_ref[1]
        moves, count = [], 0
        for piece, views in enumerate(pieces):
            moves.append([])
            for term, view in enumerate(views):
                source = inputs[index_of[id(view.array)]]
                starts, rows = view.runs(ha, ba)
                for k, start in enumerate(starts):
                    target = buffers[piece].at[term, pl.ds(k * rows, rows), :]
                    move = pltpu.make_async_copy(source.at[pl.ds(start, rows), :], target, sems.at[count])
                    move.start()
                    moves[-1].append(move)
                    count += 1
        values, waited, leaving = [], set(), []
        for out, group in enumerate(groups):
            row = 0
            for views in group:
                piece = piece_of[id(views)]
                if piece not in waited:
                    waited.add(piece)
                    for move in moves[piece]:
                        move.wait()
                value = buffers[piece][0]
                for term in range(1, len(views)):
                    value = value + buffers[piece][term]
                if plain:
                    results[out][row : row + value.shape[0], :] = value
                values.append(value)
                row += value.shape[0]
            if plain:
                leaving.append(pltpu.make_async_copy(results[out], outs[out], out_sems.at[out]))
                leaving[-1].start()
        if not plain:
            epilogue(ha, ba, values, outs)
        for move in leaving:
            move.wait()

    moved = sum(view.size() for views in pieces for view in views) + sum(sizes)
    scratch = [pltpu.VMEM((len(views), views[0].size(), LANES), F32) for views in pieces]
    scratch.append(pltpu.SemaphoreType.DMA((copies,)))
    if plain:
        scratch += [pltpu.VMEM((size, LANES), F32) for size in sizes]
    scratch.append(pltpu.SemaphoreType.DMA((len(groups),)))
    return pl.pallas_call(
        kernel,
        in_specs=[in_smem()] + [in_hbm()] * (len(arrays) + len(ties)),
        out_specs=[in_hbm() if plain else pl.BlockSpec(memory_space=pltpu.VMEM)] * len(out_shape),
        out_shape=out_shape,
        scratch_shapes=scratch,
        compiler_params=params(),
        cost_estimate=lasting(1 + moved * LANES * 4 / 3.0e6),
    )(place, *arrays, *ties)


def tied(arrays, ties):
    return pl.pallas_call(
        lambda *refs: None,
        in_specs=[pl.BlockSpec(memory_space=pl.ANY)] * (len(arrays) + len(ties)),
        out_specs=[pl.BlockSpec(memory_space=pl.ANY)] * len(arrays),
        out_shape=[shape_of(*array.shape) for array in arrays],
        input_output_aliases={k: k for k in range(len(arrays))},
        compiler_params=params(),
        cost_estimate=lasting(0.5),
    )(*arrays, *ties)


class Sum:
    def __init__(self, arrays, names):
        self.views = []
        near = lax.axis_size("ha") // 4
        sizes = {"plane": lax.axis_size("ba"), "far": 2, "near": near}
        for array in arrays:
            flat = array.reshape(-1, LANES)
            stride, ways = flat.shape[0], []
            for name in names:
                stride //= sizes[name]
                ways.append((name, sizes[name], stride))
            self.views.append(View(flat, 0, ways, [], stride))

    def leaving(self, way, step):
        return [view.fix(way, step) for view in self.views]

    def keep(self, way, sent, arrived):
        self.views = [view.fix(way, 0) for view in self.views]
        rows = self.views[0].rows
        stride, ways = rows, []
        for name, size, _ in reversed(self.views[0].ways):
            ways.insert(0, (name, size, stride))
            stride *= size
        self.views += [View(array, start, ways, [], rows) for array, start in arrived]

    def part(self, first, rows):
        return [View(view.array, view.start + first, view.ways, view.fixed, rows) for view in self.views]


class Rider:
    def __init__(self, views):
        self.views = views

    def leaving(self, way, step):
        return self.views

    def keep(self, way, sent, arrived):
        rows = self.views[0].size()
        self.views = [View(array, start, [], [], rows) for array, start in [sent] + arrived]


class Gather(Rider):
    def keep(self, way, sent, arrived):
        rows = self.views[0].size()
        self.gathered = [[View(array, start, [], [], rows)] for array, start in [sent] + arrived]


class Stage:
    def __init__(self, members, way):
        self.members, self.way = members, way
        line, near = lax.axis_size("ha") // 2, lax.axis_size("ha") // 4
        self.steps = {
            "plane": list(range(1, lax.axis_size("ba"))),
            "line": list(range(1, line)),
            "near last": list(range(near, line)) + list(range(1, near)),
            "far": [near],
        }[way]
        self.near = near

    def taking(self, step):
        takes = {"plane": True, "line": True, "near": step < self.near, "far": step == self.near}
        return [(one, way) for one, way in self.members if takes[way]]

    def groups(self):
        return [
            [one.leaving(way, step // self.near if way == "far" else step) for one, way in self.taking(step)]
            for step in self.steps
        ]

    def go(self, payloads, in_turn=False):
        axis, unit = ("ba", 1) if self.way == "plane" else ("ha", 2)
        arrived = []
        for step, part in zip(self.steps, payloads):
            if in_turn and len(arrived) == 2:
                (part,) = tied([part], arrived[1:])
            arrived.append(exchange(part, axis, unit * step))
        places = {}
        for step, sent, part in zip(self.steps, payloads, arrived):
            row = 0
            for one, way in self.taking(step):
                places.setdefault(id(one), []).append(((sent, row), (part, row)))
                row += one.leaving(way, 1)[0].size()
        for one, way in self.members:
            mine = places.get(id(one), [])
            one.keep(way, mine[0][0] if mine else None, [part for _, part in mine])
        return arrived


def run(place, stage, ties=(), in_turn=False, late_ties=()):
    made = list(combine(place, stage.groups(), ties))
    if late_ties:
        made = list(tied(made, late_ties))
    return made, stage.go(made, in_turn)


def neighbour_rows(top, bottom):
    count = lax.axis_size("ha")
    up = [(i, i + 1) for i in range(count - 1)]
    down = [(i + 1, i) for i in range(count - 1)]
    return lax.ppermute(bottom, "ha", up), lax.ppermute(top, "ha", down)


def lay_beside(value, ref):
    tall, width = ref.shape
    for k in range(lane_blocks(width)):
        columns = slice(k * LANES, min(width, (k + 1) * LANES))
        ref[:, columns] = value[k * tall : (k + 1) * tall, : columns.stop - columns.start]


def lay_large(ha, ba, values, outs):
    up_first, up_second, down_first, down_second, out = values
    lay_beside(jnp.concatenate([up_first, up_second], axis=0), outs[0])
    lay_beside(jnp.concatenate([down_first, down_second], axis=0), outs[1])
    lay_beside(out, outs[2])


def lay_small(ha, ba, values, outs, blocks):
    din_ref, dk_ref, gain_ref = outs[:3]
    scratch = outs[-1]
    lay_beside(values[0], din_ref)
    own, other = values[1], values[2]
    small = small_rows(blocks, gain_ref.shape[1]) // 2
    mine = ha % 2 == 0
    first, second = jnp.where(mine, own, other), jnp.where(mine, other, own)
    dkern = jnp.concatenate([first[:small], second[:small]], axis=0)
    joined = jnp.concatenate([dkern[k * TAPS : (k + 1) * TAPS] for k in range(blocks)], axis=1)
    dk_ref[...] = joined[:, joined.shape[1] - dk_ref.shape[1] :]
    half = own.shape[0] - small
    count = lax.axis_size("ba")
    part = half // count
    for core, rows in ((0, first), (1, second)):
        for step in range(count):
            start = core * half + (ba ^ step) * part
            source = small + step * part
            scratch[pl.ds(pl.multiple_of(start, 8), part), :] = rows[source : source + part]
    dim = gain_ref.shape[1]
    for k in range(dim // LANES):
        columns = slice(k * LANES, (k + 1) * LANES)
        row = blocks * TAPS + k
        gain_ref[:, columns] = dkern[row : row + 1]
        for vector, ref in enumerate(outs[3:6]):
            ref[:, columns] = scratch[vector * dim // LANES + k : vector * dim // LANES + k + 1, :]
    row = scratch.shape[0]
    for ref in reversed(outs[6:-1]):
        tall, width = ref.shape
        row -= tall * width // LANES
        for k in range(width // LANES):
            ref[:, k * LANES : (k + 1) * LANES] = scratch[row + k * tall : row + (k + 1) * tall, :]


def shards(
    canvas,
    image_id,
    keep_first,
    keep_second,
    first_gain,
    weight_in,
    depth_kernel,
    gate_first,
    gate_second,
    gate_third,
    weight_out,
    scale_first,
    second_gain,
    weight_up,
    weight_down,
    scale_second,
    cotangent,
):
    _, rows, cols, dim = canvas.shape
    cells = rows * cols
    reach = REACH * cols
    count_ha, count_ba = lax.axis_size("ha"), lax.axis_size("ba")
    hidden = weight_up.shape[1]
    blocks = weight_in.shape[1] // LANES
    place = jnp.stack([lax.axis_index("ha"), lax.axis_index("ba")])
    own = canvas.reshape(cells, dim)
    gates = (gate_first, gate_second, gate_third)
    gain = first_gain[None]
    vectors = (gain, scale_first[None], second_gain[None], scale_second[None])
    ids = image_id[0]
    above, below = neighbour_rows(own[:reach], own[cells - reach :])
    ahead = head(place, ids, keep_first, keep_second, own, gain, weight_in, rows, cols)
    joined = ahead[0]
    (
        output, dmiddle, dconv, dconv_top, dconv_bottom, plane_kept, plane_sent, line_kept, line_sent,
        packed_kept, packed_sent,
    ) = forward(
        place, ids, ahead, above, own, below, cotangent.reshape(cells, dim), vectors,
        weight_in, depth_kernel, gates, weight_out, weight_up, weight_down, rows, cols, count_ha, count_ba,
    )
    above, below = neighbour_rows(dconv_top, dconv_bottom)

    plane_sum = Sum([plane_kept, exchange(plane_sent, "ha", 1)], ["plane", "far", "near"])
    line_sum = Sum([line_kept, exchange(line_sent, "ha", 1)], ["far", "near", "plane"])
    packed = Sum([packed_kept, exchange(packed_sent, "ha", 1)], ["plane"])
    made, arrived = run(place, Stage([(plane_sum, "plane"), (packed, "plane")], "plane"))
    more, far = run(place, Stage([(line_sum, "far")], "far"), ties=made, late_ties=[above, below])
    made, arrived = made + more, arrived + far
    dcanvas, in_kept, in_sent, small_kept, small_sent = backward(
        place, ids, above, dconv, below, joined, depth_kernel, own, gain, dmiddle, weight_in, made,
        rows, cols, count_ha, count_ba,
    )
    in_sent, small_sent = tied([in_sent, small_sent], arrived)
    in_sum = Sum([in_kept, exchange(in_sent, "ha", 1)], ["plane", "far", "near"])
    small = Rider([flat_view(small_kept), flat_view(exchange(small_sent, "ha", 1))])
    packed = Rider(packed.views)
    packed = Rider(packed.views)
    made, arrived = run(
        place, Stage([(plane_sum, "far"), (line_sum, "near"), (packed, "line")], "near last"), in_turn=True
    )
    run(place, Stage([(in_sum, "plane"), (small, "plane")], "plane"), ties=made)
    made, _ = run(
        place, Stage([(plane_sum, "near"), (in_sum, "line"), (small, "line")], "line"), ties=arrived, in_turn=True
    )
    packed = Gather(packed.views)
    run(place, Stage([(line_sum, "plane"), (packed, "plane")], "plane"), ties=made)
    cut = plane_sum.views[0].rows // 2
    rest = (line_sum.views[0].rows - dim // count_ha * lane_blocks(dim // count_ba)) // 2
    dup, ddown, dout = combine(
        place,
        [
            [
                plane_sum.part(0, cut),
                line_sum.part(0, rest),
                plane_sum.part(cut, cut),
                line_sum.part(rest, rest),
                line_sum.part(2 * rest, line_sum.views[0].rows - 2 * rest),
            ]
        ],
        epilogue=lay_large,
        out_shape=[
            shape_of(dim // count_ba, hidden // count_ha),
            shape_of(dim // count_ha, hidden // count_ba),
            shape_of(dim // count_ha, dim // count_ba),
        ],
    )
    (halves_of,) = combine(place, [[small.views] + packed.gathered], ties=[dup])
    din, dkern, dgain_one, dscale_one, dgain_two, dscale_two, dfirst, dsecond, dthird, _ = combine(
        place,
        [[in_sum.views, [flat_view(halves_of)], [flat_view(exchange(halves_of, "ha", 1))]]],
        epilogue=functools.partial(lay_small, blocks=blocks),
        out_shape=[shape_of(dim // count_ba, weight_in.shape[1] // count_ha), shape_of(*depth_kernel.shape)]
        + [shape_of(1, dim)] * 4
        + [shape_of(*gate.shape) for gate in gates]
        + [shape_of(packed_rows(gates, dim, count_ba), LANES)],
    )
    return (
        output.reshape(canvas.shape),
        dcanvas.reshape(canvas.shape),
        dgain_one[0],
        din,
        dkern,
        dfirst,
        dsecond,
        dthird,
        dout.T,
        dscale_one[0],
        dgain_two[0],
        dup,
        ddown.T,
        dscale_two[0],
    )


def solution(mesh):
    in_specs = (
        P("ba", "ha", None, None),
        P("ba", None, None),
        P("ba", None),
        P("ba", None),
    ) + (P(),) * 12 + (P("ba", "ha", None, None),)
    tiled = P("ba", "ha")
    out_specs = (
        P("ba", "ha", None, None),
        P("ba", "ha", None, None),
        P(),
        tiled,
        P(),
        P(),
        P(),
        P(),
        tiled,
        P(),
        P(),
        tiled,
        tiled,
        P(),
    )
    return jax.shard_map(shards, mesh=mesh, in_specs=in_specs, out_specs=out_specs, check_vma=False)
```

```python
import functools

import jax
import jax.numpy as jnp
from jax import lax
from jax.experimental import pallas as pl
from jax.experimental.pallas import tpu as pltpu
from jax.sharding import PartitionSpec as P

KERN = 7
TAPS = KERN * KERN
REACH = KERN // 2
KEEP_RATE = 0.8
SPREAD = 1.0 / 3.0
EPSILON = 1e-06
LANES = 128
EDGE = 8
VMEM_BYTES = 64 << 20
F32 = jnp.float32
INV_SQRT_2 = 0.7071067811865476
INV_SQRT_2PI = 0.3989422804014327
NN = (((1,), (0,)), ((), ()))
NT = (((1,), (1,)), ((), ()))
TN = (((0,), (0,)), ((), ()))


def dot(left, right, dims=NN):
    return lax.dot_general(left, right, dims, precision=lax.Precision.HIGH, preferred_element_type=F32)


def normalized(values):
    centered = values - jnp.mean(values, axis=-1, keepdims=True)
    scale = lax.rsqrt(jnp.mean(centered * centered, axis=-1, keepdims=True) + EPSILON)
    return centered * scale, scale


def norm_backward(grad_hat, hat, scale):
    return scale * (
        grad_hat
        - jnp.mean(grad_hat, axis=-1, keepdims=True)
        - hat * jnp.mean(grad_hat * hat, axis=-1, keepdims=True)
    )


def params():
    return pltpu.CompilerParams(vmem_limit_bytes=VMEM_BYTES)


def lasting(microseconds):
    return pl.CostEstimate(flops=int(microseconds * 1.1e9), bytes_accessed=0, transcendentals=0)


def whole(shape):
    return pl.BlockSpec(tuple(shape), lambda *_: (0,) * len(shape), pipeline_mode=pl.Buffered(1))


def in_smem():
    return pl.BlockSpec(memory_space=pltpu.SMEM)


def in_hbm():
    return pl.BlockSpec(memory_space=pltpu.HBM)


def shape_of(*shape):
    return jax.ShapeDtypeStruct(shape, F32)


def lane_blocks(width):
    return -(-width // LANES)


def image_ids(ids_ref, padded, place, rows):
    height, cols = ids_ref.shape
    padded[...] = jnp.full(padded.shape, -1, jnp.int32)
    padded[EDGE : EDGE + height, :] = ids_ref[...]
    ids = padded[pl.ds(place * rows + (EDGE - REACH), rows + 2 * REACH), :]
    return jnp.concatenate([ids, jnp.full((-ids.shape[0] % 8, cols), -1, jnp.int32)], axis=0).T


def spread_cells(factors, out_ref, first, rows):
    cols = factors.shape[0]
    for r in range(rows):
        column = factors[:, first + r : first + r + 1]
        out_ref[r * cols : (r + 1) * cols, :] = jnp.broadcast_to(column, (cols, LANES))


def keep_factors(turned, table_ref):
    result = jnp.zeros(turned.shape, F32)
    for slot in range(table_ref.shape[1]):
        result = jnp.where(turned == slot, table_ref[0, slot].astype(F32) / KEEP_RATE, result)
    return result


def conv_masks(ids_scalar, ids_ref, place, row_taps, col_mask, rows):
    height, cols = ids_ref.shape
    column_masks(ids_ref, col_mask)
    row_masks(ids_scalar, place, row_taps, rows, height, cols)


def column_masks(ids_ref, col_mask):
    height, cols = ids_ref.shape
    wide_ids = jnp.broadcast_to(ids_ref[...].T[:, height // 2 : height // 2 + 1], (cols, LANES))
    column = lax.broadcasted_iota(jnp.int32, (cols, LANES), 0)
    for b in range(KERN):
        shift = b - REACH
        moved = pltpu.roll(wide_ids, (-shift) % cols, 0)
        inside = (column + shift >= 0) & (column + shift < cols)
        same = (moved == wide_ids) & inside
        col_mask[b] = same.astype(F32).reshape(cols // 8, 8, LANES)


def row_masks(ids_scalar, place, row_taps, rows, height, cols):
    def one(r, _):
        own = ids_scalar[place * rows + r, cols // 2]
        row_taps[r, 0] = KERN
        row_taps[r, KERN + 1] = KERN
        for a in range(KERN):
            other = place * rows + r + a - REACH
            inside = (other >= 0) & (other < height)
            same = ids_scalar[jnp.clip(other, 0, height - 1), cols // 2] == own
            row_taps[r, a + 1] = jnp.where(inside & same, a, KERN)
        return 0

    lax.fori_loop(0, rows, one, 0)


def lay_kernel(kern_ref, laid, split):
    tap = lax.broadcasted_iota(jnp.int32, (TAPS, split), 0)
    own = jnp.where(tap == TAPS // 2, 1.0 / SPREAD, 0.0).astype(F32)
    for k in range(laid.shape[0]):
        start = k * LANES - split
        left = own if k == 0 else kern_ref[:, start : start + split]
        laid[k] = jnp.concatenate([left, kern_ref[:, start + split : start + LANES]], axis=1) * SPREAD


def fill_shifted(flat, col_ref, shifted, rows_ext, cols):
    for b in range(KERN):
        for g in range(cols // 8):
            mask = None if b == REACH else col_ref[b, g]
            for r in range(rows_ext):
                x = flat[pl.ds(EDGE + r * cols + 8 * g + b - REACH, 8), :]
                shifted[b, r, g] = x if b == REACH else x * mask


def spread_taps(kern, wide, turned):
    for t in range(TAPS):
        source = TAPS - 1 - t if turned else t
        wide[t] = jnp.broadcast_to(kern[source : source + 1, :], (8, LANES))
    for t in range(KERN):
        wide[TAPS + t] = jnp.zeros((8, LANES), F32)


def conv_block(row_taps, kern, shifted, wide, out_ref, rows, cols):
    groups = cols // 8
    spread_taps(kern, wide, False)

    def pair(h, _):
        r = 2 * h

        def step(i, totals):
            first, second = totals
            taps_first = row_taps[r, i + 1] * KERN
            taps_second = row_taps[r + 1, i] * KERN
            for b in range(KERN):
                x = shifted[b, r + i]
                first = first + wide[taps_first + b][None] * x
                second = second + wide[taps_second + b][None] * x
            return first, second

        zero = jnp.zeros((groups, 8, LANES), F32)
        first, second = lax.fori_loop(0, KERN + 1, step, (zero, zero), unroll=4)
        out_ref[pl.ds(pl.multiple_of(r * cols, cols), cols), :] = first.reshape(cols, LANES)
        out_ref[pl.ds(pl.multiple_of((r + 1) * cols, cols), cols), :] = second.reshape(cols, LANES)
        return 0

    lax.fori_loop(0, rows // 2, pair, 0)


def conv_grad_block(row_taps, kern, shifted, wide, dk, mix_ref, out_ref, dk_ref, rows, cols):
    groups = cols // 8
    spread_taps(kern, wide, True)
    for t in range(TAPS):
        dk[t] = jnp.zeros((8, LANES), F32)

    def one(r, _):
        start = pl.ds(pl.multiple_of(r * cols, cols), cols)
        mix = mix_ref[start, :].reshape(groups, 8, LANES)
        total = jnp.zeros((groups, 8, LANES), F32)
        for i in range(KERN):
            row = row_taps[r, i + 1]
            same = jnp.where(row < KERN, 1.0, 0.0).astype(F32)
            for b in range(KERN):
                x = shifted[b, r + i]
                total = total + wide[row * KERN + b][None] * x
                dk[i * KERN + b] += jnp.sum(mix * x, axis=0) * same
        out_ref[start, :] = total.reshape(cols, LANES)
        return 0

    lax.fori_loop(0, rows, one, 0)
    for t in range(TAPS):
        dk_ref[TAPS - 1 - t : TAPS - t, :] = jnp.sum(dk[t], axis=0, keepdims=True) * SPREAD
    dk_ref[TAPS:, :] = jnp.zeros((dk_ref.shape[0] - TAPS, LANES), F32)


def share(core, first, second, kept_ref, sent_ref, z, p):
    mine = core == 0
    tall, width = first.shape
    for ref, chunk in (
        (kept_ref, jnp.where(mine, first, second)),
        (sent_ref, jnp.where(mine, second, first)),
    ):
        for k in range(lane_blocks(width)):
            part = chunk[:, k * LANES : (k + 1) * LANES]
            if part.shape[1] < LANES:
                part = jnp.concatenate([part, jnp.zeros((tall, LANES - part.shape[1]), F32)], axis=1)
            ref[z, p, k * tall : (k + 1) * tall, :] = part


def share_columns(core, grad, kept_ref, sent_ref, width, plane_first=False):
    groups, parts = reversed(kept_ref.shape[:2]) if plane_first else kept_ref.shape[:2]
    tall = grad.shape[0] // parts
    for z in range(groups):
        for p in range(parts):
            rows = slice(p * tall, (p + 1) * tall)
            first = grad[rows, 2 * z * width : (2 * z + 1) * width]
            second = grad[rows, (2 * z + 1) * width : (2 * z + 2) * width]
            share(core, first, second, kept_ref, sent_ref, *((p, z) if plane_first else (z, p)))


def share_rows(core, grad, kept_ref, sent_ref, tall):
    groups, parts = kept_ref.shape[:2]
    width = grad.shape[1] // parts
    for z in range(groups):
        for p in range(parts):
            columns = slice(p * width, (p + 1) * width)
            first = grad[2 * z * tall : (2 * z + 1) * tall, columns]
            second = grad[(2 * z + 1) * tall : (2 * z + 2) * tall, columns]
            share(core, first, second, kept_ref, sent_ref, z, p)


class Copies:
    def __init__(self, sems):
        self.sems, self.count, self.pending = sems, 0, {}

    def start(self, name, source, target):
        copy = pltpu.make_async_copy(source, target, self.sems.at[self.count])
        self.count += 1
        copy.start()
        self.pending.setdefault(name, []).append(copy)

    def wait(self, *names):
        for name in names:
            for copy in self.pending.pop(name):
                copy.wait()

    def wait_all(self):
        self.wait(*list(self.pending))


def head_kernel(
    place_ref, ids_scalar, one_table, two_table, ids_hbm, own_hbm, gain_hbm, in_hbm_ref,
    joined_hbm, valid_hbm, one_keep_hbm, two_keep_hbm, col_hbm,
    ids_ref, rows_ref, gain_ref, in_ref, padded, valid_ref, one_keep_ref, two_keep_ref, col_ref, normed, joined, sems,
    *, rows, cols,
):
    cells = rows * cols
    reach = REACH * cols
    steps = in_ref.shape[0]
    copies = Copies(sems)
    copies.start("ids", ids_hbm, ids_ref)
    copies.start("own", own_hbm, rows_ref)
    copies.start("own", gain_hbm, gain_ref)
    for k in range(steps):
        copies.start(("in", k), in_hbm_ref.at[:, pl.ds(2 * LANES * k, 2 * LANES)], in_ref.at[k])
    copies.wait("ids")
    turned = image_ids(ids_ref, padded, place_ref[0], rows)
    spread_cells((turned >= 0).astype(F32), valid_ref, 0, rows + 2 * REACH)
    spread_cells(keep_factors(turned, one_table), one_keep_ref, REACH, rows)
    spread_cells(keep_factors(turned, two_table), two_keep_ref, REACH, rows)
    column_masks(ids_ref, col_ref)
    for source, target in (
        (valid_ref, valid_hbm), (one_keep_ref, one_keep_hbm), (two_keep_ref, two_keep_hbm), (col_ref, col_hbm)
    ):
        copies.start("outs", source, target)
    copies.wait("own")
    hat, _ = normalized(rows_ref[...] * valid_ref[reach : reach + cells, :1])
    normed[...] = hat * gain_ref[...]
    for step in range(steps):
        copies.wait(("in", step))
        part = dot(normed[...], in_ref[step])
        for k in range(2):
            joined[2 * step + k] = part[:, k * LANES : (k + 1) * LANES]
        pair = pl.ds(2 * step, 2)
        copies.start("outs", joined.at[pair], joined_hbm.at[pair])
    copies.wait_all()


def head(place, ids, keep_one, keep_two, own, gain, weight_in, rows, cols):
    cells, dim = own.shape
    cells_ext = cells + 2 * REACH * cols
    blocks = weight_in.shape[1] // LANES
    vmem = functools.partial(pltpu.VMEM, dtype=F32)
    shapes = [
        (blocks, cells, LANES), (cells_ext, LANES), (cells, LANES), (cells, LANES), (KERN, cols // 8, 8, LANES)
    ]
    return pl.pallas_call(
        functools.partial(head_kernel, rows=rows, cols=cols),
        in_specs=[in_smem()] * 4 + [in_hbm()] * 4,
        out_specs=[in_hbm()] * len(shapes),
        out_shape=[shape_of(*shape) for shape in shapes],
        scratch_shapes=[
            pltpu.VMEM(ids.shape, jnp.int32),
            vmem((cells, dim)),
            vmem((1, dim)),
            vmem((blocks // 2, dim, 2 * LANES)),
            pltpu.VMEM((ids.shape[0] + 2 * EDGE, ids.shape[1]), jnp.int32),
        ]
        + [vmem(shape) for shape in shapes[1:]]
        + [vmem((cells, dim)), vmem(shapes[0]), pltpu.SemaphoreType.DMA((7 + blocks,))],
        compiler_params=params(),
        cost_estimate=lasting(7),
    )(place, ids, keep_one, keep_two, ids, own, gain, weight_in)


def forward_kernel(
    place_ref, ids_scalar, joined_hbm, valid_hbm, one_keep_hbm, two_keep_hbm, col_hbm, above_hbm, own_hbm, below_hbm, cot_hbm,
    first_gain_hbm, first_scale_hbm, second_gain_hbm, second_scale_hbm,
    in_hbm_ref, kern_hbm, one_hbm, two_hbm, three_hbm, out_hbm, up_hbm, down_hbm,
    output_hbm, dmiddle_hbm, dconv_hbm, dconv_top_hbm, dconv_bottom_hbm,
    plane_kept_ref, plane_sent_ref, line_kept_ref, line_sent_ref, packed_kept_hbm, packed_sent_hbm,
    rows_ref, cot_ref, first_gain_ref, first_scale_ref, second_gain_ref, second_scale_ref,
    in_ref, kern_ref, one_ref, two_ref, three_ref, out_ref, up_ref, down_ref, dconv_ref, sems, chunk_sems,
    up_kept, up_sent, down_kept, down_sent, out_kept, out_sent,
    row_taps, valid_ref, one_keep_ref, two_keep_ref, col_ref, packed_ref, normed, flat, shifted, laid, wide, conv,
    mixed_ref, mapped_ref, middle_ref, result, dnorm,
    *, rows, cols, count_ha, count_ba,
):
    blocks = flat.shape[0]
    cells = rows * cols
    reach = REACH * cols
    cells_ext = cells + 2 * reach
    core = place_ref[0] % 2
    split = one_ref.shape[0]
    dim = rows_ref.shape[1]
    head_steps = blocks // 2
    ffn_steps = up_kept.shape[0]
    chunk = down_ref.shape[1]
    gate_refs = (one_ref, two_ref, three_ref)

    copies = Copies(sems)
    copies.start("rows", valid_hbm, valid_ref)
    copies.start("rows", first_gain_hbm, first_gain_ref)
    copies.start("above", above_hbm, rows_ref.at[pl.ds(0, reach)])
    copies.start("below", below_hbm, rows_ref.at[pl.ds(reach + cells, reach)])
    for k in range(head_steps):
        copies.start(("in", k), in_hbm_ref.at[:, pl.ds(2 * LANES * k, 2 * LANES)], in_ref.at[k])
    copies.start("conv", joined_hbm, flat.at[:, pl.ds(EDGE + reach, cells), :])
    copies.start("conv", col_hbm, col_ref)
    copies.start("gates", own_hbm, rows_ref.at[pl.ds(reach, cells)])
    copies.start("gates", one_keep_hbm, one_keep_ref)
    copies.start("gates", two_keep_hbm, two_keep_ref)
    copies.start("kern", kern_hbm, kern_ref)
    def weights(k):
        ends = pl.ds(pl.multiple_of(k * chunk, chunk), chunk)
        return [
            pltpu.make_async_copy(up_hbm.at[:, ends], up_ref.at[k], chunk_sems.at[k, 0]),
            pltpu.make_async_copy(down_hbm.at[ends, :], down_ref.at[k], chunk_sems.at[k, 1]),
        ]

    def chunk_copies(place):
        moves = []
        sides = ((up_kept, down_kept, plane_kept_ref, line_kept_ref), (up_sent, down_sent, plane_sent_ref, line_sent_ref))
        for up, down, plane, line in sides:
            cut = plane.shape[2] // 2
            rest = up.shape[3] - cut
            zs = pl.ds(place * up.shape[1], up.shape[1])
            bas = pl.ds(place * down.shape[2], down.shape[2])
            moves += [
                (up.at[place, :, ba, pl.ds(0, cut), :], plane.at[ba, zs, pl.ds(0, cut), :])
                for ba in range(plane.shape[0])
            ]
            moves += [
                (down.at[place, z, :, pl.ds(0, cut), :], plane.at[bas, z, pl.ds(cut, cut), :])
                for z in range(plane.shape[1])
            ]
            moves.append((up.at[place, :, :, pl.ds(cut, rest), :], line.at[zs, :, pl.ds(0, rest), :]))
            moves.append((down.at[place, :, :, pl.ds(cut, rest), :], line.at[:, bas, pl.ds(rest, rest), :]))
        return [
            pltpu.make_async_copy(source, target, chunk_sems.at[place, 2 + k])
            for k, (source, target) in enumerate(moves)
        ]

    row_masks(ids_scalar, place_ref[0], row_taps, rows, ids_scalar.shape[0], cols)
    copies.wait("rows")
    for name, start, place in (("above", 0, 0), ("below", reach + cells, reach)):
        copies.wait(name)
        hat, _ = normalized(rows_ref[start : start + reach, :] * valid_ref[start : start + reach, :1])
        normed[place : place + reach] = hat * first_gain_ref[...]

    for k in range(blocks):
        flat[k, :EDGE] = jnp.zeros((EDGE, LANES), F32)
        flat[k, EDGE + cells_ext :] = jnp.zeros((EDGE, LANES), F32)
    for step in range(head_steps):
        copies.wait(("in", step))
        joined = dot(normed[: 2 * reach], in_ref[step])
        for k in range(2):
            part = joined[:, k * LANES : (k + 1) * LANES]
            flat[2 * step + k, EDGE : EDGE + reach] = part[:reach]
            flat[2 * step + k, EDGE + reach + cells : EDGE + cells_ext] = part[reach:]
        if step == 0:
            copies.start("gates", first_scale_hbm, first_scale_ref)
            copies.start("gates", second_gain_hbm, second_gain_ref)
            copies.start("gates", second_scale_hbm, second_scale_ref)
            for source, target in zip((one_hbm, two_hbm, three_hbm, out_hbm, cot_hbm), gate_refs + (out_ref, cot_ref)):
                copies.start("gates", source, target)
            for k in range(ffn_steps):
                for copy in weights(k):
                    copy.start()

    copies.wait("conv")
    copies.wait("kern")
    lay_kernel(kern_ref, laid, split)

    def conv_step(block, _):
        fill_shifted(flat.at[block], col_ref, shifted, rows + 2 * REACH, cols)
        conv_block(row_taps, laid[block], shifted, wide, conv.at[block], rows, cols)
        return 0

    lax.fori_loop(0, blocks, conv_step, 0)

    def conv_part(start, width):
        return jnp.concatenate([conv[start // LANES + k] for k in range(width // LANES)], axis=1)

    copies.wait("gates")
    mixed = conv[0, :, :split] * conv[0, :, split:]
    mixed_ref[:, :split] = mixed
    start = 2 * split
    for ref in gate_refs:
        width = ref.shape[1]
        mapped = dot(mixed, ref[...])
        mapped_ref[:, start - 2 * split : start - 2 * split + width] = mapped
        mixed = mapped * conv_part(start, width)
        mixed_ref[:, start : start + width] = mixed
        start += width
    branch = dot(mixed, out_ref[...])
    masked = rows_ref[reach : reach + cells, :] * valid_ref[reach : reach + cells, :1]
    middle = masked + one_keep_ref[:, :1] * first_scale_ref[...] * branch
    middle_ref[...] = middle
    hat, _ = normalized(middle)
    normed[:cells] = hat * second_gain_ref[...]
    result[...] = jnp.zeros_like(result)
    dnorm[...] = jnp.zeros_like(dnorm)

    def ffn_step(place, _):
        for copy in weights(place):
            copy.wait()
        grad_result = two_keep_ref[:, :1] * second_scale_ref[...] * cot_ref[...]
        pre = dot(normed[:cells], up_ref[place])
        cdf = 0.5 + 0.5 * lax.erf(pre * INV_SQRT_2)
        slope = cdf + pre * (INV_SQRT_2PI * jnp.exp(-0.5 * pre * pre))
        hidden = pre * cdf
        result[...] += dot(hidden, down_ref[place])
        grad_pre = dot(grad_result, down_ref[place], NT) * slope
        share_rows(
            core, dot(grad_result, hidden, TN), down_kept.at[place], down_sent.at[place], dim // count_ha
        )
        width = chunk // (2 * up_kept.shape[1])
        share_columns(core, dot(normed[:cells], grad_pre, TN), up_kept.at[place], up_sent.at[place], width)
        for copy in chunk_copies(place):
            copy.start()
        dnorm[...] += dot(grad_pre, up_ref[place], NT)
        return 0

    lax.fori_loop(0, ffn_steps, ffn_step, 0)

    hat, scale = normalized(middle_ref[...])
    kept = two_keep_ref[:, :1] * result[...]
    dscale_two = jnp.sum(cot_ref[...] * kept, axis=0, keepdims=True)
    result[...] = middle_ref[...] + second_scale_ref[...] * kept
    copies.start("outs", result, output_hbm)
    dgain_two = jnp.sum(dnorm[...] * hat, axis=0, keepdims=True)
    dmiddle = cot_ref[...] + norm_backward(dnorm[...] * second_gain_ref[...], hat, scale)
    dnorm[...] = dmiddle
    copies.start("outs", dnorm, dmiddle_hbm)
    kept = one_keep_ref[:, :1] * dmiddle
    grad = dot(kept * first_scale_ref[...], out_ref[...], NT)
    row = packed_ref.shape[0]
    start = blocks * LANES
    for ref in reversed(gate_refs):
        tall, width = ref.shape
        start -= width
        source = start - tall if tall > split else 0
        columns = slice(start - 2 * split, start - 2 * split + width)
        dconv = grad * mapped_ref[:, columns]
        for k in range(width // LANES):
            dconv_ref[start // LANES + k] = dconv[:, k * LANES : (k + 1) * LANES]
        grad_mapped = grad * conv_part(start, width)
        part = dot(mixed_ref[:, source : source + tall], grad_mapped, TN)
        row -= tall * width // LANES
        for k in range(width // LANES):
            packed_ref[row + k * tall : row + (k + 1) * tall] = part[:, k * LANES : (k + 1) * LANES]
        grad = dot(grad_mapped, ref[...], NT)
    dconv_ref[0] = jnp.concatenate([grad * conv[0, :, split:], grad * conv[0, :, :split]], axis=1)
    copies.start("outs", dconv_ref.at[:, pl.ds(0, reach), :], dconv_top_hbm)
    copies.start("outs", dconv_ref.at[:, pl.ds(cells - reach, reach), :], dconv_bottom_hbm)
    copies.start("outs", dconv_ref, dconv_hbm)
    start = mixed_ref.shape[1] - out_ref.shape[0]
    crossed = dot(mixed_ref[:, start:], kept, TN)
    dscale_one = jnp.sum(crossed * out_ref[...], axis=0, keepdims=True)
    packed_ref[:row] = jnp.zeros((row, LANES), F32)
    row = 0
    for vector in (dscale_one, dgain_two, dscale_two):
        for k in range(dim // LANES):
            packed_ref[row : row + 1] = vector[:, k * LANES : (k + 1) * LANES]
            row += 1
    half = packed_kept_hbm.shape[0]
    for place, target in ((core, packed_kept_hbm), (1 - core, packed_sent_hbm)):
        copies.start("outs", packed_ref.at[pl.ds(pl.multiple_of(place * half, 8), half), :], target)
    share_rows(core, (crossed * first_scale_ref[...]).T, out_kept, out_sent, dim // count_ha)
    for source, line in ((out_kept, line_kept_ref), (out_sent, line_sent_ref)):
        tall = source.shape[2]
        copies.start("outs", source, line.at[:, :, pl.ds(line.shape[2] - tall, tall), :])
    for place in range(ffn_steps):
        for copy in chunk_copies(place):
            copy.wait()
    copies.wait_all()


def mask_scratch(ids, rows):
    height, cols = ids.shape
    return [
        pltpu.SMEM((rows, KERN + 2), jnp.int32),
        pltpu.VMEM((height + 2 * EDGE, cols), jnp.int32),
        pltpu.VMEM(((rows + 2 * REACH) * cols, LANES), F32),
    ]


def packed_rows(gates, dim, parts):
    rows = sum(gate.size for gate in gates) // LANES + 3 * dim // LANES
    return -(-rows // (16 * parts)) * 16 * parts


def plane_share(rows):
    return max(rows * 3 // 4 // 8 * 8, 8)


def forward(
    place, ids, ahead, above, own, below, cot, vectors, weight_in, kern, gates,
    weight_out, weight_up, weight_down, rows, cols, count_ha, count_ba, chunk=512,
):
    cells, dim = own.shape
    reach = above.shape[0]
    blocks = weight_in.shape[1] // LANES
    hidden = weight_up.shape[1]
    split = gates[0].shape[0]
    wide = blocks * LANES
    head_steps = blocks // 2
    ffn_steps = hidden // chunk

    up_wide, down_wide = hidden // count_ha, hidden // count_ba
    up_rows = dim // count_ba * lane_blocks(up_wide)
    down_rows = dim // count_ha * lane_blocks(down_wide)
    out_rows = dim // count_ha * lane_blocks(dim // count_ba)
    half = count_ha // 2
    assert up_rows == down_rows
    cut = plane_share(up_rows)
    rest = up_rows - cut
    plane = (count_ba, half, 2 * cut, LANES)
    line = (half, count_ba, 2 * rest + out_rows, LANES)
    packed_shape = (packed_rows(gates, dim, count_ba), LANES)
    half_packed = (packed_shape[0] // 2, LANES)
    cells_ext = cells + 2 * reach
    vmem = functools.partial(pltpu.VMEM, dtype=F32)
    operands = (
        place, ids, *ahead, above, own, below, cot, *vectors,
        weight_in, kern, *gates, weight_out, weight_up, weight_down,
    )
    out_shape = [
        shape_of(cells, dim),
        shape_of(cells, dim),
        shape_of(blocks, cells, LANES),
        shape_of(blocks, reach, LANES),
        shape_of(blocks, reach, LANES),
        shape_of(*plane),
        shape_of(*plane),
        shape_of(*line),
        shape_of(*line),
        shape_of(*half_packed),
        shape_of(*half_packed),
    ]
    return pl.pallas_call(
        functools.partial(forward_kernel, rows=rows, cols=cols, count_ha=count_ha, count_ba=count_ba),
        in_specs=[in_smem()] * 2 + [in_hbm()] * (len(operands) - 2),
        out_specs=[in_hbm()] * len(out_shape),
        out_shape=out_shape,
        scratch_shapes=[vmem((cells_ext, dim)), vmem((cells, dim))]
        + [vmem((1, dim))] * 4
        + [vmem((head_steps, dim, 2 * LANES)), vmem(kern.shape)]
        + [vmem(gate.shape) for gate in gates]
        + [
            vmem(weight_out.shape),
            vmem((ffn_steps, dim, chunk)),
            vmem((ffn_steps, chunk, dim)),
            vmem((blocks, cells, LANES)),
            pltpu.SemaphoreType.DMA((40 + head_steps,)),
            pltpu.SemaphoreType.DMA((ffn_steps, 2 + 2 * (count_ba + half + 2))),
        ]
        + [vmem((ffn_steps, chunk // (2 * up_wide), count_ba, up_rows, LANES))] * 2
        + [vmem((ffn_steps, half, chunk // down_wide, down_rows, LANES))] * 2
        + [vmem((half, count_ba, out_rows, LANES))] * 2
        + [
            pltpu.SMEM((rows, KERN + 2), jnp.int32),
            vmem((cells_ext, LANES)),
            vmem((cells, LANES)),
            vmem((cells, LANES)),
            vmem((KERN, cols // 8, 8, LANES)),
            vmem(packed_shape),
            vmem((max(cells, 2 * reach), dim)),
            vmem((blocks, cells_ext + 2 * EDGE, LANES)),
            vmem((KERN, rows + 2 * REACH, cols // 8, 8, LANES)),
            vmem((blocks, TAPS, LANES)),
            vmem((TAPS + KERN, 8, LANES)),
            vmem((blocks, cells, LANES)),
            vmem((cells, wide)),
            vmem((cells, wide - 2 * split)),
            vmem((cells, dim)),
            vmem((cells, dim)),
            vmem((cells, dim)),
        ],
        compiler_params=params(),
        cost_estimate=lasting(48),
    )(*operands)


def lay_flat(above_ref, own_ref, below_ref, flat):
    reach, cells = above_ref.shape[1], own_ref.shape[1]
    flat[:EDGE] = jnp.zeros((EDGE, LANES), F32)
    flat[EDGE : EDGE + reach] = above_ref[0]
    flat[EDGE + reach : EDGE + reach + cells] = own_ref[0]
    flat[EDGE + reach + cells : EDGE + 2 * reach + cells] = below_ref[0]
    flat[EDGE + 2 * reach + cells :] = jnp.zeros((EDGE, LANES), F32)


def backward_kernel(
    place_ref, ids_scalar, ids_ref, above_ref, own_ref, below_ref, mix_ref, kern_ref, canvas_ref, gain_ref,
    dmiddle_ref, in_ref, *rest, rows, cols,
):
    dcanvas_ref, kept_ref, sent_ref, small_kept_ref, small_sent_ref = rest[-19:-14]
    row_taps, padded, valid_ref, col_ref, flat, shifted, laid, wide, dk, sums, small, djoined, normed, dnorm = rest[-14:]
    step = pl.program_id(0)
    cells = rows * cols
    reach = REACH * cols
    core = place_ref[0] % 2
    split = laid.shape[0] * LANES - kern_ref.shape[1]
    width = in_ref.shape[1] // (2 * kept_ref.shape[1])

    @pl.when(step == 0)
    def _():
        lay_kernel(kern_ref, laid, split)
        turned = image_ids(ids_ref, padded, place_ref[0], rows)
        spread_cells((turned >= 0).astype(F32), valid_ref, 0, rows + 2 * REACH)
        conv_masks(ids_scalar, ids_ref, place_ref[0], row_taps, col_ref, rows)
        hat, _ = normalized(canvas_ref[...] * valid_ref[reach : reach + cells, :1])
        normed[...] = hat * gain_ref[...]
        dnorm[...] = jnp.zeros_like(dnorm)

    lay_flat(above_ref, own_ref, below_ref, flat)
    fill_shifted(flat, col_ref, shifted, rows + 2 * REACH, cols)
    conv_grad_block(
        row_taps, laid[step], shifted, wide, dk, mix_ref.at[0], djoined.at[step % 2], sums.at[step], rows, cols
    )

    @pl.when(step % 2 == 1)
    def _():
        grad = jnp.concatenate([djoined[0], djoined[1]], axis=1)
        share_columns(core, dot(normed[...], grad, TN), kept_ref, sent_ref, width, plane_first=True)
        dnorm[...] += dot(grad, in_ref[...], NT)

    @pl.when(step == pl.num_programs(0) - 1)
    def _():
        hat, scale = normalized(canvas_ref[...] * valid_ref[reach : reach + cells, :1])
        dgain = jnp.sum(dnorm[...] * hat, axis=0, keepdims=True)
        row = sums.shape[0] * TAPS
        for k in range(sums.shape[0]):
            small[k * TAPS : (k + 1) * TAPS, :] = sums[k, :TAPS]
        small[row:, :] = jnp.zeros((small.shape[0] - row, LANES), F32)
        for k in range(dgain.shape[1] // LANES):
            small[row + k : row + k + 1, :] = dgain[:, k * LANES : (k + 1) * LANES]
        half = small.shape[0] // 2
        for ref, start in ((small_kept_ref, core * half), (small_sent_ref, (1 - core) * half)):
            ref[...] = small[pl.ds(pl.multiple_of(start, 8), half), :]
        inner = dmiddle_ref[...] + norm_backward(dnorm[...] * gain_ref[...], hat, scale)
        dcanvas_ref[...] = inner * valid_ref[reach : reach + cells, :1]


def block_of(size):
    return pl.BlockSpec((1, size, LANES), lambda i: (i, 0, 0))


def small_rows(blocks, dim):
    return -(-(blocks * TAPS + dim // LANES) // 16) * 16


def backward(
    place, ids, above, own, below, mix, kern, canvas, gain, dmiddle, weight_in, ties, rows, cols, count_ha, count_ba
):
    cells, dim = canvas.shape
    blocks = own.shape[0]
    reach = above.shape[1]
    own_wide = weight_in.shape[1] // count_ha
    chunk_rows = dim // count_ba * lane_blocks(own_wide)
    groups = 2 * LANES // (2 * own_wide)
    chunk_spec = pl.BlockSpec((count_ba, groups, chunk_rows, LANES), lambda i: (0, i // 2, 0, 0))
    chunks = shape_of(count_ba, count_ha // 2, chunk_rows, LANES)
    tall = -(-TAPS // 8) * 8
    small = (small_rows(blocks, dim) // 2, LANES)
    return pl.pallas_call(
        functools.partial(backward_kernel, rows=rows, cols=cols),
        grid=(blocks,),
        in_specs=[in_smem(), in_smem(), whole(ids.shape)]
        + [block_of(size) for size in (reach, cells, reach, cells)]
        + [whole(kern.shape), whole(canvas.shape)]
        + [whole((1, dim)), whole((cells, dim))]
        + [pl.BlockSpec((dim, 2 * LANES), lambda i: (0, i // 2))]
        + [in_hbm()] * len(ties),
        out_specs=[whole((cells, dim)), chunk_spec, chunk_spec, whole(small), whole(small)],
        out_shape=[shape_of(cells, dim), chunks, chunks, shape_of(*small), shape_of(*small)],
        scratch_shapes=mask_scratch(ids, rows)
        + [
            pltpu.VMEM((KERN, cols // 8, 8, LANES), F32),
            pltpu.VMEM((cells + 2 * reach + 2 * EDGE, LANES), F32),
            pltpu.VMEM((KERN, rows + 2 * REACH, cols // 8, 8, LANES), F32),
            pltpu.VMEM((blocks, TAPS, LANES), F32),
            pltpu.VMEM((TAPS + KERN, 8, LANES), F32),
            pltpu.VMEM((TAPS, 8, LANES), F32),
            pltpu.VMEM((blocks, tall, LANES), F32),
            pltpu.VMEM((small_rows(blocks, dim), LANES), F32),
            pltpu.VMEM((2, cells, LANES), F32),
            pltpu.VMEM((cells, dim), F32),
            pltpu.VMEM((cells, dim), F32),
        ],
        compiler_params=params(),
        cost_estimate=lasting(25),
    )(place, ids, ids, above, own, below, mix, kern, canvas, gain, dmiddle, weight_in, *ties)


def exchange(values, axis, bit):
    return lax.ppermute(values, axis, [(i, i ^ bit) for i in range(lax.axis_size(axis))])


class View:
    def __init__(self, array, start, ways, fixed, rows):
        self.array, self.start, self.ways, self.fixed, self.rows = array, start, ways, fixed, rows

    def fix(self, way, step):
        if way == "line":
            near = lax.axis_size("ha") // 4
            return self.fix("far", step // near).fix("near", step % near)
        left = [entry for entry in self.ways if entry[0] != way]
        (stride,) = [entry[2] for entry in self.ways if entry[0] == way]
        return View(self.array, self.start, left, self.fixed + [(way, step, stride)], self.rows)

    def size(self):
        count = self.rows
        for _, size, _ in self.ways:
            count *= size
        return count

    def runs(self, ha, ba):
        start = self.start
        near = lax.axis_size("ha") // 4
        places = {"plane": ba, "far": ha // 2 // near, "near": ha // 2 % near}
        for way, step, stride in self.fixed:
            start = start + (places[way] ^ step) * stride
        rows, ways = self.rows, list(self.ways)
        while ways and ways[-1][2] == rows:
            rows *= ways.pop()[1]
        offsets = [0]
        for _, size, stride in ways:
            offsets = [offset + k * stride for offset in offsets for k in range(size)]
        return [pl.multiple_of(start + offset, 8) for offset in offsets], rows


def flat_view(array, start=0, rows=None):
    flat = array.reshape(-1, LANES)
    return View(flat, start, [], [], flat.shape[0] if rows is None else rows)


def combine(place, groups, ties=(), epilogue=None, out_shape=None):
    pieces, arrays = [], []
    for group in groups:
        for views in group:
            if not any(views is other for other in pieces):
                pieces.append(views)
    for views in pieces:
        for view in views:
            if not any(view.array is other for other in arrays):
                arrays.append(view.array)
    index_of = {id(array): k for k, array in enumerate(arrays)}
    piece_of = {id(views): k for k, views in enumerate(pieces)}
    sizes = [sum(views[0].size() for views in group) for group in groups]
    copies = sum(len(view.runs(0, 0)[0]) for views in pieces for view in views)
    plain = epilogue is None
    if plain:
        out_shape = [shape_of(size, LANES) for size in sizes]

    def kernel(place_ref, *refs):
        inputs = refs[: len(arrays)]
        refs = refs[len(arrays) + len(ties) :]
        outs, refs = refs[: len(out_shape)], refs[len(out_shape) :]
        buffers, refs = refs[: len(pieces)], refs[len(pieces) :]
        sems, results, out_sems = refs[0], refs[1:-1], refs[-1]
        ha, ba = place_ref[0], place_ref[1]
        moves, count = [], 0
        for piece, views in enumerate(pieces):
            moves.append([])
            for term, view in enumerate(views):
                source = inputs[index_of[id(view.array)]]
                starts, rows = view.runs(ha, ba)
                for k, start in enumerate(starts):
                    target = buffers[piece].at[term, pl.ds(k * rows, rows), :]
                    move = pltpu.make_async_copy(source.at[pl.ds(start, rows), :], target, sems.at[count])
                    move.start()
                    moves[-1].append(move)
                    count += 1
        values, waited, leaving = [], set(), []
        for out, group in enumerate(groups):
            row = 0
            for views in group:
                piece = piece_of[id(views)]
                if piece not in waited:
                    waited.add(piece)
                    for move in moves[piece]:
                        move.wait()
                value = buffers[piece][0]
                for term in range(1, len(views)):
                    value = value + buffers[piece][term]
                if plain:
                    results[out][row : row + value.shape[0], :] = value
                values.append(value)
                row += value.shape[0]
            if plain:
                leaving.append(pltpu.make_async_copy(results[out], outs[out], out_sems.at[out]))
                leaving[-1].start()
        if not plain:
            epilogue(ha, ba, values, outs)
        for move in leaving:
            move.wait()

    moved = sum(view.size() for views in pieces for view in views) + sum(sizes)
    scratch = [pltpu.VMEM((len(views), views[0].size(), LANES), F32) for views in pieces]
    scratch.append(pltpu.SemaphoreType.DMA((copies,)))
    if plain:
        scratch += [pltpu.VMEM((size, LANES), F32) for size in sizes]
    scratch.append(pltpu.SemaphoreType.DMA((len(groups),)))
    return pl.pallas_call(
        kernel,
        in_specs=[in_smem()] + [in_hbm()] * (len(arrays) + len(ties)),
        out_specs=[in_hbm() if plain else pl.BlockSpec(memory_space=pltpu.VMEM)] * len(out_shape),
        out_shape=out_shape,
        scratch_shapes=scratch,
        compiler_params=params(),
        cost_estimate=lasting(1 + moved * LANES * 4 / 3.0e6),
    )(place, *arrays, *ties)


def tied(arrays, ties):
    return pl.pallas_call(
        lambda *refs: None,
        in_specs=[pl.BlockSpec(memory_space=pl.ANY)] * (len(arrays) + len(ties)),
        out_specs=[pl.BlockSpec(memory_space=pl.ANY)] * len(arrays),
        out_shape=[shape_of(*array.shape) for array in arrays],
        input_output_aliases={k: k for k in range(len(arrays))},
        compiler_params=params(),
        cost_estimate=lasting(0.5),
    )(*arrays, *ties)


class Sum:
    def __init__(self, arrays, names):
        self.views = []
        near = lax.axis_size("ha") // 4
        sizes = {"plane": lax.axis_size("ba"), "far": 2, "near": near}
        for array in arrays:
            flat = array.reshape(-1, LANES)
            stride, ways = flat.shape[0], []
            for name in names:
                stride //= sizes[name]
                ways.append((name, sizes[name], stride))
            self.views.append(View(flat, 0, ways, [], stride))

    def leaving(self, way, step):
        return [view.fix(way, step) for view in self.views]

    def keep(self, way, sent, arrived):
        self.views = [view.fix(way, 0) for view in self.views]
        rows = self.views[0].rows
        stride, ways = rows, []
        for name, size, _ in reversed(self.views[0].ways):
            ways.insert(0, (name, size, stride))
            stride *= size
        self.views += [View(array, start, ways, [], rows) for array, start in arrived]

    def part(self, first, rows):
        return [View(view.array, view.start + first, view.ways, view.fixed, rows) for view in self.views]


class Rider:
    def __init__(self, views):
        self.views = views

    def leaving(self, way, step):
        return self.views

    def keep(self, way, sent, arrived):
        rows = self.views[0].size()
        self.views = [View(array, start, [], [], rows) for array, start in [sent] + arrived]


class Gather(Rider):
    def keep(self, way, sent, arrived):
        rows = self.views[0].size()
        self.gathered = [[View(array, start, [], [], rows)] for array, start in [sent] + arrived]


class Stage:
    def __init__(self, members, way):
        self.members, self.way = members, way
        line, near = lax.axis_size("ha") // 2, lax.axis_size("ha") // 4
        self.steps = {
            "plane": list(range(1, lax.axis_size("ba"))),
            "line": list(range(1, line)),
            "far": [near],
        }[way]
        self.near = near

    def taking(self, step):
        takes = {"plane": True, "line": True, "near": step < self.near, "far": step == self.near}
        return [(one, way) for one, way in self.members if takes[way]]

    def groups(self):
        return [
            [one.leaving(way, step // self.near if way == "far" else step) for one, way in self.taking(step)]
            for step in self.steps
        ]

    def go(self, payloads, in_turn=None):
        axis, unit = ("ba", 1) if self.way == "plane" else ("ha", 2)
        arrived = []
        for step, part in zip(self.steps, payloads):
            if in_turn is not None and len(arrived) == 2:
                (part,) = tied([part], [arrived[in_turn]])
            arrived.append(exchange(part, axis, unit * step))
        places = {}
        for step, sent, part in zip(self.steps, payloads, arrived):
            row = 0
            for one, way in self.taking(step):
                places.setdefault(id(one), []).append(((sent, row), (part, row)))
                row += one.leaving(way, 1)[0].size()
        for one, way in self.members:
            mine = places.get(id(one), [])
            one.keep(way, mine[0][0] if mine else None, [part for _, part in mine])
        return arrived


def run(place, stage, ties=(), in_turn=None, late_ties=()):
    made = list(combine(place, stage.groups(), ties))
    if late_ties:
        made = list(tied(made, late_ties))
    return made, stage.go(made, in_turn)


def neighbour_rows(top, bottom):
    count = lax.axis_size("ha")
    up = [(i, i + 1) for i in range(count - 1)]
    down = [(i + 1, i) for i in range(count - 1)]
    return lax.ppermute(bottom, "ha", up), lax.ppermute(top, "ha", down)


def lay_beside(value, ref):
    tall, width = ref.shape
    for k in range(lane_blocks(width)):
        columns = slice(k * LANES, min(width, (k + 1) * LANES))
        ref[:, columns] = value[k * tall : (k + 1) * tall, : columns.stop - columns.start]


def lay_large(ha, ba, values, outs):
    up_first, up_second, down_first, down_second, out = values
    lay_beside(jnp.concatenate([up_first, up_second], axis=0), outs[0])
    lay_beside(jnp.concatenate([down_first, down_second], axis=0), outs[1])
    lay_beside(out, outs[2])


def lay_small(ha, ba, values, outs, blocks):
    din_ref, dk_ref, gain_ref = outs[:3]
    scratch = outs[-1]
    lay_beside(values[0], din_ref)
    own, other = values[1], values[2]
    small = small_rows(blocks, gain_ref.shape[1]) // 2
    mine = ha % 2 == 0
    first, second = jnp.where(mine, own, other), jnp.where(mine, other, own)
    dkern = jnp.concatenate([first[:small], second[:small]], axis=0)
    joined = jnp.concatenate([dkern[k * TAPS : (k + 1) * TAPS] for k in range(blocks)], axis=1)
    dk_ref[...] = joined[:, joined.shape[1] - dk_ref.shape[1] :]
    half = own.shape[0] - small
    count = lax.axis_size("ba")
    part = half // count
    for core, rows in ((0, first), (1, second)):
        for step in range(count):
            start = core * half + (ba ^ step) * part
            source = small + step * part
            scratch[pl.ds(pl.multiple_of(start, 8), part), :] = rows[source : source + part]
    dim = gain_ref.shape[1]
    for k in range(dim // LANES):
        columns = slice(k * LANES, (k + 1) * LANES)
        row = blocks * TAPS + k
        gain_ref[:, columns] = dkern[row : row + 1]
        for vector, ref in enumerate(outs[3:6]):
            ref[:, columns] = scratch[vector * dim // LANES + k : vector * dim // LANES + k + 1, :]
    row = scratch.shape[0]
    for ref in reversed(outs[6:-1]):
        tall, width = ref.shape
        row -= tall * width // LANES
        for k in range(width // LANES):
            ref[:, k * LANES : (k + 1) * LANES] = scratch[row + k * tall : row + (k + 1) * tall, :]


def shards(
    canvas,
    image_id,
    keep_first,
    keep_second,
    first_gain,
    weight_in,
    depth_kernel,
    gate_first,
    gate_second,
    gate_third,
    weight_out,
    scale_first,
    second_gain,
    weight_up,
    weight_down,
    scale_second,
    cotangent,
):
    _, rows, cols, dim = canvas.shape
    cells = rows * cols
    reach = REACH * cols
    count_ha, count_ba = lax.axis_size("ha"), lax.axis_size("ba")
    hidden = weight_up.shape[1]
    blocks = weight_in.shape[1] // LANES
    place = jnp.stack([lax.axis_index("ha"), lax.axis_index("ba")])
    own = canvas.reshape(cells, dim)
    gates = (gate_first, gate_second, gate_third)
    gain = first_gain[None]
    vectors = (gain, scale_first[None], second_gain[None], scale_second[None])
    ids = image_id[0]
    above, below = neighbour_rows(own[:reach], own[cells - reach :])
    ahead = head(place, ids, keep_first, keep_second, own, gain, weight_in, rows, cols)
    joined = ahead[0]
    (
        output, dmiddle, dconv, dconv_top, dconv_bottom, plane_kept, plane_sent, line_kept, line_sent,
        packed_kept, packed_sent,
    ) = forward(
        place, ids, ahead, above, own, below, cotangent.reshape(cells, dim), vectors,
        weight_in, depth_kernel, gates, weight_out, weight_up, weight_down, rows, cols, count_ha, count_ba,
    )
    above, below = neighbour_rows(dconv_top, dconv_bottom)

    plane_sum = Sum([plane_kept, exchange(plane_sent, "ha", 1)], ["plane", "far", "near"])
    packed_got = exchange(packed_sent, "ha", 1)
    packed = Sum([packed_kept, packed_got], ["plane"])
    (line_sent,) = tied([line_sent], [packed_got])
    line_sum = Sum([line_kept, exchange(line_sent, "ha", 1)], ["far", "near", "plane"])
    made, arrived = run(place, Stage([(plane_sum, "plane"), (packed, "plane")], "plane"))
    more, far = run(place, Stage([(line_sum, "far")], "far"), ties=made, late_ties=[above, below])
    made, arrived = made + more, arrived + far
    dcanvas, in_kept, in_sent, small_kept, small_sent = backward(
        place, ids, above, dconv, below, joined, depth_kernel, own, gain, dmiddle, weight_in, made,
        rows, cols, count_ha, count_ba,
    )
    in_sent, small_sent = tied([in_sent, small_sent], arrived)
    in_sum = Sum([in_kept, exchange(in_sent, "ha", 1)], ["plane", "far", "near"])
    small = Rider([flat_view(small_kept), flat_view(exchange(small_sent, "ha", 1))])
    packed = Rider(packed.views)
    packed = Rider(packed.views)
    made, arrived = run(
        place, Stage([(plane_sum, "far"), (line_sum, "near"), (packed, "line")], "line"), in_turn=0
    )
    run(place, Stage([(in_sum, "plane"), (small, "plane")], "plane"), ties=made)
    made, _ = run(
        place, Stage([(plane_sum, "near"), (in_sum, "line"), (small, "line")], "line"), ties=arrived, in_turn=1
    )
    packed = Gather(packed.views)
    run(place, Stage([(line_sum, "plane"), (packed, "plane")], "plane"), ties=made)
    cut = plane_sum.views[0].rows // 2
    rest = (line_sum.views[0].rows - dim // count_ha * lane_blocks(dim // count_ba)) // 2
    dup, ddown, dout = combine(
        place,
        [
            [
                plane_sum.part(0, cut),
                line_sum.part(0, rest),
                plane_sum.part(cut, cut),
                line_sum.part(rest, rest),
                line_sum.part(2 * rest, line_sum.views[0].rows - 2 * rest),
            ]
        ],
        epilogue=lay_large,
        out_shape=[
            shape_of(dim // count_ba, hidden // count_ha),
            shape_of(dim // count_ha, hidden // count_ba),
            shape_of(dim // count_ha, dim // count_ba),
        ],
    )
    (halves_of,) = combine(place, [[small.views] + packed.gathered], ties=[dup])
    din, dkern, dgain_one, dscale_one, dgain_two, dscale_two, dfirst, dsecond, dthird, _ = combine(
        place,
        [[in_sum.views, [flat_view(halves_of)], [flat_view(exchange(halves_of, "ha", 1))]]],
        epilogue=functools.partial(lay_small, blocks=blocks),
        out_shape=[shape_of(dim // count_ba, weight_in.shape[1] // count_ha), shape_of(*depth_kernel.shape)]
        + [shape_of(1, dim)] * 4
        + [shape_of(*gate.shape) for gate in gates]
        + [shape_of(packed_rows(gates, dim, count_ba), LANES)],
    )
    return (
        output.reshape(canvas.shape),
        dcanvas.reshape(canvas.shape),
        dgain_one[0],
        din,
        dkern,
        dfirst,
        dsecond,
        dthird,
        dout.T,
        dscale_one[0],
        dgain_two[0],
        dup,
        ddown.T,
        dscale_two[0],
    )


def solution(mesh):
    in_specs = (
        P("ba", "ha", None, None),
        P("ba", None, None),
        P("ba", None),
        P("ba", None),
    ) + (P(),) * 12 + (P("ba", "ha", None, None),)
    tiled = P("ba", "ha")
    out_specs = (
        P("ba", "ha", None, None),
        P("ba", "ha", None, None),
        P(),
        tiled,
        P(),
        P(),
        P(),
        P(),
        tiled,
        P(),
        P(),
        tiled,
        tiled,
        P(),
    )
    return jax.shard_map(shards, mesh=mesh, in_specs=in_specs, out_specs=out_specs, check_vma=False)
```

```python
import functools

import jax
import jax.numpy as jnp
from jax import lax
from jax.experimental import pallas as pl
from jax.experimental.pallas import tpu as pltpu
from jax.sharding import PartitionSpec as P

KERN = 7
TAPS = KERN * KERN
REACH = KERN // 2
KEEP_RATE = 0.8
SPREAD = 1.0 / 3.0
EPSILON = 1e-06
LANES = 128
EDGE = 8
VMEM_BYTES = 64 << 20
F32 = jnp.float32
INV_SQRT_2 = 0.7071067811865476
INV_SQRT_2PI = 0.3989422804014327
NN = (((1,), (0,)), ((), ()))
NT = (((1,), (1,)), ((), ()))
TN = (((0,), (0,)), ((), ()))


def dot(left, right, dims=NN):
    return lax.dot_general(left, right, dims, precision=lax.Precision.HIGH, preferred_element_type=F32)


def normalized(values):
    centered = values - jnp.mean(values, axis=-1, keepdims=True)
    scale = lax.rsqrt(jnp.mean(centered * centered, axis=-1, keepdims=True) + EPSILON)
    return centered * scale, scale


def norm_backward(grad_hat, hat, scale):
    return scale * (
        grad_hat
        - jnp.mean(grad_hat, axis=-1, keepdims=True)
        - hat * jnp.mean(grad_hat * hat, axis=-1, keepdims=True)
    )


def params():
    return pltpu.CompilerParams(vmem_limit_bytes=VMEM_BYTES)


def lasting(microseconds):
    return pl.CostEstimate(flops=int(microseconds * 1.1e9), bytes_accessed=0, transcendentals=0)


def whole(shape):
    return pl.BlockSpec(tuple(shape), lambda *_: (0,) * len(shape), pipeline_mode=pl.Buffered(1))


def in_smem():
    return pl.BlockSpec(memory_space=pltpu.SMEM)


def in_hbm():
    return pl.BlockSpec(memory_space=pltpu.HBM)


def shape_of(*shape):
    return jax.ShapeDtypeStruct(shape, F32)


def lane_blocks(width):
    return -(-width // LANES)


def image_ids(ids_ref, padded, place, rows):
    height, cols = ids_ref.shape
    padded[...] = jnp.full(padded.shape, -1, jnp.int32)
    padded[EDGE : EDGE + height, :] = ids_ref[...]
    ids = padded[pl.ds(place * rows + (EDGE - REACH), rows + 2 * REACH), :]
    return jnp.concatenate([ids, jnp.full((-ids.shape[0] % 8, cols), -1, jnp.int32)], axis=0).T


def spread_cells(factors, out_ref, first, rows):
    cols = factors.shape[0]
    for r in range(rows):
        column = factors[:, first + r : first + r + 1]
        out_ref[r * cols : (r + 1) * cols, :] = jnp.broadcast_to(column, (cols, LANES))


def keep_factors(turned, table_ref):
    result = jnp.zeros(turned.shape, F32)
    for slot in range(table_ref.shape[1]):
        result = jnp.where(turned == slot, table_ref[0, slot].astype(F32) / KEEP_RATE, result)
    return result


def conv_masks(ids_scalar, ids_ref, place, row_taps, col_mask, rows):
    height, cols = ids_ref.shape
    column_masks(ids_ref, col_mask)
    row_masks(ids_scalar, place, row_taps, rows, height, cols)


def column_masks(ids_ref, col_mask):
    height, cols = ids_ref.shape
    wide_ids = jnp.broadcast_to(ids_ref[...].T[:, height // 2 : height // 2 + 1], (cols, LANES))
    column = lax.broadcasted_iota(jnp.int32, (cols, LANES), 0)
    for b in range(KERN):
        shift = b - REACH
        moved = pltpu.roll(wide_ids, (-shift) % cols, 0)
        inside = (column + shift >= 0) & (column + shift < cols)
        same = (moved == wide_ids) & inside
        col_mask[b] = same.astype(F32).reshape(cols // 8, 8, LANES)


def row_masks(ids_scalar, place, row_taps, rows, height, cols):
    def one(r, _):
        own = ids_scalar[place * rows + r, cols // 2]
        row_taps[r, 0] = KERN
        row_taps[r, KERN + 1] = KERN
        for a in range(KERN):
            other = place * rows + r + a - REACH
            inside = (other >= 0) & (other < height)
            same = ids_scalar[jnp.clip(other, 0, height - 1), cols // 2] == own
            row_taps[r, a + 1] = jnp.where(inside & same, a, KERN)
        return 0

    lax.fori_loop(0, rows, one, 0)


def lay_kernel(kern_ref, laid, split):
    tap = lax.broadcasted_iota(jnp.int32, (TAPS, split), 0)
    own = jnp.where(tap == TAPS // 2, 1.0 / SPREAD, 0.0).astype(F32)
    for k in range(laid.shape[0]):
        start = k * LANES - split
        left = own if k == 0 else kern_ref[:, start : start + split]
        laid[k] = jnp.concatenate([left, kern_ref[:, start + split : start + LANES]], axis=1) * SPREAD


def fill_shifted(flat, col_ref, shifted, rows_ext, cols):
    for b in range(KERN):
        for g in range(cols // 8):
            mask = None if b == REACH else col_ref[b, g]
            for r in range(rows_ext):
                x = flat[pl.ds(EDGE + r * cols + 8 * g + b - REACH, 8), :]
                shifted[b, r, g] = x if b == REACH else x * mask


def spread_taps(kern, wide, turned):
    for t in range(TAPS):
        source = TAPS - 1 - t if turned else t
        wide[t] = jnp.broadcast_to(kern[source : source + 1, :], (8, LANES))
    for t in range(KERN):
        wide[TAPS + t] = jnp.zeros((8, LANES), F32)


def conv_block(row_taps, kern, shifted, wide, out_ref, rows, cols):
    groups = cols // 8
    spread_taps(kern, wide, False)

    def pair(h, _):
        r = 2 * h

        def step(i, totals):
            first, second = totals
            taps_first = row_taps[r, i + 1] * KERN
            taps_second = row_taps[r + 1, i] * KERN
            for b in range(KERN):
                x = shifted[b, r + i]
                first = first + wide[taps_first + b][None] * x
                second = second + wide[taps_second + b][None] * x
            return first, second

        zero = jnp.zeros((groups, 8, LANES), F32)
        first, second = lax.fori_loop(0, KERN + 1, step, (zero, zero), unroll=4)
        out_ref[pl.ds(pl.multiple_of(r * cols, cols), cols), :] = first.reshape(cols, LANES)
        out_ref[pl.ds(pl.multiple_of((r + 1) * cols, cols), cols), :] = second.reshape(cols, LANES)
        return 0

    lax.fori_loop(0, rows // 2, pair, 0)


def conv_grad_block(row_taps, kern, shifted, wide, dk, mix_ref, out_ref, dk_ref, rows, cols):
    groups = cols // 8
    spread_taps(kern, wide, True)
    for t in range(TAPS):
        dk[t] = jnp.zeros((8, LANES), F32)

    def one(r, _):
        start = pl.ds(pl.multiple_of(r * cols, cols), cols)
        mix = mix_ref[start, :].reshape(groups, 8, LANES)
        total = jnp.zeros((groups, 8, LANES), F32)
        for i in range(KERN):
            row = row_taps[r, i + 1]
            same = jnp.where(row < KERN, 1.0, 0.0).astype(F32)
            for b in range(KERN):
                x = shifted[b, r + i]
                total = total + wide[row * KERN + b][None] * x
                dk[i * KERN + b] += jnp.sum(mix * x, axis=0) * same
        out_ref[start, :] = total.reshape(cols, LANES)
        return 0

    lax.fori_loop(0, rows, one, 0)
    for t in range(TAPS):
        dk_ref[TAPS - 1 - t : TAPS - t, :] = jnp.sum(dk[t], axis=0, keepdims=True) * SPREAD
    dk_ref[TAPS:, :] = jnp.zeros((dk_ref.shape[0] - TAPS, LANES), F32)


def share(core, first, second, kept_ref, sent_ref, z, p):
    mine = core == 0
    tall, width = first.shape
    for ref, chunk in (
        (kept_ref, jnp.where(mine, first, second)),
        (sent_ref, jnp.where(mine, second, first)),
    ):
        for k in range(lane_blocks(width)):
            part = chunk[:, k * LANES : (k + 1) * LANES]
            if part.shape[1] < LANES:
                part = jnp.concatenate([part, jnp.zeros((tall, LANES - part.shape[1]), F32)], axis=1)
            ref[z, p, k * tall : (k + 1) * tall, :] = part


def share_columns(core, grad, kept_ref, sent_ref, width, plane_first=False):
    groups, parts = reversed(kept_ref.shape[:2]) if plane_first else kept_ref.shape[:2]
    tall = grad.shape[0] // parts
    for z in range(groups):
        for p in range(parts):
            rows = slice(p * tall, (p + 1) * tall)
            first = grad[rows, 2 * z * width : (2 * z + 1) * width]
            second = grad[rows, (2 * z + 1) * width : (2 * z + 2) * width]
            share(core, first, second, kept_ref, sent_ref, *((p, z) if plane_first else (z, p)))


def share_rows(core, grad, kept_ref, sent_ref, tall):
    groups, parts = kept_ref.shape[:2]
    width = grad.shape[1] // parts
    for z in range(groups):
        for p in range(parts):
            columns = slice(p * width, (p + 1) * width)
            first = grad[2 * z * tall : (2 * z + 1) * tall, columns]
            second = grad[(2 * z + 1) * tall : (2 * z + 2) * tall, columns]
            share(core, first, second, kept_ref, sent_ref, z, p)


class Copies:
    def __init__(self, sems):
        self.sems, self.count, self.pending = sems, 0, {}

    def start(self, name, source, target):
        copy = pltpu.make_async_copy(source, target, self.sems.at[self.count])
        self.count += 1
        copy.start()
        self.pending.setdefault(name, []).append(copy)

    def wait(self, *names):
        for name in names:
            for copy in self.pending.pop(name):
                copy.wait()

    def wait_all(self):
        self.wait(*list(self.pending))


def head_kernel(
    place_ref, ids_scalar, one_table, two_table, ids_hbm, own_hbm, gain_hbm, in_hbm_ref,
    joined_hbm, valid_hbm, one_keep_hbm, two_keep_hbm, col_hbm,
    ids_ref, rows_ref, gain_ref, in_ref, padded, valid_ref, one_keep_ref, two_keep_ref, col_ref, normed, joined, sems,
    *, rows, cols,
):
    cells = rows * cols
    reach = REACH * cols
    steps = in_ref.shape[0]
    copies = Copies(sems)
    copies.start("ids", ids_hbm, ids_ref)
    copies.start("own", own_hbm, rows_ref)
    copies.start("own", gain_hbm, gain_ref)
    for k in range(steps):
        copies.start(("in", k), in_hbm_ref.at[:, pl.ds(2 * LANES * k, 2 * LANES)], in_ref.at[k])
    copies.wait("ids")
    turned = image_ids(ids_ref, padded, place_ref[0], rows)
    spread_cells((turned >= 0).astype(F32), valid_ref, 0, rows + 2 * REACH)
    spread_cells(keep_factors(turned, one_table), one_keep_ref, REACH, rows)
    spread_cells(keep_factors(turned, two_table), two_keep_ref, REACH, rows)
    column_masks(ids_ref, col_ref)
    for source, target in (
        (valid_ref, valid_hbm), (one_keep_ref, one_keep_hbm), (two_keep_ref, two_keep_hbm), (col_ref, col_hbm)
    ):
        copies.start("outs", source, target)
    copies.wait("own")
    hat, _ = normalized(rows_ref[...] * valid_ref[reach : reach + cells, :1])
    normed[...] = hat * gain_ref[...]
    for step in range(steps):
        copies.wait(("in", step))
        part = dot(normed[...], in_ref[step])
        for k in range(2):
            joined[2 * step + k] = part[:, k * LANES : (k + 1) * LANES]
        pair = pl.ds(2 * step, 2)
        copies.start("outs", joined.at[pair], joined_hbm.at[pair])
    copies.wait_all()


def head(place, ids, keep_one, keep_two, own, gain, weight_in, rows, cols):
    cells, dim = own.shape
    cells_ext = cells + 2 * REACH * cols
    blocks = weight_in.shape[1] // LANES
    vmem = functools.partial(pltpu.VMEM, dtype=F32)
    shapes = [
        (blocks, cells, LANES), (cells_ext, LANES), (cells, LANES), (cells, LANES), (KERN, cols // 8, 8, LANES)
    ]
    return pl.pallas_call(
        functools.partial(head_kernel, rows=rows, cols=cols),
        in_specs=[in_smem()] * 4 + [in_hbm()] * 4,
        out_specs=[in_hbm()] * len(shapes),
        out_shape=[shape_of(*shape) for shape in shapes],
        scratch_shapes=[
            pltpu.VMEM(ids.shape, jnp.int32),
            vmem((cells, dim)),
            vmem((1, dim)),
            vmem((blocks // 2, dim, 2 * LANES)),
            pltpu.VMEM((ids.shape[0] + 2 * EDGE, ids.shape[1]), jnp.int32),
        ]
        + [vmem(shape) for shape in shapes[1:]]
        + [vmem((cells, dim)), vmem(shapes[0]), pltpu.SemaphoreType.DMA((7 + blocks,))],
        compiler_params=params(),
        cost_estimate=lasting(7),
    )(place, ids, keep_one, keep_two, ids, own, gain, weight_in)


def forward_kernel(
    place_ref, ids_scalar, joined_hbm, valid_hbm, one_keep_hbm, two_keep_hbm, col_hbm, above_hbm, own_hbm, below_hbm, cot_hbm,
    first_gain_hbm, first_scale_hbm, second_gain_hbm, second_scale_hbm,
    in_hbm_ref, kern_hbm, one_hbm, two_hbm, three_hbm, out_hbm, up_hbm, down_hbm,
    output_hbm, dmiddle_hbm, dconv_hbm, dconv_top_hbm, dconv_bottom_hbm,
    plane_kept_ref, plane_sent_ref, line_kept_ref, line_sent_ref, packed_kept_hbm, packed_sent_hbm,
    rows_ref, cot_ref, first_gain_ref, first_scale_ref, second_gain_ref, second_scale_ref,
    in_ref, kern_ref, one_ref, two_ref, three_ref, out_ref, up_ref, down_ref, dconv_ref, sems, chunk_sems,
    up_kept, up_sent, down_kept, down_sent, out_kept, out_sent,
    row_taps, valid_ref, one_keep_ref, two_keep_ref, col_ref, packed_ref, normed, flat, shifted, laid, wide, conv,
    mixed_ref, mapped_ref, middle_ref, result, dnorm,
    *, rows, cols, count_ha, count_ba,
):
    blocks = flat.shape[0]
    cells = rows * cols
    reach = REACH * cols
    cells_ext = cells + 2 * reach
    core = place_ref[0] % 2
    split = one_ref.shape[0]
    dim = rows_ref.shape[1]
    head_steps = blocks // 2
    ffn_steps = up_kept.shape[0]
    chunk = down_ref.shape[1]
    gate_refs = (one_ref, two_ref, three_ref)

    copies = Copies(sems)
    copies.start("rows", valid_hbm, valid_ref)
    copies.start("rows", first_gain_hbm, first_gain_ref)
    copies.start("above", above_hbm, rows_ref.at[pl.ds(0, reach)])
    copies.start("below", below_hbm, rows_ref.at[pl.ds(reach + cells, reach)])
    for k in range(head_steps):
        copies.start(("in", k), in_hbm_ref.at[:, pl.ds(2 * LANES * k, 2 * LANES)], in_ref.at[k])
    copies.start("conv", joined_hbm, flat.at[:, pl.ds(EDGE + reach, cells), :])
    copies.start("conv", col_hbm, col_ref)
    copies.start("gates", own_hbm, rows_ref.at[pl.ds(reach, cells)])
    copies.start("gates", one_keep_hbm, one_keep_ref)
    copies.start("gates", two_keep_hbm, two_keep_ref)
    copies.start("kern", kern_hbm, kern_ref)
    def weights(k):
        ends = pl.ds(pl.multiple_of(k * chunk, chunk), chunk)
        return [
            pltpu.make_async_copy(up_hbm.at[:, ends], up_ref.at[k], chunk_sems.at[k, 0]),
            pltpu.make_async_copy(down_hbm.at[ends, :], down_ref.at[k], chunk_sems.at[k, 1]),
        ]

    def chunk_copies(place):
        moves = []
        sides = ((up_kept, down_kept, plane_kept_ref, line_kept_ref), (up_sent, down_sent, plane_sent_ref, line_sent_ref))
        for up, down, plane, line in sides:
            cut = plane.shape[2] // 2
            rest = up.shape[3] - cut
            zs = pl.ds(place * up.shape[1], up.shape[1])
            bas = pl.ds(place * down.shape[2], down.shape[2])
            moves += [
                (up.at[place, :, ba, pl.ds(0, cut), :], plane.at[ba, zs, pl.ds(0, cut), :])
                for ba in range(plane.shape[0])
            ]
            moves += [
                (down.at[place, z, :, pl.ds(0, cut), :], plane.at[bas, z, pl.ds(cut, cut), :])
                for z in range(plane.shape[1])
            ]
            moves.append((up.at[place, :, :, pl.ds(cut, rest), :], line.at[zs, :, pl.ds(0, rest), :]))
            moves.append((down.at[place, :, :, pl.ds(cut, rest), :], line.at[:, bas, pl.ds(rest, rest), :]))
        return [
            pltpu.make_async_copy(source, target, chunk_sems.at[place, 2 + k])
            for k, (source, target) in enumerate(moves)
        ]

    row_masks(ids_scalar, place_ref[0], row_taps, rows, ids_scalar.shape[0], cols)
    copies.wait("rows")
    for name, start, place in (("above", 0, 0), ("below", reach + cells, reach)):
        copies.wait(name)
        hat, _ = normalized(rows_ref[start : start + reach, :] * valid_ref[start : start + reach, :1])
        normed[place : place + reach] = hat * first_gain_ref[...]

    for k in range(blocks):
        flat[k, :EDGE] = jnp.zeros((EDGE, LANES), F32)
        flat[k, EDGE + cells_ext :] = jnp.zeros((EDGE, LANES), F32)
    for step in range(head_steps):
        copies.wait(("in", step))
        joined = dot(normed[: 2 * reach], in_ref[step])
        for k in range(2):
            part = joined[:, k * LANES : (k + 1) * LANES]
            flat[2 * step + k, EDGE : EDGE + reach] = part[:reach]
            flat[2 * step + k, EDGE + reach + cells : EDGE + cells_ext] = part[reach:]
        if step == 0:
            copies.start("gates", first_scale_hbm, first_scale_ref)
            copies.start("gates", second_gain_hbm, second_gain_ref)
            copies.start("gates", second_scale_hbm, second_scale_ref)
            for source, target in zip((one_hbm, two_hbm, three_hbm, out_hbm, cot_hbm), gate_refs + (out_ref, cot_ref)):
                copies.start("gates", source, target)
            for k in range(ffn_steps):
                for copy in weights(k):
                    copy.start()

    copies.wait("conv")
    copies.wait("kern")
    lay_kernel(kern_ref, laid, split)

    def conv_step(block, _):
        fill_shifted(flat.at[block], col_ref, shifted, rows + 2 * REACH, cols)
        conv_block(row_taps, laid[block], shifted, wide, conv.at[block], rows, cols)
        return 0

    lax.fori_loop(0, blocks, conv_step, 0)

    def conv_part(start, width):
        return jnp.concatenate([conv[start // LANES + k] for k in range(width // LANES)], axis=1)

    copies.wait("gates")
    mixed = conv[0, :, :split] * conv[0, :, split:]
    mixed_ref[:, :split] = mixed
    start = 2 * split
    for ref in gate_refs:
        width = ref.shape[1]
        mapped = dot(mixed, ref[...])
        mapped_ref[:, start - 2 * split : start - 2 * split + width] = mapped
        mixed = mapped * conv_part(start, width)
        mixed_ref[:, start : start + width] = mixed
        start += width
    branch = dot(mixed, out_ref[...])
    masked = rows_ref[reach : reach + cells, :] * valid_ref[reach : reach + cells, :1]
    middle = masked + one_keep_ref[:, :1] * first_scale_ref[...] * branch
    middle_ref[...] = middle
    hat, _ = normalized(middle)
    normed[:cells] = hat * second_gain_ref[...]
    result[...] = jnp.zeros_like(result)
    dnorm[...] = jnp.zeros_like(dnorm)

    def ffn_step(place, _):
        for copy in weights(place):
            copy.wait()
        grad_result = two_keep_ref[:, :1] * second_scale_ref[...] * cot_ref[...]
        pre = dot(normed[:cells], up_ref[place])
        cdf = 0.5 + 0.5 * lax.erf(pre * INV_SQRT_2)
        slope = cdf + pre * (INV_SQRT_2PI * jnp.exp(-0.5 * pre * pre))
        hidden = pre * cdf
        result[...] += dot(hidden, down_ref[place])
        grad_pre = dot(grad_result, down_ref[place], NT) * slope
        share_rows(
            core, dot(grad_result, hidden, TN), down_kept.at[place], down_sent.at[place], dim // count_ha
        )
        width = chunk // (2 * up_kept.shape[1])
        share_columns(core, dot(normed[:cells], grad_pre, TN), up_kept.at[place], up_sent.at[place], width)
        for copy in chunk_copies(place):
            copy.start()
        dnorm[...] += dot(grad_pre, up_ref[place], NT)
        return 0

    lax.fori_loop(0, ffn_steps, ffn_step, 0)

    hat, scale = normalized(middle_ref[...])
    kept = two_keep_ref[:, :1] * result[...]
    dscale_two = jnp.sum(cot_ref[...] * kept, axis=0, keepdims=True)
    result[...] = middle_ref[...] + second_scale_ref[...] * kept
    copies.start("outs", result, output_hbm)
    dgain_two = jnp.sum(dnorm[...] * hat, axis=0, keepdims=True)
    dmiddle = cot_ref[...] + norm_backward(dnorm[...] * second_gain_ref[...], hat, scale)
    dnorm[...] = dmiddle
    copies.start("outs", dnorm, dmiddle_hbm)
    kept = one_keep_ref[:, :1] * dmiddle
    grad = dot(kept * first_scale_ref[...], out_ref[...], NT)
    row = packed_ref.shape[0]
    start = blocks * LANES
    for ref in reversed(gate_refs):
        tall, width = ref.shape
        start -= width
        source = start - tall if tall > split else 0
        columns = slice(start - 2 * split, start - 2 * split + width)
        dconv = grad * mapped_ref[:, columns]
        for k in range(width // LANES):
            dconv_ref[start // LANES + k] = dconv[:, k * LANES : (k + 1) * LANES]
        grad_mapped = grad * conv_part(start, width)
        part = dot(mixed_ref[:, source : source + tall], grad_mapped, TN)
        row -= tall * width // LANES
        for k in range(width // LANES):
            packed_ref[row + k * tall : row + (k + 1) * tall] = part[:, k * LANES : (k + 1) * LANES]
        grad = dot(grad_mapped, ref[...], NT)
    dconv_ref[0] = jnp.concatenate([grad * conv[0, :, split:], grad * conv[0, :, :split]], axis=1)
    copies.start("outs", dconv_ref.at[:, pl.ds(0, reach), :], dconv_top_hbm)
    copies.start("outs", dconv_ref.at[:, pl.ds(cells - reach, reach), :], dconv_bottom_hbm)
    copies.start("outs", dconv_ref, dconv_hbm)
    start = mixed_ref.shape[1] - out_ref.shape[0]
    crossed = dot(mixed_ref[:, start:], kept, TN)
    dscale_one = jnp.sum(crossed * out_ref[...], axis=0, keepdims=True)
    packed_ref[:row] = jnp.zeros((row, LANES), F32)
    row = 0
    for vector in (dscale_one, dgain_two, dscale_two):
        for k in range(dim // LANES):
            packed_ref[row : row + 1] = vector[:, k * LANES : (k + 1) * LANES]
            row += 1
    half = packed_kept_hbm.shape[0]
    for place, target in ((core, packed_kept_hbm), (1 - core, packed_sent_hbm)):
        copies.start("outs", packed_ref.at[pl.ds(pl.multiple_of(place * half, 8), half), :], target)
    share_rows(core, (crossed * first_scale_ref[...]).T, out_kept, out_sent, dim // count_ha)
    for source, line in ((out_kept, line_kept_ref), (out_sent, line_sent_ref)):
        tall = source.shape[2]
        copies.start("outs", source, line.at[:, :, pl.ds(line.shape[2] - tall, tall), :])
    for place in range(ffn_steps):
        for copy in chunk_copies(place):
            copy.wait()
    copies.wait_all()


def mask_scratch(ids, rows):
    height, cols = ids.shape
    return [
        pltpu.SMEM((rows, KERN + 2), jnp.int32),
        pltpu.VMEM((height + 2 * EDGE, cols), jnp.int32),
        pltpu.VMEM(((rows + 2 * REACH) * cols, LANES), F32),
    ]


def packed_rows(gates, dim, parts):
    rows = sum(gate.size for gate in gates) // LANES + 3 * dim // LANES
    return -(-rows // (16 * parts)) * 16 * parts


def plane_share(rows):
    return max(rows * 3 // 4 // 8 * 8, 8)


def forward(
    place, ids, ahead, above, own, below, cot, vectors, weight_in, kern, gates,
    weight_out, weight_up, weight_down, rows, cols, count_ha, count_ba, chunk=512,
):
    cells, dim = own.shape
    reach = above.shape[0]
    blocks = weight_in.shape[1] // LANES
    hidden = weight_up.shape[1]
    split = gates[0].shape[0]
    wide = blocks * LANES
    head_steps = blocks // 2
    ffn_steps = hidden // chunk

    up_wide, down_wide = hidden // count_ha, hidden // count_ba
    up_rows = dim // count_ba * lane_blocks(up_wide)
    down_rows = dim // count_ha * lane_blocks(down_wide)
    out_rows = dim // count_ha * lane_blocks(dim // count_ba)
    half = count_ha // 2
    assert up_rows == down_rows
    cut = plane_share(up_rows)
    rest = up_rows - cut
    plane = (count_ba, half, 2 * cut, LANES)
    line = (half, count_ba, 2 * rest + out_rows, LANES)
    packed_shape = (packed_rows(gates, dim, count_ba), LANES)
    half_packed = (packed_shape[0] // 2, LANES)
    cells_ext = cells + 2 * reach
    vmem = functools.partial(pltpu.VMEM, dtype=F32)
    operands = (
        place, ids, *ahead, above, own, below, cot, *vectors,
        weight_in, kern, *gates, weight_out, weight_up, weight_down,
    )
    out_shape = [
        shape_of(cells, dim),
        shape_of(cells, dim),
        shape_of(blocks, cells, LANES),
        shape_of(blocks, reach, LANES),
        shape_of(blocks, reach, LANES),
        shape_of(*plane),
        shape_of(*plane),
        shape_of(*line),
        shape_of(*line),
        shape_of(*half_packed),
        shape_of(*half_packed),
    ]
    return pl.pallas_call(
        functools.partial(forward_kernel, rows=rows, cols=cols, count_ha=count_ha, count_ba=count_ba),
        in_specs=[in_smem()] * 2 + [in_hbm()] * (len(operands) - 2),
        out_specs=[in_hbm()] * len(out_shape),
        out_shape=out_shape,
        scratch_shapes=[vmem((cells_ext, dim)), vmem((cells, dim))]
        + [vmem((1, dim))] * 4
        + [vmem((head_steps, dim, 2 * LANES)), vmem(kern.shape)]
        + [vmem(gate.shape) for gate in gates]
        + [
            vmem(weight_out.shape),
            vmem((ffn_steps, dim, chunk)),
            vmem((ffn_steps, chunk, dim)),
            vmem((blocks, cells, LANES)),
            pltpu.SemaphoreType.DMA((40 + head_steps,)),
            pltpu.SemaphoreType.DMA((ffn_steps, 2 + 2 * (count_ba + half + 2))),
        ]
        + [vmem((ffn_steps, chunk // (2 * up_wide), count_ba, up_rows, LANES))] * 2
        + [vmem((ffn_steps, half, chunk // down_wide, down_rows, LANES))] * 2
        + [vmem((half, count_ba, out_rows, LANES))] * 2
        + [
            pltpu.SMEM((rows, KERN + 2), jnp.int32),
            vmem((cells_ext, LANES)),
            vmem((cells, LANES)),
            vmem((cells, LANES)),
            vmem((KERN, cols // 8, 8, LANES)),
            vmem(packed_shape),
            vmem((max(cells, 2 * reach), dim)),
            vmem((blocks, cells_ext + 2 * EDGE, LANES)),
            vmem((KERN, rows + 2 * REACH, cols // 8, 8, LANES)),
            vmem((blocks, TAPS, LANES)),
            vmem((TAPS + KERN, 8, LANES)),
            vmem((blocks, cells, LANES)),
            vmem((cells, wide)),
            vmem((cells, wide - 2 * split)),
            vmem((cells, dim)),
            vmem((cells, dim)),
            vmem((cells, dim)),
        ],
        compiler_params=params(),
        cost_estimate=lasting(48),
    )(*operands)


def lay_flat(above_ref, own_ref, below_ref, flat):
    reach, cells = above_ref.shape[1], own_ref.shape[1]
    flat[:EDGE] = jnp.zeros((EDGE, LANES), F32)
    flat[EDGE : EDGE + reach] = above_ref[0]
    flat[EDGE + reach : EDGE + reach + cells] = own_ref[0]
    flat[EDGE + reach + cells : EDGE + 2 * reach + cells] = below_ref[0]
    flat[EDGE + 2 * reach + cells :] = jnp.zeros((EDGE, LANES), F32)


def backward_kernel(
    place_ref, ids_scalar, ids_ref, above_ref, own_ref, below_ref, mix_ref, kern_ref, canvas_ref, gain_ref,
    dmiddle_ref, in_ref, *rest, rows, cols,
):
    dcanvas_ref, kept_ref, sent_ref, small_kept_ref, small_sent_ref = rest[-19:-14]
    row_taps, padded, valid_ref, col_ref, flat, shifted, laid, wide, dk, sums, small, djoined, normed, dnorm = rest[-14:]
    step = pl.program_id(0)
    cells = rows * cols
    reach = REACH * cols
    core = place_ref[0] % 2
    split = laid.shape[0] * LANES - kern_ref.shape[1]
    width = in_ref.shape[1] // (2 * kept_ref.shape[1])

    @pl.when(step == 0)
    def _():
        lay_kernel(kern_ref, laid, split)
        turned = image_ids(ids_ref, padded, place_ref[0], rows)
        spread_cells((turned >= 0).astype(F32), valid_ref, 0, rows + 2 * REACH)
        conv_masks(ids_scalar, ids_ref, place_ref[0], row_taps, col_ref, rows)
        hat, _ = normalized(canvas_ref[...] * valid_ref[reach : reach + cells, :1])
        normed[...] = hat * gain_ref[...]
        dnorm[...] = jnp.zeros_like(dnorm)

    lay_flat(above_ref, own_ref, below_ref, flat)
    fill_shifted(flat, col_ref, shifted, rows + 2 * REACH, cols)
    conv_grad_block(
        row_taps, laid[step], shifted, wide, dk, mix_ref.at[0], djoined.at[step % 2], sums.at[step], rows, cols
    )

    @pl.when(step % 2 == 1)
    def _():
        grad = jnp.concatenate([djoined[0], djoined[1]], axis=1)
        share_columns(core, dot(normed[...], grad, TN), kept_ref, sent_ref, width, plane_first=True)
        dnorm[...] += dot(grad, in_ref[...], NT)

    @pl.when(step == pl.num_programs(0) - 1)
    def _():
        hat, scale = normalized(canvas_ref[...] * valid_ref[reach : reach + cells, :1])
        dgain = jnp.sum(dnorm[...] * hat, axis=0, keepdims=True)
        row = sums.shape[0] * TAPS
        for k in range(sums.shape[0]):
            small[k * TAPS : (k + 1) * TAPS, :] = sums[k, :TAPS]
        small[row:, :] = jnp.zeros((small.shape[0] - row, LANES), F32)
        for k in range(dgain.shape[1] // LANES):
            small[row + k : row + k + 1, :] = dgain[:, k * LANES : (k + 1) * LANES]
        half = small.shape[0] // 2
        for ref, start in ((small_kept_ref, core * half), (small_sent_ref, (1 - core) * half)):
            ref[...] = small[pl.ds(pl.multiple_of(start, 8), half), :]
        inner = dmiddle_ref[...] + norm_backward(dnorm[...] * gain_ref[...], hat, scale)
        dcanvas_ref[...] = inner * valid_ref[reach : reach + cells, :1]


def block_of(size):
    return pl.BlockSpec((1, size, LANES), lambda i: (i, 0, 0))


def small_rows(blocks, dim):
    return -(-(blocks * TAPS + dim // LANES) // 16) * 16


def backward(
    place, ids, above, own, below, mix, kern, canvas, gain, dmiddle, weight_in, ties, rows, cols, count_ha, count_ba
):
    cells, dim = canvas.shape
    blocks = own.shape[0]
    reach = above.shape[1]
    own_wide = weight_in.shape[1] // count_ha
    chunk_rows = dim // count_ba * lane_blocks(own_wide)
    groups = 2 * LANES // (2 * own_wide)
    chunk_spec = pl.BlockSpec((count_ba, groups, chunk_rows, LANES), lambda i: (0, i // 2, 0, 0))
    chunks = shape_of(count_ba, count_ha // 2, chunk_rows, LANES)
    tall = -(-TAPS // 8) * 8
    small = (small_rows(blocks, dim) // 2, LANES)
    return pl.pallas_call(
        functools.partial(backward_kernel, rows=rows, cols=cols),
        grid=(blocks,),
        in_specs=[in_smem(), in_smem(), whole(ids.shape)]
        + [block_of(size) for size in (reach, cells, reach, cells)]
        + [whole(kern.shape), whole(canvas.shape)]
        + [whole((1, dim)), whole((cells, dim))]
        + [pl.BlockSpec((dim, 2 * LANES), lambda i: (0, i // 2))]
        + [in_hbm()] * len(ties),
        out_specs=[whole((cells, dim)), chunk_spec, chunk_spec, whole(small), whole(small)],
        out_shape=[shape_of(cells, dim), chunks, chunks, shape_of(*small), shape_of(*small)],
        scratch_shapes=mask_scratch(ids, rows)
        + [
            pltpu.VMEM((KERN, cols // 8, 8, LANES), F32),
            pltpu.VMEM((cells + 2 * reach + 2 * EDGE, LANES), F32),
            pltpu.VMEM((KERN, rows + 2 * REACH, cols // 8, 8, LANES), F32),
            pltpu.VMEM((blocks, TAPS, LANES), F32),
            pltpu.VMEM((TAPS + KERN, 8, LANES), F32),
            pltpu.VMEM((TAPS, 8, LANES), F32),
            pltpu.VMEM((blocks, tall, LANES), F32),
            pltpu.VMEM((small_rows(blocks, dim), LANES), F32),
            pltpu.VMEM((2, cells, LANES), F32),
            pltpu.VMEM((cells, dim), F32),
            pltpu.VMEM((cells, dim), F32),
        ],
        compiler_params=params(),
        cost_estimate=lasting(25),
    )(place, ids, ids, above, own, below, mix, kern, canvas, gain, dmiddle, weight_in, *ties)


def exchange(values, axis, bit):
    return lax.ppermute(values, axis, [(i, i ^ bit) for i in range(lax.axis_size(axis))])


class View:
    def __init__(self, array, start, ways, fixed, rows):
        self.array, self.start, self.ways, self.fixed, self.rows = array, start, ways, fixed, rows

    def fix(self, way, step):
        if way == "line":
            near = lax.axis_size("ha") // 4
            return self.fix("far", step // near).fix("near", step % near)
        left = [entry for entry in self.ways if entry[0] != way]
        (stride,) = [entry[2] for entry in self.ways if entry[0] == way]
        return View(self.array, self.start, left, self.fixed + [(way, step, stride)], self.rows)

    def size(self):
        count = self.rows
        for _, size, _ in self.ways:
            count *= size
        return count

    def runs(self, ha, ba):
        start = self.start
        near = lax.axis_size("ha") // 4
        places = {"plane": ba, "far": ha // 2 // near, "near": ha // 2 % near}
        for way, step, stride in self.fixed:
            start = start + (places[way] ^ step) * stride
        rows, ways = self.rows, list(self.ways)
        while ways and ways[-1][2] == rows:
            rows *= ways.pop()[1]
        offsets = [0]
        for _, size, stride in ways:
            offsets = [offset + k * stride for offset in offsets for k in range(size)]
        return [pl.multiple_of(start + offset, 8) for offset in offsets], rows


def flat_view(array, start=0, rows=None):
    flat = array.reshape(-1, LANES)
    return View(flat, start, [], [], flat.shape[0] if rows is None else rows)


def combine(place, groups, ties=(), epilogue=None, out_shape=None):
    pieces, arrays = [], []
    for group in groups:
        for views in group:
            if not any(views is other for other in pieces):
                pieces.append(views)
    for views in pieces:
        for view in views:
            if not any(view.array is other for other in arrays):
                arrays.append(view.array)
    index_of = {id(array): k for k, array in enumerate(arrays)}
    piece_of = {id(views): k for k, views in enumerate(pieces)}
    sizes = [sum(views[0].size() for views in group) for group in groups]
    copies = sum(len(view.runs(0, 0)[0]) for views in pieces for view in views)
    plain = epilogue is None
    if plain:
        out_shape = [shape_of(size, LANES) for size in sizes]

    def kernel(place_ref, *refs):
        inputs = refs[: len(arrays)]
        refs = refs[len(arrays) + len(ties) :]
        outs, refs = refs[: len(out_shape)], refs[len(out_shape) :]
        buffers, refs = refs[: len(pieces)], refs[len(pieces) :]
        sems, results, out_sems = refs[0], refs[1:-1], refs[-1]
        ha, ba = place_ref[0], place_ref[1]
        moves, count = [], 0
        for piece, views in enumerate(pieces):
            moves.append([])
            for term, view in enumerate(views):
                source = inputs[index_of[id(view.array)]]
                starts, rows = view.runs(ha, ba)
                for k, start in enumerate(starts):
                    target = buffers[piece].at[term, pl.ds(k * rows, rows), :]
                    move = pltpu.make_async_copy(source.at[pl.ds(start, rows), :], target, sems.at[count])
                    move.start()
                    moves[-1].append(move)
                    count += 1
        values, waited, leaving = [], set(), []
        for out, group in enumerate(groups):
            row = 0
            for views in group:
                piece = piece_of[id(views)]
                if piece not in waited:
                    waited.add(piece)
                    for move in moves[piece]:
                        move.wait()
                value = buffers[piece][0]
                for term in range(1, len(views)):
                    value = value + buffers[piece][term]
                if plain:
                    results[out][row : row + value.shape[0], :] = value
                values.append(value)
                row += value.shape[0]
            if plain:
                leaving.append(pltpu.make_async_copy(results[out], outs[out], out_sems.at[out]))
                leaving[-1].start()
        if not plain:
            epilogue(ha, ba, values, outs)
        for move in leaving:
            move.wait()

    moved = sum(view.size() for views in pieces for view in views) + sum(sizes)
    scratch = [pltpu.VMEM((len(views), views[0].size(), LANES), F32) for views in pieces]
    scratch.append(pltpu.SemaphoreType.DMA((copies,)))
    if plain:
        scratch += [pltpu.VMEM((size, LANES), F32) for size in sizes]
    scratch.append(pltpu.SemaphoreType.DMA((len(groups),)))
    return pl.pallas_call(
        kernel,
        in_specs=[in_smem()] + [in_hbm()] * (len(arrays) + len(ties)),
        out_specs=[in_hbm() if plain else pl.BlockSpec(memory_space=pltpu.VMEM)] * len(out_shape),
        out_shape=out_shape,
        scratch_shapes=scratch,
        compiler_params=params(),
        cost_estimate=lasting(1 + moved * LANES * 4 / 3.0e6),
    )(place, *arrays, *ties)


def tied(arrays, ties):
    return pl.pallas_call(
        lambda *refs: None,
        in_specs=[pl.BlockSpec(memory_space=pl.ANY)] * (len(arrays) + len(ties)),
        out_specs=[pl.BlockSpec(memory_space=pl.ANY)] * len(arrays),
        out_shape=[shape_of(*array.shape) for array in arrays],
        input_output_aliases={k: k for k in range(len(arrays))},
        compiler_params=params(),
        cost_estimate=lasting(0.5),
    )(*arrays, *ties)


class Sum:
    def __init__(self, arrays, names):
        self.views = []
        near = lax.axis_size("ha") // 4
        sizes = {"plane": lax.axis_size("ba"), "far": 2, "near": near}
        for array in arrays:
            flat = array.reshape(-1, LANES)
            stride, ways = flat.shape[0], []
            for name in names:
                stride //= sizes[name]
                ways.append((name, sizes[name], stride))
            self.views.append(View(flat, 0, ways, [], stride))

    def leaving(self, way, step):
        return [view.fix(way, step) for view in self.views]

    def keep(self, way, sent, arrived):
        self.views = [view.fix(way, 0) for view in self.views]
        rows = self.views[0].rows
        stride, ways = rows, []
        for name, size, _ in reversed(self.views[0].ways):
            ways.insert(0, (name, size, stride))
            stride *= size
        self.views += [View(array, start, ways, [], rows) for array, start in arrived]

    def part(self, first, rows):
        return [View(view.array, view.start + first, view.ways, view.fixed, rows) for view in self.views]


class Rider:
    def __init__(self, views):
        self.views = views

    def leaving(self, way, step):
        return self.views

    def keep(self, way, sent, arrived):
        rows = self.views[0].size()
        self.views = [View(array, start, [], [], rows) for array, start in [sent] + arrived]


class Gather(Rider):
    def keep(self, way, sent, arrived):
        rows = self.views[0].size()
        self.gathered = [[View(array, start, [], [], rows)] for array, start in [sent] + arrived]


class Stage:
    def __init__(self, members, way):
        self.members, self.way = members, way
        line, near = lax.axis_size("ha") // 2, lax.axis_size("ha") // 4
        self.steps = {
            "plane": list(range(1, lax.axis_size("ba"))),
            "line": list(range(1, line)),
            "far": [near],
        }[way]
        self.near = near

    def taking(self, step):
        takes = {"plane": True, "line": True, "near": step < self.near, "far": step == self.near}
        return [(one, way) for one, way in self.members if takes[way]]

    def groups(self):
        return [
            [one.leaving(way, step // self.near if way == "far" else step) for one, way in self.taking(step)]
            for step in self.steps
        ]

    def go(self, payloads, in_turn=None):
        axis, unit = ("ba", 1) if self.way == "plane" else ("ha", 2)
        arrived = []
        for step, part in zip(self.steps, payloads):
            if in_turn is not None and len(arrived) == 2:
                (part,) = tied([part], [arrived[in_turn]])
            arrived.append(exchange(part, axis, unit * step))
        places = {}
        for step, sent, part in zip(self.steps, payloads, arrived):
            row = 0
            for one, way in self.taking(step):
                places.setdefault(id(one), []).append(((sent, row), (part, row)))
                row += one.leaving(way, 1)[0].size()
        for one, way in self.members:
            mine = places.get(id(one), [])
            one.keep(way, mine[:2][-1][0] if mine else None, [part for _, part in mine])
        return arrived


def run(place, stage, ties=(), in_turn=None, late_ties=(), extra=()):
    groups = stage.groups()
    made = list(combine(place, groups + list(extra), ties))
    made, more = made[: len(groups)], made[len(groups) :]
    if late_ties:
        made = list(tied(made, late_ties))
    return made, stage.go(made, in_turn), more


def neighbour_rows(top, bottom):
    count = lax.axis_size("ha")
    up = [(i, i + 1) for i in range(count - 1)]
    down = [(i + 1, i) for i in range(count - 1)]
    return lax.ppermute(bottom, "ha", up), lax.ppermute(top, "ha", down)


def lay_beside(value, ref):
    tall, width = ref.shape
    for k in range(lane_blocks(width)):
        columns = slice(k * LANES, min(width, (k + 1) * LANES))
        ref[:, columns] = value[k * tall : (k + 1) * tall, : columns.stop - columns.start]


def lay_large(ha, ba, values, outs):
    up_first, up_second, down_first, down_second, out = values
    lay_beside(jnp.concatenate([up_first, up_second], axis=0), outs[0])
    lay_beside(jnp.concatenate([down_first, down_second], axis=0), outs[1])
    lay_beside(out, outs[2])


def lay_small(ha, ba, values, outs, blocks):
    din_ref, dk_ref, gain_ref = outs[:3]
    scratch = outs[-1]
    lay_beside(values[0], din_ref)
    count = lax.axis_size("ba")
    own, other = values[1 : 2 + count], values[2 + count :]
    mine = ha % 2 == 0
    dkern = jnp.concatenate([jnp.where(mine, own[0], other[0]), jnp.where(mine, other[0], own[0])], axis=0)
    joined = jnp.concatenate([dkern[k * TAPS : (k + 1) * TAPS] for k in range(blocks)], axis=1)
    dk_ref[...] = joined[:, joined.shape[1] - dk_ref.shape[1] :]
    part = own[1].shape[0]
    for side, parts in ((ha % 2, own[1:]), (1 - ha % 2, other[1:])):
        for step, rows in enumerate(parts):
            start = (side * count + (ba ^ step)) * part
            scratch[pl.ds(pl.multiple_of(start, 8), part), :] = rows
    dim = gain_ref.shape[1]
    for k in range(dim // LANES):
        columns = slice(k * LANES, (k + 1) * LANES)
        row = blocks * TAPS + k
        gain_ref[:, columns] = dkern[row : row + 1]
        for vector, ref in enumerate(outs[3:6]):
            ref[:, columns] = scratch[vector * dim // LANES + k : vector * dim // LANES + k + 1, :]
    row = scratch.shape[0]
    for ref in reversed(outs[6:-1]):
        tall, width = ref.shape
        row -= tall * width // LANES
        for k in range(width // LANES):
            ref[:, k * LANES : (k + 1) * LANES] = scratch[row + k * tall : row + (k + 1) * tall, :]


def shards(
    canvas,
    image_id,
    keep_first,
    keep_second,
    first_gain,
    weight_in,
    depth_kernel,
    gate_first,
    gate_second,
    gate_third,
    weight_out,
    scale_first,
    second_gain,
    weight_up,
    weight_down,
    scale_second,
    cotangent,
):
    _, rows, cols, dim = canvas.shape
    cells = rows * cols
    reach = REACH * cols
    count_ha, count_ba = lax.axis_size("ha"), lax.axis_size("ba")
    hidden = weight_up.shape[1]
    blocks = weight_in.shape[1] // LANES
    place = jnp.stack([lax.axis_index("ha"), lax.axis_index("ba")])
    own = canvas.reshape(cells, dim)
    gates = (gate_first, gate_second, gate_third)
    gain = first_gain[None]
    vectors = (gain, scale_first[None], second_gain[None], scale_second[None])
    ids = image_id[0]
    above, below = neighbour_rows(own[:reach], own[cells - reach :])
    ahead = head(place, ids, keep_first, keep_second, own, gain, weight_in, rows, cols)
    joined = ahead[0]
    (
        output, dmiddle, dconv, dconv_top, dconv_bottom, plane_kept, plane_sent, line_kept, line_sent,
        packed_kept, packed_sent,
    ) = forward(
        place, ids, ahead, above, own, below, cotangent.reshape(cells, dim), vectors,
        weight_in, depth_kernel, gates, weight_out, weight_up, weight_down, rows, cols, count_ha, count_ba,
    )
    above, below = neighbour_rows(dconv_top, dconv_bottom)

    plane_sum = Sum([plane_kept, exchange(plane_sent, "ha", 1)], ["plane", "far", "near"])
    line_sum = Sum([line_kept, exchange(line_sent, "ha", 1)], ["far", "near", "plane"])
    packed = Sum([packed_kept, exchange(packed_sent, "ha", 1)], ["plane"])
    made, arrived, _ = run(place, Stage([(plane_sum, "plane"), (packed, "plane")], "plane"))
    more, far, _ = run(place, Stage([(line_sum, "far")], "far"), ties=made, late_ties=[above, below])
    made, arrived = made + more, arrived + far
    dcanvas, in_kept, in_sent, small_kept, small_sent = backward(
        place, ids, above, dconv, below, joined, depth_kernel, own, gain, dmiddle, weight_in, made,
        rows, cols, count_ha, count_ba,
    )
    in_sent, small_sent = tied([in_sent, small_sent], arrived)
    in_sum = Sum([in_kept, exchange(in_sent, "ha", 1)], ["plane", "far", "near"])
    small = Rider([flat_view(small_kept), flat_view(exchange(small_sent, "ha", 1))])
    packed = Rider(packed.views)
    packed = Rider(packed.views)
    made, arrived, _ = run(
        place, Stage([(plane_sum, "far"), (line_sum, "near"), (packed, "line")], "line"), in_turn=0
    )
    run(place, Stage([(in_sum, "plane"), (small, "plane")], "plane"), ties=made)
    along = Stage([(plane_sum, "near"), (in_sum, "line"), (small, "line")], "line")
    made, arrived, (own_small,) = run(place, along, ties=arrived, in_turn=1, extra=[[small.views]])
    packed = Gather(packed.views)
    across = Stage([(line_sum, "plane"), (packed, "plane")], "plane")
    _, crossed, (own_packed,) = run(place, across, ties=made, extra=[[packed.views]])
    cut = plane_sum.views[0].rows // 2
    rest = (line_sum.views[0].rows - dim // count_ha * lane_blocks(dim // count_ba)) // 2
    dup, ddown, dout = combine(
        place,
        [
            [
                plane_sum.part(0, cut),
                line_sum.part(0, rest),
                plane_sum.part(cut, cut),
                line_sum.part(rest, rest),
                line_sum.part(2 * rest, line_sum.views[0].rows - 2 * rest),
            ]
        ],
        epilogue=lay_large,
        out_shape=[
            shape_of(dim // count_ba, hidden // count_ha),
            shape_of(dim // count_ha, hidden // count_ba),
            shape_of(dim // count_ha, dim // count_ba),
        ],
    )
    sent = list(tied([own_small, own_packed], arrived[1:2]))
    others = [exchange(part, "ha", 1) for part in sent + arrived + crossed]
    other_of = {id(part): other for part, other in zip(arrived + crossed, others[2:])}

    def from_other(view):
        return View(other_of[id(view.array)], view.start, view.ways, view.fixed, view.rows)

    own_parts = [small.views] + packed.gathered
    other_parts = [[flat_view(others[0])] + [from_other(view) for view in small.views[1:]], [flat_view(others[1])]]
    other_parts += [[from_other(view) for view in views] for views in packed.gathered[1:]]
    din, dkern, dgain_one, dscale_one, dgain_two, dscale_two, dfirst, dsecond, dthird, _ = combine(
        place,
        [[in_sum.views] + own_parts + other_parts],
        ties=[dup],
        epilogue=functools.partial(lay_small, blocks=blocks),
        out_shape=[shape_of(dim // count_ba, weight_in.shape[1] // count_ha), shape_of(*depth_kernel.shape)]
        + [shape_of(1, dim)] * 4
        + [shape_of(*gate.shape) for gate in gates]
        + [shape_of(packed_rows(gates, dim, count_ba), LANES)],
    )
    return (
        output.reshape(canvas.shape),
        dcanvas.reshape(canvas.shape),
        dgain_one[0],
        din,
        dkern,
        dfirst,
        dsecond,
        dthird,
        dout.T,
        dscale_one[0],
        dgain_two[0],
        dup,
        ddown.T,
        dscale_two[0],
    )


def solution(mesh):
    in_specs = (
        P("ba", "ha", None, None),
        P("ba", None, None),
        P("ba", None),
        P("ba", None),
    ) + (P(),) * 12 + (P("ba", "ha", None, None),)
    tiled = P("ba", "ha")
    out_specs = (
        P("ba", "ha", None, None),
        P("ba", "ha", None, None),
        P(),
        tiled,
        P(),
        P(),
        P(),
        P(),
        tiled,
        P(),
        P(),
        tiled,
        tiled,
        P(),
    )
    return jax.shard_map(shards, mesh=mesh, in_specs=in_specs, out_specs=out_specs, check_vma=False)
```

```python
import functools

import jax
import jax.numpy as jnp
from jax import lax
from jax.experimental import pallas as pl
from jax.experimental.pallas import tpu as pltpu
from jax.sharding import PartitionSpec as P

KERN = 7
TAPS = KERN * KERN
REACH = KERN // 2
KEEP_RATE = 0.8
SPREAD = 1.0 / 3.0
EPSILON = 1e-06
LANES = 128
EDGE = 8
VMEM_BYTES = 64 << 20
F32 = jnp.float32
INV_SQRT_2 = 0.7071067811865476
INV_SQRT_2PI = 0.3989422804014327
NN = (((1,), (0,)), ((), ()))
NT = (((1,), (1,)), ((), ()))
TN = (((0,), (0,)), ((), ()))


def dot(left, right, dims=NN):
    return lax.dot_general(left, right, dims, precision=lax.Precision.HIGH, preferred_element_type=F32)


def normalized(values):
    centered = values - jnp.mean(values, axis=-1, keepdims=True)
    scale = lax.rsqrt(jnp.mean(centered * centered, axis=-1, keepdims=True) + EPSILON)
    return centered * scale, scale


def norm_backward(grad_hat, hat, scale):
    return scale * (
        grad_hat
        - jnp.mean(grad_hat, axis=-1, keepdims=True)
        - hat * jnp.mean(grad_hat * hat, axis=-1, keepdims=True)
    )


def params():
    return pltpu.CompilerParams(vmem_limit_bytes=VMEM_BYTES)


def lasting(microseconds):
    return pl.CostEstimate(flops=int(microseconds * 1.1e9), bytes_accessed=0, transcendentals=0)


def whole(shape):
    return pl.BlockSpec(tuple(shape), lambda *_: (0,) * len(shape), pipeline_mode=pl.Buffered(1))


def in_smem():
    return pl.BlockSpec(memory_space=pltpu.SMEM)


def in_hbm():
    return pl.BlockSpec(memory_space=pltpu.HBM)


def shape_of(*shape):
    return jax.ShapeDtypeStruct(shape, F32)


def lane_blocks(width):
    return -(-width // LANES)


def image_ids(ids_ref, padded, place, rows):
    height, cols = ids_ref.shape
    padded[...] = jnp.full(padded.shape, -1, jnp.int32)
    padded[EDGE : EDGE + height, :] = ids_ref[...]
    ids = padded[pl.ds(place * rows + (EDGE - REACH), rows + 2 * REACH), :]
    return jnp.concatenate([ids, jnp.full((-ids.shape[0] % 8, cols), -1, jnp.int32)], axis=0).T


def spread_cells(factors, out_ref, first, rows):
    cols = factors.shape[0]
    for r in range(rows):
        column = factors[:, first + r : first + r + 1]
        out_ref[r * cols : (r + 1) * cols, :] = jnp.broadcast_to(column, (cols, LANES))


def keep_factors(turned, table_ref):
    result = jnp.zeros(turned.shape, F32)
    for slot in range(table_ref.shape[1]):
        result = jnp.where(turned == slot, table_ref[0, slot].astype(F32) / KEEP_RATE, result)
    return result


def conv_masks(ids_scalar, ids_ref, place, row_taps, col_mask, rows):
    height, cols = ids_ref.shape
    column_masks(ids_ref, col_mask)
    row_masks(ids_scalar, place, row_taps, rows, height, cols)


def column_masks(ids_ref, col_mask):
    height, cols = ids_ref.shape
    wide_ids = jnp.broadcast_to(ids_ref[...].T[:, height // 2 : height // 2 + 1], (cols, LANES))
    column = lax.broadcasted_iota(jnp.int32, (cols, LANES), 0)
    for b in range(KERN):
        shift = b - REACH
        moved = pltpu.roll(wide_ids, (-shift) % cols, 0)
        inside = (column + shift >= 0) & (column + shift < cols)
        same = (moved == wide_ids) & inside
        col_mask[b] = same.astype(F32).reshape(cols // 8, 8, LANES)


def row_masks(ids_scalar, place, row_taps, rows, height, cols):
    def one(r, _):
        own = ids_scalar[place * rows + r, cols // 2]
        row_taps[r, 0] = KERN
        row_taps[r, KERN + 1] = KERN
        for a in range(KERN):
            other = place * rows + r + a - REACH
            inside = (other >= 0) & (other < height)
            same = ids_scalar[jnp.clip(other, 0, height - 1), cols // 2] == own
            row_taps[r, a + 1] = jnp.where(inside & same, a, KERN)
        return 0

    lax.fori_loop(0, rows, one, 0)


def lay_kernel(kern_ref, laid, split):
    tap = lax.broadcasted_iota(jnp.int32, (TAPS, split), 0)
    own = jnp.where(tap == TAPS // 2, 1.0 / SPREAD, 0.0).astype(F32)
    for k in range(laid.shape[0]):
        start = k * LANES - split
        left = own if k == 0 else kern_ref[:, start : start + split]
        laid[k] = jnp.concatenate([left, kern_ref[:, start + split : start + LANES]], axis=1) * SPREAD


def fill_shifted(flat, col_ref, shifted, rows_ext, cols):
    for b in range(KERN):
        for g in range(cols // 8):
            mask = None if b == REACH else col_ref[b, g]
            for r in range(rows_ext):
                x = flat[pl.ds(EDGE + r * cols + 8 * g + b - REACH, 8), :]
                shifted[b, r, g] = x if b == REACH else x * mask


def spread_taps(kern, wide, turned):
    for t in range(TAPS):
        source = TAPS - 1 - t if turned else t
        wide[t] = jnp.broadcast_to(kern[source : source + 1, :], (8, LANES))
    for t in range(KERN):
        wide[TAPS + t] = jnp.zeros((8, LANES), F32)


def conv_block(row_taps, kern, shifted, wide, out_ref, rows, cols):
    groups = cols // 8
    spread_taps(kern, wide, False)

    def pair(h, _):
        r = 2 * h

        def step(i, totals):
            first, second = totals
            taps_first = row_taps[r, i + 1] * KERN
            taps_second = row_taps[r + 1, i] * KERN
            for b in range(KERN):
                x = shifted[b, r + i]
                first = first + wide[taps_first + b][None] * x
                second = second + wide[taps_second + b][None] * x
            return first, second

        zero = jnp.zeros((groups, 8, LANES), F32)
        first, second = lax.fori_loop(0, KERN + 1, step, (zero, zero), unroll=4)
        out_ref[pl.ds(pl.multiple_of(r * cols, cols), cols), :] = first.reshape(cols, LANES)
        out_ref[pl.ds(pl.multiple_of((r + 1) * cols, cols), cols), :] = second.reshape(cols, LANES)
        return 0

    lax.fori_loop(0, rows // 2, pair, 0)


def conv_grad_block(row_taps, kern, shifted, wide, dk, mix_ref, out_ref, dk_ref, rows, cols):
    groups = cols // 8
    spread_taps(kern, wide, True)
    for t in range(TAPS):
        dk[t] = jnp.zeros((8, LANES), F32)

    def one(r, _):
        start = pl.ds(pl.multiple_of(r * cols, cols), cols)
        mix = mix_ref[start, :].reshape(groups, 8, LANES)
        total = jnp.zeros((groups, 8, LANES), F32)
        for i in range(KERN):
            row = row_taps[r, i + 1]
            same = jnp.where(row < KERN, 1.0, 0.0).astype(F32)
            for b in range(KERN):
                x = shifted[b, r + i]
                total = total + wide[row * KERN + b][None] * x
                dk[i * KERN + b] += jnp.sum(mix * x, axis=0) * same
        out_ref[start, :] = total.reshape(cols, LANES)
        return 0

    lax.fori_loop(0, rows, one, 0)
    for t in range(TAPS):
        dk_ref[TAPS - 1 - t : TAPS - t, :] = jnp.sum(dk[t], axis=0, keepdims=True) * SPREAD
    dk_ref[TAPS:, :] = jnp.zeros((dk_ref.shape[0] - TAPS, LANES), F32)


def share(core, first, second, kept_ref, sent_ref, z, p):
    mine = core == 0
    tall, width = first.shape
    for ref, chunk in (
        (kept_ref, jnp.where(mine, first, second)),
        (sent_ref, jnp.where(mine, second, first)),
    ):
        for k in range(lane_blocks(width)):
            part = chunk[:, k * LANES : (k + 1) * LANES]
            if part.shape[1] < LANES:
                part = jnp.concatenate([part, jnp.zeros((tall, LANES - part.shape[1]), F32)], axis=1)
            ref[z, p, k * tall : (k + 1) * tall, :] = part


def share_columns(core, grad, kept_ref, sent_ref, width, plane_first=False):
    groups, parts = reversed(kept_ref.shape[:2]) if plane_first else kept_ref.shape[:2]
    tall = grad.shape[0] // parts
    for z in range(groups):
        for p in range(parts):
            rows = slice(p * tall, (p + 1) * tall)
            first = grad[rows, 2 * z * width : (2 * z + 1) * width]
            second = grad[rows, (2 * z + 1) * width : (2 * z + 2) * width]
            share(core, first, second, kept_ref, sent_ref, *((p, z) if plane_first else (z, p)))


def share_rows(core, grad, kept_ref, sent_ref, tall):
    groups, parts = kept_ref.shape[:2]
    width = grad.shape[1] // parts
    for z in range(groups):
        for p in range(parts):
            columns = slice(p * width, (p + 1) * width)
            first = grad[2 * z * tall : (2 * z + 1) * tall, columns]
            second = grad[(2 * z + 1) * tall : (2 * z + 2) * tall, columns]
            share(core, first, second, kept_ref, sent_ref, z, p)


class Copies:
    def __init__(self, sems):
        self.sems, self.count, self.pending = sems, 0, {}

    def start(self, name, source, target):
        copy = pltpu.make_async_copy(source, target, self.sems.at[self.count])
        self.count += 1
        copy.start()
        self.pending.setdefault(name, []).append(copy)

    def wait(self, *names):
        for name in names:
            for copy in self.pending.pop(name):
                copy.wait()

    def wait_all(self):
        self.wait(*list(self.pending))


def head_kernel(
    place_ref, ids_scalar, one_table, two_table, ids_hbm, own_hbm, gain_hbm, in_hbm_ref,
    joined_hbm, valid_hbm, one_keep_hbm, two_keep_hbm, col_hbm,
    ids_ref, rows_ref, gain_ref, in_ref, padded, valid_ref, one_keep_ref, two_keep_ref, col_ref, normed, joined, sems,
    *, rows, cols,
):
    cells = rows * cols
    reach = REACH * cols
    steps = in_ref.shape[0]
    copies = Copies(sems)
    copies.start("ids", ids_hbm, ids_ref)
    copies.start("own", own_hbm, rows_ref)
    copies.start("own", gain_hbm, gain_ref)
    for k in range(steps):
        copies.start(("in", k), in_hbm_ref.at[:, pl.ds(2 * LANES * k, 2 * LANES)], in_ref.at[k])
    copies.wait("ids")
    turned = image_ids(ids_ref, padded, place_ref[0], rows)
    spread_cells((turned >= 0).astype(F32), valid_ref, 0, rows + 2 * REACH)
    spread_cells(keep_factors(turned, one_table), one_keep_ref, REACH, rows)
    spread_cells(keep_factors(turned, two_table), two_keep_ref, REACH, rows)
    column_masks(ids_ref, col_ref)
    for source, target in (
        (valid_ref, valid_hbm), (one_keep_ref, one_keep_hbm), (two_keep_ref, two_keep_hbm), (col_ref, col_hbm)
    ):
        copies.start("outs", source, target)
    copies.wait("own")
    hat, _ = normalized(rows_ref[...] * valid_ref[reach : reach + cells, :1])
    normed[...] = hat * gain_ref[...]
    for step in range(steps):
        copies.wait(("in", step))
        part = dot(normed[...], in_ref[step])
        for k in range(2):
            joined[2 * step + k] = part[:, k * LANES : (k + 1) * LANES]
        pair = pl.ds(2 * step, 2)
        copies.start("outs", joined.at[pair], joined_hbm.at[pair])
    copies.wait_all()


def head(place, ids, keep_one, keep_two, own, gain, weight_in, rows, cols):
    cells, dim = own.shape
    cells_ext = cells + 2 * REACH * cols
    blocks = weight_in.shape[1] // LANES
    vmem = functools.partial(pltpu.VMEM, dtype=F32)
    shapes = [
        (blocks, cells, LANES), (cells_ext, LANES), (cells, LANES), (cells, LANES), (KERN, cols // 8, 8, LANES)
    ]
    return pl.pallas_call(
        functools.partial(head_kernel, rows=rows, cols=cols),
        in_specs=[in_smem()] * 4 + [in_hbm()] * 4,
        out_specs=[in_hbm()] * len(shapes),
        out_shape=[shape_of(*shape) for shape in shapes],
        scratch_shapes=[
            pltpu.VMEM(ids.shape, jnp.int32),
            vmem((cells, dim)),
            vmem((1, dim)),
            vmem((blocks // 2, dim, 2 * LANES)),
            pltpu.VMEM((ids.shape[0] + 2 * EDGE, ids.shape[1]), jnp.int32),
        ]
        + [vmem(shape) for shape in shapes[1:]]
        + [vmem((cells, dim)), vmem(shapes[0]), pltpu.SemaphoreType.DMA((7 + blocks,))],
        compiler_params=params(),
        cost_estimate=lasting(7),
    )(place, ids, keep_one, keep_two, ids, own, gain, weight_in)


def forward_kernel(
    place_ref, ids_scalar, joined_hbm, valid_hbm, one_keep_hbm, two_keep_hbm, col_hbm, above_hbm, own_hbm, below_hbm, cot_hbm,
    first_gain_hbm, first_scale_hbm, second_gain_hbm, second_scale_hbm,
    in_hbm_ref, kern_hbm, one_hbm, two_hbm, three_hbm, out_hbm, up_hbm, down_hbm,
    output_hbm, dmiddle_hbm, dconv_hbm, dconv_top_hbm, dconv_bottom_hbm,
    plane_kept_ref, plane_sent_ref, line_kept_ref, line_sent_ref, packed_kept_hbm, packed_sent_hbm,
    rows_ref, cot_ref, first_gain_ref, first_scale_ref, second_gain_ref, second_scale_ref,
    in_ref, kern_ref, one_ref, two_ref, three_ref, out_ref, up_ref, down_ref, dconv_ref, sems, chunk_sems,
    up_kept, up_sent, down_kept, down_sent, out_kept, out_sent,
    row_taps, valid_ref, one_keep_ref, two_keep_ref, col_ref, packed_ref, normed, flat, shifted, laid, wide, conv,
    mixed_ref, mapped_ref, middle_ref, result, dnorm,
    *, rows, cols, count_ha, count_ba,
):
    blocks = flat.shape[0]
    cells = rows * cols
    reach = REACH * cols
    cells_ext = cells + 2 * reach
    core = place_ref[0] % 2
    split = one_ref.shape[0]
    dim = rows_ref.shape[1]
    head_steps = blocks // 2
    ffn_steps = up_kept.shape[0]
    chunk = down_ref.shape[1]
    gate_refs = (one_ref, two_ref, three_ref)

    copies = Copies(sems)
    copies.start("rows", valid_hbm, valid_ref)
    copies.start("rows", first_gain_hbm, first_gain_ref)
    copies.start("above", above_hbm, rows_ref.at[pl.ds(0, reach)])
    copies.start("below", below_hbm, rows_ref.at[pl.ds(reach + cells, reach)])
    for k in range(head_steps):
        copies.start(("in", k), in_hbm_ref.at[:, pl.ds(2 * LANES * k, 2 * LANES)], in_ref.at[k])
    copies.start("conv", joined_hbm, flat.at[:, pl.ds(EDGE + reach, cells), :])
    copies.start("conv", col_hbm, col_ref)
    copies.start("gates", own_hbm, rows_ref.at[pl.ds(reach, cells)])
    copies.start("gates", one_keep_hbm, one_keep_ref)
    copies.start("gates", two_keep_hbm, two_keep_ref)
    copies.start("kern", kern_hbm, kern_ref)
    def weights(k):
        ends = pl.ds(pl.multiple_of(k * chunk, chunk), chunk)
        return [
            pltpu.make_async_copy(up_hbm.at[:, ends], up_ref.at[k], chunk_sems.at[k, 0]),
            pltpu.make_async_copy(down_hbm.at[ends, :], down_ref.at[k], chunk_sems.at[k, 1]),
        ]

    def chunk_copies(place):
        moves = []
        sides = ((up_kept, down_kept, plane_kept_ref, line_kept_ref), (up_sent, down_sent, plane_sent_ref, line_sent_ref))
        for up, down, plane, line in sides:
            cut = plane.shape[2] // 2
            rest = up.shape[3] - cut
            zs = pl.ds(place * up.shape[1], up.shape[1])
            bas = pl.ds(place * down.shape[2], down.shape[2])
            moves += [
                (up.at[place, :, ba, pl.ds(0, cut), :], plane.at[ba, zs, pl.ds(0, cut), :])
                for ba in range(plane.shape[0])
            ]
            moves += [
                (down.at[place, z, :, pl.ds(0, cut), :], plane.at[bas, z, pl.ds(cut, cut), :])
                for z in range(plane.shape[1])
            ]
            moves.append((up.at[place, :, :, pl.ds(cut, rest), :], line.at[zs, :, pl.ds(0, rest), :]))
            moves.append((down.at[place, :, :, pl.ds(cut, rest), :], line.at[:, bas, pl.ds(rest, rest), :]))
        return [
            pltpu.make_async_copy(source, target, chunk_sems.at[place, 2 + k])
            for k, (source, target) in enumerate(moves)
        ]

    row_masks(ids_scalar, place_ref[0], row_taps, rows, ids_scalar.shape[0], cols)
    copies.wait("rows")
    for name, start, place in (("above", 0, 0), ("below", reach + cells, reach)):
        copies.wait(name)
        hat, _ = normalized(rows_ref[start : start + reach, :] * valid_ref[start : start + reach, :1])
        normed[place : place + reach] = hat * first_gain_ref[...]

    for k in range(blocks):
        flat[k, :EDGE] = jnp.zeros((EDGE, LANES), F32)
        flat[k, EDGE + cells_ext :] = jnp.zeros((EDGE, LANES), F32)
    for step in range(head_steps):
        copies.wait(("in", step))
        joined = dot(normed[: 2 * reach], in_ref[step])
        for k in range(2):
            part = joined[:, k * LANES : (k + 1) * LANES]
            flat[2 * step + k, EDGE : EDGE + reach] = part[:reach]
            flat[2 * step + k, EDGE + reach + cells : EDGE + cells_ext] = part[reach:]
        if step == 0:
            copies.start("gates", first_scale_hbm, first_scale_ref)
            copies.start("gates", second_gain_hbm, second_gain_ref)
            copies.start("gates", second_scale_hbm, second_scale_ref)
            for source, target in zip((one_hbm, two_hbm, three_hbm, out_hbm, cot_hbm), gate_refs + (out_ref, cot_ref)):
                copies.start("gates", source, target)
            for k in range(ffn_steps):
                for copy in weights(k):
                    copy.start()

    copies.wait("conv")
    copies.wait("kern")
    lay_kernel(kern_ref, laid, split)

    def conv_step(block, _):
        fill_shifted(flat.at[block], col_ref, shifted, rows + 2 * REACH, cols)
        conv_block(row_taps, laid[block], shifted, wide, conv.at[block], rows, cols)
        return 0

    lax.fori_loop(0, blocks, conv_step, 0)

    def conv_part(start, width):
        return jnp.concatenate([conv[start // LANES + k] for k in range(width // LANES)], axis=1)

    copies.wait("gates")
    mixed = conv[0, :, :split] * conv[0, :, split:]
    mixed_ref[:, :split] = mixed
    start = 2 * split
    for ref in gate_refs:
        width = ref.shape[1]
        mapped = dot(mixed, ref[...])
        mapped_ref[:, start - 2 * split : start - 2 * split + width] = mapped
        mixed = mapped * conv_part(start, width)
        mixed_ref[:, start : start + width] = mixed
        start += width
    branch = dot(mixed, out_ref[...])
    masked = rows_ref[reach : reach + cells, :] * valid_ref[reach : reach + cells, :1]
    middle = masked + one_keep_ref[:, :1] * first_scale_ref[...] * branch
    middle_ref[...] = middle
    hat, _ = normalized(middle)
    normed[:cells] = hat * second_gain_ref[...]
    result[...] = jnp.zeros_like(result)
    dnorm[...] = jnp.zeros_like(dnorm)

    def ffn_step(place, _):
        for copy in weights(place):
            copy.wait()
        grad_result = two_keep_ref[:, :1] * second_scale_ref[...] * cot_ref[...]
        pre = dot(normed[:cells], up_ref[place])
        cdf = 0.5 + 0.5 * lax.erf(pre * INV_SQRT_2)
        slope = cdf + pre * (INV_SQRT_2PI * jnp.exp(-0.5 * pre * pre))
        hidden = pre * cdf
        result[...] += dot(hidden, down_ref[place])
        grad_pre = dot(grad_result, down_ref[place], NT) * slope
        share_rows(
            core, dot(grad_result, hidden, TN), down_kept.at[place], down_sent.at[place], dim // count_ha
        )
        width = chunk // (2 * up_kept.shape[1])
        share_columns(core, dot(normed[:cells], grad_pre, TN), up_kept.at[place], up_sent.at[place], width)
        for copy in chunk_copies(place):
            copy.start()
        dnorm[...] += dot(grad_pre, up_ref[place], NT)
        return 0

    lax.fori_loop(0, ffn_steps, ffn_step, 0)

    hat, scale = normalized(middle_ref[...])
    kept = two_keep_ref[:, :1] * result[...]
    dscale_two = jnp.sum(cot_ref[...] * kept, axis=0, keepdims=True)
    result[...] = middle_ref[...] + second_scale_ref[...] * kept
    copies.start("outs", result, output_hbm)
    dgain_two = jnp.sum(dnorm[...] * hat, axis=0, keepdims=True)
    dmiddle = cot_ref[...] + norm_backward(dnorm[...] * second_gain_ref[...], hat, scale)
    dnorm[...] = dmiddle
    copies.start("outs", dnorm, dmiddle_hbm)
    kept = one_keep_ref[:, :1] * dmiddle
    grad = dot(kept * first_scale_ref[...], out_ref[...], NT)
    row = packed_ref.shape[0]
    start = blocks * LANES
    for ref in reversed(gate_refs):
        tall, width = ref.shape
        start -= width
        source = start - tall if tall > split else 0
        columns = slice(start - 2 * split, start - 2 * split + width)
        dconv = grad * mapped_ref[:, columns]
        for k in range(width // LANES):
            dconv_ref[start // LANES + k] = dconv[:, k * LANES : (k + 1) * LANES]
        grad_mapped = grad * conv_part(start, width)
        part = dot(mixed_ref[:, source : source + tall], grad_mapped, TN)
        row -= tall * width // LANES
        for k in range(width // LANES):
            packed_ref[row + k * tall : row + (k + 1) * tall] = part[:, k * LANES : (k + 1) * LANES]
        grad = dot(grad_mapped, ref[...], NT)
    dconv_ref[0] = jnp.concatenate([grad * conv[0, :, split:], grad * conv[0, :, :split]], axis=1)
    copies.start("outs", dconv_ref.at[:, pl.ds(0, reach), :], dconv_top_hbm)
    copies.start("outs", dconv_ref.at[:, pl.ds(cells - reach, reach), :], dconv_bottom_hbm)
    copies.start("outs", dconv_ref, dconv_hbm)
    start = mixed_ref.shape[1] - out_ref.shape[0]
    crossed = dot(mixed_ref[:, start:], kept, TN)
    dscale_one = jnp.sum(crossed * out_ref[...], axis=0, keepdims=True)
    packed_ref[:row] = jnp.zeros((row, LANES), F32)
    row = 0
    for vector in (dscale_one, dgain_two, dscale_two):
        for k in range(dim // LANES):
            packed_ref[row : row + 1] = vector[:, k * LANES : (k + 1) * LANES]
            row += 1
    half = packed_kept_hbm.shape[0]
    for place, target in ((core, packed_kept_hbm), (1 - core, packed_sent_hbm)):
        copies.start("outs", packed_ref.at[pl.ds(pl.multiple_of(place * half, 8), half), :], target)
    share_rows(core, (crossed * first_scale_ref[...]).T, out_kept, out_sent, dim // count_ha)
    for source, line in ((out_kept, line_kept_ref), (out_sent, line_sent_ref)):
        tall = source.shape[2]
        copies.start("outs", source, line.at[:, :, pl.ds(line.shape[2] - tall, tall), :])
    for place in range(ffn_steps):
        for copy in chunk_copies(place):
            copy.wait()
    copies.wait_all()


def mask_scratch(ids, rows):
    height, cols = ids.shape
    return [
        pltpu.SMEM((rows, KERN + 2), jnp.int32),
        pltpu.VMEM((height + 2 * EDGE, cols), jnp.int32),
        pltpu.VMEM(((rows + 2 * REACH) * cols, LANES), F32),
    ]


def packed_rows(gates, dim, parts):
    rows = sum(gate.size for gate in gates) // LANES + 3 * dim // LANES
    return -(-rows // (16 * parts)) * 16 * parts


def plane_share(rows):
    return max(rows * 3 // 4 // 8 * 8, 8)


def forward(
    place, ids, ahead, above, own, below, cot, vectors, weight_in, kern, gates,
    weight_out, weight_up, weight_down, rows, cols, count_ha, count_ba, chunk=512,
):
    cells, dim = own.shape
    reach = above.shape[0]
    blocks = weight_in.shape[1] // LANES
    hidden = weight_up.shape[1]
    split = gates[0].shape[0]
    wide = blocks * LANES
    head_steps = blocks // 2
    ffn_steps = hidden // chunk

    up_wide, down_wide = hidden // count_ha, hidden // count_ba
    up_rows = dim // count_ba * lane_blocks(up_wide)
    down_rows = dim // count_ha * lane_blocks(down_wide)
    out_rows = dim // count_ha * lane_blocks(dim // count_ba)
    half = count_ha // 2
    assert up_rows == down_rows
    cut = plane_share(up_rows)
    rest = up_rows - cut
    plane = (count_ba, half, 2 * cut, LANES)
    line = (half, count_ba, 2 * rest + out_rows, LANES)
    packed_shape = (packed_rows(gates, dim, count_ba), LANES)
    half_packed = (packed_shape[0] // 2, LANES)
    cells_ext = cells + 2 * reach
    vmem = functools.partial(pltpu.VMEM, dtype=F32)
    operands = (
        place, ids, *ahead, above, own, below, cot, *vectors,
        weight_in, kern, *gates, weight_out, weight_up, weight_down,
    )
    out_shape = [
        shape_of(cells, dim),
        shape_of(cells, dim),
        shape_of(blocks, cells, LANES),
        shape_of(blocks, reach, LANES),
        shape_of(blocks, reach, LANES),
        shape_of(*plane),
        shape_of(*plane),
        shape_of(*line),
        shape_of(*line),
        shape_of(*half_packed),
        shape_of(*half_packed),
    ]
    return pl.pallas_call(
        functools.partial(forward_kernel, rows=rows, cols=cols, count_ha=count_ha, count_ba=count_ba),
        in_specs=[in_smem()] * 2 + [in_hbm()] * (len(operands) - 2),
        out_specs=[in_hbm()] * len(out_shape),
        out_shape=out_shape,
        scratch_shapes=[vmem((cells_ext, dim)), vmem((cells, dim))]
        + [vmem((1, dim))] * 4
        + [vmem((head_steps, dim, 2 * LANES)), vmem(kern.shape)]
        + [vmem(gate.shape) for gate in gates]
        + [
            vmem(weight_out.shape),
            vmem((ffn_steps, dim, chunk)),
            vmem((ffn_steps, chunk, dim)),
            vmem((blocks, cells, LANES)),
            pltpu.SemaphoreType.DMA((40 + head_steps,)),
            pltpu.SemaphoreType.DMA((ffn_steps, 2 + 2 * (count_ba + half + 2))),
        ]
        + [vmem((ffn_steps, chunk // (2 * up_wide), count_ba, up_rows, LANES))] * 2
        + [vmem((ffn_steps, half, chunk // down_wide, down_rows, LANES))] * 2
        + [vmem((half, count_ba, out_rows, LANES))] * 2
        + [
            pltpu.SMEM((rows, KERN + 2), jnp.int32),
            vmem((cells_ext, LANES)),
            vmem((cells, LANES)),
            vmem((cells, LANES)),
            vmem((KERN, cols // 8, 8, LANES)),
            vmem(packed_shape),
            vmem((max(cells, 2 * reach), dim)),
            vmem((blocks, cells_ext + 2 * EDGE, LANES)),
            vmem((KERN, rows + 2 * REACH, cols // 8, 8, LANES)),
            vmem((blocks, TAPS, LANES)),
            vmem((TAPS + KERN, 8, LANES)),
            vmem((blocks, cells, LANES)),
            vmem((cells, wide)),
            vmem((cells, wide - 2 * split)),
            vmem((cells, dim)),
            vmem((cells, dim)),
            vmem((cells, dim)),
        ],
        compiler_params=params(),
        cost_estimate=lasting(48),
    )(*operands)


def lay_flat(above_ref, own_ref, below_ref, flat):
    reach, cells = above_ref.shape[1], own_ref.shape[1]
    flat[:EDGE] = jnp.zeros((EDGE, LANES), F32)
    flat[EDGE : EDGE + reach] = above_ref[0]
    flat[EDGE + reach : EDGE + reach + cells] = own_ref[0]
    flat[EDGE + reach + cells : EDGE + 2 * reach + cells] = below_ref[0]
    flat[EDGE + 2 * reach + cells :] = jnp.zeros((EDGE, LANES), F32)


def backward_kernel(
    place_ref, ids_scalar, ids_ref, above_ref, own_ref, below_ref, mix_ref, kern_ref, canvas_ref, gain_ref,
    dmiddle_ref, in_ref, *rest, rows, cols,
):
    dcanvas_ref, kept_ref, sent_ref, small_kept_ref, small_sent_ref = rest[-19:-14]
    row_taps, padded, valid_ref, col_ref, flat, shifted, laid, wide, dk, sums, small, djoined, normed, dnorm = rest[-14:]
    step = pl.program_id(0)
    cells = rows * cols
    reach = REACH * cols
    core = place_ref[0] % 2
    split = laid.shape[0] * LANES - kern_ref.shape[1]
    width = in_ref.shape[1] // (2 * kept_ref.shape[1])

    @pl.when(step == 0)
    def _():
        lay_kernel(kern_ref, laid, split)
        turned = image_ids(ids_ref, padded, place_ref[0], rows)
        spread_cells((turned >= 0).astype(F32), valid_ref, 0, rows + 2 * REACH)
        conv_masks(ids_scalar, ids_ref, place_ref[0], row_taps, col_ref, rows)
        hat, _ = normalized(canvas_ref[...] * valid_ref[reach : reach + cells, :1])
        normed[...] = hat * gain_ref[...]
        dnorm[...] = jnp.zeros_like(dnorm)

    lay_flat(above_ref, own_ref, below_ref, flat)
    fill_shifted(flat, col_ref, shifted, rows + 2 * REACH, cols)
    conv_grad_block(
        row_taps, laid[step], shifted, wide, dk, mix_ref.at[0], djoined.at[step % 2], sums.at[step], rows, cols
    )

    @pl.when(step % 2 == 1)
    def _():
        grad = jnp.concatenate([djoined[0], djoined[1]], axis=1)
        share_columns(core, dot(normed[...], grad, TN), kept_ref, sent_ref, width, plane_first=True)
        dnorm[...] += dot(grad, in_ref[...], NT)

    @pl.when(step == pl.num_programs(0) - 1)
    def _():
        hat, scale = normalized(canvas_ref[...] * valid_ref[reach : reach + cells, :1])
        dgain = jnp.sum(dnorm[...] * hat, axis=0, keepdims=True)
        row = sums.shape[0] * TAPS
        for k in range(sums.shape[0]):
            small[k * TAPS : (k + 1) * TAPS, :] = sums[k, :TAPS]
        small[row:, :] = jnp.zeros((small.shape[0] - row, LANES), F32)
        for k in range(dgain.shape[1] // LANES):
            small[row + k : row + k + 1, :] = dgain[:, k * LANES : (k + 1) * LANES]
        half = small.shape[0] // 2
        for ref, start in ((small_kept_ref, core * half), (small_sent_ref, (1 - core) * half)):
            ref[...] = small[pl.ds(pl.multiple_of(start, 8), half), :]
        inner = dmiddle_ref[...] + norm_backward(dnorm[...] * gain_ref[...], hat, scale)
        dcanvas_ref[...] = inner * valid_ref[reach : reach + cells, :1]


def block_of(size):
    return pl.BlockSpec((1, size, LANES), lambda i: (i, 0, 0))


def small_rows(blocks, dim):
    return -(-(blocks * TAPS + dim // LANES) // 16) * 16


def backward(
    place, ids, above, own, below, mix, kern, canvas, gain, dmiddle, weight_in, ties, rows, cols, count_ha, count_ba
):
    cells, dim = canvas.shape
    blocks = own.shape[0]
    reach = above.shape[1]
    own_wide = weight_in.shape[1] // count_ha
    chunk_rows = dim // count_ba * lane_blocks(own_wide)
    groups = 2 * LANES // (2 * own_wide)
    chunk_spec = pl.BlockSpec((count_ba, groups, chunk_rows, LANES), lambda i: (0, i // 2, 0, 0))
    chunks = shape_of(count_ba, count_ha // 2, chunk_rows, LANES)
    tall = -(-TAPS // 8) * 8
    small = (small_rows(blocks, dim) // 2, LANES)
    return pl.pallas_call(
        functools.partial(backward_kernel, rows=rows, cols=cols),
        grid=(blocks,),
        in_specs=[in_smem(), in_smem(), whole(ids.shape)]
        + [block_of(size) for size in (reach, cells, reach, cells)]
        + [whole(kern.shape), whole(canvas.shape)]
        + [whole((1, dim)), whole((cells, dim))]
        + [pl.BlockSpec((dim, 2 * LANES), lambda i: (0, i // 2))]
        + [in_hbm()] * len(ties),
        out_specs=[whole((cells, dim)), chunk_spec, chunk_spec, whole(small), whole(small)],
        out_shape=[shape_of(cells, dim), chunks, chunks, shape_of(*small), shape_of(*small)],
        scratch_shapes=mask_scratch(ids, rows)
        + [
            pltpu.VMEM((KERN, cols // 8, 8, LANES), F32),
            pltpu.VMEM((cells + 2 * reach + 2 * EDGE, LANES), F32),
            pltpu.VMEM((KERN, rows + 2 * REACH, cols // 8, 8, LANES), F32),
            pltpu.VMEM((blocks, TAPS, LANES), F32),
            pltpu.VMEM((TAPS + KERN, 8, LANES), F32),
            pltpu.VMEM((TAPS, 8, LANES), F32),
            pltpu.VMEM((blocks, tall, LANES), F32),
            pltpu.VMEM((small_rows(blocks, dim), LANES), F32),
            pltpu.VMEM((2, cells, LANES), F32),
            pltpu.VMEM((cells, dim), F32),
            pltpu.VMEM((cells, dim), F32),
        ],
        compiler_params=params(),
        cost_estimate=lasting(25),
    )(place, ids, ids, above, own, below, mix, kern, canvas, gain, dmiddle, weight_in, *ties)


def exchange(values, axis, bit):
    return lax.ppermute(values, axis, [(i, i ^ bit) for i in range(lax.axis_size(axis))])


class View:
    def __init__(self, array, start, ways, fixed, rows):
        self.array, self.start, self.ways, self.fixed, self.rows = array, start, ways, fixed, rows

    def fix(self, way, step):
        if way == "line":
            near = lax.axis_size("ha") // 4
            return self.fix("far", step // near).fix("near", step % near)
        left = [entry for entry in self.ways if entry[0] != way]
        (stride,) = [entry[2] for entry in self.ways if entry[0] == way]
        return View(self.array, self.start, left, self.fixed + [(way, step, stride)], self.rows)

    def size(self):
        count = self.rows
        for _, size, _ in self.ways:
            count *= size
        return count

    def runs(self, ha, ba):
        start = self.start
        near = lax.axis_size("ha") // 4
        places = {"plane": ba, "far": ha // 2 // near, "near": ha // 2 % near}
        for way, step, stride in self.fixed:
            start = start + (places[way] ^ step) * stride
        rows, ways = self.rows, list(self.ways)
        while ways and ways[-1][2] == rows:
            rows *= ways.pop()[1]
        offsets = [0]
        for _, size, stride in ways:
            offsets = [offset + k * stride for offset in offsets for k in range(size)]
        return [pl.multiple_of(start + offset, 8) for offset in offsets], rows


def flat_view(array, start=0, rows=None):
    flat = array.reshape(-1, LANES)
    return View(flat, start, [], [], flat.shape[0] if rows is None else rows)


def combine(place, groups, ties=(), epilogue=None, out_shape=None):
    pieces, arrays = [], []
    for group in groups:
        for views in group:
            if not any(views is other for other in pieces):
                pieces.append(views)
    for views in pieces:
        for view in views:
            if not any(view.array is other for other in arrays):
                arrays.append(view.array)
    index_of = {id(array): k for k, array in enumerate(arrays)}
    piece_of = {id(views): k for k, views in enumerate(pieces)}
    sizes = [sum(views[0].size() for views in group) for group in groups]
    copies = sum(len(view.runs(0, 0)[0]) for views in pieces for view in views)
    plain = epilogue is None
    if plain:
        out_shape = [shape_of(size, LANES) for size in sizes]

    def kernel(place_ref, *refs):
        inputs = refs[: len(arrays)]
        refs = refs[len(arrays) + len(ties) :]
        outs, refs = refs[: len(out_shape)], refs[len(out_shape) :]
        buffers, refs = refs[: len(pieces)], refs[len(pieces) :]
        sems, results, out_sems = refs[0], refs[1:-1], refs[-1]
        ha, ba = place_ref[0], place_ref[1]
        moves, count = [], 0
        for piece, views in enumerate(pieces):
            moves.append([])
            for term, view in enumerate(views):
                source = inputs[index_of[id(view.array)]]
                starts, rows = view.runs(ha, ba)
                for k, start in enumerate(starts):
                    target = buffers[piece].at[term, pl.ds(k * rows, rows), :]
                    move = pltpu.make_async_copy(source.at[pl.ds(start, rows), :], target, sems.at[count])
                    move.start()
                    moves[-1].append(move)
                    count += 1
        values, waited, leaving = [], set(), []
        for out, group in enumerate(groups):
            row = 0
            for views in group:
                piece = piece_of[id(views)]
                if piece not in waited:
                    waited.add(piece)
                    for move in moves[piece]:
                        move.wait()
                value = buffers[piece][0]
                for term in range(1, len(views)):
                    value = value + buffers[piece][term]
                if plain:
                    results[out][row : row + value.shape[0], :] = value
                values.append(value)
                row += value.shape[0]
            if plain:
                leaving.append(pltpu.make_async_copy(results[out], outs[out], out_sems.at[out]))
                leaving[-1].start()
        if not plain:
            epilogue(ha, ba, values, outs)
        for move in leaving:
            move.wait()

    moved = sum(view.size() for views in pieces for view in views) + sum(sizes)
    scratch = [pltpu.VMEM((len(views), views[0].size(), LANES), F32) for views in pieces]
    scratch.append(pltpu.SemaphoreType.DMA((copies,)))
    if plain:
        scratch += [pltpu.VMEM((size, LANES), F32) for size in sizes]
    scratch.append(pltpu.SemaphoreType.DMA((len(groups),)))
    return pl.pallas_call(
        kernel,
        in_specs=[in_smem()] + [in_hbm()] * (len(arrays) + len(ties)),
        out_specs=[in_hbm() if plain else pl.BlockSpec(memory_space=pltpu.VMEM)] * len(out_shape),
        out_shape=out_shape,
        scratch_shapes=scratch,
        compiler_params=params(),
        cost_estimate=lasting(1 + moved * LANES * 4 / 3.0e6),
    )(place, *arrays, *ties)


def tied(arrays, ties):
    return pl.pallas_call(
        lambda *refs: None,
        in_specs=[pl.BlockSpec(memory_space=pl.ANY)] * (len(arrays) + len(ties)),
        out_specs=[pl.BlockSpec(memory_space=pl.ANY)] * len(arrays),
        out_shape=[shape_of(*array.shape) for array in arrays],
        input_output_aliases={k: k for k in range(len(arrays))},
        compiler_params=params(),
        cost_estimate=lasting(0.5),
    )(*arrays, *ties)


class Sum:
    def __init__(self, arrays, names):
        self.views = []
        near = lax.axis_size("ha") // 4
        sizes = {"plane": lax.axis_size("ba"), "far": 2, "near": near}
        for array in arrays:
            flat = array.reshape(-1, LANES)
            stride, ways = flat.shape[0], []
            for name in names:
                stride //= sizes[name]
                ways.append((name, sizes[name], stride))
            self.views.append(View(flat, 0, ways, [], stride))

    def leaving(self, way, step):
        return [view.fix(way, step) for view in self.views]

    def keep(self, way, sent, arrived):
        self.views = [view.fix(way, 0) for view in self.views]
        rows = self.views[0].rows
        stride, ways = rows, []
        for name, size, _ in reversed(self.views[0].ways):
            ways.insert(0, (name, size, stride))
            stride *= size
        self.views += [View(array, start, ways, [], rows) for array, start in arrived]

    def part(self, first, rows):
        return [View(view.array, view.start + first, view.ways, view.fixed, rows) for view in self.views]


class Rider:
    def __init__(self, views):
        self.views = views

    def leaving(self, way, step):
        return self.views

    def keep(self, way, sent, arrived):
        rows = self.views[0].size()
        self.views = [View(array, start, [], [], rows) for array, start in [sent] + arrived]


class Gather(Rider):
    def keep(self, way, sent, arrived):
        rows = self.views[0].size()
        self.gathered = [[View(array, start, [], [], rows)] for array, start in [sent] + arrived]


class Stage:
    def __init__(self, members, way):
        self.members, self.way = members, way
        line, near = lax.axis_size("ha") // 2, lax.axis_size("ha") // 4
        self.steps = {
            "plane": list(range(1, lax.axis_size("ba"))),
            "line": list(range(1, line)),
            "far": [near],
        }[way]
        self.near = near

    def taking(self, step):
        takes = {"plane": True, "line": True, "near": step < self.near, "far": step == self.near}
        return [(one, way) for one, way in self.members if takes[way]]

    def groups(self):
        return [
            [one.leaving(way, step // self.near if way == "far" else step) for one, way in self.taking(step)]
            for step in self.steps
        ]

    def go(self, payloads, in_turn=None):
        axis, unit = ("ba", 1) if self.way == "plane" else ("ha", 2)
        arrived = []
        for step, part in zip(self.steps, payloads):
            if in_turn is not None and len(arrived) == 2:
                (part,) = tied([part], [arrived[in_turn]])
            arrived.append(exchange(part, axis, unit * step))
        places = {}
        for step, sent, part in zip(self.steps, payloads, arrived):
            row = 0
            for one, way in self.taking(step):
                places.setdefault(id(one), []).append(((sent, row), (part, row)))
                row += one.leaving(way, 1)[0].size()
        for one, way in self.members:
            mine = places.get(id(one), [])
            one.keep(way, mine[:2][-1][0] if mine else None, [part for _, part in mine])
        return arrived


def run(place, stage, ties=(), in_turn=None, extra=()):
    groups = stage.groups()
    made = list(combine(place, groups + list(extra), ties))
    made, more = made[: len(groups)], made[len(groups) :]
    return made, stage.go(made, in_turn), more


def neighbour_rows(top, bottom):
    count = lax.axis_size("ha")
    up = [(i, i + 1) for i in range(count - 1)]
    down = [(i + 1, i) for i in range(count - 1)]
    return lax.ppermute(bottom, "ha", up), lax.ppermute(top, "ha", down)


def lay_beside(value, ref):
    tall, width = ref.shape
    for k in range(lane_blocks(width)):
        columns = slice(k * LANES, min(width, (k + 1) * LANES))
        ref[:, columns] = value[k * tall : (k + 1) * tall, : columns.stop - columns.start]


def lay_large(ha, ba, values, outs):
    up_first, up_second, down_first, down_second, out = values
    lay_beside(jnp.concatenate([up_first, up_second], axis=0), outs[0])
    lay_beside(jnp.concatenate([down_first, down_second], axis=0), outs[1])
    lay_beside(out, outs[2])


def lay_small(ha, ba, values, outs, blocks):
    din_ref, dk_ref, gain_ref = outs[:3]
    scratch = outs[-1]
    lay_beside(values[0], din_ref)
    count = lax.axis_size("ba")
    own, other = values[1 : 2 + count], values[2 + count :]
    mine = ha % 2 == 0
    dkern = jnp.concatenate([jnp.where(mine, own[0], other[0]), jnp.where(mine, other[0], own[0])], axis=0)
    joined = jnp.concatenate([dkern[k * TAPS : (k + 1) * TAPS] for k in range(blocks)], axis=1)
    dk_ref[...] = joined[:, joined.shape[1] - dk_ref.shape[1] :]
    part = own[1].shape[0]
    for side, parts in ((ha % 2, own[1:]), (1 - ha % 2, other[1:])):
        for step, rows in enumerate(parts):
            start = (side * count + (ba ^ step)) * part
            scratch[pl.ds(pl.multiple_of(start, 8), part), :] = rows
    dim = gain_ref.shape[1]
    for k in range(dim // LANES):
        columns = slice(k * LANES, (k + 1) * LANES)
        row = blocks * TAPS + k
        gain_ref[:, columns] = dkern[row : row + 1]
        for vector, ref in enumerate(outs[3:6]):
            ref[:, columns] = scratch[vector * dim // LANES + k : vector * dim // LANES + k + 1, :]
    row = scratch.shape[0]
    for ref in reversed(outs[6:-1]):
        tall, width = ref.shape
        row -= tall * width // LANES
        for k in range(width // LANES):
            ref[:, k * LANES : (k + 1) * LANES] = scratch[row + k * tall : row + (k + 1) * tall, :]


def shards(
    canvas,
    image_id,
    keep_first,
    keep_second,
    first_gain,
    weight_in,
    depth_kernel,
    gate_first,
    gate_second,
    gate_third,
    weight_out,
    scale_first,
    second_gain,
    weight_up,
    weight_down,
    scale_second,
    cotangent,
):
    _, rows, cols, dim = canvas.shape
    cells = rows * cols
    reach = REACH * cols
    count_ha, count_ba = lax.axis_size("ha"), lax.axis_size("ba")
    hidden = weight_up.shape[1]
    blocks = weight_in.shape[1] // LANES
    place = jnp.stack([lax.axis_index("ha"), lax.axis_index("ba")])
    own = canvas.reshape(cells, dim)
    gates = (gate_first, gate_second, gate_third)
    gain = first_gain[None]
    vectors = (gain, scale_first[None], second_gain[None], scale_second[None])
    ids = image_id[0]
    above, below = neighbour_rows(own[:reach], own[cells - reach :])
    ahead = head(place, ids, keep_first, keep_second, own, gain, weight_in, rows, cols)
    joined = ahead[0]
    (
        output, dmiddle, dconv, dconv_top, dconv_bottom, plane_kept, plane_sent, line_kept, line_sent,
        packed_kept, packed_sent,
    ) = forward(
        place, ids, ahead, above, own, below, cotangent.reshape(cells, dim), vectors,
        weight_in, depth_kernel, gates, weight_out, weight_up, weight_down, rows, cols, count_ha, count_ba,
    )
    above, below = neighbour_rows(dconv_top, dconv_bottom)

    plane_sum = Sum([plane_kept, exchange(plane_sent, "ha", 1)], ["plane", "far", "near"])
    line_sum = Sum([line_kept, exchange(line_sent, "ha", 1)], ["far", "near", "plane"])
    packed = Sum([packed_kept, exchange(packed_sent, "ha", 1)], ["plane"])
    across = Stage([(plane_sum, "plane"), (packed, "plane")], "plane")
    apart = Stage([(line_sum, "far")], "far")
    made = list(combine(place, across.groups() + apart.groups()))
    arrived = across.go(made[: len(across.steps)])
    made[len(across.steps) :] = tied(made[len(across.steps) :], [above, below])
    arrived += apart.go(made[len(across.steps) :])
    dcanvas, in_kept, in_sent, small_kept, small_sent = backward(
        place, ids, above, dconv, below, joined, depth_kernel, own, gain, dmiddle, weight_in, made,
        rows, cols, count_ha, count_ba,
    )
    in_sent, small_sent = tied([in_sent, small_sent], arrived)
    in_sum = Sum([in_kept, exchange(in_sent, "ha", 1)], ["plane", "far", "near"])
    small = Rider([flat_view(small_kept), flat_view(exchange(small_sent, "ha", 1))])
    packed = Rider(packed.views)
    packed = Rider(packed.views)
    made, arrived, _ = run(
        place, Stage([(plane_sum, "far"), (line_sum, "near"), (packed, "line")], "line"), in_turn=0
    )
    run(place, Stage([(in_sum, "plane"), (small, "plane")], "plane"), ties=made)
    along = Stage([(plane_sum, "near"), (in_sum, "line"), (small, "line")], "line")
    made, arrived, (own_small,) = run(place, along, ties=arrived[:2], in_turn=1, extra=[[small.views]])
    packed = Gather(packed.views)
    across = Stage([(line_sum, "plane"), (packed, "plane")], "plane")
    _, crossed, (own_packed,) = run(place, across, ties=made, extra=[[packed.views]])
    cut = plane_sum.views[0].rows // 2
    rest = (line_sum.views[0].rows - dim // count_ha * lane_blocks(dim // count_ba)) // 2
    dup, ddown, dout = combine(
        place,
        [
            [
                plane_sum.part(0, cut),
                line_sum.part(0, rest),
                plane_sum.part(cut, cut),
                line_sum.part(rest, rest),
                line_sum.part(2 * rest, line_sum.views[0].rows - 2 * rest),
            ]
        ],
        epilogue=lay_large,
        out_shape=[
            shape_of(dim // count_ba, hidden // count_ha),
            shape_of(dim // count_ha, hidden // count_ba),
            shape_of(dim // count_ha, dim // count_ba),
        ],
    )
    sent = list(tied([own_small, own_packed], arrived[1:2]))
    others = [exchange(part, "ha", 1) for part in sent + arrived + crossed]
    other_of = {id(part): other for part, other in zip(arrived + crossed, others[2:])}

    def from_other(view):
        return View(other_of[id(view.array)], view.start, view.ways, view.fixed, view.rows)

    own_parts = [small.views] + packed.gathered
    other_parts = [[flat_view(others[0])] + [from_other(view) for view in small.views[1:]], [flat_view(others[1])]]
    other_parts += [[from_other(view) for view in views] for views in packed.gathered[1:]]
    din, dkern, dgain_one, dscale_one, dgain_two, dscale_two, dfirst, dsecond, dthird, _ = combine(
        place,
        [[in_sum.views] + own_parts + other_parts],
        ties=[dup],
        epilogue=functools.partial(lay_small, blocks=blocks),
        out_shape=[shape_of(dim // count_ba, weight_in.shape[1] // count_ha), shape_of(*depth_kernel.shape)]
        + [shape_of(1, dim)] * 4
        + [shape_of(*gate.shape) for gate in gates]
        + [shape_of(packed_rows(gates, dim, count_ba), LANES)],
    )
    return (
        output.reshape(canvas.shape),
        dcanvas.reshape(canvas.shape),
        dgain_one[0],
        din,
        dkern,
        dfirst,
        dsecond,
        dthird,
        dout.T,
        dscale_one[0],
        dgain_two[0],
        dup,
        ddown.T,
        dscale_two[0],
    )


def solution(mesh):
    in_specs = (
        P("ba", "ha", None, None),
        P("ba", None, None),
        P("ba", None),
        P("ba", None),
    ) + (P(),) * 12 + (P("ba", "ha", None, None),)
    tiled = P("ba", "ha")
    out_specs = (
        P("ba", "ha", None, None),
        P("ba", "ha", None, None),
        P(),
        tiled,
        P(),
        P(),
        P(),
        P(),
        tiled,
        P(),
        P(),
        tiled,
        tiled,
        P(),
    )
    return jax.shard_map(shards, mesh=mesh, in_specs=in_specs, out_specs=out_specs, check_vma=False)
```

```python
import functools

import jax
import jax.numpy as jnp
from jax import lax
from jax.experimental import pallas as pl
from jax.experimental.pallas import tpu as pltpu
from jax.sharding import PartitionSpec as P

KERN = 7
TAPS = KERN * KERN
REACH = KERN // 2
KEEP_RATE = 0.8
SPREAD = 1.0 / 3.0
EPSILON = 1e-06
LANES = 128
EDGE = 8
VMEM_BYTES = 64 << 20
F32 = jnp.float32
INV_SQRT_2 = 0.7071067811865476
INV_SQRT_2PI = 0.3989422804014327
NN = (((1,), (0,)), ((), ()))
NT = (((1,), (1,)), ((), ()))
TN = (((0,), (0,)), ((), ()))


def dot(left, right, dims=NN):
    return lax.dot_general(left, right, dims, precision=lax.Precision.HIGH, preferred_element_type=F32)


def normalized(values):
    centered = values - jnp.mean(values, axis=-1, keepdims=True)
    scale = lax.rsqrt(jnp.mean(centered * centered, axis=-1, keepdims=True) + EPSILON)
    return centered * scale, scale


def norm_backward(grad_hat, hat, scale):
    return scale * (
        grad_hat
        - jnp.mean(grad_hat, axis=-1, keepdims=True)
        - hat * jnp.mean(grad_hat * hat, axis=-1, keepdims=True)
    )


def params():
    return pltpu.CompilerParams(vmem_limit_bytes=VMEM_BYTES)


def lasting(microseconds):
    return pl.CostEstimate(flops=int(microseconds * 1.1e9), bytes_accessed=0, transcendentals=0)


def whole(shape):
    return pl.BlockSpec(tuple(shape), lambda *_: (0,) * len(shape), pipeline_mode=pl.Buffered(1))


def in_smem():
    return pl.BlockSpec(memory_space=pltpu.SMEM)


def in_hbm():
    return pl.BlockSpec(memory_space=pltpu.HBM)


def shape_of(*shape):
    return jax.ShapeDtypeStruct(shape, F32)


def lane_blocks(width):
    return -(-width // LANES)


def image_ids(ids_ref, padded, place, rows):
    height, cols = ids_ref.shape
    padded[...] = jnp.full(padded.shape, -1, jnp.int32)
    padded[EDGE : EDGE + height, :] = ids_ref[...]
    ids = padded[pl.ds(place * rows + (EDGE - REACH), rows + 2 * REACH), :]
    return jnp.concatenate([ids, jnp.full((-ids.shape[0] % 8, cols), -1, jnp.int32)], axis=0).T


def spread_cells(factors, out_ref, first, rows):
    cols = factors.shape[0]
    for r in range(rows):
        column = factors[:, first + r : first + r + 1]
        out_ref[r * cols : (r + 1) * cols, :] = jnp.broadcast_to(column, (cols, LANES))


def keep_factors(turned, table_ref):
    result = jnp.zeros(turned.shape, F32)
    for slot in range(table_ref.shape[1]):
        result = jnp.where(turned == slot, table_ref[0, slot].astype(F32) / KEEP_RATE, result)
    return result


def conv_masks(ids_scalar, ids_ref, place, row_taps, col_mask, rows):
    height, cols = ids_ref.shape
    column_masks(ids_ref, col_mask)
    row_masks(ids_scalar, place, row_taps, rows, height, cols)


def column_masks(ids_ref, col_mask):
    height, cols = ids_ref.shape
    wide_ids = jnp.broadcast_to(ids_ref[...].T[:, height // 2 : height // 2 + 1], (cols, LANES))
    column = lax.broadcasted_iota(jnp.int32, (cols, LANES), 0)
    for b in range(KERN):
        shift = b - REACH
        moved = pltpu.roll(wide_ids, (-shift) % cols, 0)
        inside = (column + shift >= 0) & (column + shift < cols)
        same = (moved == wide_ids) & inside
        col_mask[b] = same.astype(F32).reshape(cols // 8, 8, LANES)


def row_masks(ids_scalar, place, row_taps, rows, height, cols):
    def one(r, _):
        own = ids_scalar[place * rows + r, cols // 2]
        row_taps[r, 0] = KERN
        row_taps[r, KERN + 1] = KERN
        for a in range(KERN):
            other = place * rows + r + a - REACH
            inside = (other >= 0) & (other < height)
            same = ids_scalar[jnp.clip(other, 0, height - 1), cols // 2] == own
            row_taps[r, a + 1] = jnp.where(inside & same, a, KERN)
        return 0

    lax.fori_loop(0, rows, one, 0)


def lay_kernel(kern_ref, laid, split):
    tap = lax.broadcasted_iota(jnp.int32, (TAPS, split), 0)
    own = jnp.where(tap == TAPS // 2, 1.0 / SPREAD, 0.0).astype(F32)
    for k in range(laid.shape[0]):
        start = k * LANES - split
        left = own if k == 0 else kern_ref[:, start : start + split]
        laid[k] = jnp.concatenate([left, kern_ref[:, start + split : start + LANES]], axis=1) * SPREAD


def fill_shifted(flat, col_ref, shifted, rows_ext, cols):
    for b in range(KERN):
        for g in range(cols // 8):
            mask = None if b == REACH else col_ref[b, g]
            for r in range(rows_ext):
                x = flat[pl.ds(EDGE + r * cols + 8 * g + b - REACH, 8), :]
                shifted[b, r, g] = x if b == REACH else x * mask


def spread_taps(kern, wide, turned):
    for t in range(TAPS):
        source = TAPS - 1 - t if turned else t
        wide[t] = jnp.broadcast_to(kern[source : source + 1, :], (8, LANES))
    for t in range(KERN):
        wide[TAPS + t] = jnp.zeros((8, LANES), F32)


def conv_block(row_taps, kern, shifted, wide, out_ref, rows, cols):
    groups = cols // 8
    spread_taps(kern, wide, False)

    def pair(h, _):
        r = 2 * h

        def step(i, totals):
            first, second = totals
            taps_first = row_taps[r, i + 1] * KERN
            taps_second = row_taps[r + 1, i] * KERN
            for b in range(KERN):
                x = shifted[b, r + i]
                first = first + wide[taps_first + b][None] * x
                second = second + wide[taps_second + b][None] * x
            return first, second

        zero = jnp.zeros((groups, 8, LANES), F32)
        first, second = lax.fori_loop(0, KERN + 1, step, (zero, zero), unroll=4)
        out_ref[pl.ds(pl.multiple_of(r * cols, cols), cols), :] = first.reshape(cols, LANES)
        out_ref[pl.ds(pl.multiple_of((r + 1) * cols, cols), cols), :] = second.reshape(cols, LANES)
        return 0

    lax.fori_loop(0, rows // 2, pair, 0)


def conv_grad_block(row_taps, kern, shifted, wide, dk, mix_ref, out_ref, dk_ref, rows, cols):
    groups = cols // 8
    spread_taps(kern, wide, True)
    for t in range(TAPS):
        dk[t] = jnp.zeros((8, LANES), F32)

    def one(r, _):
        start = pl.ds(pl.multiple_of(r * cols, cols), cols)
        mix = mix_ref[start, :].reshape(groups, 8, LANES)
        total = jnp.zeros((groups, 8, LANES), F32)
        for i in range(KERN):
            row = row_taps[r, i + 1]
            same = jnp.where(row < KERN, 1.0, 0.0).astype(F32)
            for b in range(KERN):
                x = shifted[b, r + i]
                total = total + wide[row * KERN + b][None] * x
                dk[i * KERN + b] += jnp.sum(mix * x, axis=0) * same
        out_ref[start, :] = total.reshape(cols, LANES)
        return 0

    lax.fori_loop(0, rows, one, 0)
    for t in range(TAPS):
        dk_ref[TAPS - 1 - t : TAPS - t, :] = jnp.sum(dk[t], axis=0, keepdims=True) * SPREAD
    dk_ref[TAPS:, :] = jnp.zeros((dk_ref.shape[0] - TAPS, LANES), F32)


def share(core, first, second, kept_ref, sent_ref, z, p):
    mine = core == 0
    tall, width = first.shape
    for ref, chunk in (
        (kept_ref, jnp.where(mine, first, second)),
        (sent_ref, jnp.where(mine, second, first)),
    ):
        for k in range(lane_blocks(width)):
            part = chunk[:, k * LANES : (k + 1) * LANES]
            if part.shape[1] < LANES:
                part = jnp.concatenate([part, jnp.zeros((tall, LANES - part.shape[1]), F32)], axis=1)
            ref[z, p, k * tall : (k + 1) * tall, :] = part


def share_columns(core, grad, kept_ref, sent_ref, width, plane_first=False):
    groups, parts = reversed(kept_ref.shape[:2]) if plane_first else kept_ref.shape[:2]
    tall = grad.shape[0] // parts
    for z in range(groups):
        for p in range(parts):
            rows = slice(p * tall, (p + 1) * tall)
            first = grad[rows, 2 * z * width : (2 * z + 1) * width]
            second = grad[rows, (2 * z + 1) * width : (2 * z + 2) * width]
            share(core, first, second, kept_ref, sent_ref, *((p, z) if plane_first else (z, p)))


def share_rows(core, grad, kept_ref, sent_ref, tall):
    groups, parts = kept_ref.shape[:2]
    width = grad.shape[1] // parts
    for z in range(groups):
        for p in range(parts):
            columns = slice(p * width, (p + 1) * width)
            first = grad[2 * z * tall : (2 * z + 1) * tall, columns]
            second = grad[(2 * z + 1) * tall : (2 * z + 2) * tall, columns]
            share(core, first, second, kept_ref, sent_ref, z, p)


class Copies:
    def __init__(self, sems):
        self.sems, self.count, self.pending = sems, 0, {}

    def start(self, name, source, target):
        copy = pltpu.make_async_copy(source, target, self.sems.at[self.count])
        self.count += 1
        copy.start()
        self.pending.setdefault(name, []).append(copy)

    def wait(self, *names):
        for name in names:
            for copy in self.pending.pop(name):
                copy.wait()

    def wait_all(self):
        self.wait(*list(self.pending))


def head_kernel(
    place_ref, ids_scalar, one_table, two_table, ids_hbm, own_hbm, gain_hbm, in_hbm_ref,
    joined_hbm, valid_hbm, one_keep_hbm, two_keep_hbm, col_hbm,
    ids_ref, rows_ref, gain_ref, in_ref, padded, valid_ref, one_keep_ref, two_keep_ref, col_ref, normed, joined, sems,
    *, rows, cols,
):
    cells = rows * cols
    reach = REACH * cols
    steps = in_ref.shape[0]
    copies = Copies(sems)
    copies.start("ids", ids_hbm, ids_ref)
    copies.start("own", own_hbm, rows_ref)
    copies.start("own", gain_hbm, gain_ref)
    for k in range(steps):
        copies.start(("in", k), in_hbm_ref.at[:, pl.ds(2 * LANES * k, 2 * LANES)], in_ref.at[k])
    copies.wait("ids")
    turned = image_ids(ids_ref, padded, place_ref[0], rows)
    spread_cells((turned >= 0).astype(F32), valid_ref, 0, rows + 2 * REACH)
    copies.start("outs", valid_ref, valid_hbm)
    copies.wait("own")
    hat, _ = normalized(rows_ref[...] * valid_ref[reach : reach + cells, :1])
    normed[...] = hat * gain_ref[...]
    for step in range(steps):
        copies.wait(("in", step))
        part = dot(normed[...], in_ref[step])
        for k in range(2):
            joined[2 * step + k] = part[:, k * LANES : (k + 1) * LANES]
        pair = pl.ds(2 * step, 2)
        copies.start("outs", joined.at[pair], joined_hbm.at[pair])
    spread_cells(keep_factors(turned, one_table), one_keep_ref, REACH, rows)
    spread_cells(keep_factors(turned, two_table), two_keep_ref, REACH, rows)
    column_masks(ids_ref, col_ref)
    for source, target in ((one_keep_ref, one_keep_hbm), (two_keep_ref, two_keep_hbm), (col_ref, col_hbm)):
        copies.start("outs", source, target)
    copies.wait_all()


def head(place, ids, keep_one, keep_two, own, gain, weight_in, rows, cols):
    cells, dim = own.shape
    cells_ext = cells + 2 * REACH * cols
    blocks = weight_in.shape[1] // LANES
    vmem = functools.partial(pltpu.VMEM, dtype=F32)
    shapes = [
        (blocks, cells, LANES), (cells_ext, LANES), (cells, LANES), (cells, LANES), (KERN, cols // 8, 8, LANES)
    ]
    return pl.pallas_call(
        functools.partial(head_kernel, rows=rows, cols=cols),
        in_specs=[in_smem()] * 4 + [in_hbm()] * 4,
        out_specs=[in_hbm()] * len(shapes),
        out_shape=[shape_of(*shape) for shape in shapes],
        scratch_shapes=[
            pltpu.VMEM(ids.shape, jnp.int32),
            vmem((cells, dim)),
            vmem((1, dim)),
            vmem((blocks // 2, dim, 2 * LANES)),
            pltpu.VMEM((ids.shape[0] + 2 * EDGE, ids.shape[1]), jnp.int32),
        ]
        + [vmem(shape) for shape in shapes[1:]]
        + [vmem((cells, dim)), vmem(shapes[0]), pltpu.SemaphoreType.DMA((7 + blocks,))],
        compiler_params=params(),
        cost_estimate=lasting(7),
    )(place, ids, keep_one, keep_two, ids, own, gain, weight_in)


def forward_kernel(
    place_ref, ids_scalar, joined_hbm, valid_hbm, one_keep_hbm, two_keep_hbm, col_hbm, above_hbm, own_hbm, below_hbm, cot_hbm,
    first_gain_hbm, first_scale_hbm, second_gain_hbm, second_scale_hbm,
    in_hbm_ref, kern_hbm, one_hbm, two_hbm, three_hbm, out_hbm, up_hbm, down_hbm,
    output_hbm, dmiddle_hbm, dconv_hbm, dconv_top_hbm, dconv_bottom_hbm,
    plane_kept_ref, plane_sent_ref, line_kept_ref, line_sent_ref, packed_kept_hbm, packed_sent_hbm,
    rows_ref, cot_ref, first_gain_ref, first_scale_ref, second_gain_ref, second_scale_ref,
    in_ref, kern_ref, one_ref, two_ref, three_ref, out_ref, up_ref, down_ref, dconv_ref, sems, chunk_sems,
    up_kept, up_sent, down_kept, down_sent, out_kept, out_sent,
    row_taps, valid_ref, one_keep_ref, two_keep_ref, col_ref, packed_ref, normed, flat, shifted, laid, wide, conv,
    mixed_ref, mapped_ref, middle_ref, result, dnorm,
    *, rows, cols, count_ha, count_ba,
):
    blocks = flat.shape[0]
    cells = rows * cols
    reach = REACH * cols
    cells_ext = cells + 2 * reach
    core = place_ref[0] % 2
    split = one_ref.shape[0]
    dim = rows_ref.shape[1]
    head_steps = blocks // 2
    ffn_steps = up_kept.shape[0]
    chunk = down_ref.shape[1]
    gate_refs = (one_ref, two_ref, three_ref)

    copies = Copies(sems)
    copies.start("rows", valid_hbm, valid_ref)
    copies.start("rows", first_gain_hbm, first_gain_ref)
    copies.start("above", above_hbm, rows_ref.at[pl.ds(0, reach)])
    copies.start("below", below_hbm, rows_ref.at[pl.ds(reach + cells, reach)])
    for k in range(head_steps):
        copies.start(("in", k), in_hbm_ref.at[:, pl.ds(2 * LANES * k, 2 * LANES)], in_ref.at[k])
    copies.start("conv", joined_hbm, flat.at[:, pl.ds(EDGE + reach, cells), :])
    copies.start("conv", col_hbm, col_ref)
    copies.start("gates", own_hbm, rows_ref.at[pl.ds(reach, cells)])
    copies.start("gates", one_keep_hbm, one_keep_ref)
    copies.start("gates", two_keep_hbm, two_keep_ref)
    copies.start("kern", kern_hbm, kern_ref)
    def weights(k):
        ends = pl.ds(pl.multiple_of(k * chunk, chunk), chunk)
        return [
            pltpu.make_async_copy(up_hbm.at[:, ends], up_ref.at[k], chunk_sems.at[k, 0]),
            pltpu.make_async_copy(down_hbm.at[ends, :], down_ref.at[k], chunk_sems.at[k, 1]),
        ]

    def chunk_copies(place):
        moves = []
        sides = ((up_kept, down_kept, plane_kept_ref, line_kept_ref), (up_sent, down_sent, plane_sent_ref, line_sent_ref))
        for up, down, plane, line in sides:
            cut = plane.shape[2] // 2
            rest = up.shape[3] - cut
            zs = pl.ds(place * up.shape[1], up.shape[1])
            bas = pl.ds(place * down.shape[2], down.shape[2])
            moves += [
                (up.at[place, :, ba, pl.ds(0, cut), :], plane.at[ba, zs, pl.ds(0, cut), :])
                for ba in range(plane.shape[0])
            ]
            moves += [
                (down.at[place, z, :, pl.ds(0, cut), :], plane.at[bas, z, pl.ds(cut, cut), :])
                for z in range(plane.shape[1])
            ]
            moves.append((up.at[place, :, :, pl.ds(cut, rest), :], line.at[zs, :, pl.ds(0, rest), :]))
            moves.append((down.at[place, :, :, pl.ds(cut, rest), :], line.at[:, bas, pl.ds(rest, rest), :]))
        return [
            pltpu.make_async_copy(source, target, chunk_sems.at[place, 2 + k])
            for k, (source, target) in enumerate(moves)
        ]

    row_masks(ids_scalar, place_ref[0], row_taps, rows, ids_scalar.shape[0], cols)
    copies.wait("rows")
    for name, start, place in (("above", 0, 0), ("below", reach + cells, reach)):
        copies.wait(name)
        hat, _ = normalized(rows_ref[start : start + reach, :] * valid_ref[start : start + reach, :1])
        normed[place : place + reach] = hat * first_gain_ref[...]

    for k in range(blocks):
        flat[k, :EDGE] = jnp.zeros((EDGE, LANES), F32)
        flat[k, EDGE + cells_ext :] = jnp.zeros((EDGE, LANES), F32)
    for step in range(head_steps):
        copies.wait(("in", step))
        joined = dot(normed[: 2 * reach], in_ref[step])
        for k in range(2):
            part = joined[:, k * LANES : (k + 1) * LANES]
            flat[2 * step + k, EDGE : EDGE + reach] = part[:reach]
            flat[2 * step + k, EDGE + reach + cells : EDGE + cells_ext] = part[reach:]
        if step == 0:
            copies.start("gates", first_scale_hbm, first_scale_ref)
            copies.start("gates", second_gain_hbm, second_gain_ref)
            copies.start("gates", second_scale_hbm, second_scale_ref)
            for source, target in zip((one_hbm, two_hbm, three_hbm, out_hbm, cot_hbm), gate_refs + (out_ref, cot_ref)):
                copies.start("gates", source, target)
            for k in range(ffn_steps):
                for copy in weights(k):
                    copy.start()

    copies.wait("conv")
    copies.wait("kern")
    lay_kernel(kern_ref, laid, split)

    def conv_step(block, _):
        fill_shifted(flat.at[block], col_ref, shifted, rows + 2 * REACH, cols)
        conv_block(row_taps, laid[block], shifted, wide, conv.at[block], rows, cols)
        return 0

    lax.fori_loop(0, blocks, conv_step, 0)

    def conv_part(start, width):
        return jnp.concatenate([conv[start // LANES + k] for k in range(width // LANES)], axis=1)

    copies.wait("gates")
    mixed = conv[0, :, :split] * conv[0, :, split:]
    mixed_ref[:, :split] = mixed
    start = 2 * split
    for ref in gate_refs:
        width = ref.shape[1]
        mapped = dot(mixed, ref[...])
        mapped_ref[:, start - 2 * split : start - 2 * split + width] = mapped
        mixed = mapped * conv_part(start, width)
        mixed_ref[:, start : start + width] = mixed
        start += width
    branch = dot(mixed, out_ref[...])
    masked = rows_ref[reach : reach + cells, :] * valid_ref[reach : reach + cells, :1]
    middle = masked + one_keep_ref[:, :1] * first_scale_ref[...] * branch
    middle_ref[...] = middle
    hat, _ = normalized(middle)
    normed[:cells] = hat * second_gain_ref[...]
    result[...] = jnp.zeros_like(result)
    dnorm[...] = jnp.zeros_like(dnorm)

    def ffn_step(place, _):
        for copy in weights(place):
            copy.wait()
        grad_result = two_keep_ref[:, :1] * second_scale_ref[...] * cot_ref[...]
        pre = dot(normed[:cells], up_ref[place])
        cdf = 0.5 + 0.5 * lax.erf(pre * INV_SQRT_2)
        slope = cdf + pre * (INV_SQRT_2PI * jnp.exp(-0.5 * pre * pre))
        hidden = pre * cdf
        result[...] += dot(hidden, down_ref[place])
        grad_pre = dot(grad_result, down_ref[place], NT) * slope
        share_rows(
            core, dot(grad_result, hidden, TN), down_kept.at[place], down_sent.at[place], dim // count_ha
        )
        width = chunk // (2 * up_kept.shape[1])
        share_columns(core, dot(normed[:cells], grad_pre, TN), up_kept.at[place], up_sent.at[place], width)
        for copy in chunk_copies(place):
            copy.start()
        dnorm[...] += dot(grad_pre, up_ref[place], NT)
        return 0

    lax.fori_loop(0, ffn_steps, ffn_step, 0)

    hat, scale = normalized(middle_ref[...])
    kept = two_keep_ref[:, :1] * result[...]
    dscale_two = jnp.sum(cot_ref[...] * kept, axis=0, keepdims=True)
    result[...] = middle_ref[...] + second_scale_ref[...] * kept
    copies.start("outs", result, output_hbm)
    dgain_two = jnp.sum(dnorm[...] * hat, axis=0, keepdims=True)
    dmiddle = cot_ref[...] + norm_backward(dnorm[...] * second_gain_ref[...], hat, scale)
    dnorm[...] = dmiddle
    copies.start("outs", dnorm, dmiddle_hbm)
    kept = one_keep_ref[:, :1] * dmiddle
    grad = dot(kept * first_scale_ref[...], out_ref[...], NT)
    row = packed_ref.shape[0]
    start = blocks * LANES
    for ref in reversed(gate_refs):
        tall, width = ref.shape
        start -= width
        source = start - tall if tall > split else 0
        columns = slice(start - 2 * split, start - 2 * split + width)
        dconv = grad * mapped_ref[:, columns]
        for k in range(width // LANES):
            dconv_ref[start // LANES + k] = dconv[:, k * LANES : (k + 1) * LANES]
        grad_mapped = grad * conv_part(start, width)
        part = dot(mixed_ref[:, source : source + tall], grad_mapped, TN)
        row -= tall * width // LANES
        for k in range(width // LANES):
            packed_ref[row + k * tall : row + (k + 1) * tall] = part[:, k * LANES : (k + 1) * LANES]
        grad = dot(grad_mapped, ref[...], NT)
    dconv_ref[0] = jnp.concatenate([grad * conv[0, :, split:], grad * conv[0, :, :split]], axis=1)
    copies.start("outs", dconv_ref.at[:, pl.ds(0, reach), :], dconv_top_hbm)
    copies.start("outs", dconv_ref.at[:, pl.ds(cells - reach, reach), :], dconv_bottom_hbm)
    copies.start("outs", dconv_ref, dconv_hbm)
    start = mixed_ref.shape[1] - out_ref.shape[0]
    crossed = dot(mixed_ref[:, start:], kept, TN)
    dscale_one = jnp.sum(crossed * out_ref[...], axis=0, keepdims=True)
    packed_ref[:row] = jnp.zeros((row, LANES), F32)
    row = 0
    for vector in (dscale_one, dgain_two, dscale_two):
        for k in range(dim // LANES):
            packed_ref[row : row + 1] = vector[:, k * LANES : (k + 1) * LANES]
            row += 1
    half = packed_kept_hbm.shape[0]
    for place, target in ((core, packed_kept_hbm), (1 - core, packed_sent_hbm)):
        copies.start("outs", packed_ref.at[pl.ds(pl.multiple_of(place * half, 8), half), :], target)
    share_rows(core, (crossed * first_scale_ref[...]).T, out_kept, out_sent, dim // count_ha)
    for source, line in ((out_kept, line_kept_ref), (out_sent, line_sent_ref)):
        tall = source.shape[2]
        copies.start("outs", source, line.at[:, :, pl.ds(line.shape[2] - tall, tall), :])
    for place in range(ffn_steps):
        for copy in chunk_copies(place):
            copy.wait()
    copies.wait_all()


def mask_scratch(ids, rows):
    height, cols = ids.shape
    return [
        pltpu.SMEM((rows, KERN + 2), jnp.int32),
        pltpu.VMEM((height + 2 * EDGE, cols), jnp.int32),
        pltpu.VMEM(((rows + 2 * REACH) * cols, LANES), F32),
    ]


def packed_rows(gates, dim, parts):
    rows = sum(gate.size for gate in gates) // LANES + 3 * dim // LANES
    return -(-rows // (16 * parts)) * 16 * parts


def plane_share(rows):
    return max(rows * 3 // 4 // 8 * 8, 8)


def forward(
    place, ids, ahead, above, own, below, cot, vectors, weight_in, kern, gates,
    weight_out, weight_up, weight_down, rows, cols, count_ha, count_ba, chunk=512,
):
    cells, dim = own.shape
    reach = above.shape[0]
    blocks = weight_in.shape[1] // LANES
    hidden = weight_up.shape[1]
    split = gates[0].shape[0]
    wide = blocks * LANES
    head_steps = blocks // 2
    ffn_steps = hidden // chunk

    up_wide, down_wide = hidden // count_ha, hidden // count_ba
    up_rows = dim // count_ba * lane_blocks(up_wide)
    down_rows = dim // count_ha * lane_blocks(down_wide)
    out_rows = dim // count_ha * lane_blocks(dim // count_ba)
    half = count_ha // 2
    assert up_rows == down_rows
    cut = plane_share(up_rows)
    rest = up_rows - cut
    plane = (count_ba, half, 2 * cut, LANES)
    line = (half, count_ba, 2 * rest + out_rows, LANES)
    packed_shape = (packed_rows(gates, dim, count_ba), LANES)
    half_packed = (packed_shape[0] // 2, LANES)
    cells_ext = cells + 2 * reach
    vmem = functools.partial(pltpu.VMEM, dtype=F32)
    operands = (
        place, ids, *ahead, above, own, below, cot, *vectors,
        weight_in, kern, *gates, weight_out, weight_up, weight_down,
    )
    out_shape = [
        shape_of(cells, dim),
        shape_of(cells, dim),
        shape_of(blocks, cells, LANES),
        shape_of(blocks, reach, LANES),
        shape_of(blocks, reach, LANES),
        shape_of(*plane),
        shape_of(*plane),
        shape_of(*line),
        shape_of(*line),
        shape_of(*half_packed),
        shape_of(*half_packed),
    ]
    return pl.pallas_call(
        functools.partial(forward_kernel, rows=rows, cols=cols, count_ha=count_ha, count_ba=count_ba),
        in_specs=[in_smem()] * 2 + [in_hbm()] * (len(operands) - 2),
        out_specs=[in_hbm()] * len(out_shape),
        out_shape=out_shape,
        scratch_shapes=[vmem((cells_ext, dim)), vmem((cells, dim))]
        + [vmem((1, dim))] * 4
        + [vmem((head_steps, dim, 2 * LANES)), vmem(kern.shape)]
        + [vmem(gate.shape) for gate in gates]
        + [
            vmem(weight_out.shape),
            vmem((ffn_steps, dim, chunk)),
            vmem((ffn_steps, chunk, dim)),
            vmem((blocks, cells, LANES)),
            pltpu.SemaphoreType.DMA((40 + head_steps,)),
            pltpu.SemaphoreType.DMA((ffn_steps, 2 + 2 * (count_ba + half + 2))),
        ]
        + [vmem((ffn_steps, chunk // (2 * up_wide), count_ba, up_rows, LANES))] * 2
        + [vmem((ffn_steps, half, chunk // down_wide, down_rows, LANES))] * 2
        + [vmem((half, count_ba, out_rows, LANES))] * 2
        + [
            pltpu.SMEM((rows, KERN + 2), jnp.int32),
            vmem((cells_ext, LANES)),
            vmem((cells, LANES)),
            vmem((cells, LANES)),
            vmem((KERN, cols // 8, 8, LANES)),
            vmem(packed_shape),
            vmem((max(cells, 2 * reach), dim)),
            vmem((blocks, cells_ext + 2 * EDGE, LANES)),
            vmem((KERN, rows + 2 * REACH, cols // 8, 8, LANES)),
            vmem((blocks, TAPS, LANES)),
            vmem((TAPS + KERN, 8, LANES)),
            vmem((blocks, cells, LANES)),
            vmem((cells, wide)),
            vmem((cells, wide - 2 * split)),
            vmem((cells, dim)),
            vmem((cells, dim)),
            vmem((cells, dim)),
        ],
        compiler_params=params(),
        cost_estimate=lasting(48),
    )(*operands)


def lay_flat(above_ref, own_ref, below_ref, flat):
    reach, cells = above_ref.shape[1], own_ref.shape[1]
    flat[:EDGE] = jnp.zeros((EDGE, LANES), F32)
    flat[EDGE : EDGE + reach] = above_ref[0]
    flat[EDGE + reach : EDGE + reach + cells] = own_ref[0]
    flat[EDGE + reach + cells : EDGE + 2 * reach + cells] = below_ref[0]
    flat[EDGE + 2 * reach + cells :] = jnp.zeros((EDGE, LANES), F32)


def backward_kernel(
    place_ref, ids_scalar, ids_ref, above_ref, own_ref, below_ref, mix_ref, kern_ref, canvas_ref, gain_ref,
    dmiddle_ref, in_ref, *rest, rows, cols,
):
    dcanvas_ref, kept_ref, sent_ref, small_kept_ref, small_sent_ref = rest[-19:-14]
    row_taps, padded, valid_ref, col_ref, flat, shifted, laid, wide, dk, sums, small, djoined, normed, dnorm = rest[-14:]
    step = pl.program_id(0)
    cells = rows * cols
    reach = REACH * cols
    core = place_ref[0] % 2
    split = laid.shape[0] * LANES - kern_ref.shape[1]
    width = in_ref.shape[1] // (2 * kept_ref.shape[1])

    @pl.when(step == 0)
    def _():
        lay_kernel(kern_ref, laid, split)
        turned = image_ids(ids_ref, padded, place_ref[0], rows)
        spread_cells((turned >= 0).astype(F32), valid_ref, 0, rows + 2 * REACH)
        conv_masks(ids_scalar, ids_ref, place_ref[0], row_taps, col_ref, rows)
        hat, _ = normalized(canvas_ref[...] * valid_ref[reach : reach + cells, :1])
        normed[...] = hat * gain_ref[...]
        dnorm[...] = jnp.zeros_like(dnorm)

    lay_flat(above_ref, own_ref, below_ref, flat)
    fill_shifted(flat, col_ref, shifted, rows + 2 * REACH, cols)
    conv_grad_block(
        row_taps, laid[step], shifted, wide, dk, mix_ref.at[0], djoined.at[step % 2], sums.at[step], rows, cols
    )

    @pl.when(step % 2 == 1)
    def _():
        grad = jnp.concatenate([djoined[0], djoined[1]], axis=1)
        share_columns(core, dot(normed[...], grad, TN), kept_ref, sent_ref, width, plane_first=True)
        dnorm[...] += dot(grad, in_ref[...], NT)

    @pl.when(step == pl.num_programs(0) - 1)
    def _():
        hat, scale = normalized(canvas_ref[...] * valid_ref[reach : reach + cells, :1])
        dgain = jnp.sum(dnorm[...] * hat, axis=0, keepdims=True)
        row = sums.shape[0] * TAPS
        for k in range(sums.shape[0]):
            small[k * TAPS : (k + 1) * TAPS, :] = sums[k, :TAPS]
        small[row:, :] = jnp.zeros((small.shape[0] - row, LANES), F32)
        for k in range(dgain.shape[1] // LANES):
            small[row + k : row + k + 1, :] = dgain[:, k * LANES : (k + 1) * LANES]
        half = small.shape[0] // 2
        for ref, start in ((small_kept_ref, core * half), (small_sent_ref, (1 - core) * half)):
            ref[...] = small[pl.ds(pl.multiple_of(start, 8), half), :]
        inner = dmiddle_ref[...] + norm_backward(dnorm[...] * gain_ref[...], hat, scale)
        dcanvas_ref[...] = inner * valid_ref[reach : reach + cells, :1]


def block_of(size):
    return pl.BlockSpec((1, size, LANES), lambda i: (i, 0, 0))


def small_rows(blocks, dim):
    return -(-(blocks * TAPS + dim // LANES) // 16) * 16


def backward(
    place, ids, above, own, below, mix, kern, canvas, gain, dmiddle, weight_in, ties, rows, cols, count_ha, count_ba
):
    cells, dim = canvas.shape
    blocks = own.shape[0]
    reach = above.shape[1]
    own_wide = weight_in.shape[1] // count_ha
    chunk_rows = dim // count_ba * lane_blocks(own_wide)
    groups = 2 * LANES // (2 * own_wide)
    chunk_spec = pl.BlockSpec((count_ba, groups, chunk_rows, LANES), lambda i: (0, i // 2, 0, 0))
    chunks = shape_of(count_ba, count_ha // 2, chunk_rows, LANES)
    tall = -(-TAPS // 8) * 8
    small = (small_rows(blocks, dim) // 2, LANES)
    return pl.pallas_call(
        functools.partial(backward_kernel, rows=rows, cols=cols),
        grid=(blocks,),
        in_specs=[in_smem(), in_smem(), whole(ids.shape)]
        + [block_of(size) for size in (reach, cells, reach, cells)]
        + [whole(kern.shape), whole(canvas.shape)]
        + [whole((1, dim)), whole((cells, dim))]
        + [pl.BlockSpec((dim, 2 * LANES), lambda i: (0, i // 2))]
        + [in_hbm()] * len(ties),
        out_specs=[whole((cells, dim)), chunk_spec, chunk_spec, whole(small), whole(small)],
        out_shape=[shape_of(cells, dim), chunks, chunks, shape_of(*small), shape_of(*small)],
        scratch_shapes=mask_scratch(ids, rows)
        + [
            pltpu.VMEM((KERN, cols // 8, 8, LANES), F32),
            pltpu.VMEM((cells + 2 * reach + 2 * EDGE, LANES), F32),
            pltpu.VMEM((KERN, rows + 2 * REACH, cols // 8, 8, LANES), F32),
            pltpu.VMEM((blocks, TAPS, LANES), F32),
            pltpu.VMEM((TAPS + KERN, 8, LANES), F32),
            pltpu.VMEM((TAPS, 8, LANES), F32),
            pltpu.VMEM((blocks, tall, LANES), F32),
            pltpu.VMEM((small_rows(blocks, dim), LANES), F32),
            pltpu.VMEM((2, cells, LANES), F32),
            pltpu.VMEM((cells, dim), F32),
            pltpu.VMEM((cells, dim), F32),
        ],
        compiler_params=params(),
        cost_estimate=lasting(25),
    )(place, ids, ids, above, own, below, mix, kern, canvas, gain, dmiddle, weight_in, *ties)


def exchange(values, axis, bit):
    return lax.ppermute(values, axis, [(i, i ^ bit) for i in range(lax.axis_size(axis))])


class View:
    def __init__(self, array, start, ways, fixed, rows):
        self.array, self.start, self.ways, self.fixed, self.rows = array, start, ways, fixed, rows

    def fix(self, way, step):
        if way == "line":
            near = lax.axis_size("ha") // 4
            return self.fix("far", step // near).fix("near", step % near)
        left = [entry for entry in self.ways if entry[0] != way]
        (stride,) = [entry[2] for entry in self.ways if entry[0] == way]
        return View(self.array, self.start, left, self.fixed + [(way, step, stride)], self.rows)

    def size(self):
        count = self.rows
        for _, size, _ in self.ways:
            count *= size
        return count

    def runs(self, ha, ba):
        start = self.start
        near = lax.axis_size("ha") // 4
        places = {"plane": ba, "far": ha // 2 // near, "near": ha // 2 % near}
        for way, step, stride in self.fixed:
            start = start + (places[way] ^ step) * stride
        rows, ways = self.rows, list(self.ways)
        while ways and ways[-1][2] == rows:
            rows *= ways.pop()[1]
        offsets = [0]
        for _, size, stride in ways:
            offsets = [offset + k * stride for offset in offsets for k in range(size)]
        return [pl.multiple_of(start + offset, 8) for offset in offsets], rows


def flat_view(array, start=0, rows=None):
    flat = array.reshape(-1, LANES)
    return View(flat, start, [], [], flat.shape[0] if rows is None else rows)


def combine(place, groups, ties=(), epilogue=None, out_shape=None):
    pieces, arrays = [], []
    for group in groups:
        for views in group:
            if not any(views is other for other in pieces):
                pieces.append(views)
    for views in pieces:
        for view in views:
            if not any(view.array is other for other in arrays):
                arrays.append(view.array)
    index_of = {id(array): k for k, array in enumerate(arrays)}
    piece_of = {id(views): k for k, views in enumerate(pieces)}
    sizes = [sum(views[0].size() for views in group) for group in groups]
    copies = sum(len(view.runs(0, 0)[0]) for views in pieces for view in views)
    plain = epilogue is None
    if plain:
        out_shape = [shape_of(size, LANES) for size in sizes]

    def kernel(place_ref, *refs):
        inputs = refs[: len(arrays)]
        refs = refs[len(arrays) + len(ties) :]
        outs, refs = refs[: len(out_shape)], refs[len(out_shape) :]
        buffers, refs = refs[: len(pieces)], refs[len(pieces) :]
        sems, results, out_sems = refs[0], refs[1:-1], refs[-1]
        ha, ba = place_ref[0], place_ref[1]
        moves, count = [], 0
        for piece, views in enumerate(pieces):
            moves.append([])
            for term, view in enumerate(views):
                source = inputs[index_of[id(view.array)]]
                starts, rows = view.runs(ha, ba)
                for k, start in enumerate(starts):
                    target = buffers[piece].at[term, pl.ds(k * rows, rows), :]
                    move = pltpu.make_async_copy(source.at[pl.ds(start, rows), :], target, sems.at[count])
                    move.start()
                    moves[-1].append(move)
                    count += 1
        values, waited, leaving = [], set(), []
        for out, group in enumerate(groups):
            row = 0
            for views in group:
                piece = piece_of[id(views)]
                if piece not in waited:
                    waited.add(piece)
                    for move in moves[piece]:
                        move.wait()
                value = buffers[piece][0]
                for term in range(1, len(views)):
                    value = value + buffers[piece][term]
                if plain:
                    results[out][row : row + value.shape[0], :] = value
                values.append(value)
                row += value.shape[0]
            if plain:
                leaving.append(pltpu.make_async_copy(results[out], outs[out], out_sems.at[out]))
                leaving[-1].start()
        if not plain:
            epilogue(ha, ba, values, outs)
        for move in leaving:
            move.wait()

    moved = sum(view.size() for views in pieces for view in views) + sum(sizes)
    scratch = [pltpu.VMEM((len(views), views[0].size(), LANES), F32) for views in pieces]
    scratch.append(pltpu.SemaphoreType.DMA((copies,)))
    if plain:
        scratch += [pltpu.VMEM((size, LANES), F32) for size in sizes]
    scratch.append(pltpu.SemaphoreType.DMA((len(groups),)))
    return pl.pallas_call(
        kernel,
        in_specs=[in_smem()] + [in_hbm()] * (len(arrays) + len(ties)),
        out_specs=[in_hbm() if plain else pl.BlockSpec(memory_space=pltpu.VMEM)] * len(out_shape),
        out_shape=out_shape,
        scratch_shapes=scratch,
        compiler_params=params(),
        cost_estimate=lasting(1 + moved * LANES * 4 / 3.0e6),
    )(place, *arrays, *ties)


def tied(arrays, ties):
    return pl.pallas_call(
        lambda *refs: None,
        in_specs=[pl.BlockSpec(memory_space=pl.ANY)] * (len(arrays) + len(ties)),
        out_specs=[pl.BlockSpec(memory_space=pl.ANY)] * len(arrays),
        out_shape=[shape_of(*array.shape) for array in arrays],
        input_output_aliases={k: k for k in range(len(arrays))},
        compiler_params=params(),
        cost_estimate=lasting(0.5),
    )(*arrays, *ties)


class Sum:
    def __init__(self, arrays, names):
        self.views = []
        near = lax.axis_size("ha") // 4
        sizes = {"plane": lax.axis_size("ba"), "far": 2, "near": near}
        for array in arrays:
            flat = array.reshape(-1, LANES)
            stride, ways = flat.shape[0], []
            for name in names:
                stride //= sizes[name]
                ways.append((name, sizes[name], stride))
            self.views.append(View(flat, 0, ways, [], stride))

    def leaving(self, way, step):
        return [view.fix(way, step) for view in self.views]

    def keep(self, way, sent, arrived):
        self.views = [view.fix(way, 0) for view in self.views]
        rows = self.views[0].rows
        stride, ways = rows, []
        for name, size, _ in reversed(self.views[0].ways):
            ways.insert(0, (name, size, stride))
            stride *= size
        self.views += [View(array, start, ways, [], rows) for array, start in arrived]

    def part(self, first, rows):
        return [View(view.array, view.start + first, view.ways, view.fixed, rows) for view in self.views]


class Rider:
    def __init__(self, views):
        self.views = views

    def leaving(self, way, step):
        return self.views

    def keep(self, way, sent, arrived):
        rows = self.views[0].size()
        self.views = [View(array, start, [], [], rows) for array, start in [sent] + arrived]


class Gather(Rider):
    def keep(self, way, sent, arrived):
        rows = self.views[0].size()
        self.gathered = [[View(array, start, [], [], rows)] for array, start in [sent] + arrived]


class Stage:
    def __init__(self, members, way):
        self.members, self.way = members, way
        line, near = lax.axis_size("ha") // 2, lax.axis_size("ha") // 4
        self.steps = {
            "plane": list(range(1, lax.axis_size("ba"))),
            "line": list(range(1, line)),
            "far": [near],
        }[way]
        self.near = near

    def taking(self, step):
        takes = {"plane": True, "line": True, "near": step < self.near, "far": step == self.near}
        return [(one, way) for one, way in self.members if takes[way]]

    def groups(self):
        return [
            [one.leaving(way, step // self.near if way == "far" else step) for one, way in self.taking(step)]
            for step in self.steps
        ]

    def go(self, payloads, in_turn=None):
        axis, unit = ("ba", 1) if self.way == "plane" else ("ha", 2)
        arrived = []
        for step, part in zip(self.steps, payloads):
            if in_turn is not None and len(arrived) == 2:
                (part,) = tied([part], [arrived[in_turn]])
            arrived.append(exchange(part, axis, unit * step))
        places = {}
        for step, sent, part in zip(self.steps, payloads, arrived):
            row = 0
            for one, way in self.taking(step):
                places.setdefault(id(one), []).append(((sent, row), (part, row)))
                row += one.leaving(way, 1)[0].size()
        for one, way in self.members:
            mine = places.get(id(one), [])
            one.keep(way, mine[:2][-1][0] if mine else None, [part for _, part in mine])
        return arrived


def run(place, stage, ties=(), in_turn=None, extra=()):
    groups = stage.groups()
    made = list(combine(place, groups + list(extra), ties))
    made, more = made[: len(groups)], made[len(groups) :]
    return made, stage.go(made, in_turn), more


def neighbour_rows(top, bottom):
    count = lax.axis_size("ha")
    up = [(i, i + 1) for i in range(count - 1)]
    down = [(i + 1, i) for i in range(count - 1)]
    return lax.ppermute(bottom, "ha", up), lax.ppermute(top, "ha", down)


def lay_beside(value, ref):
    tall, width = ref.shape
    for k in range(lane_blocks(width)):
        columns = slice(k * LANES, min(width, (k + 1) * LANES))
        ref[:, columns] = value[k * tall : (k + 1) * tall, : columns.stop - columns.start]


def lay_large(ha, ba, values, outs):
    up_first, up_second, down_first, down_second, out = values
    lay_beside(jnp.concatenate([up_first, up_second], axis=0), outs[0])
    lay_beside(jnp.concatenate([down_first, down_second], axis=0), outs[1])
    lay_beside(out, outs[2])


def lay_small(ha, ba, values, outs, blocks):
    din_ref, dk_ref, gain_ref = outs[:3]
    scratch = outs[-1]
    lay_beside(values[0], din_ref)
    count = lax.axis_size("ba")
    own, other = values[1 : 2 + count], values[2 + count :]
    mine = ha % 2 == 0
    dkern = jnp.concatenate([jnp.where(mine, own[0], other[0]), jnp.where(mine, other[0], own[0])], axis=0)
    joined = jnp.concatenate([dkern[k * TAPS : (k + 1) * TAPS] for k in range(blocks)], axis=1)
    dk_ref[...] = joined[:, joined.shape[1] - dk_ref.shape[1] :]
    part = own[1].shape[0]
    for side, parts in ((ha % 2, own[1:]), (1 - ha % 2, other[1:])):
        for step, rows in enumerate(parts):
            start = (side * count + (ba ^ step)) * part
            scratch[pl.ds(pl.multiple_of(start, 8), part), :] = rows
    dim = gain_ref.shape[1]
    for k in range(dim // LANES):
        columns = slice(k * LANES, (k + 1) * LANES)
        row = blocks * TAPS + k
        gain_ref[:, columns] = dkern[row : row + 1]
        for vector, ref in enumerate(outs[3:6]):
            ref[:, columns] = scratch[vector * dim // LANES + k : vector * dim // LANES + k + 1, :]
    row = scratch.shape[0]
    for ref in reversed(outs[6:-1]):
        tall, width = ref.shape
        row -= tall * width // LANES
        for k in range(width // LANES):
            ref[:, k * LANES : (k + 1) * LANES] = scratch[row + k * tall : row + (k + 1) * tall, :]


def shards(
    canvas,
    image_id,
    keep_first,
    keep_second,
    first_gain,
    weight_in,
    depth_kernel,
    gate_first,
    gate_second,
    gate_third,
    weight_out,
    scale_first,
    second_gain,
    weight_up,
    weight_down,
    scale_second,
    cotangent,
):
    _, rows, cols, dim = canvas.shape
    cells = rows * cols
    reach = REACH * cols
    count_ha, count_ba = lax.axis_size("ha"), lax.axis_size("ba")
    hidden = weight_up.shape[1]
    blocks = weight_in.shape[1] // LANES
    place = jnp.stack([lax.axis_index("ha"), lax.axis_index("ba")])
    own = canvas.reshape(cells, dim)
    gates = (gate_first, gate_second, gate_third)
    gain = first_gain[None]
    vectors = (gain, scale_first[None], second_gain[None], scale_second[None])
    ids = image_id[0]
    above, below = neighbour_rows(own[:reach], own[cells - reach :])
    ahead = head(place, ids, keep_first, keep_second, own, gain, weight_in, rows, cols)
    joined = ahead[0]
    (
        output, dmiddle, dconv, dconv_top, dconv_bottom, plane_kept, plane_sent, line_kept, line_sent,
        packed_kept, packed_sent,
    ) = forward(
        place, ids, ahead, above, own, below, cotangent.reshape(cells, dim), vectors,
        weight_in, depth_kernel, gates, weight_out, weight_up, weight_down, rows, cols, count_ha, count_ba,
    )
    above, below = neighbour_rows(dconv_top, dconv_bottom)

    plane_sum = Sum([plane_kept, exchange(plane_sent, "ha", 1)], ["plane", "far", "near"])
    line_sum = Sum([line_kept, exchange(line_sent, "ha", 1)], ["far", "near", "plane"])
    packed = Sum([packed_kept, exchange(packed_sent, "ha", 1)], ["plane"])
    made, arrived, _ = run(place, Stage([(plane_sum, "plane"), (packed, "plane")], "plane"))
    apart = Stage([(line_sum, "far")], "far")
    more = list(tied(combine(place, apart.groups(), made), [above, below]))
    made, arrived = made + more, arrived + apart.go(more)
    dcanvas, in_kept, in_sent, small_kept, small_sent = backward(
        place, ids, above, dconv, below, joined, depth_kernel, own, gain, dmiddle, weight_in, made,
        rows, cols, count_ha, count_ba,
    )
    in_sent, small_sent = tied([in_sent, small_sent], arrived)
    in_sum = Sum([in_kept, exchange(in_sent, "ha", 1)], ["plane", "far", "near"])
    small = Rider([flat_view(small_kept), flat_view(exchange(small_sent, "ha", 1))])
    packed = Rider(packed.views)
    packed = Rider(packed.views)
    made, arrived, _ = run(
        place, Stage([(plane_sum, "far"), (line_sum, "near"), (packed, "line")], "line"), in_turn=0
    )
    run(place, Stage([(in_sum, "plane"), (small, "plane")], "plane"), ties=made)
    along = Stage([(plane_sum, "near"), (in_sum, "line"), (small, "line")], "line")
    made, arrived, (own_small,) = run(place, along, ties=arrived[:2], in_turn=1, extra=[[small.views]])
    packed = Gather(packed.views)
    across = Stage([(line_sum, "plane"), (packed, "plane")], "plane")
    _, crossed, (own_packed,) = run(place, across, ties=made, extra=[[packed.views]])
    cut = plane_sum.views[0].rows // 2
    rest = (line_sum.views[0].rows - dim // count_ha * lane_blocks(dim // count_ba)) // 2
    dup, ddown, dout = combine(
        place,
        [
            [
                plane_sum.part(0, cut),
                line_sum.part(0, rest),
                plane_sum.part(cut, cut),
                line_sum.part(rest, rest),
                line_sum.part(2 * rest, line_sum.views[0].rows - 2 * rest),
            ]
        ],
        epilogue=lay_large,
        out_shape=[
            shape_of(dim // count_ba, hidden // count_ha),
            shape_of(dim // count_ha, hidden // count_ba),
            shape_of(dim // count_ha, dim // count_ba),
        ],
    )
    sent = list(tied([own_small, own_packed], arrived[1:2]))
    others = [exchange(part, "ha", 1) for part in sent + arrived + crossed]
    other_of = {id(part): other for part, other in zip(arrived + crossed, others[2:])}

    def from_other(view):
        return View(other_of[id(view.array)], view.start, view.ways, view.fixed, view.rows)

    own_parts = [small.views] + packed.gathered
    other_parts = [[flat_view(others[0])] + [from_other(view) for view in small.views[1:]], [flat_view(others[1])]]
    other_parts += [[from_other(view) for view in views] for views in packed.gathered[1:]]
    din, dkern, dgain_one, dscale_one, dgain_two, dscale_two, dfirst, dsecond, dthird, _ = combine(
        place,
        [[in_sum.views] + own_parts + other_parts],
        ties=[dup],
        epilogue=functools.partial(lay_small, blocks=blocks),
        out_shape=[shape_of(dim // count_ba, weight_in.shape[1] // count_ha), shape_of(*depth_kernel.shape)]
        + [shape_of(1, dim)] * 4
        + [shape_of(*gate.shape) for gate in gates]
        + [shape_of(packed_rows(gates, dim, count_ba), LANES)],
    )
    return (
        output.reshape(canvas.shape),
        dcanvas.reshape(canvas.shape),
        dgain_one[0],
        din,
        dkern,
        dfirst,
        dsecond,
        dthird,
        dout.T,
        dscale_one[0],
        dgain_two[0],
        dup,
        ddown.T,
        dscale_two[0],
    )


def solution(mesh):
    in_specs = (
        P("ba", "ha", None, None),
        P("ba", None, None),
        P("ba", None),
        P("ba", None),
    ) + (P(),) * 12 + (P("ba", "ha", None, None),)
    tiled = P("ba", "ha")
    out_specs = (
        P("ba", "ha", None, None),
        P("ba", "ha", None, None),
        P(),
        tiled,
        P(),
        P(),
        P(),
        P(),
        tiled,
        P(),
        P(),
        tiled,
        tiled,
        P(),
    )
    return jax.shard_map(shards, mesh=mesh, in_specs=in_specs, out_specs=out_specs, check_vma=False)
```

```python
import functools

import jax
import jax.numpy as jnp
from jax import lax
from jax.experimental import pallas as pl
from jax.experimental.pallas import tpu as pltpu
from jax.sharding import PartitionSpec as P

KERN = 7
TAPS = KERN * KERN
REACH = KERN // 2
KEEP_RATE = 0.8
SPREAD = 1.0 / 3.0
EPSILON = 1e-06
LANES = 128
EDGE = 8
VMEM_BYTES = 64 << 20
F32 = jnp.float32
INV_SQRT_2 = 0.7071067811865476
INV_SQRT_2PI = 0.3989422804014327
NN = (((1,), (0,)), ((), ()))
NT = (((1,), (1,)), ((), ()))
TN = (((0,), (0,)), ((), ()))


def dot(left, right, dims=NN):
    return lax.dot_general(left, right, dims, precision=lax.Precision.HIGH, preferred_element_type=F32)


def normalized(values):
    centered = values - jnp.mean(values, axis=-1, keepdims=True)
    scale = lax.rsqrt(jnp.mean(centered * centered, axis=-1, keepdims=True) + EPSILON)
    return centered * scale, scale


def norm_backward(grad_hat, hat, scale):
    return scale * (
        grad_hat
        - jnp.mean(grad_hat, axis=-1, keepdims=True)
        - hat * jnp.mean(grad_hat * hat, axis=-1, keepdims=True)
    )


def params():
    return pltpu.CompilerParams(vmem_limit_bytes=VMEM_BYTES)


def lasting(microseconds):
    return pl.CostEstimate(flops=int(microseconds * 1.1e9), bytes_accessed=0, transcendentals=0)


def whole(shape):
    return pl.BlockSpec(tuple(shape), lambda *_: (0,) * len(shape), pipeline_mode=pl.Buffered(1))


def in_smem():
    return pl.BlockSpec(memory_space=pltpu.SMEM)


def in_hbm():
    return pl.BlockSpec(memory_space=pltpu.HBM)


def shape_of(*shape):
    return jax.ShapeDtypeStruct(shape, F32)


def lane_blocks(width):
    return -(-width // LANES)


def image_ids(ids_ref, padded, place, rows):
    height, cols = ids_ref.shape
    padded[...] = jnp.full(padded.shape, -1, jnp.int32)
    padded[EDGE : EDGE + height, :] = ids_ref[...]
    ids = padded[pl.ds(place * rows + (EDGE - REACH), rows + 2 * REACH), :]
    return jnp.concatenate([ids, jnp.full((-ids.shape[0] % 8, cols), -1, jnp.int32)], axis=0).T


def spread_cells(factors, out_ref, first, rows):
    cols = factors.shape[0]
    for r in range(rows):
        column = factors[:, first + r : first + r + 1]
        out_ref[r * cols : (r + 1) * cols, :] = jnp.broadcast_to(column, (cols, LANES))


def keep_factors(turned, table_ref):
    result = jnp.zeros(turned.shape, F32)
    for slot in range(table_ref.shape[1]):
        result = jnp.where(turned == slot, table_ref[0, slot].astype(F32) / KEEP_RATE, result)
    return result


def conv_masks(ids_scalar, ids_ref, place, row_taps, col_mask, rows):
    height, cols = ids_ref.shape
    column_masks(ids_ref, col_mask)
    row_masks(ids_scalar, place, row_taps, rows, height, cols)


def column_masks(ids_ref, col_mask):
    height, cols = ids_ref.shape
    wide_ids = jnp.broadcast_to(ids_ref[...].T[:, height // 2 : height // 2 + 1], (cols, LANES))
    column = lax.broadcasted_iota(jnp.int32, (cols, LANES), 0)
    for b in range(KERN):
        shift = b - REACH
        moved = pltpu.roll(wide_ids, (-shift) % cols, 0)
        inside = (column + shift >= 0) & (column + shift < cols)
        same = (moved == wide_ids) & inside
        col_mask[b] = same.astype(F32).reshape(cols // 8, 8, LANES)


def row_masks(ids_scalar, place, row_taps, rows, height, cols):
    def one(r, _):
        own = ids_scalar[place * rows + r, cols // 2]
        row_taps[r, 0] = KERN
        row_taps[r, KERN + 1] = KERN
        for a in range(KERN):
            other = place * rows + r + a - REACH
            inside = (other >= 0) & (other < height)
            same = ids_scalar[jnp.clip(other, 0, height - 1), cols // 2] == own
            row_taps[r, a + 1] = jnp.where(inside & same, a, KERN)
        return 0

    lax.fori_loop(0, rows, one, 0)


def lay_kernel(kern_ref, laid, split):
    tap = lax.broadcasted_iota(jnp.int32, (TAPS, split), 0)
    own = jnp.where(tap == TAPS // 2, 1.0 / SPREAD, 0.0).astype(F32)
    for k in range(laid.shape[0]):
        start = k * LANES - split
        left = own if k == 0 else kern_ref[:, start : start + split]
        laid[k] = jnp.concatenate([left, kern_ref[:, start + split : start + LANES]], axis=1) * SPREAD


def fill_shifted(flat, col_ref, shifted, rows_ext, cols):
    for b in range(KERN):
        for g in range(cols // 8):
            mask = None if b == REACH else col_ref[b, g]
            for r in range(rows_ext):
                x = flat[pl.ds(EDGE + r * cols + 8 * g + b - REACH, 8), :]
                shifted[b, r, g] = x if b == REACH else x * mask


def spread_taps(kern, wide, turned):
    for t in range(TAPS):
        source = TAPS - 1 - t if turned else t
        wide[t] = jnp.broadcast_to(kern[source : source + 1, :], (8, LANES))
    for t in range(KERN):
        wide[TAPS + t] = jnp.zeros((8, LANES), F32)


def conv_block(row_taps, kern, shifted, wide, out_ref, rows, cols):
    groups = cols // 8
    spread_taps(kern, wide, False)

    def pair(h, _):
        r = 2 * h

        def step(i, totals):
            first, second = totals
            taps_first = row_taps[r, i + 1] * KERN
            taps_second = row_taps[r + 1, i] * KERN
            for b in range(KERN):
                x = shifted[b, r + i]
                first = first + wide[taps_first + b][None] * x
                second = second + wide[taps_second + b][None] * x
            return first, second

        zero = jnp.zeros((groups, 8, LANES), F32)
        first, second = lax.fori_loop(0, KERN + 1, step, (zero, zero), unroll=4)
        out_ref[pl.ds(pl.multiple_of(r * cols, cols), cols), :] = first.reshape(cols, LANES)
        out_ref[pl.ds(pl.multiple_of((r + 1) * cols, cols), cols), :] = second.reshape(cols, LANES)
        return 0

    lax.fori_loop(0, rows // 2, pair, 0)


def conv_grad_block(row_taps, kern, shifted, wide, dk, mix_ref, out_ref, dk_ref, rows, cols):
    groups = cols // 8
    spread_taps(kern, wide, True)
    for t in range(TAPS):
        dk[t] = jnp.zeros((8, LANES), F32)

    def one(r, _):
        start = pl.ds(pl.multiple_of(r * cols, cols), cols)
        mix = mix_ref[start, :].reshape(groups, 8, LANES)
        total = jnp.zeros((groups, 8, LANES), F32)
        for i in range(KERN):
            row = row_taps[r, i + 1]
            same = jnp.where(row < KERN, 1.0, 0.0).astype(F32)
            for b in range(KERN):
                x = shifted[b, r + i]
                total = total + wide[row * KERN + b][None] * x
                dk[i * KERN + b] += jnp.sum(mix * x, axis=0) * same
        out_ref[start, :] = total.reshape(cols, LANES)
        return 0

    lax.fori_loop(0, rows, one, 0)
    for t in range(TAPS):
        dk_ref[TAPS - 1 - t : TAPS - t, :] = jnp.sum(dk[t], axis=0, keepdims=True) * SPREAD
    dk_ref[TAPS:, :] = jnp.zeros((dk_ref.shape[0] - TAPS, LANES), F32)


def share(core, first, second, kept_ref, sent_ref, z, p):
    mine = core == 0
    tall, width = first.shape
    for ref, chunk in (
        (kept_ref, jnp.where(mine, first, second)),
        (sent_ref, jnp.where(mine, second, first)),
    ):
        for k in range(lane_blocks(width)):
            part = chunk[:, k * LANES : (k + 1) * LANES]
            if part.shape[1] < LANES:
                part = jnp.concatenate([part, jnp.zeros((tall, LANES - part.shape[1]), F32)], axis=1)
            ref[z, p, k * tall : (k + 1) * tall, :] = part


def share_columns(core, grad, kept_ref, sent_ref, width, plane_first=False):
    groups, parts = reversed(kept_ref.shape[:2]) if plane_first else kept_ref.shape[:2]
    tall = grad.shape[0] // parts
    for z in range(groups):
        for p in range(parts):
            rows = slice(p * tall, (p + 1) * tall)
            first = grad[rows, 2 * z * width : (2 * z + 1) * width]
            second = grad[rows, (2 * z + 1) * width : (2 * z + 2) * width]
            share(core, first, second, kept_ref, sent_ref, *((p, z) if plane_first else (z, p)))


def share_rows(core, grad, kept_ref, sent_ref, tall):
    groups, parts = kept_ref.shape[:2]
    width = grad.shape[1] // parts
    for z in range(groups):
        for p in range(parts):
            columns = slice(p * width, (p + 1) * width)
            first = grad[2 * z * tall : (2 * z + 1) * tall, columns]
            second = grad[(2 * z + 1) * tall : (2 * z + 2) * tall, columns]
            share(core, first, second, kept_ref, sent_ref, z, p)


class Copies:
    def __init__(self, sems):
        self.sems, self.count, self.pending = sems, 0, {}

    def start(self, name, source, target):
        copy = pltpu.make_async_copy(source, target, self.sems.at[self.count])
        self.count += 1
        copy.start()
        self.pending.setdefault(name, []).append(copy)

    def wait(self, *names):
        for name in names:
            for copy in self.pending.pop(name):
                copy.wait()

    def wait_all(self):
        self.wait(*list(self.pending))


def head_kernel(
    ids_scalar, one_table, two_table, ids_hbm, own_hbm, gain_hbm, in_hbm_ref,
    joined_hbm, valid_hbm, one_keep_hbm, two_keep_hbm, col_hbm,
    ids_ref, rows_ref, gain_ref, in_ref, padded, valid_ref, one_keep_ref, two_keep_ref, col_ref, normed, joined, sems,
    *, rows, cols,
):
    cells = rows * cols
    reach = REACH * cols
    steps = in_ref.shape[0]
    copies = Copies(sems)
    copies.start("ids", ids_hbm, ids_ref)
    copies.start("own", own_hbm, rows_ref)
    copies.start("own", gain_hbm, gain_ref)
    for k in range(steps):
        copies.start(("in", k), in_hbm_ref.at[:, pl.ds(2 * LANES * k, 2 * LANES)], in_ref.at[k])
    copies.wait("ids")
    turned = image_ids(ids_ref, padded, lax.axis_index("ha"), rows)
    spread_cells((turned >= 0).astype(F32), valid_ref, 0, rows + 2 * REACH)
    copies.start("outs", valid_ref, valid_hbm)
    copies.wait("own")
    hat, _ = normalized(rows_ref[...] * valid_ref[reach : reach + cells, :1])
    normed[...] = hat * gain_ref[...]
    for step in range(steps):
        copies.wait(("in", step))
        part = dot(normed[...], in_ref[step])
        for k in range(2):
            joined[2 * step + k] = part[:, k * LANES : (k + 1) * LANES]
        pair = pl.ds(2 * step, 2)
        copies.start("outs", joined.at[pair], joined_hbm.at[pair])
    spread_cells(keep_factors(turned, one_table), one_keep_ref, REACH, rows)
    spread_cells(keep_factors(turned, two_table), two_keep_ref, REACH, rows)
    column_masks(ids_ref, col_ref)
    for source, target in ((one_keep_ref, one_keep_hbm), (two_keep_ref, two_keep_hbm), (col_ref, col_hbm)):
        copies.start("outs", source, target)
    copies.wait_all()


def head(ids, keep_one, keep_two, own, gain, weight_in, rows, cols):
    cells, dim = own.shape
    cells_ext = cells + 2 * REACH * cols
    blocks = weight_in.shape[1] // LANES
    vmem = functools.partial(pltpu.VMEM, dtype=F32)
    shapes = [
        (blocks, cells, LANES), (cells_ext, LANES), (cells, LANES), (cells, LANES), (KERN, cols // 8, 8, LANES)
    ]
    return pl.pallas_call(
        functools.partial(head_kernel, rows=rows, cols=cols),
        in_specs=[in_smem()] * 3 + [in_hbm()] * 4,
        out_specs=[in_hbm()] * len(shapes),
        out_shape=[shape_of(*shape) for shape in shapes],
        scratch_shapes=[
            pltpu.VMEM(ids.shape, jnp.int32),
            vmem((cells, dim)),
            vmem((1, dim)),
            vmem((blocks // 2, dim, 2 * LANES)),
            pltpu.VMEM((ids.shape[0] + 2 * EDGE, ids.shape[1]), jnp.int32),
        ]
        + [vmem(shape) for shape in shapes[1:]]
        + [vmem((cells, dim)), vmem(shapes[0]), pltpu.SemaphoreType.DMA((7 + blocks,))],
        compiler_params=params(),
        cost_estimate=lasting(7),
    )(ids, keep_one, keep_two, ids, own, gain, weight_in)


def forward_kernel(
    ids_scalar, joined_hbm, valid_hbm, one_keep_hbm, two_keep_hbm, col_hbm, above_hbm, own_hbm, below_hbm, cot_hbm,
    first_gain_hbm, first_scale_hbm, second_gain_hbm, second_scale_hbm,
    in_hbm_ref, kern_hbm, one_hbm, two_hbm, three_hbm, out_hbm, up_hbm, down_hbm,
    output_hbm, dmiddle_hbm, dconv_hbm, dconv_top_hbm, dconv_bottom_hbm,
    plane_kept_ref, plane_sent_ref, line_kept_ref, line_sent_ref, packed_kept_hbm, packed_sent_hbm,
    rows_ref, cot_ref, first_gain_ref, first_scale_ref, second_gain_ref, second_scale_ref,
    in_ref, kern_ref, one_ref, two_ref, three_ref, out_ref, up_ref, down_ref, dconv_ref, sems, chunk_sems,
    up_kept, up_sent, down_kept, down_sent, out_kept, out_sent,
    row_taps, valid_ref, one_keep_ref, two_keep_ref, col_ref, packed_ref, normed, flat, shifted, laid, wide, conv,
    mixed_ref, mapped_ref, branch_ref, middle_ref, result, dnorm,
    *, rows, cols, count_ha, count_ba,
):
    blocks = flat.shape[0]
    cells = rows * cols
    reach = REACH * cols
    cells_ext = cells + 2 * reach
    core = lax.axis_index("ha") % 2
    split = one_ref.shape[0]
    dim = rows_ref.shape[1]
    head_steps = blocks // 2
    ffn_steps = up_kept.shape[0]
    chunk = down_ref.shape[1]
    gate_refs = (one_ref, two_ref, three_ref)

    copies = Copies(sems)
    copies.start("rows", valid_hbm, valid_ref)
    copies.start("rows", first_gain_hbm, first_gain_ref)
    copies.start("above", above_hbm, rows_ref.at[pl.ds(0, reach)])
    copies.start("below", below_hbm, rows_ref.at[pl.ds(reach + cells, reach)])
    for k in range(head_steps):
        copies.start(("in", k), in_hbm_ref.at[:, pl.ds(2 * LANES * k, 2 * LANES)], in_ref.at[k])
    copies.start("conv", joined_hbm, flat.at[:, pl.ds(EDGE + reach, cells), :])
    copies.start("conv", col_hbm, col_ref)
    copies.start("gates", own_hbm, rows_ref.at[pl.ds(reach, cells)])
    copies.start("gates", one_keep_hbm, one_keep_ref)
    copies.start("gates", two_keep_hbm, two_keep_ref)
    copies.start("kern", kern_hbm, kern_ref)
    def weights(k):
        ends = pl.ds(pl.multiple_of(k * chunk, chunk), chunk)
        return [
            pltpu.make_async_copy(up_hbm.at[:, ends], up_ref.at[k], chunk_sems.at[k, 0]),
            pltpu.make_async_copy(down_hbm.at[ends, :], down_ref.at[k], chunk_sems.at[k, 1]),
        ]

    def chunk_copies(place):
        moves = []
        sides = ((up_kept, down_kept, plane_kept_ref, line_kept_ref), (up_sent, down_sent, plane_sent_ref, line_sent_ref))
        for up, down, plane, line in sides:
            cut = plane.shape[2] // 2
            rest = up.shape[3] - cut
            zs = pl.ds(place * up.shape[1], up.shape[1])
            bas = pl.ds(place * down.shape[2], down.shape[2])
            moves += [
                (up.at[place, :, ba, pl.ds(0, cut), :], plane.at[ba, zs, pl.ds(0, cut), :])
                for ba in range(plane.shape[0])
            ]
            moves += [
                (down.at[place, z, :, pl.ds(0, cut), :], plane.at[bas, z, pl.ds(cut, cut), :])
                for z in range(plane.shape[1])
            ]
            moves.append((up.at[place, :, :, pl.ds(cut, rest), :], line.at[zs, :, pl.ds(0, rest), :]))
            moves.append((down.at[place, :, :, pl.ds(cut, rest), :], line.at[:, bas, pl.ds(rest, rest), :]))
        return [
            pltpu.make_async_copy(source, target, chunk_sems.at[place, 2 + k])
            for k, (source, target) in enumerate(moves)
        ]

    row_masks(ids_scalar, lax.axis_index("ha"), row_taps, rows, ids_scalar.shape[0], cols)
    copies.wait("rows")
    for name, start, place in (("above", 0, 0), ("below", reach + cells, reach)):
        copies.wait(name)
        hat, _ = normalized(rows_ref[start : start + reach, :] * valid_ref[start : start + reach, :1])
        normed[place : place + reach] = hat * first_gain_ref[...]

    for k in range(blocks):
        flat[k, :EDGE] = jnp.zeros((EDGE, LANES), F32)
        flat[k, EDGE + cells_ext :] = jnp.zeros((EDGE, LANES), F32)
    for step in range(head_steps):
        copies.wait(("in", step))
        joined = dot(normed[: 2 * reach], in_ref[step])
        for k in range(2):
            part = joined[:, k * LANES : (k + 1) * LANES]
            flat[2 * step + k, EDGE : EDGE + reach] = part[:reach]
            flat[2 * step + k, EDGE + reach + cells : EDGE + cells_ext] = part[reach:]
        if step == 0:
            copies.start("gates", first_scale_hbm, first_scale_ref)
            copies.start("gates", second_gain_hbm, second_gain_ref)
            copies.start("gates", second_scale_hbm, second_scale_ref)
            for source, target in zip((one_hbm, two_hbm, three_hbm, out_hbm, cot_hbm), gate_refs + (out_ref, cot_ref)):
                copies.start("gates", source, target)
            for k in range(ffn_steps):
                for copy in weights(k):
                    copy.start()

    copies.wait("conv")
    copies.wait("kern")
    lay_kernel(kern_ref, laid, split)

    def conv_step(block, _):
        fill_shifted(flat.at[block], col_ref, shifted, rows + 2 * REACH, cols)
        conv_block(row_taps, laid[block], shifted, wide, conv.at[block], rows, cols)
        return 0

    lax.fori_loop(0, blocks, conv_step, 0)

    def conv_part(start, width):
        return jnp.concatenate([conv[start // LANES + k] for k in range(width // LANES)], axis=1)

    copies.wait("gates")
    mixed = conv[0, :, :split] * conv[0, :, split:]
    mixed_ref[:, :split] = mixed
    start = 2 * split
    for ref in gate_refs:
        width = ref.shape[1]
        mapped = dot(mixed, ref[...])
        mapped_ref[:, start - 2 * split : start - 2 * split + width] = mapped
        mixed = mapped * conv_part(start, width)
        mixed_ref[:, start : start + width] = mixed
        start += width
    branch = dot(mixed, out_ref[...])
    branch_ref[...] = branch
    masked = rows_ref[reach : reach + cells, :] * valid_ref[reach : reach + cells, :1]
    middle = masked + one_keep_ref[:, :1] * first_scale_ref[...] * branch
    middle_ref[...] = middle
    hat, _ = normalized(middle)
    normed[:cells] = hat * second_gain_ref[...]
    result[...] = jnp.zeros_like(result)
    dnorm[...] = jnp.zeros_like(dnorm)

    def ffn_step(place, _):
        for copy in weights(place):
            copy.wait()
        grad_result = two_keep_ref[:, :1] * second_scale_ref[...] * cot_ref[...]
        pre = dot(normed[:cells], up_ref[place])
        cdf = 0.5 + 0.5 * lax.erf(pre * INV_SQRT_2)
        slope = cdf + pre * (INV_SQRT_2PI * jnp.exp(-0.5 * pre * pre))
        hidden = pre * cdf
        result[...] += dot(hidden, down_ref[place])
        grad_pre = dot(grad_result, down_ref[place], NT) * slope
        share_rows(
            core, dot(grad_result, hidden, TN), down_kept.at[place], down_sent.at[place], dim // count_ha
        )
        width = chunk // (2 * up_kept.shape[1])
        share_columns(core, dot(normed[:cells], grad_pre, TN), up_kept.at[place], up_sent.at[place], width)
        for copy in chunk_copies(place):
            copy.start()
        dnorm[...] += dot(grad_pre, up_ref[place], NT)
        return 0

    lax.fori_loop(0, ffn_steps, ffn_step, 0)

    hat, scale = normalized(middle_ref[...])
    kept = two_keep_ref[:, :1] * result[...]
    dscale_two = jnp.sum(cot_ref[...] * kept, axis=0, keepdims=True)
    result[...] = middle_ref[...] + second_scale_ref[...] * kept
    copies.start("outs", result, output_hbm)
    dgain_two = jnp.sum(dnorm[...] * hat, axis=0, keepdims=True)
    dmiddle = cot_ref[...] + norm_backward(dnorm[...] * second_gain_ref[...], hat, scale)
    dnorm[...] = dmiddle
    copies.start("outs", dnorm, dmiddle_hbm)
    kept = one_keep_ref[:, :1] * dmiddle
    grad = dot(kept * first_scale_ref[...], out_ref[...], NT)
    row = packed_ref.shape[0]
    start = blocks * LANES
    for ref in reversed(gate_refs):
        tall, width = ref.shape
        start -= width
        source = start - tall if tall > split else 0
        columns = slice(start - 2 * split, start - 2 * split + width)
        dconv = grad * mapped_ref[:, columns]
        for k in range(width // LANES):
            dconv_ref[start // LANES + k] = dconv[:, k * LANES : (k + 1) * LANES]
        grad_mapped = grad * conv_part(start, width)
        part = dot(mixed_ref[:, source : source + tall], grad_mapped, TN)
        row -= tall * width // LANES
        for k in range(width // LANES):
            packed_ref[row + k * tall : row + (k + 1) * tall] = part[:, k * LANES : (k + 1) * LANES]
        grad = dot(grad_mapped, ref[...], NT)
    dconv_ref[0] = jnp.concatenate([grad * conv[0, :, split:], grad * conv[0, :, :split]], axis=1)
    copies.start("outs", dconv_ref.at[:, pl.ds(0, reach), :], dconv_top_hbm)
    copies.start("outs", dconv_ref.at[:, pl.ds(cells - reach, reach), :], dconv_bottom_hbm)
    copies.start("outs", dconv_ref, dconv_hbm)
    start = mixed_ref.shape[1] - out_ref.shape[0]
    turned = dot(kept * first_scale_ref[...], mixed_ref[:, start:], TN)
    dscale_one = jnp.sum(kept * branch_ref[...], axis=0, keepdims=True)
    packed_ref[:row] = jnp.zeros((row, LANES), F32)
    row = 0
    for vector in (dscale_one, dgain_two, dscale_two):
        for k in range(dim // LANES):
            packed_ref[row : row + 1] = vector[:, k * LANES : (k + 1) * LANES]
            row += 1
    half = packed_kept_hbm.shape[0]
    for place, target in ((core, packed_kept_hbm), (1 - core, packed_sent_hbm)):
        copies.start("outs", packed_ref.at[pl.ds(pl.multiple_of(place * half, 8), half), :], target)
    share_rows(core, turned, out_kept, out_sent, dim // count_ha)
    for source, line in ((out_kept, line_kept_ref), (out_sent, line_sent_ref)):
        tall = source.shape[2]
        copies.start("outs", source, line.at[:, :, pl.ds(line.shape[2] - tall, tall), :])
    for place in range(ffn_steps):
        for copy in chunk_copies(place):
            copy.wait()
    copies.wait_all()


def mask_scratch(ids, rows):
    height, cols = ids.shape
    return [
        pltpu.SMEM((rows, KERN + 2), jnp.int32),
        pltpu.VMEM((height + 2 * EDGE, cols), jnp.int32),
        pltpu.VMEM(((rows + 2 * REACH) * cols, LANES), F32),
    ]


def packed_rows(gates, dim, parts):
    rows = sum(gate.size for gate in gates) // LANES + 3 * dim // LANES
    return -(-rows // (16 * parts)) * 16 * parts


def plane_share(rows):
    return max(rows * 3 // 4 // 8 * 8, 8)


def forward(
    ids, ahead, above, own, below, cot, vectors, weight_in, kern, gates,
    weight_out, weight_up, weight_down, rows, cols, count_ha, count_ba, chunk=512,
):
    cells, dim = own.shape
    reach = above.shape[0]
    blocks = weight_in.shape[1] // LANES
    hidden = weight_up.shape[1]
    split = gates[0].shape[0]
    wide = blocks * LANES
    head_steps = blocks // 2
    ffn_steps = hidden // chunk

    up_wide, down_wide = hidden // count_ha, hidden // count_ba
    up_rows = dim // count_ba * lane_blocks(up_wide)
    down_rows = dim // count_ha * lane_blocks(down_wide)
    out_rows = dim // count_ha * lane_blocks(dim // count_ba)
    half = count_ha // 2
    assert up_rows == down_rows
    cut = plane_share(up_rows)
    rest = up_rows - cut
    plane = (count_ba, half, 2 * cut, LANES)
    line = (half, count_ba, 2 * rest + out_rows, LANES)
    packed_shape = (packed_rows(gates, dim, count_ba), LANES)
    half_packed = (packed_shape[0] // 2, LANES)
    cells_ext = cells + 2 * reach
    vmem = functools.partial(pltpu.VMEM, dtype=F32)
    operands = (
        ids, *ahead, above, own, below, cot, *vectors,
        weight_in, kern, *gates, weight_out, weight_up, weight_down,
    )
    out_shape = [
        shape_of(cells, dim),
        shape_of(cells, dim),
        shape_of(blocks, cells, LANES),
        shape_of(blocks, reach, LANES),
        shape_of(blocks, reach, LANES),
        shape_of(*plane),
        shape_of(*plane),
        shape_of(*line),
        shape_of(*line),
        shape_of(*half_packed),
        shape_of(*half_packed),
    ]
    return pl.pallas_call(
        functools.partial(forward_kernel, rows=rows, cols=cols, count_ha=count_ha, count_ba=count_ba),
        in_specs=[in_smem()] + [in_hbm()] * (len(operands) - 1),
        out_specs=[in_hbm()] * len(out_shape),
        out_shape=out_shape,
        scratch_shapes=[vmem((cells_ext, dim)), vmem((cells, dim))]
        + [vmem((1, dim))] * 4
        + [vmem((head_steps, dim, 2 * LANES)), vmem(kern.shape)]
        + [vmem(gate.shape) for gate in gates]
        + [
            vmem(weight_out.shape),
            vmem((ffn_steps, dim, chunk)),
            vmem((ffn_steps, chunk, dim)),
            vmem((blocks, cells, LANES)),
            pltpu.SemaphoreType.DMA((40 + head_steps,)),
            pltpu.SemaphoreType.DMA((ffn_steps, 2 + 2 * (count_ba + half + 2))),
        ]
        + [vmem((ffn_steps, chunk // (2 * up_wide), count_ba, up_rows, LANES))] * 2
        + [vmem((ffn_steps, half, chunk // down_wide, down_rows, LANES))] * 2
        + [vmem((half, count_ba, out_rows, LANES))] * 2
        + [
            pltpu.SMEM((rows, KERN + 2), jnp.int32),
            vmem((cells_ext, LANES)),
            vmem((cells, LANES)),
            vmem((cells, LANES)),
            vmem((KERN, cols // 8, 8, LANES)),
            vmem(packed_shape),
            vmem((max(cells, 2 * reach), dim)),
            vmem((blocks, cells_ext + 2 * EDGE, LANES)),
            vmem((KERN, rows + 2 * REACH, cols // 8, 8, LANES)),
            vmem((blocks, TAPS, LANES)),
            vmem((TAPS + KERN, 8, LANES)),
            vmem((blocks, cells, LANES)),
            vmem((cells, wide)),
            vmem((cells, wide - 2 * split)),
            vmem((cells, dim)),
            vmem((cells, dim)),
            vmem((cells, dim)),
            vmem((cells, dim)),
        ],
        compiler_params=params(),
        cost_estimate=lasting(48),
    )(*operands)


def lay_flat(above_ref, own_ref, below_ref, flat):
    reach, cells = above_ref.shape[1], own_ref.shape[1]
    flat[:EDGE] = jnp.zeros((EDGE, LANES), F32)
    flat[EDGE : EDGE + reach] = above_ref[0]
    flat[EDGE + reach : EDGE + reach + cells] = own_ref[0]
    flat[EDGE + reach + cells : EDGE + 2 * reach + cells] = below_ref[0]
    flat[EDGE + 2 * reach + cells :] = jnp.zeros((EDGE, LANES), F32)


def backward_kernel(
    place_ref, ids_scalar, ids_ref, above_ref, own_ref, below_ref, mix_ref, kern_ref, canvas_ref, gain_ref,
    dmiddle_ref, in_ref, *rest, rows, cols,
):
    dcanvas_ref, kept_ref, sent_ref, small_kept_ref, small_sent_ref = rest[-19:-14]
    row_taps, padded, valid_ref, col_ref, flat, shifted, laid, wide, dk, sums, small, djoined, normed, dnorm = rest[-14:]
    step = pl.program_id(0)
    cells = rows * cols
    reach = REACH * cols
    core = place_ref[0] % 2
    split = laid.shape[0] * LANES - kern_ref.shape[1]
    width = in_ref.shape[1] // (2 * kept_ref.shape[1])

    @pl.when(step == 0)
    def _():
        lay_kernel(kern_ref, laid, split)
        turned = image_ids(ids_ref, padded, place_ref[0], rows)
        spread_cells((turned >= 0).astype(F32), valid_ref, 0, rows + 2 * REACH)
        conv_masks(ids_scalar, ids_ref, place_ref[0], row_taps, col_ref, rows)
        hat, _ = normalized(canvas_ref[...] * valid_ref[reach : reach + cells, :1])
        normed[...] = hat * gain_ref[...]
        dnorm[...] = jnp.zeros_like(dnorm)

    lay_flat(above_ref, own_ref, below_ref, flat)
    fill_shifted(flat, col_ref, shifted, rows + 2 * REACH, cols)
    conv_grad_block(
        row_taps, laid[step], shifted, wide, dk, mix_ref.at[0], djoined.at[step % 2], sums.at[step], rows, cols
    )

    @pl.when(step % 2 == 1)
    def _():
        grad = jnp.concatenate([djoined[0], djoined[1]], axis=1)
        share_columns(core, dot(normed[...], grad, TN), kept_ref, sent_ref, width, plane_first=True)
        dnorm[...] += dot(grad, in_ref[...], NT)

    @pl.when(step == pl.num_programs(0) - 1)
    def _():
        hat, scale = normalized(canvas_ref[...] * valid_ref[reach : reach + cells, :1])
        dgain = jnp.sum(dnorm[...] * hat, axis=0, keepdims=True)
        row = sums.shape[0] * TAPS
        for k in range(sums.shape[0]):
            small[k * TAPS : (k + 1) * TAPS, :] = sums[k, :TAPS]
        small[row:, :] = jnp.zeros((small.shape[0] - row, LANES), F32)
        for k in range(dgain.shape[1] // LANES):
            small[row + k : row + k + 1, :] = dgain[:, k * LANES : (k + 1) * LANES]
        half = small.shape[0] // 2
        for ref, start in ((small_kept_ref, core * half), (small_sent_ref, (1 - core) * half)):
            ref[...] = small[pl.ds(pl.multiple_of(start, 8), half), :]
        inner = dmiddle_ref[...] + norm_backward(dnorm[...] * gain_ref[...], hat, scale)
        dcanvas_ref[...] = inner * valid_ref[reach : reach + cells, :1]


def block_of(size):
    return pl.BlockSpec((1, size, LANES), lambda i: (i, 0, 0))


def small_rows(blocks, dim):
    return -(-(blocks * TAPS + dim // LANES) // 16) * 16


def backward(
    place, ids, above, own, below, mix, kern, canvas, gain, dmiddle, weight_in, ties, rows, cols, count_ha, count_ba
):
    cells, dim = canvas.shape
    blocks = own.shape[0]
    reach = above.shape[1]
    own_wide = weight_in.shape[1] // count_ha
    chunk_rows = dim // count_ba * lane_blocks(own_wide)
    groups = 2 * LANES // (2 * own_wide)
    chunk_spec = pl.BlockSpec((count_ba, groups, chunk_rows, LANES), lambda i: (0, i // 2, 0, 0))
    chunks = shape_of(count_ba, count_ha // 2, chunk_rows, LANES)
    tall = -(-TAPS // 8) * 8
    small = (small_rows(blocks, dim) // 2, LANES)
    return pl.pallas_call(
        functools.partial(backward_kernel, rows=rows, cols=cols),
        grid=(blocks,),
        in_specs=[in_smem(), in_smem(), whole(ids.shape)]
        + [block_of(size) for size in (reach, cells, reach, cells)]
        + [whole(kern.shape), whole(canvas.shape)]
        + [whole((1, dim)), whole((cells, dim))]
        + [pl.BlockSpec((dim, 2 * LANES), lambda i: (0, i // 2))]
        + [in_hbm()] * len(ties),
        out_specs=[whole((cells, dim)), chunk_spec, chunk_spec, whole(small), whole(small)],
        out_shape=[shape_of(cells, dim), chunks, chunks, shape_of(*small), shape_of(*small)],
        scratch_shapes=mask_scratch(ids, rows)
        + [
            pltpu.VMEM((KERN, cols // 8, 8, LANES), F32),
            pltpu.VMEM((cells + 2 * reach + 2 * EDGE, LANES), F32),
            pltpu.VMEM((KERN, rows + 2 * REACH, cols // 8, 8, LANES), F32),
            pltpu.VMEM((blocks, TAPS, LANES), F32),
            pltpu.VMEM((TAPS + KERN, 8, LANES), F32),
            pltpu.VMEM((TAPS, 8, LANES), F32),
            pltpu.VMEM((blocks, tall, LANES), F32),
            pltpu.VMEM((small_rows(blocks, dim), LANES), F32),
            pltpu.VMEM((2, cells, LANES), F32),
            pltpu.VMEM((cells, dim), F32),
            pltpu.VMEM((cells, dim), F32),
        ],
        compiler_params=params(),
        cost_estimate=lasting(25),
    )(place, ids, ids, above, own, below, mix, kern, canvas, gain, dmiddle, weight_in, *ties)


def exchange(values, axis, bit):
    return lax.ppermute(values, axis, [(i, i ^ bit) for i in range(lax.axis_size(axis))])


class View:
    def __init__(self, array, start, ways, fixed, rows):
        self.array, self.start, self.ways, self.fixed, self.rows = array, start, ways, fixed, rows

    def fix(self, way, step):
        if way == "line":
            near = lax.axis_size("ha") // 4
            return self.fix("far", step // near).fix("near", step % near)
        left = [entry for entry in self.ways if entry[0] != way]
        (stride,) = [entry[2] for entry in self.ways if entry[0] == way]
        return View(self.array, self.start, left, self.fixed + [(way, step, stride)], self.rows)

    def size(self):
        count = self.rows
        for _, size, _ in self.ways:
            count *= size
        return count

    def runs(self, ha, ba):
        start = self.start
        near = lax.axis_size("ha") // 4
        places = {"plane": ba, "far": ha // 2 // near, "near": ha // 2 % near}
        for way, step, stride in self.fixed:
            start = start + (places[way] ^ step) * stride
        rows, ways = self.rows, list(self.ways)
        while ways and ways[-1][2] == rows:
            rows *= ways.pop()[1]
        offsets = [0]
        for _, size, stride in ways:
            offsets = [offset + k * stride for offset in offsets for k in range(size)]
        return [pl.multiple_of(start + offset, 8) for offset in offsets], rows


def flat_view(array, start=0, rows=None):
    flat = array.reshape(-1, LANES)
    return View(flat, start, [], [], flat.shape[0] if rows is None else rows)


def combine(place, groups, ties=(), epilogue=None, out_shape=None):
    pieces, arrays = [], []
    for group in groups:
        for views in group:
            if not any(views is other for other in pieces):
                pieces.append(views)
    for views in pieces:
        for view in views:
            if not any(view.array is other for other in arrays):
                arrays.append(view.array)
    index_of = {id(array): k for k, array in enumerate(arrays)}
    piece_of = {id(views): k for k, views in enumerate(pieces)}
    sizes = [sum(views[0].size() for views in group) for group in groups]
    copies = sum(len(view.runs(0, 0)[0]) for views in pieces for view in views)
    plain = epilogue is None
    if plain:
        out_shape = [shape_of(size, LANES) for size in sizes]

    def kernel(place_ref, *refs):
        inputs = refs[: len(arrays)]
        refs = refs[len(arrays) + len(ties) :]
        outs, refs = refs[: len(out_shape)], refs[len(out_shape) :]
        buffers, refs = refs[: len(pieces)], refs[len(pieces) :]
        sems, results, out_sems = refs[0], refs[1:-1], refs[-1]
        ha, ba = place_ref[0], place_ref[1]
        moves, count = [], 0
        for piece, views in enumerate(pieces):
            moves.append([])
            for term, view in enumerate(views):
                source = inputs[index_of[id(view.array)]]
                starts, rows = view.runs(ha, ba)
                for k, start in enumerate(starts):
                    target = buffers[piece].at[term, pl.ds(k * rows, rows), :]
                    move = pltpu.make_async_copy(source.at[pl.ds(start, rows), :], target, sems.at[count])
                    move.start()
                    moves[-1].append(move)
                    count += 1
        values, waited, leaving = [], set(), []
        for out, group in enumerate(groups):
            row = 0
            for views in group:
                piece = piece_of[id(views)]
                if piece not in waited:
                    waited.add(piece)
                    for move in moves[piece]:
                        move.wait()
                value = buffers[piece][0]
                for term in range(1, len(views)):
                    value = value + buffers[piece][term]
                if plain:
                    results[out][row : row + value.shape[0], :] = value
                values.append(value)
                row += value.shape[0]
            if plain:
                leaving.append(pltpu.make_async_copy(results[out], outs[out], out_sems.at[out]))
                leaving[-1].start()
        if not plain:
            epilogue(ha, ba, values, outs)
        for move in leaving:
            move.wait()

    moved = sum(view.size() for views in pieces for view in views) + sum(sizes)
    scratch = [pltpu.VMEM((len(views), views[0].size(), LANES), F32) for views in pieces]
    scratch.append(pltpu.SemaphoreType.DMA((copies,)))
    if plain:
        scratch += [pltpu.VMEM((size, LANES), F32) for size in sizes]
    scratch.append(pltpu.SemaphoreType.DMA((len(groups),)))
    return pl.pallas_call(
        kernel,
        in_specs=[in_smem()] + [in_hbm()] * (len(arrays) + len(ties)),
        out_specs=[in_hbm() if plain else pl.BlockSpec(memory_space=pltpu.VMEM)] * len(out_shape),
        out_shape=out_shape,
        scratch_shapes=scratch,
        compiler_params=params(),
        cost_estimate=lasting(1 + moved * LANES * 4 / 3.0e6),
    )(place, *arrays, *ties)


def tied(arrays, ties):
    return pl.pallas_call(
        lambda *refs: None,
        in_specs=[pl.BlockSpec(memory_space=pl.ANY)] * (len(arrays) + len(ties)),
        out_specs=[pl.BlockSpec(memory_space=pl.ANY)] * len(arrays),
        out_shape=[shape_of(*array.shape) for array in arrays],
        input_output_aliases={k: k for k in range(len(arrays))},
        compiler_params=params(),
        cost_estimate=lasting(0.5),
    )(*arrays, *ties)


class Sum:
    def __init__(self, arrays, names):
        self.views = []
        near = lax.axis_size("ha") // 4
        sizes = {"plane": lax.axis_size("ba"), "far": 2, "near": near}
        for array in arrays:
            flat = array.reshape(-1, LANES)
            stride, ways = flat.shape[0], []
            for name in names:
                stride //= sizes[name]
                ways.append((name, sizes[name], stride))
            self.views.append(View(flat, 0, ways, [], stride))

    def leaving(self, way, step):
        return [view.fix(way, step) for view in self.views]

    def keep(self, way, sent, arrived):
        self.views = [view.fix(way, 0) for view in self.views]
        rows = self.views[0].rows
        stride, ways = rows, []
        for name, size, _ in reversed(self.views[0].ways):
            ways.insert(0, (name, size, stride))
            stride *= size
        self.views += [View(array, start, ways, [], rows) for array, start in arrived]

    def part(self, first, rows):
        return [View(view.array, view.start + first, view.ways, view.fixed, rows) for view in self.views]


class Rider:
    def __init__(self, views):
        self.views = views

    def leaving(self, way, step):
        return self.views

    def keep(self, way, sent, arrived):
        rows = self.views[0].size()
        self.views = [View(array, start, [], [], rows) for array, start in [sent] + arrived]


class Gather(Rider):
    def keep(self, way, sent, arrived):
        rows = self.views[0].size()
        self.gathered = [[View(array, start, [], [], rows)] for array, start in [sent] + arrived]


class Stage:
    def __init__(self, members, way):
        self.members, self.way = members, way
        line, near = lax.axis_size("ha") // 2, lax.axis_size("ha") // 4
        self.steps = {
            "plane": list(range(1, lax.axis_size("ba"))),
            "line": list(range(1, line)),
            "far": [near],
        }[way]
        self.near = near

    def taking(self, step):
        takes = {"plane": True, "line": True, "near": step < self.near, "far": step == self.near}
        return [(one, way) for one, way in self.members if takes[way]]

    def groups(self):
        return [
            [one.leaving(way, step // self.near if way == "far" else step) for one, way in self.taking(step)]
            for step in self.steps
        ]

    def go(self, payloads, in_turn=None):
        axis, unit = ("ba", 1) if self.way == "plane" else ("ha", 2)
        arrived = []
        for step, part in zip(self.steps, payloads):
            if in_turn is not None and len(arrived) == 2:
                (part,) = tied([part], [arrived[in_turn]])
            arrived.append(exchange(part, axis, unit * step))
        places = {}
        for step, sent, part in zip(self.steps, payloads, arrived):
            row = 0
            for one, way in self.taking(step):
                places.setdefault(id(one), []).append(((sent, row), (part, row)))
                row += one.leaving(way, 1)[0].size()
        for one, way in self.members:
            mine = places.get(id(one), [])
            one.keep(way, mine[:2][-1][0] if mine else None, [part for _, part in mine])
        return arrived


def run(place, stage, ties=(), in_turn=None, extra=()):
    groups = stage.groups()
    made = list(combine(place, groups + list(extra), ties))
    made, more = made[: len(groups)], made[len(groups) :]
    return made, stage.go(made, in_turn), more


def neighbour_rows(top, bottom):
    count = lax.axis_size("ha")
    up = [(i, i + 1) for i in range(count - 1)]
    down = [(i + 1, i) for i in range(count - 1)]
    return lax.ppermute(bottom, "ha", up), lax.ppermute(top, "ha", down)


def lay_beside(value, ref):
    tall, width = ref.shape
    for k in range(lane_blocks(width)):
        columns = slice(k * LANES, min(width, (k + 1) * LANES))
        ref[:, columns] = value[k * tall : (k + 1) * tall, : columns.stop - columns.start]


def lay_large(ha, ba, values, outs):
    up_first, up_second, down_first, down_second, out = values
    lay_beside(jnp.concatenate([up_first, up_second], axis=0), outs[0])
    lay_beside(jnp.concatenate([down_first, down_second], axis=0), outs[1])
    lay_beside(out, outs[2])


def lay_small(ha, ba, values, outs, blocks):
    din_ref, dk_ref, gain_ref = outs[:3]
    scratch = outs[-1]
    lay_beside(values[0], din_ref)
    count = lax.axis_size("ba")
    own, other = values[1 : 2 + count], values[2 + count :]
    mine = ha % 2 == 0
    dkern = jnp.concatenate([jnp.where(mine, own[0], other[0]), jnp.where(mine, other[0], own[0])], axis=0)
    joined = jnp.concatenate([dkern[k * TAPS : (k + 1) * TAPS] for k in range(blocks)], axis=1)
    dk_ref[...] = joined[:, joined.shape[1] - dk_ref.shape[1] :]
    part = own[1].shape[0]
    for side, parts in ((ha % 2, own[1:]), (1 - ha % 2, other[1:])):
        for step, rows in enumerate(parts):
            start = (side * count + (ba ^ step)) * part
            scratch[pl.ds(pl.multiple_of(start, 8), part), :] = rows
    dim = gain_ref.shape[1]
    for k in range(dim // LANES):
        columns = slice(k * LANES, (k + 1) * LANES)
        row = blocks * TAPS + k
        gain_ref[:, columns] = dkern[row : row + 1]
        for vector, ref in enumerate(outs[3:6]):
            ref[:, columns] = scratch[vector * dim // LANES + k : vector * dim // LANES + k + 1, :]
    row = scratch.shape[0]
    for ref in reversed(outs[6:-1]):
        tall, width = ref.shape
        row -= tall * width // LANES
        for k in range(width // LANES):
            ref[:, k * LANES : (k + 1) * LANES] = scratch[row + k * tall : row + (k + 1) * tall, :]


def shards(
    canvas,
    image_id,
    keep_first,
    keep_second,
    first_gain,
    weight_in,
    depth_kernel,
    gate_first,
    gate_second,
    gate_third,
    weight_out,
    scale_first,
    second_gain,
    weight_up,
    weight_down,
    scale_second,
    cotangent,
):
    _, rows, cols, dim = canvas.shape
    cells = rows * cols
    reach = REACH * cols
    count_ha, count_ba = lax.axis_size("ha"), lax.axis_size("ba")
    hidden = weight_up.shape[1]
    blocks = weight_in.shape[1] // LANES
    place = jnp.stack([lax.axis_index("ha"), lax.axis_index("ba")])
    own = canvas.reshape(cells, dim)
    gates = (gate_first, gate_second, gate_third)
    gain = first_gain[None]
    vectors = (gain, scale_first[None], second_gain[None], scale_second[None])
    ids = image_id[0]
    above, below = neighbour_rows(own[:reach], own[cells - reach :])
    ahead = head(ids, keep_first, keep_second, own, gain, weight_in, rows, cols)
    joined = ahead[0]
    (
        output, dmiddle, dconv, dconv_top, dconv_bottom, plane_kept, plane_sent, line_kept, line_sent,
        packed_kept, packed_sent,
    ) = forward(
        ids, ahead, above, own, below, cotangent.reshape(cells, dim), vectors,
        weight_in, depth_kernel, gates, weight_out, weight_up, weight_down, rows, cols, count_ha, count_ba,
    )
    above, below = neighbour_rows(dconv_top, dconv_bottom)

    plane_sum = Sum([plane_kept, exchange(plane_sent, "ha", 1)], ["plane", "far", "near"])
    line_sum = Sum([line_kept, exchange(line_sent, "ha", 1)], ["far", "near", "plane"])
    packed = Sum([packed_kept, exchange(packed_sent, "ha", 1)], ["plane"])
    made, arrived, _ = run(place, Stage([(plane_sum, "plane"), (packed, "plane")], "plane"))
    apart = Stage([(line_sum, "far")], "far")
    more = list(tied(combine(place, apart.groups(), made), [above, below]))
    made, arrived = made + more, arrived + apart.go(more)
    dcanvas, in_kept, in_sent, small_kept, small_sent = backward(
        place, ids, above, dconv, below, joined, depth_kernel, own, gain, dmiddle, weight_in, made,
        rows, cols, count_ha, count_ba,
    )
    in_sent, small_sent = tied([in_sent, small_sent], arrived)
    in_sum = Sum([in_kept, exchange(in_sent, "ha", 1)], ["plane", "far", "near"])
    small = Rider([flat_view(small_kept), flat_view(exchange(small_sent, "ha", 1))])
    packed = Rider(packed.views)
    packed = Rider(packed.views)
    made, arrived, _ = run(
        place, Stage([(plane_sum, "far"), (line_sum, "near"), (packed, "line")], "line"), in_turn=0
    )
    run(place, Stage([(in_sum, "plane"), (small, "plane")], "plane"), ties=made)
    along = Stage([(plane_sum, "near"), (in_sum, "line"), (small, "line")], "line")
    made, arrived, (own_small,) = run(place, along, ties=arrived[:2], in_turn=1, extra=[[small.views]])
    packed = Gather(packed.views)
    across = Stage([(line_sum, "plane"), (packed, "plane")], "plane")
    _, crossed, (own_packed,) = run(place, across, ties=made, extra=[[packed.views]])
    cut = plane_sum.views[0].rows // 2
    rest = (line_sum.views[0].rows - dim // count_ha * lane_blocks(dim // count_ba)) // 2
    dup, ddown, dout = combine(
        place,
        [
            [
                plane_sum.part(0, cut),
                line_sum.part(0, rest),
                plane_sum.part(cut, cut),
                line_sum.part(rest, rest),
                line_sum.part(2 * rest, line_sum.views[0].rows - 2 * rest),
            ]
        ],
        epilogue=lay_large,
        out_shape=[
            shape_of(dim // count_ba, hidden // count_ha),
            shape_of(dim // count_ha, hidden // count_ba),
            shape_of(dim // count_ha, dim // count_ba),
        ],
    )
    sent = list(tied([own_small, own_packed], arrived[1:2]))
    others = [exchange(part, "ha", 1) for part in sent + arrived + crossed]
    other_of = {id(part): other for part, other in zip(arrived + crossed, others[2:])}

    def from_other(view):
        return View(other_of[id(view.array)], view.start, view.ways, view.fixed, view.rows)

    own_parts = [small.views] + packed.gathered
    other_parts = [[flat_view(others[0])] + [from_other(view) for view in small.views[1:]], [flat_view(others[1])]]
    other_parts += [[from_other(view) for view in views] for views in packed.gathered[1:]]
    din, dkern, dgain_one, dscale_one, dgain_two, dscale_two, dfirst, dsecond, dthird, _ = combine(
        place,
        [[in_sum.views] + own_parts + other_parts],
        ties=[dup],
        epilogue=functools.partial(lay_small, blocks=blocks),
        out_shape=[shape_of(dim // count_ba, weight_in.shape[1] // count_ha), shape_of(*depth_kernel.shape)]
        + [shape_of(1, dim)] * 4
        + [shape_of(*gate.shape) for gate in gates]
        + [shape_of(packed_rows(gates, dim, count_ba), LANES)],
    )
    return (
        output.reshape(canvas.shape),
        dcanvas.reshape(canvas.shape),
        dgain_one[0],
        din,
        dkern,
        dfirst,
        dsecond,
        dthird,
        dout.T,
        dscale_one[0],
        dgain_two[0],
        dup,
        ddown.T,
        dscale_two[0],
    )


def solution(mesh):
    in_specs = (
        P("ba", "ha", None, None),
        P("ba", None, None),
        P("ba", None),
        P("ba", None),
    ) + (P(),) * 12 + (P("ba", "ha", None, None),)
    tiled = P("ba", "ha")
    out_specs = (
        P("ba", "ha", None, None),
        P("ba", "ha", None, None),
        P(),
        tiled,
        P(),
        P(),
        P(),
        P(),
        tiled,
        P(),
        P(),
        tiled,
        tiled,
        P(),
    )
    return jax.shard_map(shards, mesh=mesh, in_specs=in_specs, out_specs=out_specs, check_vma=False)
```

```python
import functools

import jax
import jax.numpy as jnp
from jax import lax
from jax.experimental import pallas as pl
from jax.experimental.pallas import tpu as pltpu
from jax.sharding import PartitionSpec as P

KERN = 7
TAPS = KERN * KERN
REACH = KERN // 2
KEEP_RATE = 0.8
SPREAD = 1.0 / 3.0
EPSILON = 1e-06
LANES = 128
EDGE = 8
VMEM_BYTES = 64 << 20
F32 = jnp.float32
INV_SQRT_2 = 0.7071067811865476
INV_SQRT_2PI = 0.3989422804014327
NN = (((1,), (0,)), ((), ()))
NT = (((1,), (1,)), ((), ()))
TN = (((0,), (0,)), ((), ()))


def dot(left, right, dims=NN):
    return lax.dot_general(left, right, dims, precision=lax.Precision.HIGH, preferred_element_type=F32)


def normalized(values):
    centered = values - jnp.mean(values, axis=-1, keepdims=True)
    scale = lax.rsqrt(jnp.mean(centered * centered, axis=-1, keepdims=True) + EPSILON)
    return centered * scale, scale


def norm_backward(grad_hat, hat, scale):
    return scale * (
        grad_hat
        - jnp.mean(grad_hat, axis=-1, keepdims=True)
        - hat * jnp.mean(grad_hat * hat, axis=-1, keepdims=True)
    )


def params():
    return pltpu.CompilerParams(vmem_limit_bytes=VMEM_BYTES)


def lasting(microseconds):
    return pl.CostEstimate(flops=int(microseconds * 1.1e9), bytes_accessed=0, transcendentals=0)


def whole(shape):
    return pl.BlockSpec(tuple(shape), lambda *_: (0,) * len(shape), pipeline_mode=pl.Buffered(1))


def in_smem():
    return pl.BlockSpec(memory_space=pltpu.SMEM)


def in_hbm():
    return pl.BlockSpec(memory_space=pltpu.HBM)


def shape_of(*shape):
    return jax.ShapeDtypeStruct(shape, F32)


def lane_blocks(width):
    return -(-width // LANES)


def image_ids(ids_ref, padded, place, rows):
    height, cols = ids_ref.shape
    padded[...] = jnp.full(padded.shape, -1, jnp.int32)
    padded[EDGE : EDGE + height, :] = ids_ref[...]
    ids = padded[pl.ds(place * rows + (EDGE - REACH), rows + 2 * REACH), :]
    return jnp.concatenate([ids, jnp.full((-ids.shape[0] % 8, cols), -1, jnp.int32)], axis=0).T


def spread_cells(factors, out_ref, first, rows):
    cols = factors.shape[0]
    for r in range(rows):
        column = factors[:, first + r : first + r + 1]
        out_ref[r * cols : (r + 1) * cols, :] = jnp.broadcast_to(column, (cols, LANES))


def keep_factors(turned, table_ref):
    result = jnp.zeros(turned.shape, F32)
    for slot in range(table_ref.shape[1]):
        result = jnp.where(turned == slot, table_ref[0, slot].astype(F32) / KEEP_RATE, result)
    return result


def conv_masks(ids_scalar, ids_ref, place, row_taps, col_mask, rows):
    height, cols = ids_ref.shape
    column_masks(ids_ref, col_mask)
    row_masks(ids_scalar, place, row_taps, rows, height, cols)


def column_masks(ids_ref, col_mask):
    height, cols = ids_ref.shape
    wide_ids = jnp.broadcast_to(ids_ref[...].T[:, height // 2 : height // 2 + 1], (cols, LANES))
    column = lax.broadcasted_iota(jnp.int32, (cols, LANES), 0)
    for b in range(KERN):
        shift = b - REACH
        moved = pltpu.roll(wide_ids, (-shift) % cols, 0)
        inside = (column + shift >= 0) & (column + shift < cols)
        same = (moved == wide_ids) & inside
        col_mask[b] = same.astype(F32).reshape(cols // 8, 8, LANES)


def row_masks(ids_scalar, place, row_taps, rows, height, cols):
    def one(r, _):
        own = ids_scalar[place * rows + r, cols // 2]
        row_taps[r, 0] = KERN
        row_taps[r, KERN + 1] = KERN
        for a in range(KERN):
            other = place * rows + r + a - REACH
            inside = (other >= 0) & (other < height)
            same = ids_scalar[jnp.clip(other, 0, height - 1), cols // 2] == own
            row_taps[r, a + 1] = jnp.where(inside & same, a, KERN)
        return 0

    lax.fori_loop(0, rows, one, 0)


def lay_kernel(kern_ref, laid, split):
    tap = lax.broadcasted_iota(jnp.int32, (TAPS, split), 0)
    own = jnp.where(tap == TAPS // 2, 1.0 / SPREAD, 0.0).astype(F32)
    for k in range(laid.shape[0]):
        start = k * LANES - split
        left = own if k == 0 else kern_ref[:, start : start + split]
        laid[k] = jnp.concatenate([left, kern_ref[:, start + split : start + LANES]], axis=1) * SPREAD


def fill_shifted(flat, col_ref, shifted, rows_ext, cols):
    for b in range(KERN):
        for g in range(cols // 8):
            mask = None if b == REACH else col_ref[b, g]
            for r in range(rows_ext):
                x = flat[pl.ds(EDGE + r * cols + 8 * g + b - REACH, 8), :]
                shifted[b, r, g] = x if b == REACH else x * mask


def spread_taps(kern, wide, turned):
    for t in range(TAPS):
        source = TAPS - 1 - t if turned else t
        wide[t] = jnp.broadcast_to(kern[source : source + 1, :], (8, LANES))
    for t in range(KERN):
        wide[TAPS + t] = jnp.zeros((8, LANES), F32)


def conv_block(row_taps, kern, shifted, wide, out_ref, rows, cols):
    groups = cols // 8
    spread_taps(kern, wide, False)

    def pair(h, _):
        r = 2 * h

        def step(i, totals):
            first, second = totals
            taps_first = row_taps[r, i + 1] * KERN
            taps_second = row_taps[r + 1, i] * KERN
            for b in range(KERN):
                x = shifted[b, r + i]
                first = first + wide[taps_first + b][None] * x
                second = second + wide[taps_second + b][None] * x
            return first, second

        zero = jnp.zeros((groups, 8, LANES), F32)
        first, second = lax.fori_loop(0, KERN + 1, step, (zero, zero), unroll=4)
        out_ref[pl.ds(pl.multiple_of(r * cols, cols), cols), :] = first.reshape(cols, LANES)
        out_ref[pl.ds(pl.multiple_of((r + 1) * cols, cols), cols), :] = second.reshape(cols, LANES)
        return 0

    lax.fori_loop(0, rows // 2, pair, 0)


def conv_grad_block(row_taps, kern, shifted, wide, dk, mix_ref, out_ref, dk_ref, rows, cols):
    groups = cols // 8
    spread_taps(kern, wide, True)
    for t in range(TAPS):
        dk[t] = jnp.zeros((8, LANES), F32)

    def one(r, _):
        start = pl.ds(pl.multiple_of(r * cols, cols), cols)
        mix = mix_ref[start, :].reshape(groups, 8, LANES)
        total = jnp.zeros((groups, 8, LANES), F32)
        for i in range(KERN):
            row = row_taps[r, i + 1]
            same = jnp.where(row < KERN, 1.0, 0.0).astype(F32)
            for b in range(KERN):
                x = shifted[b, r + i]
                total = total + wide[row * KERN + b][None] * x
                dk[i * KERN + b] += jnp.sum(mix * x, axis=0) * same
        out_ref[start, :] = total.reshape(cols, LANES)
        return 0

    lax.fori_loop(0, rows, one, 0)
    for t in range(TAPS):
        dk_ref[TAPS - 1 - t : TAPS - t, :] = jnp.sum(dk[t], axis=0, keepdims=True) * SPREAD
    dk_ref[TAPS:, :] = jnp.zeros((dk_ref.shape[0] - TAPS, LANES), F32)


def share(core, first, second, kept_ref, sent_ref, z, p):
    mine = core == 0
    tall, width = first.shape
    for ref, chunk in (
        (kept_ref, jnp.where(mine, first, second)),
        (sent_ref, jnp.where(mine, second, first)),
    ):
        for k in range(lane_blocks(width)):
            part = chunk[:, k * LANES : (k + 1) * LANES]
            if part.shape[1] < LANES:
                part = jnp.concatenate([part, jnp.zeros((tall, LANES - part.shape[1]), F32)], axis=1)
            ref[z, p, k * tall : (k + 1) * tall, :] = part


def share_columns(core, grad, kept_ref, sent_ref, width, plane_first=False):
    groups, parts = reversed(kept_ref.shape[:2]) if plane_first else kept_ref.shape[:2]
    tall = grad.shape[0] // parts
    for z in range(groups):
        for p in range(parts):
            rows = slice(p * tall, (p + 1) * tall)
            first = grad[rows, 2 * z * width : (2 * z + 1) * width]
            second = grad[rows, (2 * z + 1) * width : (2 * z + 2) * width]
            share(core, first, second, kept_ref, sent_ref, *((p, z) if plane_first else (z, p)))


def share_rows(core, grad, kept_ref, sent_ref, tall):
    groups, parts = kept_ref.shape[:2]
    width = grad.shape[1] // parts
    for z in range(groups):
        for p in range(parts):
            columns = slice(p * width, (p + 1) * width)
            first = grad[2 * z * tall : (2 * z + 1) * tall, columns]
            second = grad[(2 * z + 1) * tall : (2 * z + 2) * tall, columns]
            share(core, first, second, kept_ref, sent_ref, z, p)


class Copies:
    def __init__(self, sems):
        self.sems, self.count, self.pending = sems, 0, {}

    def start(self, name, source, target):
        copy = pltpu.make_async_copy(source, target, self.sems.at[self.count])
        self.count += 1
        copy.start()
        self.pending.setdefault(name, []).append(copy)

    def wait(self, *names):
        for name in names:
            for copy in self.pending.pop(name):
                copy.wait()

    def wait_all(self):
        self.wait(*list(self.pending))


def head_kernel(
    ids_scalar, one_table, two_table, ids_hbm, own_hbm, gain_hbm, in_hbm_ref,
    joined_hbm, valid_hbm, one_keep_hbm, two_keep_hbm, col_hbm,
    ids_ref, rows_ref, gain_ref, in_ref, padded, valid_ref, one_keep_ref, two_keep_ref, col_ref, normed, joined, sems,
    *, rows, cols,
):
    cells = rows * cols
    reach = REACH * cols
    steps = in_ref.shape[0]
    copies = Copies(sems)
    copies.start("own", own_hbm, rows_ref)
    copies.start("own", gain_hbm, gain_ref)
    copies.start("ids", ids_hbm, ids_ref)
    for k in range(steps):
        copies.start(("in", k), in_hbm_ref.at[:, pl.ds(2 * LANES * k, 2 * LANES)], in_ref.at[k])
    copies.wait("own")
    hat, _ = normalized(rows_ref[...])
    normed[...] = hat * gain_ref[...]
    copies.wait("ids")
    turned = image_ids(ids_ref, padded, lax.axis_index("ha"), rows)
    spread_cells((turned >= 0).astype(F32), valid_ref, 0, rows + 2 * REACH)
    copies.start("outs", valid_ref, valid_hbm)
    normed[...] *= valid_ref[reach : reach + cells, :1]
    for step in range(steps):
        copies.wait(("in", step))
        part = dot(normed[...], in_ref[step])
        for k in range(2):
            joined[2 * step + k] = part[:, k * LANES : (k + 1) * LANES]
        pair = pl.ds(2 * step, 2)
        copies.start("outs", joined.at[pair], joined_hbm.at[pair])
    spread_cells(keep_factors(turned, one_table), one_keep_ref, REACH, rows)
    spread_cells(keep_factors(turned, two_table), two_keep_ref, REACH, rows)
    column_masks(ids_ref, col_ref)
    for source, target in ((one_keep_ref, one_keep_hbm), (two_keep_ref, two_keep_hbm), (col_ref, col_hbm)):
        copies.start("outs", source, target)
    copies.wait_all()


def head(ids, keep_one, keep_two, own, gain, weight_in, rows, cols):
    cells, dim = own.shape
    cells_ext = cells + 2 * REACH * cols
    blocks = weight_in.shape[1] // LANES
    vmem = functools.partial(pltpu.VMEM, dtype=F32)
    shapes = [
        (blocks, cells, LANES), (cells_ext, LANES), (cells, LANES), (cells, LANES), (KERN, cols // 8, 8, LANES)
    ]
    return pl.pallas_call(
        functools.partial(head_kernel, rows=rows, cols=cols),
        in_specs=[in_smem()] * 3 + [in_hbm()] * 4,
        out_specs=[in_hbm()] * len(shapes),
        out_shape=[shape_of(*shape) for shape in shapes],
        scratch_shapes=[
            pltpu.VMEM(ids.shape, jnp.int32),
            vmem((cells, dim)),
            vmem((1, dim)),
            vmem((blocks // 2, dim, 2 * LANES)),
            pltpu.VMEM((ids.shape[0] + 2 * EDGE, ids.shape[1]), jnp.int32),
        ]
        + [vmem(shape) for shape in shapes[1:]]
        + [vmem((cells, dim)), vmem(shapes[0]), pltpu.SemaphoreType.DMA((7 + blocks,))],
        compiler_params=params(),
        cost_estimate=lasting(7),
    )(ids, keep_one, keep_two, ids, own, gain, weight_in)


def forward_kernel(
    ids_scalar, joined_hbm, valid_hbm, one_keep_hbm, two_keep_hbm, col_hbm, above_hbm, own_hbm, below_hbm, cot_hbm,
    first_gain_hbm, first_scale_hbm, second_gain_hbm, second_scale_hbm,
    in_hbm_ref, kern_hbm, one_hbm, two_hbm, three_hbm, out_hbm, up_hbm, down_hbm,
    output_hbm, dmiddle_hbm, dconv_hbm, dconv_top_hbm, dconv_bottom_hbm,
    plane_kept_ref, plane_sent_ref, line_kept_ref, line_sent_ref, packed_kept_hbm, packed_sent_hbm,
    rows_ref, cot_ref, first_gain_ref, first_scale_ref, second_gain_ref, second_scale_ref,
    in_ref, kern_ref, one_ref, two_ref, three_ref, out_ref, up_ref, down_ref, dconv_ref, sems, chunk_sems,
    up_kept, up_sent, down_kept, down_sent, out_kept, out_sent,
    row_taps, valid_ref, one_keep_ref, two_keep_ref, col_ref, packed_ref, normed, flat, shifted, laid, wide, conv,
    mixed_ref, mapped_ref, middle_ref, result, dnorm,
    *, rows, cols, count_ha, count_ba,
):
    blocks = flat.shape[0]
    cells = rows * cols
    reach = REACH * cols
    cells_ext = cells + 2 * reach
    core = lax.axis_index("ha") % 2
    split = one_ref.shape[0]
    dim = rows_ref.shape[1]
    head_steps = blocks // 2
    ffn_steps = up_kept.shape[0]
    chunk = down_ref.shape[1]
    gate_refs = (one_ref, two_ref, three_ref)

    copies = Copies(sems)
    copies.start("rows", valid_hbm, valid_ref)
    copies.start("rows", first_gain_hbm, first_gain_ref)
    copies.start("above", above_hbm, rows_ref.at[pl.ds(0, reach)])
    copies.start("below", below_hbm, rows_ref.at[pl.ds(reach + cells, reach)])
    for k in range(head_steps):
        copies.start(("in", k), in_hbm_ref.at[:, pl.ds(2 * LANES * k, 2 * LANES)], in_ref.at[k])
    copies.start("conv", joined_hbm, flat.at[:, pl.ds(EDGE + reach, cells), :])
    copies.start("conv", col_hbm, col_ref)
    copies.start("gates", own_hbm, rows_ref.at[pl.ds(reach, cells)])
    copies.start("gates", one_keep_hbm, one_keep_ref)
    copies.start("gates", two_keep_hbm, two_keep_ref)
    copies.start("kern", kern_hbm, kern_ref)
    def weights(k):
        ends = pl.ds(pl.multiple_of(k * chunk, chunk), chunk)
        return [
            pltpu.make_async_copy(up_hbm.at[:, ends], up_ref.at[k], chunk_sems.at[k, 0]),
            pltpu.make_async_copy(down_hbm.at[ends, :], down_ref.at[k], chunk_sems.at[k, 1]),
        ]

    def chunk_copies(place):
        moves = []
        sides = ((up_kept, down_kept, plane_kept_ref, line_kept_ref), (up_sent, down_sent, plane_sent_ref, line_sent_ref))
        for up, down, plane, line in sides:
            cut = plane.shape[2] // 2
            rest = up.shape[3] - cut
            zs = pl.ds(place * up.shape[1], up.shape[1])
            bas = pl.ds(place * down.shape[2], down.shape[2])
            moves += [
                (up.at[place, :, ba, pl.ds(0, cut), :], plane.at[ba, zs, pl.ds(0, cut), :])
                for ba in range(plane.shape[0])
            ]
            moves += [
                (down.at[place, z, :, pl.ds(0, cut), :], plane.at[bas, z, pl.ds(cut, cut), :])
                for z in range(plane.shape[1])
            ]
            moves.append((up.at[place, :, :, pl.ds(cut, rest), :], line.at[zs, :, pl.ds(0, rest), :]))
            moves.append((down.at[place, :, :, pl.ds(cut, rest), :], line.at[:, bas, pl.ds(rest, rest), :]))
        return [
            pltpu.make_async_copy(source, target, chunk_sems.at[place, 2 + k])
            for k, (source, target) in enumerate(moves)
        ]

    row_masks(ids_scalar, lax.axis_index("ha"), row_taps, rows, ids_scalar.shape[0], cols)
    copies.wait("rows")
    for name, start, place in (("above", 0, 0), ("below", reach + cells, reach)):
        copies.wait(name)
        hat, _ = normalized(rows_ref[start : start + reach, :] * valid_ref[start : start + reach, :1])
        normed[place : place + reach] = hat * first_gain_ref[...]

    for k in range(blocks):
        flat[k, :EDGE] = jnp.zeros((EDGE, LANES), F32)
        flat[k, EDGE + cells_ext :] = jnp.zeros((EDGE, LANES), F32)
    for step in range(head_steps):
        copies.wait(("in", step))
        joined = dot(normed[: 2 * reach], in_ref[step])
        for k in range(2):
            part = joined[:, k * LANES : (k + 1) * LANES]
            flat[2 * step + k, EDGE : EDGE + reach] = part[:reach]
            flat[2 * step + k, EDGE + reach + cells : EDGE + cells_ext] = part[reach:]
        if step == 0:
            copies.start("gates", first_scale_hbm, first_scale_ref)
            copies.start("gates", second_gain_hbm, second_gain_ref)
            copies.start("gates", second_scale_hbm, second_scale_ref)
            for source, target in zip((one_hbm, two_hbm, three_hbm, out_hbm, cot_hbm), gate_refs + (out_ref, cot_ref)):
                copies.start("gates", source, target)
            for k in range(ffn_steps):
                for copy in weights(k):
                    copy.start()

    copies.wait("conv")
    copies.wait("kern")
    lay_kernel(kern_ref, laid, split)

    def conv_step(block, _):
        fill_shifted(flat.at[block], col_ref, shifted, rows + 2 * REACH, cols)
        conv_block(row_taps, laid[block], shifted, wide, conv.at[block], rows, cols)
        return 0

    lax.fori_loop(0, blocks, conv_step, 0)

    def conv_part(start, width):
        return jnp.concatenate([conv[start // LANES + k] for k in range(width // LANES)], axis=1)

    copies.wait("gates")
    mixed = conv[0, :, :split] * conv[0, :, split:]
    mixed_ref[:, :split] = mixed
    start = 2 * split
    for ref in gate_refs:
        width = ref.shape[1]
        mapped = dot(mixed, ref[...])
        mapped_ref[:, start - 2 * split : start - 2 * split + width] = mapped
        mixed = mapped * conv_part(start, width)
        mixed_ref[:, start : start + width] = mixed
        start += width
    branch = dot(mixed, out_ref[...])
    masked = rows_ref[reach : reach + cells, :] * valid_ref[reach : reach + cells, :1]
    middle = masked + one_keep_ref[:, :1] * first_scale_ref[...] * branch
    middle_ref[...] = middle
    hat, _ = normalized(middle)
    normed[:cells] = hat * second_gain_ref[...]
    result[...] = jnp.zeros_like(result)
    dnorm[...] = jnp.zeros_like(dnorm)

    def ffn_step(place, _):
        for copy in weights(place):
            copy.wait()
        grad_result = two_keep_ref[:, :1] * second_scale_ref[...] * cot_ref[...]
        pre = dot(normed[:cells], up_ref[place])
        cdf = 0.5 + 0.5 * lax.erf(pre * INV_SQRT_2)
        slope = cdf + pre * (INV_SQRT_2PI * jnp.exp(-0.5 * pre * pre))
        hidden = pre * cdf
        result[...] += dot(hidden, down_ref[place])
        grad_pre = dot(grad_result, down_ref[place], NT) * slope
        share_rows(
            core, dot(grad_result, hidden, TN), down_kept.at[place], down_sent.at[place], dim // count_ha
        )
        width = chunk // (2 * up_kept.shape[1])
        share_columns(core, dot(normed[:cells], grad_pre, TN), up_kept.at[place], up_sent.at[place], width)
        for copy in chunk_copies(place):
            copy.start()
        dnorm[...] += dot(grad_pre, up_ref[place], NT)
        return 0

    lax.fori_loop(0, ffn_steps, ffn_step, 0)

    hat, scale = normalized(middle_ref[...])
    kept = two_keep_ref[:, :1] * result[...]
    dscale_two = jnp.sum(cot_ref[...] * kept, axis=0, keepdims=True)
    result[...] = middle_ref[...] + second_scale_ref[...] * kept
    copies.start("outs", result, output_hbm)
    dgain_two = jnp.sum(dnorm[...] * hat, axis=0, keepdims=True)
    dmiddle = cot_ref[...] + norm_backward(dnorm[...] * second_gain_ref[...], hat, scale)
    dnorm[...] = dmiddle
    copies.start("outs", dnorm, dmiddle_hbm)
    kept = one_keep_ref[:, :1] * dmiddle
    grad = dot(kept * first_scale_ref[...], out_ref[...], NT)
    row = packed_ref.shape[0]
    start = blocks * LANES
    for ref in reversed(gate_refs):
        tall, width = ref.shape
        start -= width
        source = start - tall if tall > split else 0
        columns = slice(start - 2 * split, start - 2 * split + width)
        dconv = grad * mapped_ref[:, columns]
        for k in range(width // LANES):
            dconv_ref[start // LANES + k] = dconv[:, k * LANES : (k + 1) * LANES]
        grad_mapped = grad * conv_part(start, width)
        part = dot(mixed_ref[:, source : source + tall], grad_mapped, TN)
        row -= tall * width // LANES
        for k in range(width // LANES):
            packed_ref[row + k * tall : row + (k + 1) * tall] = part[:, k * LANES : (k + 1) * LANES]
        grad = dot(grad_mapped, ref[...], NT)
    dconv_ref[0] = jnp.concatenate([grad * conv[0, :, split:], grad * conv[0, :, :split]], axis=1)
    copies.start("outs", dconv_ref.at[:, pl.ds(0, reach), :], dconv_top_hbm)
    copies.start("outs", dconv_ref.at[:, pl.ds(cells - reach, reach), :], dconv_bottom_hbm)
    copies.start("outs", dconv_ref, dconv_hbm)
    start = mixed_ref.shape[1] - out_ref.shape[0]
    crossed = dot(mixed_ref[:, start:], kept, TN)
    dscale_one = jnp.sum(crossed * out_ref[...], axis=0, keepdims=True)
    packed_ref[:row] = jnp.zeros((row, LANES), F32)
    row = 0
    for vector in (dscale_one, dgain_two, dscale_two):
        for k in range(dim // LANES):
            packed_ref[row : row + 1] = vector[:, k * LANES : (k + 1) * LANES]
            row += 1
    half = packed_kept_hbm.shape[0]
    for place, target in ((core, packed_kept_hbm), (1 - core, packed_sent_hbm)):
        copies.start("outs", packed_ref.at[pl.ds(pl.multiple_of(place * half, 8), half), :], target)
    share_rows(core, (crossed * first_scale_ref[...]).T, out_kept, out_sent, dim // count_ha)
    for source, line in ((out_kept, line_kept_ref), (out_sent, line_sent_ref)):
        tall = source.shape[2]
        copies.start("outs", source, line.at[:, :, pl.ds(line.shape[2] - tall, tall), :])
    for place in range(ffn_steps):
        for copy in chunk_copies(place):
            copy.wait()
    copies.wait_all()


def mask_scratch(ids, rows):
    height, cols = ids.shape
    return [
        pltpu.SMEM((rows, KERN + 2), jnp.int32),
        pltpu.VMEM((height + 2 * EDGE, cols), jnp.int32),
        pltpu.VMEM(((rows + 2 * REACH) * cols, LANES), F32),
    ]


def packed_rows(gates, dim, parts):
    rows = sum(gate.size for gate in gates) // LANES + 3 * dim // LANES
    return -(-rows // (16 * parts)) * 16 * parts


def plane_share(rows):
    return max(rows * 3 // 4 // 8 * 8, 8)


def forward(
    ids, ahead, above, own, below, cot, vectors, weight_in, kern, gates,
    weight_out, weight_up, weight_down, rows, cols, count_ha, count_ba, chunk=512,
):
    cells, dim = own.shape
    reach = above.shape[0]
    blocks = weight_in.shape[1] // LANES
    hidden = weight_up.shape[1]
    split = gates[0].shape[0]
    wide = blocks * LANES
    head_steps = blocks // 2
    ffn_steps = hidden // chunk

    up_wide, down_wide = hidden // count_ha, hidden // count_ba
    up_rows = dim // count_ba * lane_blocks(up_wide)
    down_rows = dim // count_ha * lane_blocks(down_wide)
    out_rows = dim // count_ha * lane_blocks(dim // count_ba)
    half = count_ha // 2
    assert up_rows == down_rows
    cut = plane_share(up_rows)
    rest = up_rows - cut
    plane = (count_ba, half, 2 * cut, LANES)
    line = (half, count_ba, 2 * rest + out_rows, LANES)
    packed_shape = (packed_rows(gates, dim, count_ba), LANES)
    half_packed = (packed_shape[0] // 2, LANES)
    cells_ext = cells + 2 * reach
    vmem = functools.partial(pltpu.VMEM, dtype=F32)
    operands = (
        ids, *ahead, above, own, below, cot, *vectors,
        weight_in, kern, *gates, weight_out, weight_up, weight_down,
    )
    out_shape = [
        shape_of(cells, dim),
        shape_of(cells, dim),
        shape_of(blocks, cells, LANES),
        shape_of(blocks, reach, LANES),
        shape_of(blocks, reach, LANES),
        shape_of(*plane),
        shape_of(*plane),
        shape_of(*line),
        shape_of(*line),
        shape_of(*half_packed),
        shape_of(*half_packed),
    ]
    return pl.pallas_call(
        functools.partial(forward_kernel, rows=rows, cols=cols, count_ha=count_ha, count_ba=count_ba),
        in_specs=[in_smem()] + [in_hbm()] * (len(operands) - 1),
        out_specs=[in_hbm()] * len(out_shape),
        out_shape=out_shape,
        scratch_shapes=[vmem((cells_ext, dim)), vmem((cells, dim))]
        + [vmem((1, dim))] * 4
        + [vmem((head_steps, dim, 2 * LANES)), vmem(kern.shape)]
        + [vmem(gate.shape) for gate in gates]
        + [
            vmem(weight_out.shape),
            vmem((ffn_steps, dim, chunk)),
            vmem((ffn_steps, chunk, dim)),
            vmem((blocks, cells, LANES)),
            pltpu.SemaphoreType.DMA((40 + head_steps,)),
            pltpu.SemaphoreType.DMA((ffn_steps, 2 + 2 * (count_ba + half + 2))),
        ]
        + [vmem((ffn_steps, chunk // (2 * up_wide), count_ba, up_rows, LANES))] * 2
        + [vmem((ffn_steps, half, chunk // down_wide, down_rows, LANES))] * 2
        + [vmem((half, count_ba, out_rows, LANES))] * 2
        + [
            pltpu.SMEM((rows, KERN + 2), jnp.int32),
            vmem((cells_ext, LANES)),
            vmem((cells, LANES)),
            vmem((cells, LANES)),
            vmem((KERN, cols // 8, 8, LANES)),
            vmem(packed_shape),
            vmem((max(cells, 2 * reach), dim)),
            vmem((blocks, cells_ext + 2 * EDGE, LANES)),
            vmem((KERN, rows + 2 * REACH, cols // 8, 8, LANES)),
            vmem((blocks, TAPS, LANES)),
            vmem((TAPS + KERN, 8, LANES)),
            vmem((blocks, cells, LANES)),
            vmem((cells, wide)),
            vmem((cells, wide - 2 * split)),
            vmem((cells, dim)),
            vmem((cells, dim)),
            vmem((cells, dim)),
        ],
        compiler_params=params(),
        cost_estimate=lasting(48),
    )(*operands)


def lay_flat(above_ref, own_ref, below_ref, flat):
    reach, cells = above_ref.shape[1], own_ref.shape[1]
    flat[:EDGE] = jnp.zeros((EDGE, LANES), F32)
    flat[EDGE : EDGE + reach] = above_ref[0]
    flat[EDGE + reach : EDGE + reach + cells] = own_ref[0]
    flat[EDGE + reach + cells : EDGE + 2 * reach + cells] = below_ref[0]
    flat[EDGE + 2 * reach + cells :] = jnp.zeros((EDGE, LANES), F32)


def backward_kernel(
    place_ref, ids_scalar, ids_ref, above_ref, own_ref, below_ref, mix_ref, kern_ref, canvas_ref, gain_ref,
    dmiddle_ref, in_ref, *rest, rows, cols,
):
    dcanvas_ref, kept_ref, sent_ref, small_kept_ref, small_sent_ref = rest[-19:-14]
    row_taps, padded, valid_ref, col_ref, flat, shifted, laid, wide, dk, sums, small, djoined, normed, dnorm = rest[-14:]
    step = pl.program_id(0)
    cells = rows * cols
    reach = REACH * cols
    core = place_ref[0] % 2
    split = laid.shape[0] * LANES - kern_ref.shape[1]
    width = in_ref.shape[1] // (2 * kept_ref.shape[1])

    @pl.when(step == 0)
    def _():
        lay_kernel(kern_ref, laid, split)
        turned = image_ids(ids_ref, padded, place_ref[0], rows)
        spread_cells((turned >= 0).astype(F32), valid_ref, 0, rows + 2 * REACH)
        conv_masks(ids_scalar, ids_ref, place_ref[0], row_taps, col_ref, rows)
        hat, _ = normalized(canvas_ref[...] * valid_ref[reach : reach + cells, :1])
        normed[...] = hat * gain_ref[...]
        dnorm[...] = jnp.zeros_like(dnorm)

    lay_flat(above_ref, own_ref, below_ref, flat)
    fill_shifted(flat, col_ref, shifted, rows + 2 * REACH, cols)
    conv_grad_block(
        row_taps, laid[step], shifted, wide, dk, mix_ref.at[0], djoined.at[step % 2], sums.at[step], rows, cols
    )

    @pl.when(step % 2 == 1)
    def _():
        grad = jnp.concatenate([djoined[0], djoined[1]], axis=1)
        share_columns(core, dot(normed[...], grad, TN), kept_ref, sent_ref, width, plane_first=True)
        dnorm[...] += dot(grad, in_ref[...], NT)

    @pl.when(step == pl.num_programs(0) - 1)
    def _():
        hat, scale = normalized(canvas_ref[...] * valid_ref[reach : reach + cells, :1])
        dgain = jnp.sum(dnorm[...] * hat, axis=0, keepdims=True)
        row = sums.shape[0] * TAPS
        for k in range(sums.shape[0]):
            small[k * TAPS : (k + 1) * TAPS, :] = sums[k, :TAPS]
        small[row:, :] = jnp.zeros((small.shape[0] - row, LANES), F32)
        for k in range(dgain.shape[1] // LANES):
            small[row + k : row + k + 1, :] = dgain[:, k * LANES : (k + 1) * LANES]
        half = small.shape[0] // 2
        for ref, start in ((small_kept_ref, core * half), (small_sent_ref, (1 - core) * half)):
            ref[...] = small[pl.ds(pl.multiple_of(start, 8), half), :]
        inner = dmiddle_ref[...] + norm_backward(dnorm[...] * gain_ref[...], hat, scale)
        dcanvas_ref[...] = inner * valid_ref[reach : reach + cells, :1]


def block_of(size):
    return pl.BlockSpec((1, size, LANES), lambda i: (i, 0, 0))


def small_rows(blocks, dim):
    return -(-(blocks * TAPS + dim // LANES) // 16) * 16


def backward(
    place, ids, above, own, below, mix, kern, canvas, gain, dmiddle, weight_in, ties, rows, cols, count_ha, count_ba
):
    cells, dim = canvas.shape
    blocks = own.shape[0]
    reach = above.shape[1]
    own_wide = weight_in.shape[1] // count_ha
    chunk_rows = dim // count_ba * lane_blocks(own_wide)
    groups = 2 * LANES // (2 * own_wide)
    chunk_spec = pl.BlockSpec((count_ba, groups, chunk_rows, LANES), lambda i: (0, i // 2, 0, 0))
    chunks = shape_of(count_ba, count_ha // 2, chunk_rows, LANES)
    tall = -(-TAPS // 8) * 8
    small = (small_rows(blocks, dim) // 2, LANES)
    return pl.pallas_call(
        functools.partial(backward_kernel, rows=rows, cols=cols),
        grid=(blocks,),
        in_specs=[in_smem(), in_smem(), whole(ids.shape)]
        + [block_of(size) for size in (reach, cells, reach, cells)]
        + [whole(kern.shape), whole(canvas.shape)]
        + [whole((1, dim)), whole((cells, dim))]
        + [pl.BlockSpec((dim, 2 * LANES), lambda i: (0, i // 2))]
        + [in_hbm()] * len(ties),
        out_specs=[whole((cells, dim)), chunk_spec, chunk_spec, whole(small), whole(small)],
        out_shape=[shape_of(cells, dim), chunks, chunks, shape_of(*small), shape_of(*small)],
        scratch_shapes=mask_scratch(ids, rows)
        + [
            pltpu.VMEM((KERN, cols // 8, 8, LANES), F32),
            pltpu.VMEM((cells + 2 * reach + 2 * EDGE, LANES), F32),
            pltpu.VMEM((KERN, rows + 2 * REACH, cols // 8, 8, LANES), F32),
            pltpu.VMEM((blocks, TAPS, LANES), F32),
            pltpu.VMEM((TAPS + KERN, 8, LANES), F32),
            pltpu.VMEM((TAPS, 8, LANES), F32),
            pltpu.VMEM((blocks, tall, LANES), F32),
            pltpu.VMEM((small_rows(blocks, dim), LANES), F32),
            pltpu.VMEM((2, cells, LANES), F32),
            pltpu.VMEM((cells, dim), F32),
            pltpu.VMEM((cells, dim), F32),
        ],
        compiler_params=params(),
        cost_estimate=lasting(25),
    )(place, ids, ids, above, own, below, mix, kern, canvas, gain, dmiddle, weight_in, *ties)


def exchange(values, axis, bit):
    return lax.ppermute(values, axis, [(i, i ^ bit) for i in range(lax.axis_size(axis))])


class View:
    def __init__(self, array, start, ways, fixed, rows):
        self.array, self.start, self.ways, self.fixed, self.rows = array, start, ways, fixed, rows

    def fix(self, way, step):
        if way == "line":
            near = lax.axis_size("ha") // 4
            return self.fix("far", step // near).fix("near", step % near)
        left = [entry for entry in self.ways if entry[0] != way]
        (stride,) = [entry[2] for entry in self.ways if entry[0] == way]
        return View(self.array, self.start, left, self.fixed + [(way, step, stride)], self.rows)

    def size(self):
        count = self.rows
        for _, size, _ in self.ways:
            count *= size
        return count

    def runs(self, ha, ba):
        start = self.start
        near = lax.axis_size("ha") // 4
        places = {"plane": ba, "far": ha // 2 // near, "near": ha // 2 % near}
        for way, step, stride in self.fixed:
            start = start + (places[way] ^ step) * stride
        rows, ways = self.rows, list(self.ways)
        while ways and ways[-1][2] == rows:
            rows *= ways.pop()[1]
        offsets = [0]
        for _, size, stride in ways:
            offsets = [offset + k * stride for offset in offsets for k in range(size)]
        return [pl.multiple_of(start + offset, 8) for offset in offsets], rows


def flat_view(array, start=0, rows=None):
    flat = array.reshape(-1, LANES)
    return View(flat, start, [], [], flat.shape[0] if rows is None else rows)


def combine(place, groups, ties=(), epilogue=None, out_shape=None):
    pieces, arrays = [], []
    for group in groups:
        for views in group:
            if not any(views is other for other in pieces):
                pieces.append(views)
    for views in pieces:
        for view in views:
            if not any(view.array is other for other in arrays):
                arrays.append(view.array)
    index_of = {id(array): k for k, array in enumerate(arrays)}
    piece_of = {id(views): k for k, views in enumerate(pieces)}
    sizes = [sum(views[0].size() for views in group) for group in groups]
    copies = sum(len(view.runs(0, 0)[0]) for views in pieces for view in views)
    plain = epilogue is None
    if plain:
        out_shape = [shape_of(size, LANES) for size in sizes]

    def kernel(place_ref, *refs):
        inputs = refs[: len(arrays)]
        refs = refs[len(arrays) + len(ties) :]
        outs, refs = refs[: len(out_shape)], refs[len(out_shape) :]
        buffers, refs = refs[: len(pieces)], refs[len(pieces) :]
        sems, results, out_sems = refs[0], refs[1:-1], refs[-1]
        ha, ba = place_ref[0], place_ref[1]
        moves, count = [], 0
        for piece, views in enumerate(pieces):
            moves.append([])
            for term, view in enumerate(views):
                source = inputs[index_of[id(view.array)]]
                starts, rows = view.runs(ha, ba)
                for k, start in enumerate(starts):
                    target = buffers[piece].at[term, pl.ds(k * rows, rows), :]
                    move = pltpu.make_async_copy(source.at[pl.ds(start, rows), :], target, sems.at[count])
                    move.start()
                    moves[-1].append(move)
                    count += 1
        values, waited, leaving = [], set(), []
        for out, group in enumerate(groups):
            row = 0
            for views in group:
                piece = piece_of[id(views)]
                if piece not in waited:
                    waited.add(piece)
                    for move in moves[piece]:
                        move.wait()
                value = buffers[piece][0]
                for term in range(1, len(views)):
                    value = value + buffers[piece][term]
                if plain:
                    results[out][row : row + value.shape[0], :] = value
                values.append(value)
                row += value.shape[0]
            if plain:
                leaving.append(pltpu.make_async_copy(results[out], outs[out], out_sems.at[out]))
                leaving[-1].start()
        if not plain:
            epilogue(ha, ba, values, outs)
        for move in leaving:
            move.wait()

    moved = sum(view.size() for views in pieces for view in views) + sum(sizes)
    scratch = [pltpu.VMEM((len(views), views[0].size(), LANES), F32) for views in pieces]
    scratch.append(pltpu.SemaphoreType.DMA((copies,)))
    if plain:
        scratch += [pltpu.VMEM((size, LANES), F32) for size in sizes]
    scratch.append(pltpu.SemaphoreType.DMA((len(groups),)))
    return pl.pallas_call(
        kernel,
        in_specs=[in_smem()] + [in_hbm()] * (len(arrays) + len(ties)),
        out_specs=[in_hbm() if plain else pl.BlockSpec(memory_space=pltpu.VMEM)] * len(out_shape),
        out_shape=out_shape,
        scratch_shapes=scratch,
        compiler_params=params(),
        cost_estimate=lasting(1 + moved * LANES * 4 / 3.0e6),
    )(place, *arrays, *ties)


def tied(arrays, ties):
    return pl.pallas_call(
        lambda *refs: None,
        in_specs=[pl.BlockSpec(memory_space=pl.ANY)] * (len(arrays) + len(ties)),
        out_specs=[pl.BlockSpec(memory_space=pl.ANY)] * len(arrays),
        out_shape=[shape_of(*array.shape) for array in arrays],
        input_output_aliases={k: k for k in range(len(arrays))},
        compiler_params=params(),
        cost_estimate=lasting(0.5),
    )(*arrays, *ties)


class Sum:
    def __init__(self, arrays, names):
        self.views = []
        near = lax.axis_size("ha") // 4
        sizes = {"plane": lax.axis_size("ba"), "far": 2, "near": near}
        for array in arrays:
            flat = array.reshape(-1, LANES)
            stride, ways = flat.shape[0], []
            for name in names:
                stride //= sizes[name]
                ways.append((name, sizes[name], stride))
            self.views.append(View(flat, 0, ways, [], stride))

    def leaving(self, way, step):
        return [view.fix(way, step) for view in self.views]

    def keep(self, way, sent, arrived):
        self.views = [view.fix(way, 0) for view in self.views]
        rows = self.views[0].rows
        stride, ways = rows, []
        for name, size, _ in reversed(self.views[0].ways):
            ways.insert(0, (name, size, stride))
            stride *= size
        self.views += [View(array, start, ways, [], rows) for array, start in arrived]

    def part(self, first, rows):
        return [View(view.array, view.start + first, view.ways, view.fixed, rows) for view in self.views]


class Rider:
    def __init__(self, views):
        self.views = views

    def leaving(self, way, step):
        return self.views

    def keep(self, way, sent, arrived):
        rows = self.views[0].size()
        self.views = [View(array, start, [], [], rows) for array, start in [sent] + arrived]


class Gather(Rider):
    def keep(self, way, sent, arrived):
        rows = self.views[0].size()
        self.gathered = [[View(array, start, [], [], rows)] for array, start in [sent] + arrived]


class Stage:
    def __init__(self, members, way):
        self.members, self.way = members, way
        line, near = lax.axis_size("ha") // 2, lax.axis_size("ha") // 4
        self.steps = {
            "plane": list(range(1, lax.axis_size("ba"))),
            "line": list(range(1, line)),
            "far": [near],
        }[way]
        self.near = near

    def taking(self, step):
        takes = {"plane": True, "line": True, "near": step < self.near, "far": step == self.near}
        return [(one, way) for one, way in self.members if takes[way]]

    def groups(self):
        return [
            [one.leaving(way, step // self.near if way == "far" else step) for one, way in self.taking(step)]
            for step in self.steps
        ]

    def go(self, payloads, in_turn=None):
        axis, unit = ("ba", 1) if self.way == "plane" else ("ha", 2)
        arrived = []
        for step, part in zip(self.steps, payloads):
            if in_turn is not None and len(arrived) == 2:
                (part,) = tied([part], [arrived[in_turn]])
            arrived.append(exchange(part, axis, unit * step))
        places = {}
        for step, sent, part in zip(self.steps, payloads, arrived):
            row = 0
            for one, way in self.taking(step):
                places.setdefault(id(one), []).append(((sent, row), (part, row)))
                row += one.leaving(way, 1)[0].size()
        for one, way in self.members:
            mine = places.get(id(one), [])
            one.keep(way, mine[:2][-1][0] if mine else None, [part for _, part in mine])
        return arrived


def run(place, stage, ties=(), in_turn=None, extra=()):
    groups = stage.groups()
    made = list(combine(place, groups + list(extra), ties))
    made, more = made[: len(groups)], made[len(groups) :]
    return made, stage.go(made, in_turn), more


def neighbour_rows(top, bottom):
    count = lax.axis_size("ha")
    up = [(i, i + 1) for i in range(count - 1)]
    down = [(i + 1, i) for i in range(count - 1)]
    return lax.ppermute(bottom, "ha", up), lax.ppermute(top, "ha", down)


def lay_beside(value, ref):
    tall, width = ref.shape
    for k in range(lane_blocks(width)):
        columns = slice(k * LANES, min(width, (k + 1) * LANES))
        ref[:, columns] = value[k * tall : (k + 1) * tall, : columns.stop - columns.start]


def lay_large(ha, ba, values, outs):
    up_first, up_second, down_first, down_second, out = values
    lay_beside(jnp.concatenate([up_first, up_second], axis=0), outs[0])
    lay_beside(jnp.concatenate([down_first, down_second], axis=0), outs[1])
    lay_beside(out, outs[2])


def lay_small(ha, ba, values, outs, blocks):
    din_ref, dk_ref, gain_ref = outs[:3]
    scratch = outs[-1]
    lay_beside(values[0], din_ref)
    count = lax.axis_size("ba")
    own, other = values[1 : 2 + count], values[2 + count :]
    mine = ha % 2 == 0
    dkern = jnp.concatenate([jnp.where(mine, own[0], other[0]), jnp.where(mine, other[0], own[0])], axis=0)
    joined = jnp.concatenate([dkern[k * TAPS : (k + 1) * TAPS] for k in range(blocks)], axis=1)
    dk_ref[...] = joined[:, joined.shape[1] - dk_ref.shape[1] :]
    part = own[1].shape[0]
    for side, parts in ((ha % 2, own[1:]), (1 - ha % 2, other[1:])):
        for step, rows in enumerate(parts):
            start = (side * count + (ba ^ step)) * part
            scratch[pl.ds(pl.multiple_of(start, 8), part), :] = rows
    dim = gain_ref.shape[1]
    for k in range(dim // LANES):
        columns = slice(k * LANES, (k + 1) * LANES)
        row = blocks * TAPS + k
        gain_ref[:, columns] = dkern[row : row + 1]
        for vector, ref in enumerate(outs[3:6]):
            ref[:, columns] = scratch[vector * dim // LANES + k : vector * dim // LANES + k + 1, :]
    row = scratch.shape[0]
    for ref in reversed(outs[6:-1]):
        tall, width = ref.shape
        row -= tall * width // LANES
        for k in range(width // LANES):
            ref[:, k * LANES : (k + 1) * LANES] = scratch[row + k * tall : row + (k + 1) * tall, :]


def shards(
    canvas,
    image_id,
    keep_first,
    keep_second,
    first_gain,
    weight_in,
    depth_kernel,
    gate_first,
    gate_second,
    gate_third,
    weight_out,
    scale_first,
    second_gain,
    weight_up,
    weight_down,
    scale_second,
    cotangent,
):
    _, rows, cols, dim = canvas.shape
    cells = rows * cols
    reach = REACH * cols
    count_ha, count_ba = lax.axis_size("ha"), lax.axis_size("ba")
    hidden = weight_up.shape[1]
    blocks = weight_in.shape[1] // LANES
    place = jnp.stack([lax.axis_index("ha"), lax.axis_index("ba")])
    own = canvas.reshape(cells, dim)
    gates = (gate_first, gate_second, gate_third)
    gain = first_gain[None]
    vectors = (gain, scale_first[None], second_gain[None], scale_second[None])
    ids = image_id[0]
    above, below = neighbour_rows(own[:reach], own[cells - reach :])
    ahead = head(ids, keep_first, keep_second, own, gain, weight_in, rows, cols)
    joined = ahead[0]
    (
        output, dmiddle, dconv, dconv_top, dconv_bottom, plane_kept, plane_sent, line_kept, line_sent,
        packed_kept, packed_sent,
    ) = forward(
        ids, ahead, above, own, below, cotangent.reshape(cells, dim), vectors,
        weight_in, depth_kernel, gates, weight_out, weight_up, weight_down, rows, cols, count_ha, count_ba,
    )
    above, below = neighbour_rows(dconv_top, dconv_bottom)

    plane_sum = Sum([plane_kept, exchange(plane_sent, "ha", 1)], ["plane", "far", "near"])
    line_sum = Sum([line_kept, exchange(line_sent, "ha", 1)], ["far", "near", "plane"])
    packed = Sum([packed_kept, exchange(packed_sent, "ha", 1)], ["plane"])
    made, arrived, _ = run(place, Stage([(plane_sum, "plane"), (packed, "plane")], "plane"))
    apart = Stage([(line_sum, "far")], "far")
    more = list(tied(combine(place, apart.groups(), made), [above, below]))
    made, arrived = made + more, arrived + apart.go(more)
    dcanvas, in_kept, in_sent, small_kept, small_sent = backward(
        place, ids, above, dconv, below, joined, depth_kernel, own, gain, dmiddle, weight_in, made,
        rows, cols, count_ha, count_ba,
    )
    in_sent, small_sent = tied([in_sent, small_sent], arrived)
    in_sum = Sum([in_kept, exchange(in_sent, "ha", 1)], ["plane", "far", "near"])
    small = Rider([flat_view(small_kept), flat_view(exchange(small_sent, "ha", 1))])
    packed = Rider(packed.views)
    packed = Rider(packed.views)
    made, arrived, _ = run(
        place, Stage([(plane_sum, "far"), (line_sum, "near"), (packed, "line")], "line"), in_turn=0
    )
    run(place, Stage([(in_sum, "plane"), (small, "plane")], "plane"), ties=made)
    along = Stage([(plane_sum, "near"), (in_sum, "line"), (small, "line")], "line")
    made, arrived, (own_small,) = run(place, along, ties=arrived[:2], in_turn=1, extra=[[small.views]])
    packed = Gather(packed.views)
    across = Stage([(line_sum, "plane"), (packed, "plane")], "plane")
    _, crossed, (own_packed,) = run(place, across, ties=made, extra=[[packed.views]])
    cut = plane_sum.views[0].rows // 2
    rest = (line_sum.views[0].rows - dim // count_ha * lane_blocks(dim // count_ba)) // 2
    dup, ddown, dout = combine(
        place,
        [
            [
                plane_sum.part(0, cut),
                line_sum.part(0, rest),
                plane_sum.part(cut, cut),
                line_sum.part(rest, rest),
                line_sum.part(2 * rest, line_sum.views[0].rows - 2 * rest),
            ]
        ],
        epilogue=lay_large,
        out_shape=[
            shape_of(dim // count_ba, hidden // count_ha),
            shape_of(dim // count_ha, hidden // count_ba),
            shape_of(dim // count_ha, dim // count_ba),
        ],
    )
    sent = list(tied([own_small, own_packed], arrived[1:2]))
    others = [exchange(part, "ha", 1) for part in sent + arrived + crossed]
    other_of = {id(part): other for part, other in zip(arrived + crossed, others[2:])}

    def from_other(view):
        return View(other_of[id(view.array)], view.start, view.ways, view.fixed, view.rows)

    own_parts = [small.views] + packed.gathered
    other_parts = [[flat_view(others[0])] + [from_other(view) for view in small.views[1:]], [flat_view(others[1])]]
    other_parts += [[from_other(view) for view in views] for views in packed.gathered[1:]]
    din, dkern, dgain_one, dscale_one, dgain_two, dscale_two, dfirst, dsecond, dthird, _ = combine(
        place,
        [[in_sum.views] + own_parts + other_parts],
        ties=[dup],
        epilogue=functools.partial(lay_small, blocks=blocks),
        out_shape=[shape_of(dim // count_ba, weight_in.shape[1] // count_ha), shape_of(*depth_kernel.shape)]
        + [shape_of(1, dim)] * 4
        + [shape_of(*gate.shape) for gate in gates]
        + [shape_of(packed_rows(gates, dim, count_ba), LANES)],
    )
    return (
        output.reshape(canvas.shape),
        dcanvas.reshape(canvas.shape),
        dgain_one[0],
        din,
        dkern,
        dfirst,
        dsecond,
        dthird,
        dout.T,
        dscale_one[0],
        dgain_two[0],
        dup,
        ddown.T,
        dscale_two[0],
    )


def solution(mesh):
    in_specs = (
        P("ba", "ha", None, None),
        P("ba", None, None),
        P("ba", None),
        P("ba", None),
    ) + (P(),) * 12 + (P("ba", "ha", None, None),)
    tiled = P("ba", "ha")
    out_specs = (
        P("ba", "ha", None, None),
        P("ba", "ha", None, None),
        P(),
        tiled,
        P(),
        P(),
        P(),
        P(),
        tiled,
        P(),
        P(),
        tiled,
        tiled,
        P(),
    )
    return jax.shard_map(shards, mesh=mesh, in_specs=in_specs, out_specs=out_specs, check_vma=False)
```
